32 devices in a mesh: dp: 8 (over y, x, core), seq: 4 (over z).
Axes of the slice: x: 2, y: 2, z: 4, core: 2. Of those that a mesh axis runs over, the one named last changes fastest.
Arguments:
- tokens: bfloat16 [16, 2048, 768], P('dp', 'seq'), may hold values from -6 to 6
- timesteps: int32 [16], P('dp'), may hold values from 0 to 2047, as said below
- time_table: bfloat16 [2048, 768], replicated, may hold values from -3 to 3
- ln1_gain: bfloat16 [768], replicated, may hold values from 0.5 to 1.5
- ln1_bias: bfloat16 [768], replicated, may hold values from -1.25 to 1.25
- qkv_weight: bfloat16 [768, 2304], replicated, may hold values from -0.21875 to 0.21875
- q_bias: bfloat16 [768], replicated, may hold values from -1.25 to 1.25
- v_bias: bfloat16 [768], replicated, may hold values from -1.25 to 1.25
- out_weight: bfloat16 [768, 768], replicated, may hold values from -1.75 to 1.75
- out_bias: bfloat16 [768], replicated, may hold values from -1.25 to 1.25
- ln2_gain: bfloat16 [768], replicated, may hold values from 0.5 to 1.5
- ln2_bias: bfloat16 [768], replicated, may hold values from -1.25 to 1.25
- up_weight: bfloat16 [768, 3072], replicated, may hold values from -0.21875 to 0.21875
- up_bias: bfloat16 [3072], replicated, may hold values from -1.25 to 1.25
- down_weight: bfloat16 [3072, 768], replicated, may hold values from -0.109375 to 0.109375
- down_bias: bfloat16 [768], replicated, may hold values from -1.25 to 1.25
- cotangent: bfloat16 [16, 2048, 768], P('dp', 'seq'), may hold values from -6 to 6
Outputs:
- layer_out: bfloat16 [16, 2048, 768], P('dp', 'seq')
- tokens_grad: float32 [16, 2048, 768], P('dp', 'seq')
- time_table_grad: float32 [2048, 768], P('dp')
- ln1_gain_grad: float32 [768], P('dp')
- ln1_bias_grad: float32 [768], P('dp')
- qkv_weight_grad: float32 [768, 2304], P('dp')
- q_bias_grad: float32 [768], P('dp')
- v_bias_grad: float32 [768], P('dp')
- out_weight_grad: float32 [768, 768], P('dp')
- out_bias_grad: float32 [768], P('dp')
- ln2_gain_grad: float32 [768], P('dp')
- ln2_bias_grad: float32 [768], P('dp')
- up_weight_grad: float32 [768, 3072], P('dp')
- up_bias_grad: float32 [3072], P('dp')
- down_weight_grad: float32 [3072, 768], P('dp')
- down_bias_grad: float32 [768], P('dp')
- bucket_energy: float32 [4], replicated
- bucket_counts: float32 [4], replicated
The draws below stay inside these ranges and needn't reach their ends.
Inputs may be any that keep to these rules, and one draw needn't show every extreme that they name: `timesteps`: one diffusion timestep per sequence; some sequence has timestep 0 and some has 2047.
All inputs are finite; a program needn't handle non-finite values.
Results may differ from the reference program's by a relative error of at most 0.015.
Values may be sent and summed in bfloat16 or wider, within the bound.
A program may use at most 192 MiB of HBM per device.

```python
import math
import jax
import jax.numpy as jnp
from jax import lax

D = 768
HEAD_DIM = 64
FF = 3072
TSTEPS = 2048
BUCKETS = 4
LENGTH = 2048
SEQS = 16


def draw_timesteps(key, part):
    key = jax.random.fold_in(key, 7)
    first_key, second_key, third_key, fourth_key, place_key = jax.random.split(key, 5)
    first_draw = jax.random.randint(first_key, (SEQS,), 0, 1024)
    second_draw = jax.random.randint(second_key, (SEQS,), 0, 1024)
    anywhere = first_draw * second_draw // (1048576 // TSTEPS)
    span = TSTEPS // BUCKETS
    third_draw = jax.random.randint(third_key, (SEQS,), 0, 1024)
    fourth_draw = jax.random.randint(fourth_key, (SEQS,), 0, 1024)
    offset = third_draw * fourth_draw // (1048576 // span)
    order = jax.random.permutation(place_key, SEQS)
    ranks = jnp.zeros((SEQS,), jnp.int32).at[order].set(jnp.arange(SEQS, dtype=jnp.int32))
    spread_out = ranks % BUCKETS * span + offset
    drawn = jnp.where(ranks < SEQS // 2, spread_out, anywhere)
    drawn = drawn.at[order[0]].set(0)
    drawn = drawn.at[order[BUCKETS - 1]].set(TSTEPS - 1)
    return drawn.astype(jnp.int32)


def block_scale(stream_key, shape, pieces, least, top_value):
    gain = 1.0
    for position, shards_of in pieces:
        steps = jax.random.uniform(jax.random.fold_in(jax.random.fold_in(stream_key, 6), position), (shards_of,), jnp.float32, least / len(pieces), top_value / len(pieces))
        gain = gain * jnp.repeat(jnp.exp(steps), shape[position] // shards_of).reshape((-1,) + (1,) * (len(shape) - 1 - position))
    return gain


def noise(stream_key, extent, scale, reach, cuts=(), kind=jnp.bfloat16):
    values = scale * jax.random.normal(stream_key, extent, jnp.float32)
    if cuts:
        values = values * block_scale(stream_key, extent, cuts, -0.22, 0.18)
    return jnp.clip(values, -reach, reach).astype(kind)


def setup_inputs(seed: int = 0) -> dict:
    key_of = jax.random.split(jax.random.key(seed), 18)
    return {
        "tokens": noise(key_of[0], (SEQS, LENGTH, D), 1.0, 6.0, ((0, 8), (1, 4))),
        "timesteps": draw_timesteps(jax.random.fold_in(key_of[17], 71), 0),
        "time_table": noise(key_of[2], (TSTEPS, D), 0.5, 3.0),
        "ln1_gain": jnp.clip(1.0 + 0.1 * jax.random.normal(key_of[3], (D,), jnp.float32), 0.5, 1.5).astype(jnp.bfloat16),
        "ln1_bias": noise(key_of[4], (D,), 0.2, 1.25),
        "qkv_weight": noise(key_of[5], (D, 3 * D), D ** -0.5, 0.21875),
        "q_bias": noise(key_of[6], (D,), 0.2, 1.25),
        "v_bias": noise(key_of[7], (D,), 0.2, 1.25),
        "out_weight": noise(key_of[8], (D, D), (D // 64) ** -0.5, 1.75),
        "out_bias": noise(key_of[9], (D,), 0.2, 1.25),
        "ln2_gain": jnp.clip(1.0 + 0.1 * jax.random.normal(key_of[10], (D,), jnp.float32), 0.5, 1.5).astype(jnp.bfloat16),
        "ln2_bias": noise(key_of[11], (D,), 0.2, 1.25),
        "up_weight": noise(key_of[12], (D, FF), D ** -0.5, 0.21875),
        "up_bias": noise(key_of[13], (FF,), 0.2, 1.25),
        "down_weight": noise(key_of[14], (FF, D), FF ** -0.5, 0.109375),
        "down_bias": noise(key_of[15], (D,), 0.2, 1.25),
        "cotangent": noise(key_of[16], (SEQS, LENGTH, D), 1.0, 6.0, ((0, 8), (1, 4))),
    }


norm_eps = 1e-05
top_precision = lax.Precision.HIGHEST

@jax.custom_vjp
def low(v):
    return lax.optimization_barrier(v.astype(jnp.bfloat16)).astype(jnp.float32)

@jax.custom_vjp
def low_back(v):
    return v

def low_keep(v):
    return (low(v), None)

def low_pass(kept, grad):
    return (grad,)

def back_keep(v):
    return (v, None)

def back_low(kept, grad):
    return (low(grad),)
low.defvjp(low_keep, low_pass)
low_back.defvjp(back_keep, back_low)

def layer_norm(inputs, norm_gain, norm_shift):
    centered = inputs - lax.optimization_barrier(jnp.mean(inputs, -1, keepdims=True))
    variance = lax.optimization_barrier(jnp.mean(centered * centered, -1, keepdims=True))
    return centered * lax.rsqrt(variance + norm_eps) * norm_gain + norm_shift

def attend(triple):
    queries, keys_all, values_all = triple
    scores = jnp.einsum('qhd,khd->hqk', queries, keys_all, precision=top_precision) * HEAD_DIM ** (-0.5)
    scores = low_back(scores)
    row_max = lax.optimization_barrier(jnp.max(scores, -1, keepdims=True))
    shifted = jnp.exp(scores - row_max)
    weights = low(shifted / lax.optimization_barrier(jnp.sum(shifted, -1, keepdims=True)))
    return jnp.einsum('hqk,khd->qhd', weights, values_all, precision=top_precision)

def forward(times_in, tokens_in, time_table, ln1_gain, ln1_bias, qkv_weight, q_bias, v_bias, out_weight, out_bias, ln2_gain, ln2_bias, up_weight, up_bias, down_weight, down_bias):
    group_seqs, length, model_width = tokens_in.shape
    head_count = model_width // HEAD_DIM
    start_sum = tokens_in + jnp.take(time_table, times_in, axis=0)[:, None, :]
    normed = low(layer_norm(start_sum, ln1_gain, ln1_bias))
    bias_all = jnp.concatenate([q_bias, jnp.zeros_like(q_bias), v_bias])
    projected = jnp.einsum('gld,dk->glk', normed, qkv_weight, precision=top_precision) + bias_all
    projected = low(low_back(projected)).reshape(group_seqs, length, 3, head_count, HEAD_DIM)
    context = lax.map(jax.checkpoint(attend), (projected[:, :, 0], projected[:, :, 1], projected[:, :, 2]))
    context = low(low_back(context.reshape(group_seqs, length, model_width)))
    attn_out = low_back(jnp.einsum('gld,de->gle', context, out_weight, precision=top_precision) + out_bias)
    middle = start_sum + attn_out
    normed_two = low(layer_norm(middle, ln2_gain, ln2_bias))
    hidden = low_back(jnp.einsum('gld,df->glf', normed_two, up_weight, precision=top_precision) + up_bias)
    active = low(jax.nn.gelu(hidden, approximate=False))
    branch = low_back(jnp.einsum('glf,fe->gle', active, down_weight, precision=top_precision) + down_bias)
    return middle + branch

def reference(tokens, timesteps, time_table, ln1_gain, ln1_bias, qkv_weight, q_bias, v_bias, out_weight, out_bias, ln2_gain, ln2_bias, up_weight, up_bias, down_weight, down_bias, cotangent):
    params = tuple((weight_arg.astype(jnp.float32) for weight_arg in (time_table, ln1_gain, ln1_bias, qkv_weight, q_bias, v_bias, out_weight, out_bias, ln2_gain, ln2_bias, up_weight, up_bias, down_weight, down_bias)))
    group_seqs = math.gcd(SEQS, max(1, 4096 // LENGTH))
    group_count = SEQS // group_seqs
    tokens_all = tokens.astype(jnp.float32).reshape(group_count, group_seqs, LENGTH, D)
    times_all = timesteps.reshape(group_count, group_seqs)
    cot_all = cotangent.astype(jnp.float32).reshape(group_count, group_seqs, LENGTH, D)

    def one_group(totals, slices):
        tokens_in, times_in, grad_in = slices

        def apply_layer(tokens_arg, *weight_args):
            return forward(times_in, tokens_arg, *weight_args)
        result, pullback = jax.vjp(apply_layer, tokens_in, *params)
        grads_all = pullback(grad_in)
        totals = tuple((summed + update for summed, update in zip(totals, grads_all[1:])))
        energy = lax.optimization_barrier(jnp.sum(lax.optimization_barrier(jnp.mean(result * result, -1)), -1))
        return (totals, (result.astype(jnp.bfloat16), grads_all[0], energy))
    start_totals = tuple((jnp.zeros_like(weight_arg) for weight_arg in params))
    totals, (outputs, input_grads, energies) = lax.scan(one_group, start_totals, (tokens_all, times_all, cot_all))
    table_grad, gain_one_grad, shift_one_grad, qkv_weight_grad, q_bias_grad, v_bias_grad, out_weight_grad, out_bias_grad, gain_two_grad, shift_two_grad, up_weight_grad, up_bias_grad, down_weight_grad, down_bias_grad = totals
    buckets = timesteps * BUCKETS // TSTEPS
    member = (buckets[:, None] == jnp.arange(BUCKETS)[None, :]).astype(jnp.float32)
    energies = energies.reshape(SEQS)
    bucket_energy = lax.optimization_barrier(jnp.sum(member * energies[:, None], 0)) / (SEQS * LENGTH)
    bucket_counts = lax.optimization_barrier(jnp.sum(member, 0)) * LENGTH / (SEQS * LENGTH)
    return (outputs.reshape(SEQS, LENGTH, D), input_grads.reshape(SEQS, LENGTH, D), table_grad, gain_one_grad, shift_one_grad, qkv_weight_grad, q_bias_grad, v_bias_grad, out_weight_grad, out_bias_grad, gain_two_grad, shift_two_grad, up_weight_grad, up_bias_grad, down_weight_grad, down_bias_grad, bucket_energy, bucket_counts)
```

```python
import functools

import jax
import jax.numpy as jnp
from jax import lax
from jax.experimental import pallas as pl
from jax.experimental.pallas import tpu as pltpu
from jax.sharding import PartitionSpec as P

HEAD_DIM = 64
TSTEPS = 2048
BUCKETS = 4
EPS = 1e-05
LANES = 128
VMEM_BYTES = 56 * 1024 * 1024
BOTH = ("dp", "seq")
F32 = jnp.float32
BF16 = jnp.bfloat16
NN = (((1,), (0,)), ((), ()))
NT = (((1,), (1,)), ((), ()))
TN = (((0,), (0,)), ((), ()))


def dot(a, b, dims):
    return lax.dot_general(a, b, dims, preferred_element_type=F32)


def wide(ref):
    return ref[...].astype(F32)


def column_sum(v):
    return jnp.sum(v, 0, keepdims=True)


def fixed(shape):
    return pl.BlockSpec(shape, lambda *i: (0,) * len(shape), pipeline_mode=pl.Buffered(1))


def rows(block, width):
    return pl.BlockSpec((block, width), lambda i: (i, 0))


def shape_of(shape, dtype=BF16):
    return jax.ShapeDtypeStruct(shape, dtype)


def cost(us):
    return pl.CostEstimate(flops=int(us * 1.15e9), bytes_accessed=0, transcendentals=0)


def params():
    return pltpu.CompilerParams(vmem_limit_bytes=VMEM_BYTES)


def norm_parts(v):
    centered = v - jnp.mean(v, -1, keepdims=True)
    scale = lax.rsqrt(jnp.mean(centered * centered, -1, keepdims=True) + EPS)
    return centered * scale, scale


def norm_backward(grad, gain, unit, scale):
    scaled = grad * gain
    return scale * (
        scaled
        - jnp.mean(scaled, -1, keepdims=True)
        - unit * jnp.mean(scaled * unit, -1, keepdims=True)
    )


def project_kernel(x_ref, time_ref, gain_ref, shift_ref, weight_ref, bias_ref, *refs):
    normed_ref, query_ref, kv_ref = refs[-3:]
    width = x_ref.shape[1]
    unit, _ = norm_parts(wide(x_ref) + wide(time_ref))
    normed = (unit * wide(gain_ref) + wide(shift_ref)).astype(BF16)
    normed_ref[...] = normed
    for part in range(3):
        columns = slice(part * width, (part + 1) * width)
        made = (dot(normed, weight_ref[:, columns], NN) + bias_ref[:, columns]).astype(BF16)
        if part == 0:
            query_ref[...] = made * jnp.asarray(HEAD_DIM ** (-0.5), BF16)
        else:
            kv_ref[:, (part - 1) * width : part * width] = made


def project(x, time_row, gain, shift, weight, bias, total, begun=None, block=256):
    count, width = x.shape
    first = 0 if begun is None else total // block - count // block
    later = pl.BlockSpec((block, width), lambda i: (i + first, 0))
    extra = [] if begun is None else list(begun)
    return pl.pallas_call(
        project_kernel,
        grid=(count // block,),
        in_specs=[
            rows(block, width),
            fixed((1, width)),
            fixed((1, width)),
            fixed((1, width)),
            fixed(weight.shape),
            fixed(bias.shape),
        ]
        + [pl.BlockSpec(memory_space=pl.ANY)] * len(extra),
        out_specs=[later, later, rows(block, 2 * width)],
        out_shape=[
            shape_of((total, width)),
            shape_of((total, width)),
            shape_of((count, 2 * width)),
        ],
        input_output_aliases={6: 0, 7: 1} if extra else {},
        compiler_params=params(),
        cost_estimate=cost(5),
        name="project",
    )(x, time_row, gain, shift, weight, bias, *extra)


def lane_parts():
    lane = lax.broadcasted_iota(jnp.int32, (1, LANES), 1)
    return lane < HEAD_DIM, lane % HEAD_DIM


def with_offset(own, place, base, offset):
    high = offset.astype(BF16)
    left = offset - high.astype(F32)
    mid = left.astype(BF16)
    low = (left - mid.astype(F32)).astype(BF16)
    zero = jnp.zeros_like(low)
    parts = jnp.where(place == 0, high, jnp.where(place == 1, mid, jnp.where(place == 2, low, zero)))
    return jnp.where(own, base, parts)


def attend_kernel(query_ref, *refs, pieces):
    key_refs, value_refs = refs[:pieces], refs[pieces : 2 * pieces]
    context_ref, logsum_ref = refs[2 * pieces :]
    count = query_ref.shape[0]
    low, place = lane_parts()
    row_half = lax.broadcasted_iota(jnp.int32, (LANES, LANES), 0) // HEAD_DIM
    lane_half = lax.broadcasted_iota(jnp.int32, (LANES, LANES), 1) // HEAD_DIM
    swapped = jnp.where(row_half != lane_half, 1.0, 0.0).astype(BF16)
    query = query_ref[...]

    def norms(v):
        v = v.astype(F32)
        return dot((v * v).astype(BF16), swapped, NN)

    key_norm = functools.reduce(
        jnp.maximum, [jnp.max(norms(ref[...]), 0, keepdims=True) for ref in key_refs]
    )
    bound = jnp.sqrt(norms(query) * key_norm) * 1.01
    ones_key = jnp.where(place < 3, 1.0, 0.0).astype(BF16)
    values = [ref[...].T for ref in value_refs]
    ones = jnp.ones((16, value_refs[0].shape[0]), BF16)

    def value_of(piece, head):
        return jnp.concatenate([values[piece][head * HEAD_DIM : (head + 1) * HEAD_DIM], ones], 0)

    def finish(mixed, offset):
        totals = [m[HEAD_DIM : HEAD_DIM + 1] for m in mixed]
        context = jnp.concatenate([m[:HEAD_DIM] / t for m, t in zip(mixed, totals)], 0)
        context_ref[...] = context.T.astype(BF16)
        logs = [jnp.broadcast_to(jnp.log(t), (HEAD_DIM, count)) for t in reversed(totals)]
        logsum_ref[...] = jnp.concatenate(logs, 0).T + offset

    mixed = []
    for head in range(2):
        own = low if head == 0 else ~low
        query_own = with_offset(own, place, query, -bound)
        out = 0.0
        for piece in range(pieces):
            key_own = jnp.where(own, key_refs[piece][...], ones_key)
            weights = jnp.exp(dot(key_own, query_own, NT)).astype(BF16)
            out = out + dot(value_of(piece, head), weights, NN)
        mixed.append(out)
    finish(mixed, bound)
    smallest = jnp.min(jnp.minimum(mixed[0][HEAD_DIM], mixed[1][HEAD_DIM]))

    @pl.when(smallest < 1e-25)
    def _():
        again, tops = [], []
        for head in range(2):
            own = low if head == 0 else ~low
            query_own = jnp.where(own, query, jnp.zeros_like(query))
            top = jnp.full((1, count), -jnp.inf, F32)
            for piece in range(pieces):
                scores = dot(key_refs[piece][...], query_own, NT)
                top = jnp.maximum(top, jnp.max(scores, 0, keepdims=True))
            out = 0.0
            for piece in range(pieces):
                scores = dot(key_refs[piece][...], query_own, NT)
                out = out + dot(value_of(piece, head), jnp.exp(scores - top).astype(BF16), NN)
            again.append(out)
            tops.append(jnp.broadcast_to(top, (HEAD_DIM, count)))
        finish(again, jnp.concatenate(tops[::-1], 0).T)


def attend(query, kvs):
    count, width = query.shape
    pairs, pieces, length = width // LANES, len(kvs), kvs[0].shape[0]
    row = pl.BlockSpec((count, LANES), lambda p: (0, p))
    return pl.pallas_call(
        functools.partial(attend_kernel, pieces=pieces),
        grid=(pairs,),
        in_specs=[row]
        + [pl.BlockSpec((length, LANES), lambda p: (0, p))] * pieces
        + [pl.BlockSpec((length, LANES), lambda p: (0, pairs + p))] * pieces,
        out_specs=[row, row],
        out_shape=[shape_of((count, width)), shape_of((count, width), F32)],
        compiler_params=params(),
        cost_estimate=cost(32),
        name="attend",
    )(query, *kvs, *kvs)


def attend_back_kernel(query_ref, grad_ref, context_ref, logsum_ref, *refs, pieces):
    key_refs, value_refs = refs[:pieces], refs[pieces : 2 * pieces]
    query_grad_ref = refs[2 * pieces]
    key_grad_refs = refs[2 * pieces + 1 : 3 * pieces + 1]
    value_grad_refs = refs[3 * pieces + 1 :]
    low, place = lane_parts()
    query, grad = query_ref[...], grad_ref[...]
    product = grad.astype(F32) * wide(context_ref)
    logsum = logsum_ref[...]
    ones_key = jnp.where(place < 3, 1.0, 0.0).astype(BF16)
    zero = jnp.zeros_like(query)
    heads = []
    for head in range(2):
        own = low if head == 0 else ~low
        inner = jnp.sum(jnp.where(own, product, 0.0), -1, keepdims=True)
        heads.append(
            (
                own,
                with_offset(own, place, query, -logsum),
                with_offset(own, place, grad, jnp.broadcast_to(-inner, logsum.shape)),
                jnp.where(own, query, zero),
                jnp.where(own, grad, zero),
            )
        )
    query_grads = [0.0, 0.0]
    for piece in range(pieces):
        key, value = key_refs[piece][...], value_refs[piece][...]
        key_turned = key.T
        key_grad, value_grad = 0.0, 0.0
        for head, (own, query_off, grad_off, query_own, grad_own) in enumerate(heads):
            scores = dot(jnp.where(own, key, ones_key), query_off, NT)
            probs = jnp.exp(scores)
            prob_grad = dot(jnp.where(own, value, ones_key), grad_off, NT)
            score_grad = (probs * prob_grad).astype(BF16)
            value_grad = value_grad + dot(probs.astype(BF16), grad_own, NN)
            key_grad = key_grad + dot(score_grad, query_own, NN)
            lanes = slice(head * HEAD_DIM, (head + 1) * HEAD_DIM)
            query_grads[head] = query_grads[head] + dot(key_turned[lanes], score_grad, NN)
        key_grad_refs[piece][...] = key_grad.astype(BF16)
        value_grad_refs[piece][...] = value_grad.astype(BF16)
    turned = jnp.concatenate(query_grads, 0) * HEAD_DIM ** (-0.5)
    query_grad_ref[...] = turned.T.astype(BF16)


def attend_back(query, grad, context, logsum, kvs):
    count, width = query.shape
    pairs, pieces, length = width // LANES, len(kvs), kvs[0].shape[0]
    row = pl.BlockSpec((count, LANES), lambda p: (0, p))
    piece = pl.BlockSpec((length, LANES), lambda p: (0, p))
    return pl.pallas_call(
        functools.partial(attend_back_kernel, pieces=pieces),
        grid=(pairs,),
        in_specs=[row] * 4
        + [piece] * pieces
        + [pl.BlockSpec((length, LANES), lambda p: (0, pairs + p))] * pieces,
        out_specs=[row] + [piece] * (2 * pieces),
        out_shape=[shape_of((count, width))] + [shape_of((length, width))] * (2 * pieces),
        compiler_params=params(),
        cost_estimate=cost(75),
        name="attend_back",
    )(query, grad, context, logsum, *kvs, *kvs)


def gelu_parts(hidden):
    share = 0.5 + 0.5 * lax.erf(hidden * 2**-0.5)
    bell = jnp.exp(-0.5 * hidden * hidden) * 0.3989422804014327
    return hidden * share, share + hidden * bell


def feed_kernel(
    context_ref, x0_ref, x1_ref, time_ref, cot0_ref, cot1_ref, out_weight_ref, out_bias_ref,
    gain_ref, shift_ref, up_ref, up_bias_ref, down_ref, down_bias_ref,
    out_ref, active_ref, hidden_grad_ref, normed_ref, middle_grad_ref, branch_ref, context_grad_ref, sums_ref,
):
    step = pl.program_id(0)
    width, hidden_width = x0_ref.shape[1], up_ref.shape[1]

    @pl.when(step == 0)
    def _():
        sums_ref[...] = jnp.zeros_like(sums_ref)

    x = jnp.where(step == 0, x0_ref[...], x1_ref[...])
    cot = jnp.where(step == 0, cot0_ref[...], cot1_ref[...])
    middle = x.astype(F32) + wide(time_ref) + dot(context_ref[...], out_weight_ref[...], NN) + wide(out_bias_ref)
    unit, scale = norm_parts(middle)
    gain = wide(gain_ref)
    normed = (unit * gain + wide(shift_ref)).astype(BF16)
    normed_ref[...] = normed
    out = middle + wide(down_bias_ref)
    normed_grad = jnp.zeros_like(out)
    for part in range(hidden_width // width):
        columns = slice(part * width, (part + 1) * width)
        hidden = dot(normed, up_ref[:, columns], NN) + up_bias_ref[:, columns].astype(F32)
        active, slope = gelu_parts(hidden)
        active = active.astype(BF16)
        active_ref[:, columns] = active
        out = out + dot(active, down_ref[columns, :], NN)
        hidden_grad = (dot(cot, down_ref[columns, :], NT) * slope).astype(BF16)
        hidden_grad_ref[:, columns] = hidden_grad
        sums_ref[8 + part : 9 + part] += column_sum(hidden_grad.astype(F32))
        normed_grad = normed_grad + dot(hidden_grad, up_ref[:, columns], NT)
    out_ref[...] = out.astype(BF16)
    cot = cot.astype(F32)
    middle_grad = cot + norm_backward(normed_grad, gain, unit, scale)
    middle_grad_ref[...] = middle_grad
    branch = middle_grad.astype(BF16)
    branch_ref[...] = branch
    context_grad_ref[...] = dot(branch, out_weight_ref[...], NT).astype(BF16)
    sums_ref[0:1] += column_sum(cot)
    sums_ref[1:2] += column_sum(normed_grad * unit)
    sums_ref[2:3] += column_sum(normed_grad)
    sums_ref[3:4] += column_sum(branch.astype(F32))
    sums_ref[4:5] += column_sum(out * out)


def feed(context, xs, time_row, cots, out_weight, out_bias, gain, shift, up, up_bias, down, down_bias):
    block, width = xs[0].shape
    count, hidden_width = 2 * block, up.shape[1]
    sums_rows = 8 + hidden_width // width + (-(hidden_width // width)) % 8
    row = fixed((1, width))
    whole = fixed((block, width))
    return pl.pallas_call(
        feed_kernel,
        grid=(2,),
        in_specs=[
            rows(block, width), whole, whole, row, whole, whole, fixed(out_weight.shape), row, row, row,
            fixed(up.shape), fixed((1, hidden_width)), fixed(down.shape), row,
        ],
        out_specs=[
            rows(block, width), rows(block, hidden_width), rows(block, hidden_width), rows(block, width),
            rows(block, width), rows(block, width), rows(block, width),
            pl.BlockSpec((sums_rows, width), lambda i: (0, 0)),
        ],
        out_shape=[
            shape_of((count, width)), shape_of((count, hidden_width)), shape_of((count, hidden_width)),
            shape_of((count, width)), shape_of((count, width), F32), shape_of((count, width)),
            shape_of((count, width)), shape_of((sums_rows, width), F32),
        ],
        compiler_params=params(),
        cost_estimate=cost(34),
        name="feed",
    )(context, *xs, time_row, *cots, out_weight, out_bias, gain, shift, up, up_bias, down, down_bias)


def down_grad_kernel(active_ref, cot0_ref, cot1_ref, out_ref):
    block = cot0_ref.shape[0]
    out_ref[...] = (
        dot(active_ref[:block], cot0_ref[...], TN) + dot(active_ref[block:], cot1_ref[...], TN)
    ).astype(BF16)


def down_grad(active, cots):
    block, width = cots[0].shape
    count, hidden_width = active.shape
    return pl.pallas_call(
        down_grad_kernel,
        grid=(hidden_width // width,),
        in_specs=[pl.BlockSpec((count, width), lambda i: (0, i))] + [fixed((block, width))] * 2,
        out_specs=rows(width, width),
        out_shape=shape_of((hidden_width, width)),
        compiler_params=params(),
        cost_estimate=cost(8),
        name="down_grad",
    )(active, *cots)


def up_out_grad_kernel(normed_ref, hidden_grad_ref, context_ref, branch_ref, out_ref):
    last = pl.num_programs(0) - 1

    @pl.when(pl.program_id(0) < last)
    def _():
        out_ref[0] = dot(normed_ref[...], hidden_grad_ref[...], TN).astype(BF16)

    @pl.when(pl.program_id(0) == last)
    def _():
        out_ref[0] = dot(context_ref[...], branch_ref[...], TN).astype(BF16)


def up_out_grad(normed, hidden_grad, context, branch):
    count, width = normed.shape
    parts = hidden_grad.shape[1] // width
    whole = fixed((count, width))
    return pl.pallas_call(
        up_out_grad_kernel,
        grid=(parts + 1,),
        in_specs=[
            whole,
            pl.BlockSpec((count, width), lambda i: (0, jnp.minimum(i, parts - 1))),
            whole,
            whole,
        ],
        out_specs=pl.BlockSpec((1, width, width), lambda i: (i, 0, 0)),
        out_shape=shape_of((parts + 1, width, width)),
        compiler_params=params(),
        cost_estimate=cost(10),
        name="up_out_grad",
    )(normed, hidden_grad, context, branch)


def qkv_grad_kernel(normed_ref, grad_ref, out_ref):
    out_ref[0] = dot(normed_ref[...], grad_ref[...], TN).astype(BF16)


def qkv_grad(normed, grads):
    count, width = normed.shape
    parts = grads.shape[1] // width
    return pl.pallas_call(
        qkv_grad_kernel,
        grid=(parts,),
        in_specs=[fixed((count, width)), pl.BlockSpec((count, width), lambda i: (0, i))],
        out_specs=pl.BlockSpec((1, width, width), lambda i: (i, 0, 0)),
        out_shape=shape_of((parts, width, width)),
        compiler_params=params(),
        cost_estimate=cost(7),
        name="qkv_grad",
    )(normed, grads)


def start_kernel(
    query_grad_ref, key0_ref, key1_ref, far_key0_ref, far_key1_ref, value0_ref, value1_ref, far_value0_ref,
    far_value1_ref, x0_ref, x1_ref, time_ref, middle_grad_ref, gain_ref, weight_ref,
    token0_ref, token1_ref, grads_ref, sums_ref,
):
    step = pl.program_id(0)
    width = x0_ref.shape[1]

    @pl.when(step == 0)
    def _():
        sums_ref[...] = jnp.zeros_like(sums_ref)

    def pick(first, second):
        return jnp.where(step == 0, first[...], second[...])

    query_grad = query_grad_ref[...]
    key_grad = (pick(key0_ref, key1_ref).astype(F32) + pick(far_key0_ref, far_key1_ref).astype(F32)).astype(BF16)
    value_grad = (
        pick(value0_ref, value1_ref).astype(F32) + pick(far_value0_ref, far_value1_ref).astype(F32)
    ).astype(BF16)
    normed_grad = 0.0
    for part, grad in enumerate((query_grad, key_grad, value_grad)):
        columns = slice(part * width, (part + 1) * width)
        grads_ref[:, columns] = grad
        normed_grad = normed_grad + dot(grad, weight_ref[:, columns], NT)
    unit, scale = norm_parts(pick(x0_ref, x1_ref).astype(F32) + wide(time_ref))
    token_grad = middle_grad_ref[...] + norm_backward(normed_grad, wide(gain_ref), unit, scale)

    @pl.when(step == 0)
    def _():
        token0_ref[...] = token_grad.astype(BF16)

    @pl.when(step == 1)
    def _():
        token1_ref[...] = token_grad.astype(BF16)

    sums_ref[0:1] += column_sum(normed_grad * unit)
    sums_ref[1:2] += column_sum(normed_grad)
    sums_ref[2:3] += column_sum(query_grad.astype(F32))
    sums_ref[3:4] += column_sum(value_grad.astype(F32))
    sums_ref[4:5] += column_sum(token_grad)


def start_back(query_grad, key_grads, value_grads, xs, time_row, middle_grad, gain, weight):
    block, width = xs[0].shape
    count = 2 * block
    whole = fixed((block, width))
    row = fixed((1, width))
    kept = pl.BlockSpec((block, width), lambda i: (0, 0))
    return pl.pallas_call(
        start_kernel,
        grid=(2,),
        in_specs=[rows(block, width)]
        + [whole] * 10
        + [row, rows(block, width), row, fixed(weight.shape)],
        out_specs=[kept, kept, rows(block, 3 * width), pl.BlockSpec((8, width), lambda i: (0, 0))],
        out_shape=[
            shape_of((block, width)), shape_of((block, width)), shape_of((count, 3 * width)),
            shape_of((8, width), F32),
        ],
        compiler_params=params(),
        cost_estimate=cost(10),
        name="start_back",
    )(query_grad, *key_grads, *value_grads, *xs, time_row, middle_grad, gain, weight)


class Places:
    def __init__(self, dp, seq):
        self.dp, self.seq = dp, seq
        self.bits = dp.bit_length() - 1

    def flat(self, d, z):
        return d * self.seq + z

    def pairs(self, to):
        return [
            (self.flat(d, z), self.flat(*to(d, z))) for d in range(self.dp) for z in range(self.seq)
        ]

    def gather_order(self, turn):
        def to(d, z):
            core, j = d % 2, (z + turn) % 2
            return d - core + z // 2, 2 * core + j

        return self.pairs(to)

    def scatter_order(self, turn):
        return [(b, a) for a, b in self.gather_order(turn)]

    def swap(self, bit):
        return self.pairs(lambda d, z: (d ^ (1 << bit), z))

    def swap_seq(self, step):
        return self.pairs(lambda d, z: (d, z ^ step))


def send(x, order):
    return lax.ppermute(x, BOTH, order)


def add(a, b):
    return (a.astype(F32) + b.astype(F32)).astype(BF16)


def reduce_parts(parts, places):
    d, z = lax.axis_index("dp"), lax.axis_index("seq")
    count, height, width = parts.shape
    block = height // places.dp
    grid = parts.reshape((count,) + (2,) * places.bits + (block, width))

    def halve(value, bit, axes):
        axis = 1 + axes.index(bit)
        mine = (d >> bit) & 1
        kept = lax.dynamic_index_in_dim(value, mine, axis, keepdims=False)
        sent = lax.dynamic_index_in_dim(value, 1 - mine, axis, keepdims=False)
        axes.remove(bit)
        return add(kept, send(sent, places.swap(bit)))

    axes = list(range(places.bits - 1, -1, -1))
    grid = halve(grid, 0, axes)
    halves = []
    for number, order in enumerate((range(1, places.bits), range(places.bits - 1, 0, -1))):
        at = block // 2
        value = lax.slice_in_dim(grid, number * at, (number + 1) * at, axis=grid.ndim - 2)
        left = list(axes)
        for bit in order:
            value = halve(value, bit, left)
        halves.append(sum_along_seq(value, z, places))
    return jnp.concatenate(halves, 1)


def sum_along_seq(value, z, places):
    count, block, width = value.shape
    mine = z % 2
    grid = value.reshape(count, block, 2, width // 2)
    kept = lax.dynamic_index_in_dim(grid, mine, 2, keepdims=False)
    sent = lax.dynamic_index_in_dim(grid, 1 - mine, 2, keepdims=False)
    half = add(kept, send(sent, places.swap_seq(1)))
    half = add(half, send(half, places.swap_seq(2)))
    other = send(half, places.swap_seq(1))
    first = jnp.where(mine == 0, half, other)
    second = jnp.where(mine == 0, other, half)
    return jnp.concatenate([first, second], 2).astype(F32)


def sum_everywhere(value, places):
    for bit in range(places.bits):
        value = value + send(value, places.swap(bit))
    for step in (1, 2):
        value = value + send(value, places.swap_seq(step))
    return value


def per_device(
    tokens, timesteps, time_table, ln1_gain, ln1_bias, qkv_weight, q_bias, v_bias, out_weight, out_bias,
    ln2_gain, ln2_bias, up_weight, up_bias, down_weight, down_bias, cotangent,
):
    places = Places(lax.axis_size("dp"), lax.axis_size("seq"))
    seq_count, local_len, width = tokens.shape
    hidden_width = up_weight.shape[1]
    assert places.seq == 4 and seq_count == 2 and places.dp == 1 << places.bits
    d, z = lax.axis_index("dp"), lax.axis_index("seq")
    core = d % 2
    total_seqs = seq_count * places.dp
    total_tokens = total_seqs * local_len * places.seq

    def gathered(array):
        blocks = []
        for turn in range(2):
            mine = lax.dynamic_index_in_dim(array, (z + turn) % 2, 0, keepdims=False)
            blocks.append(send(mine, places.gather_order(turn)))
        return blocks

    far_steps = send(timesteps, places.swap(0))
    xs = gathered(tokens)
    cots = gathered(cotangent)
    here = z // 2 == core
    step_value = lax.dynamic_index_in_dim(jnp.where(here, timesteps, far_steps), z % 2, 0, keepdims=False)
    sequence = (d - core + z // 2) * seq_count + z % 2
    time_row = lax.dynamic_slice_in_dim(time_table, step_value, 1, 0)

    def row(v):
        return v.reshape(1, -1)

    bias_all = jnp.concatenate(
        [q_bias.astype(F32), jnp.zeros((width,), F32), v_bias.astype(F32)]
    ).reshape(1, -1)
    count = 2 * local_len
    normed, query, kv0 = project(xs[0], time_row, row(ln1_gain), row(ln1_bias), qkv_weight, bias_all, count)
    far0 = send(kv0, places.swap(0))
    normed, query, kv1 = project(
        xs[1], time_row, row(ln1_gain), row(ln1_bias), qkv_weight, bias_all, count, (normed, query)
    )
    far1 = send(kv1, places.swap(0))
    kvs = [kv0, kv1, far0, far1]
    context, logsum = attend(query, kvs)
    out, active, hidden_grad, normed_two, middle_grad, branch, context_grad, feed_sums = feed(
        context, xs, time_row, cots, out_weight, row(out_bias), row(ln2_gain), row(ln2_bias),
        up_weight, row(up_bias), down_weight, row(down_bias),
    )

    def scattered(blocks, dtype):
        back = [send(block, places.scatter_order(turn)) for turn, block in enumerate(blocks)]
        even = z % 2 == 0
        return jnp.stack(
            [jnp.where(even, back[0], back[1]), jnp.where(even, back[1], back[0])]
        ).astype(dtype)

    layer_out = scattered([out[:local_len], out[local_len:]], BF16)
    parts = hidden_width // width
    down_sum = reduce_parts(down_grad(active, cots)[None], places)[0]
    up_out_sum = reduce_parts(up_out_grad(normed_two, hidden_grad, context, branch), places)
    back = attend_back(query, context_grad, context, logsum, kvs)
    query_grad, key_grads, value_grads = back[0], back[1:5], back[5:9]
    far_key = [send(g, places.swap(0)) for g in key_grads[2:]]
    far_value = [send(g, places.swap(0)) for g in value_grads[2:]]
    token0, token1, projected_grad, start_sums = start_back(
        query_grad, list(key_grads[:2]) + far_key, list(value_grads[:2]) + far_value, xs, time_row,
        middle_grad, row(ln1_gain), qkv_weight,
    )
    tokens_grad = scattered([token0, token1], F32)
    qkv_sum = reduce_parts(qkv_grad(normed, projected_grad), places)

    bucket = step_value * BUCKETS // TSTEPS
    lane = jnp.arange(width)
    energy = jnp.sum(feed_sums[4]) / (width * total_tokens)
    stats_row = jnp.where(lane == bucket, energy, 0.0) + jnp.where(
        lane == BUCKETS + bucket, count / total_tokens, 0.0
    )
    sequence_rows = jnp.where(jnp.arange(total_seqs)[:, None] == sequence, start_sums[4][None], 0.0)
    step_row = jnp.where(lane[:total_seqs] == sequence, step_value, 0).astype(F32) * jnp.where(core == 0, 1.0, 0.0)
    packed = jnp.concatenate(
        [
            feed_sums[0:4], feed_sums[8 : 8 + parts], start_sums[0:4], stats_row[None],
            jnp.pad(step_row, (0, width - total_seqs))[None], sequence_rows,
        ]
    )
    packed = sum_everywhere(packed, places)
    piece = width // places.dp
    mine = lax.dynamic_slice_in_dim(packed[: 8 + parts], d * piece, piece, 1)
    up_piece = hidden_width // places.dp
    up_bias_sum = lax.dynamic_slice_in_dim(packed[4 : 4 + parts].reshape(-1), d * up_piece, up_piece, 0)
    stats = packed[8 + parts]
    steps = packed[9 + parts, :total_seqs].astype(jnp.int32)
    sums = packed[10 + parts :]
    table_rows = time_table.shape[0] // places.dp
    chosen = (steps[None, :] == (jnp.arange(table_rows) + d * table_rows)[:, None]).astype(F32)
    table_grad = jnp.dot(chosen, sums, precision=lax.Precision.HIGHEST)

    def side_by_side(stacked):
        return jnp.moveaxis(stacked, 0, 1).reshape(stacked.shape[1], -1)

    return (
        layer_out,
        tokens_grad,
        table_grad,
        mine[4 + parts],
        mine[5 + parts],
        side_by_side(qkv_sum),
        mine[6 + parts],
        mine[7 + parts],
        up_out_sum[parts],
        mine[3],
        mine[1],
        mine[2],
        side_by_side(up_out_sum[:parts]),
        up_bias_sum,
        down_sum,
        mine[0],
        stats[:BUCKETS],
        stats[BUCKETS : 2 * BUCKETS],
    )


def solution(mesh):
    split = P("dp", "seq", None)
    return jax.shard_map(
        per_device,
        mesh=mesh,
        in_specs=(split, P("dp")) + (P(),) * 14 + (split,),
        out_specs=(
            split, split, P("dp", None), P("dp"), P("dp"), P("dp", None), P("dp"), P("dp"), P("dp", None),
            P("dp"), P("dp"), P("dp"), P("dp", None), P("dp"), P("dp", None), P("dp"), P(), P(),
        ),
        check_vma=False,
    )
```

```python
import functools

import jax
import jax.numpy as jnp
from jax import lax
from jax.experimental import pallas as pl
from jax.experimental.pallas import tpu as pltpu
from jax.sharding import PartitionSpec as P

HEAD_DIM = 64
TSTEPS = 2048
BUCKETS = 4
EPS = 1e-05
LANES = 128
VMEM_BYTES = 56 * 1024 * 1024
BOTH = ("dp", "seq")
F32 = jnp.float32
BF16 = jnp.bfloat16
NN = (((1,), (0,)), ((), ()))
NT = (((1,), (1,)), ((), ()))
TN = (((0,), (0,)), ((), ()))


def dot(a, b, dims):
    return lax.dot_general(a, b, dims, preferred_element_type=F32)


def wide(ref):
    return ref[...].astype(F32)


def column_sum(v):
    return jnp.sum(v, 0, keepdims=True)


def fixed(shape):
    return pl.BlockSpec(shape, lambda *i: (0,) * len(shape), pipeline_mode=pl.Buffered(1))


def rows(block, width):
    return pl.BlockSpec((block, width), lambda i: (i, 0))


def shape_of(shape, dtype=BF16):
    return jax.ShapeDtypeStruct(shape, dtype)


def cost(us):
    return pl.CostEstimate(flops=int(us * 1.15e9), bytes_accessed=0, transcendentals=0)


def params():
    return pltpu.CompilerParams(vmem_limit_bytes=VMEM_BYTES)


def norm_parts(v):
    centered = v - jnp.mean(v, -1, keepdims=True)
    scale = lax.rsqrt(jnp.mean(centered * centered, -1, keepdims=True) + EPS)
    return centered * scale, scale


def norm_backward(grad, gain, unit, scale):
    scaled = grad * gain
    return scale * (
        scaled
        - jnp.mean(scaled, -1, keepdims=True)
        - unit * jnp.mean(scaled * unit, -1, keepdims=True)
    )


def project_kernel(x_ref, time_ref, gain_ref, shift_ref, weight_ref, bias_ref, *refs):
    normed_ref, query_ref, kv_ref = refs[-3:]
    width = x_ref.shape[1]
    unit, _ = norm_parts(wide(x_ref) + wide(time_ref))
    normed = (unit * wide(gain_ref) + wide(shift_ref)).astype(BF16)
    normed_ref[...] = normed
    for part in range(3):
        columns = slice(part * width, (part + 1) * width)
        made = (dot(normed, weight_ref[:, columns], NN) + bias_ref[:, columns]).astype(BF16)
        if part == 0:
            query_ref[...] = made * jnp.asarray(HEAD_DIM ** (-0.5), BF16)
        else:
            kv_ref[:, (part - 1) * width : part * width] = made


def project(x, time_row, gain, shift, weight, bias, total, begun=None, block=256):
    count, width = x.shape
    first = 0 if begun is None else total // block - count // block
    later = pl.BlockSpec((block, width), lambda i: (i + first, 0))
    extra = [] if begun is None else list(begun)
    return pl.pallas_call(
        project_kernel,
        grid=(count // block,),
        in_specs=[
            rows(block, width),
            fixed((1, width)),
            fixed((1, width)),
            fixed((1, width)),
            fixed(weight.shape),
            fixed(bias.shape),
        ]
        + [pl.BlockSpec(memory_space=pl.ANY)] * len(extra),
        out_specs=[later, later, rows(block, 2 * width)],
        out_shape=[
            shape_of((total, width)),
            shape_of((total, width)),
            shape_of((count, 2 * width)),
        ],
        input_output_aliases={6: 0, 7: 1} if extra else {},
        compiler_params=params(),
        cost_estimate=cost(5),
        name="project",
    )(x, time_row, gain, shift, weight, bias, *extra)


def lane_parts():
    lane = lax.broadcasted_iota(jnp.int32, (1, LANES), 1)
    return lane < HEAD_DIM, lane % HEAD_DIM


def with_offset(own, place, base, offset):
    high = offset.astype(BF16)
    left = offset - high.astype(F32)
    mid = left.astype(BF16)
    low = (left - mid.astype(F32)).astype(BF16)
    zero = jnp.zeros_like(low)
    parts = jnp.where(place == 0, high, jnp.where(place == 1, mid, jnp.where(place == 2, low, zero)))
    return jnp.where(own, base, parts)


def attend_kernel(query_ref, *refs, pieces):
    key_refs, value_refs = refs[:pieces], refs[pieces : 2 * pieces]
    context_ref, logsum_ref = refs[2 * pieces :]
    count = query_ref.shape[0]
    low, place = lane_parts()
    row_half = lax.broadcasted_iota(jnp.int32, (LANES, LANES), 0) // HEAD_DIM
    lane_half = lax.broadcasted_iota(jnp.int32, (LANES, LANES), 1) // HEAD_DIM
    swapped = jnp.where(row_half != lane_half, 1.0, 0.0).astype(BF16)
    query = query_ref[...]

    def norms(v):
        v = v.astype(F32)
        return dot((v * v).astype(BF16), swapped, NN)

    key_norm = functools.reduce(
        jnp.maximum, [jnp.max(norms(ref[...]), 0, keepdims=True) for ref in key_refs]
    )
    bound = jnp.sqrt(norms(query) * key_norm) * 1.01
    ones_key = jnp.where(place < 3, 1.0, 0.0).astype(BF16)
    values = [ref[...].T for ref in value_refs]
    ones = jnp.ones((16, value_refs[0].shape[0]), BF16)

    def value_of(piece, head):
        return jnp.concatenate([values[piece][head * HEAD_DIM : (head + 1) * HEAD_DIM], ones], 0)

    def finish(mixed, offset):
        totals = [m[HEAD_DIM : HEAD_DIM + 1] for m in mixed]
        context = jnp.concatenate([m[:HEAD_DIM] / t for m, t in zip(mixed, totals)], 0)
        context_ref[...] = context.T.astype(BF16)
        logs = [jnp.broadcast_to(jnp.log(t), (HEAD_DIM, count)) for t in reversed(totals)]
        logsum_ref[...] = jnp.concatenate(logs, 0).T + offset

    mixed = []
    for head in range(2):
        own = low if head == 0 else ~low
        query_own = with_offset(own, place, query, -bound)
        out = 0.0
        for piece in range(pieces):
            key_own = jnp.where(own, key_refs[piece][...], ones_key)
            weights = jnp.exp(dot(key_own, query_own, NT)).astype(BF16)
            out = out + dot(value_of(piece, head), weights, NN)
        mixed.append(out)
    finish(mixed, bound)
    smallest = jnp.min(jnp.minimum(mixed[0][HEAD_DIM], mixed[1][HEAD_DIM]))

    @pl.when(smallest < 1e-25)
    def _():
        again, tops = [], []
        for head in range(2):
            own = low if head == 0 else ~low
            query_own = jnp.where(own, query, jnp.zeros_like(query))
            top = jnp.full((1, count), -jnp.inf, F32)
            for piece in range(pieces):
                scores = dot(key_refs[piece][...], query_own, NT)
                top = jnp.maximum(top, jnp.max(scores, 0, keepdims=True))
            out = 0.0
            for piece in range(pieces):
                scores = dot(key_refs[piece][...], query_own, NT)
                out = out + dot(value_of(piece, head), jnp.exp(scores - top).astype(BF16), NN)
            again.append(out)
            tops.append(jnp.broadcast_to(top, (HEAD_DIM, count)))
        finish(again, jnp.concatenate(tops[::-1], 0).T)


def attend(query, kvs):
    count, width = query.shape
    pairs, pieces, length = width // LANES, len(kvs), kvs[0].shape[0]
    row = pl.BlockSpec((count, LANES), lambda p: (0, p))
    return pl.pallas_call(
        functools.partial(attend_kernel, pieces=pieces),
        grid=(pairs,),
        in_specs=[row]
        + [pl.BlockSpec((length, LANES), lambda p: (0, p))] * pieces
        + [pl.BlockSpec((length, LANES), lambda p: (0, pairs + p))] * pieces,
        out_specs=[row, row],
        out_shape=[shape_of((count, width)), shape_of((count, width), F32)],
        compiler_params=params(),
        cost_estimate=cost(32),
        name="attend",
    )(query, *kvs, *kvs)


def attend_back_step(query_ref, grad_ref, context_ref, logsum_ref, pieces, query_grad_ref):
    low, place = lane_parts()
    query, grad = query_ref[...], grad_ref[...]
    count = query.shape[0]
    product = grad.astype(F32) * wide(context_ref)
    logsum = logsum_ref[...]
    ones_key = jnp.where(place < 3, 1.0, 0.0).astype(BF16)
    zero = jnp.zeros_like(query)
    heads = []
    for head in range(2):
        own = low if head == 0 else ~low
        inner = jnp.sum(jnp.where(own, product, 0.0), -1, keepdims=True)
        heads.append(
            (
                own,
                with_offset(own, place, query, -logsum),
                with_offset(own, place, grad, jnp.broadcast_to(-inner, logsum.shape)),
                jnp.where(own, query, zero),
                jnp.where(own, grad, zero),
            )
        )
    length = sum(piece[0].shape[0] for piece in pieces)
    query_grads = [0.0, 0.0]
    key_mean = 0.0
    for key_ref, value_ref, key_grad_ref, value_grad_ref, before in pieces:
        if before is not None:
            before()
        key, value = key_ref[...], value_ref[...]
        key_turned = key.T
        key_mean = key_mean + jnp.sum(key_turned.astype(F32), 1, keepdims=True) / length
        ones = jnp.ones((16, key.shape[0]), BF16)
        key_grad, value_grad = 0.0, 0.0
        for head, (own, query_off, grad_off, query_own, grad_own) in enumerate(heads):
            scores = dot(jnp.where(own, key, ones_key), query_off, NT)
            probs = jnp.exp(scores)
            prob_grad = dot(jnp.where(own, value, ones_key), grad_off, NT)
            score_grad = (probs * prob_grad).astype(BF16)
            value_grad = value_grad + dot(probs.astype(BF16), grad_own, NN)
            key_grad = key_grad + dot(score_grad, query_own, NN)
            lanes = slice(head * HEAD_DIM, (head + 1) * HEAD_DIM)
            turned = jnp.concatenate([key_turned[lanes], ones], 0)
            query_grads[head] = query_grads[head] + dot(turned, score_grad, NN)
        key_grad_ref[...] = key_grad.astype(BF16)
        value_grad_ref[...] = value_grad.astype(BF16)
    parts = [
        made[:HEAD_DIM]
        - key_mean[head * HEAD_DIM : (head + 1) * HEAD_DIM]
        * jnp.broadcast_to(made[HEAD_DIM : HEAD_DIM + 1], (HEAD_DIM, count))
        for head, made in enumerate(query_grads)
    ]
    query_grad_ref[...] = (jnp.concatenate(parts, 0) * HEAD_DIM ** (-0.5)).T.astype(BF16)


def attend_back_kernel(query_ref, grad_ref, context_ref, logsum_ref, *refs, pieces):
    key_refs, value_refs = refs[:pieces], refs[pieces : 2 * pieces]
    query_grad_ref = refs[2 * pieces]
    key_grad_refs = refs[2 * pieces + 1 : 3 * pieces + 1]
    value_grad_refs = refs[3 * pieces + 1 :]
    steps = list(zip(key_refs, value_refs, key_grad_refs, value_grad_refs, [None] * pieces))
    attend_back_step(query_ref, grad_ref, context_ref, logsum_ref, steps, query_grad_ref)


def attend_back(query, grad, context, logsum, kvs):
    count, width = query.shape
    pairs, pieces, length = width // LANES, len(kvs), kvs[0].shape[0]
    row = pl.BlockSpec((count, LANES), lambda p: (0, p))
    piece = pl.BlockSpec((length, LANES), lambda p: (0, p))
    return pl.pallas_call(
        functools.partial(attend_back_kernel, pieces=pieces),
        grid=(pairs,),
        in_specs=[row] * 4
        + [piece] * pieces
        + [pl.BlockSpec((length, LANES), lambda p: (0, pairs + p))] * pieces,
        out_specs=[row] + [piece] * (2 * pieces),
        out_shape=[shape_of((count, width))] + [shape_of((length, width))] * (2 * pieces),
        compiler_params=params(),
        cost_estimate=cost(75),
        name="attend_back",
    )(query, grad, context, logsum, *kvs, *kvs)


def here():
    d, z = lax.axis_index("dp"), lax.axis_index("seq")
    return d, z, d // 4, (d // 2) % 2, d % 2


def partners():
    d, z, y, x, core = here()
    return {
        "core": (d + 1 - 2 * core, z),
        "x": (d + 2 - 4 * x, z),
        "y": (d + 4 - 8 * y, z),
        "near": (d, z + 1 - 2 * (z % 2)),
        "far": (d, (z + 2) % 4),
    }


def remote(source, target, sends, receives, send_index, receive_index, device):
    return pltpu.make_async_remote_copy(
        src_ref=source,
        dst_ref=target,
        send_sem=sends.at[send_index],
        recv_sem=receives.at[receive_index],
        device_id=device,
        device_id_type=pl.DeviceIdType.MESH,
    )


class Reduction:
    COPIES = 8

    def __init__(self, source, out, scratch, at):
        self.source, self.out = source, out
        self.own, self.from_core, self.first, self.second, self.near, self.far, self.other = scratch[:7]
        self.sends, self.receives, self.local = scratch[7:10]
        self.at = at
        self.parts, _, _, self.rows, self.width = self.own.shape
        self.half, self.top = self.width // 2, self.rows // 2

    @staticmethod
    def scratch(parts, block, width):
        half, top = width // 2, block // 2
        return [
            pltpu.VMEM((parts, 2, 2, block, width), BF16),
            pltpu.VMEM((parts, 2, 2, block, width), BF16),
            pltpu.VMEM((2, parts, 2, block, half), BF16),
            pltpu.VMEM((2, parts, block, half), BF16),
            pltpu.VMEM((parts, top, width), BF16),
            pltpu.VMEM((parts, top, width), BF16),
            pltpu.VMEM((parts, top, width), BF16),
            pltpu.SemaphoreType.DMA((8,)),
            pltpu.SemaphoreType.DMA((8,)),
            pltpu.SemaphoreType.DMA((3,)),
        ]

    def copy(self, number):
        d, z, y, x, core = here()
        to = partners()
        left, right = pl.ds(0, self.half), pl.ds(self.half, self.half)
        kept = pl.ds(pl.multiple_of((z % 2) * self.top, self.top), self.top)
        given = pl.ds(pl.multiple_of((1 - z % 2) * self.top, self.top), self.top)
        source, target, device = (
            lambda: (self.source.at[:, :, :, 1 - core], self.from_core, to["core"]),
            lambda: (self.own.at[:, :, 1 - x, :, left], self.first.at[0], to["x"]),
            lambda: (self.own.at[:, 1 - y, :, :, right], self.first.at[1], to["y"]),
            lambda: (self.own.at[:, 1 - y, x, :, left], self.second.at[0], to["y"]),
            lambda: (self.own.at[:, y, 1 - x, :, right], self.second.at[1], to["x"]),
            lambda: (self.own.at[:, y, x, given], self.near, to["near"]),
            lambda: (self.own.at[:, y, x, kept], self.far, to["far"]),
            lambda: (self.own.at[:, y, x, kept], self.other, to["near"]),
        )[number]()
        return remote(source, target, self.sends, self.receives, number, number, device)

    def load(self):
        core = here()[4]
        return pltpu.make_async_copy(self.source.at[:, :, :, core], self.own, self.local.at[0])

    def to_cores(self):
        self.copy(0).start()
        self.load().start()

    def to_first(self):
        self.load().wait()
        self.copy(0).wait()
        for part in range(self.parts):
            for i in range(2):
                for j in range(2):
                    self.own[part, i, j] = self.own[part, i, j] + self.from_core[part, i, j]
        self.copy(1).start()
        self.copy(2).start()

    def to_second(self):
        _, _, y, x, _ = here()
        self.copy(1).wait()
        self.copy(2).wait()
        left, right = slice(0, self.half), slice(self.half, self.width)
        for part in range(self.parts):
            for i in range(2):
                self.own[part, i, x, :, left] = self.own[part, i, x, :, left] + self.first[0, part, i]
                self.own[part, y, i, :, right] = self.own[part, y, i, :, right] + self.first[1, part, i]
        self.copy(3).start()
        self.copy(4).start()

    def to_near(self):
        _, _, y, x, _ = here()
        self.copy(3).wait()
        self.copy(4).wait()
        left, right = slice(0, self.half), slice(self.half, self.width)
        for part in range(self.parts):
            self.own[part, y, x, :, left] = self.own[part, y, x, :, left] + self.second[0, part]
            self.own[part, y, x, :, right] = self.own[part, y, x, :, right] + self.second[1, part]
        self.copy(5).start()

    def add_rows(self, received):
        _, z, y, x, _ = here()
        kept = pl.ds(pl.multiple_of((z % 2) * self.top, self.top), self.top)
        for part in range(self.parts):
            self.own[part, y, x, kept] = self.own[part, y, x, kept] + received[part]

    def to_far(self):
        self.copy(5).wait()
        self.add_rows(self.near)
        self.copy(6).start()

    def to_other(self):
        self.copy(6).wait()
        self.add_rows(self.far)
        self.copy(7).start()

    def stores(self):
        _, z, y, x, _ = here()
        kept = pl.ds(pl.multiple_of((z % 2) * self.top, self.top), self.top)
        given = pl.ds(pl.multiple_of((1 - z % 2) * self.top, self.top), self.top)
        return (
            pltpu.make_async_copy(self.own.at[:, y, x, kept], self.out.at[:, kept], self.local.at[1]),
            pltpu.make_async_copy(self.other, self.out.at[:, given], self.local.at[2]),
        )

    def to_out(self):
        self.copy(7).wait()
        for copy in self.stores():
            copy.start()

    def finish(self):
        for copy in self.stores():
            copy.wait()


class Return:
    def __init__(self, out, sends, receives, local):
        self.out, self.sends, self.receives, self.local = out, sends, receives, local

    def targets(self):
        d, z, _, _, core = here()
        return [(d - core + z // 2, 2 * core + (z + p) % 2) for p in range(2)]

    def sources(self):
        d, z, _, _, core = here()
        return [(d - core + z // 2, 2 * core + j) for j in range(2)]

    def stays(self):
        _, z, _, _, core = here()
        return z // 2 == core

    def greet(self, barrier):
        _, z, _, _, _ = here()
        for j, source in enumerate(self.sources()):

            @pl.when(jnp.logical_not(self.stays() & (z % 2 == j)))
            def _():
                pl.semaphore_signal(barrier, inc=1, device_id=source, device_id_type=pl.DeviceIdType.MESH)

        return jnp.where(self.stays(), 1, 2)

    def keep(self, block):
        z = lax.axis_index("seq")
        return pltpu.make_async_copy(block, self.out.at[z % 2], self.local.at[0])

    def copy(self, p, block):
        z = lax.axis_index("seq")
        return remote(block, self.out.at[z % 2], self.sends, self.receives, p, z % 2, self.targets()[p])

    def begin(self, p, block):
        if p == 1:
            self.copy(1, block).start()
            return

        @pl.when(self.stays())
        def _():
            self.keep(block).start()

        @pl.when(jnp.logical_not(self.stays()))
        def _():
            self.copy(0, block).start()

    def finish(self, blocks):
        z = lax.axis_index("seq")
        self.copy(1, blocks[1]).wait_send()

        @pl.when(self.stays())
        def _():
            self.keep(blocks[0]).wait()

        @pl.when(jnp.logical_not(self.stays()))
        def _():
            self.copy(0, blocks[0]).wait_send()

        for j in range(2):

            @pl.when(jnp.logical_not(self.stays() & (z % 2 == j)))
            def _():
                remote(
                    blocks[0], self.out.at[j], self.sends, self.receives, 0, j, self.sources()[j]
                ).wait_recv()


def meet(names, *returns):
    barrier = pltpu.get_barrier_semaphore()
    to = partners()
    for name in names:
        pl.semaphore_signal(barrier, inc=1, device_id=to[name], device_id_type=pl.DeviceIdType.MESH)
    expected = len(names)
    for one in returns:
        expected = expected + one.greet(barrier)
    pl.semaphore_wait(barrier, expected)


def back_kernel(
    query_ref, grad_ref, context_ref, logsum_ref, *refs, pieces
):
    key_refs, value_refs = refs[:pieces], refs[pieces : 2 * pieces]
    down_ref, up_ref, layer_ref = refs[2 * pieces : 2 * pieces + 3]
    refs = refs[2 * pieces + 3 :]
    near = pieces // 2
    query_grad_ref = refs[0]
    key_grad_refs, value_grad_refs = refs[1 : 1 + near], refs[1 + near : 1 + 2 * near]
    far_out, layer_out, down_out, up_out = refs[1 + 2 * near : 5 + 2 * near]
    refs = refs[5 + 2 * near :]
    down = Reduction(down_ref, down_out, refs[:10], 0)
    up = Reduction(up_ref, up_out, refs[10:20], 0)
    far_grads, far_sends, far_receives, layer_sends, layer_receives, layer_local = refs[20:]
    back = Return(layer_out, layer_sends, layer_receives, layer_local)
    block = key_refs[0].shape[0]
    layer_blocks = [layer_ref.at[pl.ds(p * block, block)] for p in range(2)]
    pair, pairs = pl.program_id(0), pl.num_programs(0)

    def far_copy(which):
        return remote(
            far_grads, far_out.at[which], far_sends, far_receives, 0, which, partners()["core"]
        )

    def begin():
        meet(("core", "x", "y", "near", "far"), back)
        down.to_cores()
        up.to_cores()
        back.begin(0, layer_blocks[0])
        back.begin(1, layer_blocks[1])

    def far_free():
        far_copy(pair - 1).wait_send()

    def far_send():
        far_copy(pair).start()

    plan = {
        (0, 0): [begin],
        (0, 2): [down.to_first],
        (1, 0): [up.to_first],
        (1, 3): [down.to_second],
        (3, 0): [down.to_near],
        (3, 1): [up.to_second],
        (3, 3): [down.to_far],
        (4, 1): [up.to_near],
        (5, 0): [up.to_far, down.to_other],
        (5, 3): [down.to_out],
    }

    def before(place):
        def run():
            for (step, at), actions in plan.items():
                if at == place:

                    @pl.when(pair == step)
                    def _():
                        for action in actions:
                            action()

            if place == 0:
                pl.when(pair > 0)(far_free)
            if place == near:
                far_send()

        return run

    order = []
    for i in range(near):
        order.append((key_refs[near + i], value_refs[near + i], far_grads.at[0, pl.ds(i * block, block)], far_grads.at[1, pl.ds(i * block, block)]))
    for i in range(near):
        order.append((key_refs[i], value_refs[i], key_grad_refs[i], value_grad_refs[i]))
    steps = [one + (before(place),) for place, one in enumerate(order)]
    attend_back_step(query_ref, grad_ref, context_ref, logsum_ref, steps, query_grad_ref)

    @pl.when(pair == pairs - 1)
    def _():
        up.to_other()
        far_copy(pair).wait_send()

        def received(which, carry):
            far_copy(which).wait_recv()
            return carry

        lax.fori_loop(0, pairs, received, 0)
        back.finish(layer_blocks)
        down.finish()
        up.to_out()
        up.finish()


def back(query, grad, context, logsum, kvs, down_parts, up_parts, layer_out):
    count, width = query.shape
    pairs, pieces, length = width // LANES, len(kvs), kvs[0].shape[0]
    near = pieces // 2
    row = pl.BlockSpec((count, LANES), lambda p: (0, p))
    piece = pl.BlockSpec((length, LANES), lambda p: (0, p))
    anywhere = pl.BlockSpec(memory_space=pl.ANY)
    sizes = [(parts.shape[0], parts.shape[1] // 8) for parts in (down_parts, up_parts)]
    split = [
        parts.reshape(n, 2, 2, 2, block, width) for parts, (n, block) in zip((down_parts, up_parts), sizes)
    ]
    return pl.pallas_call(
        functools.partial(back_kernel, pieces=pieces),
        grid=(pairs,),
        in_specs=[row] * 4
        + [piece] * pieces
        + [pl.BlockSpec((length, LANES), lambda p: (0, pairs + p))] * pieces
        + [anywhere] * 3,
        out_specs=[row] + [piece] * (2 * near) + [anywhere] * 4,
        out_shape=[shape_of((count, width))]
        + [shape_of((length, width))] * (2 * near)
        + [shape_of((pairs, 2, near * length, LANES)), shape_of((2, length, width))]
        + [shape_of((n, block, width)) for n, block in sizes],
        scratch_shapes=Reduction.scratch(*sizes[0], width)
        + Reduction.scratch(*sizes[1], width)
        + [
            pltpu.VMEM((2, near * length, LANES), BF16),
            pltpu.SemaphoreType.DMA((1,)),
            pltpu.SemaphoreType.DMA((pairs,)),
            pltpu.SemaphoreType.DMA((2,)),
            pltpu.SemaphoreType.DMA((2,)),
            pltpu.SemaphoreType.DMA((1,)),
        ],
        compiler_params=pltpu.CompilerParams(
            vmem_limit_bytes=VMEM_BYTES, collective_id=0, has_side_effects=True
        ),
        cost_estimate=cost(80),
        name="back",
    )(query, grad, context, logsum, *kvs, *kvs, *split, layer_out)


def gelu_parts(hidden):
    share = 0.5 + 0.5 * lax.erf(hidden * 2**-0.5)
    bell = jnp.exp(-0.5 * hidden * hidden) * 0.3989422804014327
    return hidden * share, share + hidden * bell


def feed_kernel(
    context_ref, x0_ref, x1_ref, time_ref, cot0_ref, cot1_ref, out_weight_ref, out_bias_ref,
    gain_ref, shift_ref, up_ref, up_bias_ref, down_ref, down_bias_ref,
    out_ref, active_ref, hidden_grad_ref, normed_ref, middle_grad_ref, branch_ref, context_grad_ref, sums_ref,
):
    step = pl.program_id(0)
    width, hidden_width = x0_ref.shape[1], up_ref.shape[1]

    @pl.when(step == 0)
    def _():
        sums_ref[...] = jnp.zeros_like(sums_ref)

    x = jnp.where(step == 0, x0_ref[...], x1_ref[...])
    cot = jnp.where(step == 0, cot0_ref[...], cot1_ref[...])
    middle = x.astype(F32) + wide(time_ref) + dot(context_ref[...], out_weight_ref[...], NN) + wide(out_bias_ref)
    unit, scale = norm_parts(middle)
    gain = wide(gain_ref)
    normed = (unit * gain + wide(shift_ref)).astype(BF16)
    normed_ref[...] = normed
    out = middle + wide(down_bias_ref)
    normed_grad = jnp.zeros_like(out)
    for part in range(hidden_width // width):
        columns = slice(part * width, (part + 1) * width)
        hidden = dot(normed, up_ref[:, columns], NN) + up_bias_ref[:, columns].astype(F32)
        active, slope = gelu_parts(hidden)
        active = active.astype(BF16)
        active_ref[:, columns] = active
        out = out + dot(active, down_ref[columns, :], NN)
        hidden_grad = (dot(cot, down_ref[columns, :], NT) * slope).astype(BF16)
        hidden_grad_ref[:, columns] = hidden_grad
        sums_ref[8 + part : 9 + part] += column_sum(hidden_grad.astype(F32))
        normed_grad = normed_grad + dot(hidden_grad, up_ref[:, columns], NT)
    out_ref[...] = out.astype(BF16)
    cot = cot.astype(F32)
    middle_grad = cot + norm_backward(normed_grad, gain, unit, scale)
    middle_grad_ref[...] = middle_grad
    branch = middle_grad.astype(BF16)
    branch_ref[...] = branch
    context_grad_ref[...] = dot(branch, out_weight_ref[...], NT).astype(BF16)
    sums_ref[0:1] += column_sum(cot)
    sums_ref[1:2] += column_sum(normed_grad * unit)
    sums_ref[2:3] += column_sum(normed_grad)
    sums_ref[3:4] += column_sum(branch.astype(F32))
    sums_ref[4:5] += column_sum(out * out)


def feed(context, xs, time_row, cots, out_weight, out_bias, gain, shift, up, up_bias, down, down_bias):
    block, width = xs[0].shape
    count, hidden_width = 2 * block, up.shape[1]
    sums_rows = 8 + hidden_width // width + (-(hidden_width // width)) % 8
    row = fixed((1, width))
    whole = fixed((block, width))
    return pl.pallas_call(
        feed_kernel,
        grid=(2,),
        in_specs=[
            rows(block, width), whole, whole, row, whole, whole, fixed(out_weight.shape), row, row, row,
            fixed(up.shape), fixed((1, hidden_width)), fixed(down.shape), row,
        ],
        out_specs=[
            rows(block, width), rows(block, hidden_width), rows(block, hidden_width), rows(block, width),
            rows(block, width), rows(block, width), rows(block, width),
            pl.BlockSpec((sums_rows, width), lambda i: (0, 0)),
        ],
        out_shape=[
            shape_of((count, width)), shape_of((count, hidden_width)), shape_of((count, hidden_width)),
            shape_of((count, width)), shape_of((count, width), F32), shape_of((count, width)),
            shape_of((count, width)), shape_of((sums_rows, width), F32),
        ],
        compiler_params=params(),
        cost_estimate=cost(34),
        name="feed",
    )(context, *xs, time_row, *cots, out_weight, out_bias, gain, shift, up, up_bias, down, down_bias)


def down_grad_kernel(active_ref, cot0_ref, cot1_ref, out_ref):
    block = cot0_ref.shape[0]
    out_ref[...] = (
        dot(active_ref[:block], cot0_ref[...], TN) + dot(active_ref[block:], cot1_ref[...], TN)
    ).astype(BF16)


def down_grad(active, cots):
    block, width = cots[0].shape
    count, hidden_width = active.shape
    return pl.pallas_call(
        down_grad_kernel,
        grid=(hidden_width // width,),
        in_specs=[pl.BlockSpec((count, width), lambda i: (0, i))] + [fixed((block, width))] * 2,
        out_specs=rows(width, width),
        out_shape=shape_of((hidden_width, width)),
        compiler_params=params(),
        cost_estimate=cost(8),
        name="down_grad",
    )(active, *cots)


def up_out_grad_kernel(normed_ref, hidden_grad_ref, context_ref, branch_ref, out_ref):
    last = pl.num_programs(0) - 1

    @pl.when(pl.program_id(0) < last)
    def _():
        out_ref[0] = dot(normed_ref[...], hidden_grad_ref[...], TN).astype(BF16)

    @pl.when(pl.program_id(0) == last)
    def _():
        out_ref[0] = dot(context_ref[...], branch_ref[...], TN).astype(BF16)


def up_out_grad(normed, hidden_grad, context, branch):
    count, width = normed.shape
    parts = hidden_grad.shape[1] // width
    whole = fixed((count, width))
    return pl.pallas_call(
        up_out_grad_kernel,
        grid=(parts + 1,),
        in_specs=[
            whole,
            pl.BlockSpec((count, width), lambda i: (0, jnp.minimum(i, parts - 1))),
            whole,
            whole,
        ],
        out_specs=pl.BlockSpec((1, width, width), lambda i: (i, 0, 0)),
        out_shape=shape_of((parts + 1, width, width)),
        compiler_params=params(),
        cost_estimate=cost(10),
        name="up_out_grad",
    )(normed, hidden_grad, context, branch)


def qkv_grad_kernel(normed_ref, grad_ref, out_ref):
    out_ref[0] = dot(normed_ref[...], grad_ref[...], TN).astype(BF16)


def qkv_grad(normed, grads):
    count, width = normed.shape
    parts = grads.shape[1] // width
    return pl.pallas_call(
        qkv_grad_kernel,
        grid=(parts,),
        in_specs=[fixed((count, width)), pl.BlockSpec((count, width), lambda i: (0, i))],
        out_specs=pl.BlockSpec((1, width, width), lambda i: (i, 0, 0)),
        out_shape=shape_of((parts, width, width)),
        compiler_params=params(),
        cost_estimate=cost(7),
        name="qkv_grad",
    )(normed, grads)


def start_kernel(
    query_grad_ref, key0_ref, key1_ref, far_key0_ref, far_key1_ref, value0_ref, value1_ref, far_value0_ref,
    far_value1_ref, x0_ref, x1_ref, time_ref, middle_grad_ref, gain_ref, weight_ref,
    token0_ref, token1_ref, grads_ref, sums_ref,
):
    step = pl.program_id(0)
    width = x0_ref.shape[1]

    @pl.when(step == 0)
    def _():
        sums_ref[...] = jnp.zeros_like(sums_ref)

    def pick(first, second):
        return jnp.where(step == 0, first[...], second[...])

    query_grad = query_grad_ref[...]
    key_grad = (pick(key0_ref, key1_ref).astype(F32) + pick(far_key0_ref, far_key1_ref).astype(F32)).astype(BF16)
    value_grad = (
        pick(value0_ref, value1_ref).astype(F32) + pick(far_value0_ref, far_value1_ref).astype(F32)
    ).astype(BF16)
    normed_grad = 0.0
    for part, grad in enumerate((query_grad, key_grad, value_grad)):
        columns = slice(part * width, (part + 1) * width)
        grads_ref[:, columns] = grad
        normed_grad = normed_grad + dot(grad, weight_ref[:, columns], NT)
    unit, scale = norm_parts(pick(x0_ref, x1_ref).astype(F32) + wide(time_ref))
    token_grad = middle_grad_ref[...] + norm_backward(normed_grad, wide(gain_ref), unit, scale)

    @pl.when(step == 0)
    def _():
        token0_ref[...] = token_grad.astype(BF16)

    @pl.when(step == 1)
    def _():
        token1_ref[...] = token_grad.astype(BF16)

    sums_ref[0:1] += column_sum(normed_grad * unit)
    sums_ref[1:2] += column_sum(normed_grad)
    sums_ref[2:3] += column_sum(query_grad.astype(F32))
    sums_ref[3:4] += column_sum(value_grad.astype(F32))
    sums_ref[4:5] += column_sum(token_grad)


def start_back(query_grad, key_grads, value_grads, xs, time_row, middle_grad, gain, weight):
    block, width = xs[0].shape
    count = 2 * block
    whole = fixed((block, width))
    row = fixed((1, width))
    kept = pl.BlockSpec((block, width), lambda i: (0, 0))
    return pl.pallas_call(
        start_kernel,
        grid=(2,),
        in_specs=[rows(block, width)]
        + [whole] * 10
        + [row, rows(block, width), row, fixed(weight.shape)],
        out_specs=[kept, kept, rows(block, 3 * width), pl.BlockSpec((8, width), lambda i: (0, 0))],
        out_shape=[
            shape_of((block, width)), shape_of((block, width)), shape_of((count, 3 * width)),
            shape_of((8, width), F32),
        ],
        compiler_params=params(),
        cost_estimate=cost(10),
        name="start_back",
    )(query_grad, *key_grads, *value_grads, *xs, time_row, middle_grad, gain, weight)


class Places:
    def __init__(self, dp, seq):
        self.dp, self.seq = dp, seq
        self.bits = dp.bit_length() - 1

    def flat(self, d, z):
        return d * self.seq + z

    def pairs(self, to):
        return [
            (self.flat(d, z), self.flat(*to(d, z))) for d in range(self.dp) for z in range(self.seq)
        ]

    def gather_order(self, turn):
        def to(d, z):
            core, j = d % 2, (z + turn) % 2
            return d - core + z // 2, 2 * core + j

        return self.pairs(to)

    def scatter_order(self, turn):
        return [(b, a) for a, b in self.gather_order(turn)]

    def swap(self, bit):
        return self.pairs(lambda d, z: (d ^ (1 << bit), z))

    def swap_seq(self, step):
        return self.pairs(lambda d, z: (d, z ^ step))


def send(x, order):
    return lax.ppermute(x, BOTH, order)


def add(a, b):
    return (a.astype(F32) + b.astype(F32)).astype(BF16)


def reduce_parts(parts, places):
    d, z = lax.axis_index("dp"), lax.axis_index("seq")
    count, height, width = parts.shape
    block = height // places.dp
    grid = parts.reshape((count,) + (2,) * places.bits + (block, width))

    def halve(value, bit, axes):
        axis = 1 + axes.index(bit)
        mine = (d >> bit) & 1
        kept = lax.dynamic_index_in_dim(value, mine, axis, keepdims=False)
        sent = lax.dynamic_index_in_dim(value, 1 - mine, axis, keepdims=False)
        axes.remove(bit)
        return add(kept, send(sent, places.swap(bit)))

    axes = list(range(places.bits - 1, -1, -1))
    grid = halve(grid, 0, axes)
    halves = []
    for number, order in enumerate((range(1, places.bits), range(places.bits - 1, 0, -1))):
        at = block // 2
        value = lax.slice_in_dim(grid, number * at, (number + 1) * at, axis=grid.ndim - 2)
        left = list(axes)
        for bit in order:
            value = halve(value, bit, left)
        halves.append(sum_along_seq(value, z, places))
    return jnp.concatenate(halves, 1)


def sum_along_seq(value, z, places):
    count, block, width = value.shape
    mine = z % 2
    grid = value.reshape(count, block, 2, width // 2)
    kept = lax.dynamic_index_in_dim(grid, mine, 2, keepdims=False)
    sent = lax.dynamic_index_in_dim(grid, 1 - mine, 2, keepdims=False)
    half = add(kept, send(sent, places.swap_seq(1)))
    half = add(half, send(half, places.swap_seq(2)))
    other = send(half, places.swap_seq(1))
    first = jnp.where(mine == 0, half, other)
    second = jnp.where(mine == 0, other, half)
    return jnp.concatenate([first, second], 2).astype(F32)


def sum_everywhere(value, places):
    for bit in range(places.bits):
        value = value + send(value, places.swap(bit))
    for step in (1, 2):
        value = value + send(value, places.swap_seq(step))
    return value


def per_device(
    tokens, timesteps, time_table, ln1_gain, ln1_bias, qkv_weight, q_bias, v_bias, out_weight, out_bias,
    ln2_gain, ln2_bias, up_weight, up_bias, down_weight, down_bias, cotangent,
):
    places = Places(lax.axis_size("dp"), lax.axis_size("seq"))
    seq_count, local_len, width = tokens.shape
    hidden_width = up_weight.shape[1]
    assert places.seq == 4 and seq_count == 2 and places.dp == 1 << places.bits
    d, z = lax.axis_index("dp"), lax.axis_index("seq")
    core = d % 2
    total_seqs = seq_count * places.dp
    total_tokens = total_seqs * local_len * places.seq

    def gathered(array):
        blocks = []
        for turn in range(2):
            mine = lax.dynamic_index_in_dim(array, (z + turn) % 2, 0, keepdims=False)
            blocks.append(send(mine, places.gather_order(turn)))
        return blocks

    far_steps = send(timesteps, places.swap(0))
    xs = gathered(tokens)
    cots = gathered(cotangent)
    here = z // 2 == core
    step_value = lax.dynamic_index_in_dim(jnp.where(here, timesteps, far_steps), z % 2, 0, keepdims=False)
    sequence = (d - core + z // 2) * seq_count + z % 2
    time_row = lax.dynamic_slice_in_dim(time_table, step_value, 1, 0)

    def row(v):
        return v.reshape(1, -1)

    bias_all = jnp.concatenate(
        [q_bias.astype(F32), jnp.zeros((width,), F32), v_bias.astype(F32)]
    ).reshape(1, -1)
    count = 2 * local_len
    normed, query, kv0 = project(xs[0], time_row, row(ln1_gain), row(ln1_bias), qkv_weight, bias_all, count)
    far0 = send(kv0, places.swap(0))
    normed, query, kv1 = project(
        xs[1], time_row, row(ln1_gain), row(ln1_bias), qkv_weight, bias_all, count, (normed, query)
    )
    far1 = send(kv1, places.swap(0))
    kvs = [kv0, kv1, far0, far1]
    context, logsum = attend(query, kvs)
    out, active, hidden_grad, normed_two, middle_grad, branch, context_grad, feed_sums = feed(
        context, xs, time_row, cots, out_weight, row(out_bias), row(ln2_gain), row(ln2_bias),
        up_weight, row(up_bias), down_weight, row(down_bias),
    )

    def scattered(blocks, dtype):
        back = [send(block, places.scatter_order(turn)) for turn, block in enumerate(blocks)]
        even = z % 2 == 0
        return jnp.stack(
            [jnp.where(even, back[0], back[1]), jnp.where(even, back[1], back[0])]
        ).astype(dtype)

    parts = hidden_width // width
    down_parts = down_grad(active, cots)[None]
    up_out_parts = up_out_grad(normed_two, hidden_grad, context, branch)
    if places.dp == 8:
        made = back(query, context_grad, context, logsum, kvs, down_parts, up_out_parts, out)
        query_grad, key_grads, value_grads = made[0], list(made[1:3]), list(made[3:5])
        far_grads, layer_out = made[5], made[6]
        down_sum, up_out_sum = made[7][0].astype(F32), made[8].astype(F32)
        far = jnp.moveaxis(far_grads.reshape(-1, 2, 2, local_len, LANES), 0, 3).reshape(2, 2, local_len, width)
        far_key, far_value = [far[0, 0], far[0, 1]], [far[1, 0], far[1, 1]]
    else:
        layer_out = scattered([out[:local_len], out[local_len:]], BF16)
        down_sum = reduce_parts(down_parts, places)[0]
        up_out_sum = reduce_parts(up_out_parts, places)
        made = attend_back(query, context_grad, context, logsum, kvs)
        query_grad, key_grads, value_grads = made[0], list(made[1:3]), list(made[5:7])
        far_key = [send(g, places.swap(0)) for g in made[3:5]]
        far_value = [send(g, places.swap(0)) for g in made[7:9]]
    token0, token1, projected_grad, start_sums = start_back(
        query_grad, key_grads + far_key, value_grads + far_value, xs, time_row,
        middle_grad, row(ln1_gain), qkv_weight,
    )
    tokens_grad = scattered([token0, token1], F32)
    qkv_sum = reduce_parts(qkv_grad(normed, projected_grad), places)

    bucket = step_value * BUCKETS // TSTEPS
    lane = jnp.arange(width)
    energy = jnp.sum(feed_sums[4]) / (width * total_tokens)
    stats_row = jnp.where(lane == bucket, energy, 0.0) + jnp.where(
        lane == BUCKETS + bucket, count / total_tokens, 0.0
    )
    sequence_rows = jnp.where(jnp.arange(total_seqs)[:, None] == sequence, start_sums[4][None], 0.0)
    step_row = jnp.where(lane[:total_seqs] == sequence, step_value, 0).astype(F32) * jnp.where(core == 0, 1.0, 0.0)
    packed = jnp.concatenate(
        [
            feed_sums[0:4], feed_sums[8 : 8 + parts], start_sums[0:4], stats_row[None],
            jnp.pad(step_row, (0, width - total_seqs))[None], sequence_rows,
        ]
    )
    packed = sum_everywhere(packed, places)
    piece = width // places.dp
    mine = lax.dynamic_slice_in_dim(packed[: 8 + parts], d * piece, piece, 1)
    up_piece = hidden_width // places.dp
    up_bias_sum = lax.dynamic_slice_in_dim(packed[4 : 4 + parts].reshape(-1), d * up_piece, up_piece, 0)
    stats = packed[8 + parts]
    steps = packed[9 + parts, :total_seqs].astype(jnp.int32)
    sums = packed[10 + parts :]
    table_rows = time_table.shape[0] // places.dp
    chosen = (steps[None, :] == (jnp.arange(table_rows) + d * table_rows)[:, None]).astype(F32)
    table_grad = jnp.dot(chosen, sums, precision=lax.Precision.HIGHEST)

    def side_by_side(stacked):
        return jnp.moveaxis(stacked, 0, 1).reshape(stacked.shape[1], -1)

    return (
        layer_out,
        tokens_grad,
        table_grad,
        mine[4 + parts],
        mine[5 + parts],
        side_by_side(qkv_sum),
        mine[6 + parts],
        mine[7 + parts],
        up_out_sum[parts],
        mine[3],
        mine[1],
        mine[2],
        side_by_side(up_out_sum[:parts]),
        up_bias_sum,
        down_sum,
        mine[0],
        stats[:BUCKETS],
        stats[BUCKETS : 2 * BUCKETS],
    )


def solution(mesh):
    split = P("dp", "seq", None)
    return jax.shard_map(
        per_device,
        mesh=mesh,
        in_specs=(split, P("dp")) + (P(),) * 14 + (split,),
        out_specs=(
            split, split, P("dp", None), P("dp"), P("dp"), P("dp", None), P("dp"), P("dp"), P("dp", None),
            P("dp"), P("dp"), P("dp"), P("dp", None), P("dp"), P("dp", None), P("dp"), P(), P(),
        ),
        check_vma=False,
    )
```

```python
import functools

import jax
import jax.numpy as jnp
from jax import lax
from jax.experimental import pallas as pl
from jax.experimental.pallas import tpu as pltpu
from jax.sharding import PartitionSpec as P

HEAD_DIM = 64
TSTEPS = 2048
BUCKETS = 4
EPS = 1e-05
LANES = 128
VMEM_BYTES = 56 * 1024 * 1024
BOTH = ("dp", "seq")
F32 = jnp.float32
BF16 = jnp.bfloat16
NN = (((1,), (0,)), ((), ()))
NT = (((1,), (1,)), ((), ()))
TN = (((0,), (0,)), ((), ()))


def dot(a, b, dims):
    return lax.dot_general(a, b, dims, preferred_element_type=F32)


def wide(ref):
    return ref[...].astype(F32)


def column_sum(v):
    return jnp.sum(v, 0, keepdims=True)


def fixed(shape):
    return pl.BlockSpec(shape, lambda *i: (0,) * len(shape), pipeline_mode=pl.Buffered(1))


def rows(block, width):
    return pl.BlockSpec((block, width), lambda i: (i, 0))


def shape_of(shape, dtype=BF16):
    return jax.ShapeDtypeStruct(shape, dtype)


def cost(us):
    return pl.CostEstimate(flops=int(us * 1.15e9), bytes_accessed=0, transcendentals=0)


def params():
    return pltpu.CompilerParams(vmem_limit_bytes=VMEM_BYTES)


def norm_parts(v):
    centered = v - jnp.mean(v, -1, keepdims=True)
    scale = lax.rsqrt(jnp.mean(centered * centered, -1, keepdims=True) + EPS)
    return centered * scale, scale


def norm_backward(grad, gain, unit, scale):
    scaled = grad * gain
    return scale * (
        scaled
        - jnp.mean(scaled, -1, keepdims=True)
        - unit * jnp.mean(scaled * unit, -1, keepdims=True)
    )


def project_kernel(x_ref, time_ref, gain_ref, shift_ref, weight_ref, bias_ref, *refs):
    normed_ref, query_ref, kv_ref = refs[-3:]
    width = x_ref.shape[1]
    unit, _ = norm_parts(wide(x_ref) + wide(time_ref))
    normed = (unit * wide(gain_ref) + wide(shift_ref)).astype(BF16)
    normed_ref[...] = normed
    for part in range(3):
        columns = slice(part * width, (part + 1) * width)
        made = (dot(normed, weight_ref[:, columns], NN) + bias_ref[:, columns]).astype(BF16)
        if part == 0:
            query_ref[...] = made * jnp.asarray(HEAD_DIM ** (-0.5), BF16)
        else:
            kv_ref[:, (part - 1) * width : part * width] = made


def project(x, time_row, gain, shift, weight, bias, total, begun=None, block=256):
    count, width = x.shape
    first = 0 if begun is None else total // block - count // block
    later = pl.BlockSpec((block, width), lambda i: (i + first, 0))
    extra = [] if begun is None else list(begun)
    return pl.pallas_call(
        project_kernel,
        grid=(count // block,),
        in_specs=[
            rows(block, width),
            fixed((1, width)),
            fixed((1, width)),
            fixed((1, width)),
            fixed(weight.shape),
            fixed(bias.shape),
        ]
        + [pl.BlockSpec(memory_space=pl.ANY)] * len(extra),
        out_specs=[later, later, rows(block, 2 * width)],
        out_shape=[
            shape_of((total, width)),
            shape_of((total, width)),
            shape_of((count, 2 * width)),
        ],
        input_output_aliases={6: 0, 7: 1} if extra else {},
        compiler_params=params(),
        cost_estimate=cost(5),
        name="project",
    )(x, time_row, gain, shift, weight, bias, *extra)


def lane_parts():
    lane = lax.broadcasted_iota(jnp.int32, (1, LANES), 1)
    return lane < HEAD_DIM, lane % HEAD_DIM


def with_offset(own, place, base, offset):
    high = offset.astype(BF16)
    left = offset - high.astype(F32)
    mid = left.astype(BF16)
    low = (left - mid.astype(F32)).astype(BF16)
    zero = jnp.zeros_like(low)
    parts = jnp.where(place == 0, high, jnp.where(place == 1, mid, jnp.where(place == 2, low, zero)))
    return jnp.where(own, base, parts)


def attend_kernel(query_ref, *refs, pieces):
    key_refs, value_refs = refs[:pieces], refs[pieces : 2 * pieces]
    context_ref, logsum_ref = refs[2 * pieces :]
    count = query_ref.shape[0]
    low, place = lane_parts()
    row_half = lax.broadcasted_iota(jnp.int32, (LANES, LANES), 0) // HEAD_DIM
    lane_half = lax.broadcasted_iota(jnp.int32, (LANES, LANES), 1) // HEAD_DIM
    swapped = jnp.where(row_half != lane_half, 1.0, 0.0).astype(BF16)
    query = query_ref[...]

    def norms(v):
        v = v.astype(F32)
        return dot((v * v).astype(BF16), swapped, NN)

    key_norm = functools.reduce(
        jnp.maximum, [jnp.max(norms(ref[...]), 0, keepdims=True) for ref in key_refs]
    )
    bound = jnp.sqrt(norms(query) * key_norm) * 1.01
    ones_key = jnp.where(place < 3, 1.0, 0.0).astype(BF16)
    values = [ref[...].T for ref in value_refs]
    ones = jnp.ones((16, value_refs[0].shape[0]), BF16)

    def value_of(piece, head):
        return jnp.concatenate([values[piece][head * HEAD_DIM : (head + 1) * HEAD_DIM], ones], 0)

    def finish(mixed, offset):
        totals = [m[HEAD_DIM : HEAD_DIM + 1] for m in mixed]
        context = jnp.concatenate([m[:HEAD_DIM] / t for m, t in zip(mixed, totals)], 0)
        context_ref[...] = context.T.astype(BF16)
        logs = [jnp.broadcast_to(jnp.log(t), (HEAD_DIM, count)) for t in reversed(totals)]
        logsum_ref[...] = jnp.concatenate(logs, 0).T + offset

    mixed = []
    for head in range(2):
        own = low if head == 0 else ~low
        query_own = with_offset(own, place, query, -bound)
        out = 0.0
        for piece in range(pieces):
            key_own = jnp.where(own, key_refs[piece][...], ones_key)
            weights = jnp.exp(dot(key_own, query_own, NT)).astype(BF16)
            out = out + dot(value_of(piece, head), weights, NN)
        mixed.append(out)
    finish(mixed, bound)
    smallest = jnp.min(jnp.minimum(mixed[0][HEAD_DIM], mixed[1][HEAD_DIM]))

    @pl.when(smallest < 1e-25)
    def _():
        again, tops = [], []
        for head in range(2):
            own = low if head == 0 else ~low
            query_own = jnp.where(own, query, jnp.zeros_like(query))
            top = jnp.full((1, count), -jnp.inf, F32)
            for piece in range(pieces):
                scores = dot(key_refs[piece][...], query_own, NT)
                top = jnp.maximum(top, jnp.max(scores, 0, keepdims=True))
            out = 0.0
            for piece in range(pieces):
                scores = dot(key_refs[piece][...], query_own, NT)
                out = out + dot(value_of(piece, head), jnp.exp(scores - top).astype(BF16), NN)
            again.append(out)
            tops.append(jnp.broadcast_to(top, (HEAD_DIM, count)))
        finish(again, jnp.concatenate(tops[::-1], 0).T)


def attend(query, kvs):
    count, width = query.shape
    pairs, pieces, length = width // LANES, len(kvs), kvs[0].shape[0]
    row = pl.BlockSpec((count, LANES), lambda p: (0, p))
    return pl.pallas_call(
        functools.partial(attend_kernel, pieces=pieces),
        grid=(pairs,),
        in_specs=[row]
        + [pl.BlockSpec((length, LANES), lambda p: (0, p))] * pieces
        + [pl.BlockSpec((length, LANES), lambda p: (0, pairs + p))] * pieces,
        out_specs=[row, row],
        out_shape=[shape_of((count, width)), shape_of((count, width), F32)],
        compiler_params=params(),
        cost_estimate=cost(32),
        name="attend",
    )(query, *kvs, *kvs)


def attend_back_step(query_ref, grad_ref, context_ref, logsum_ref, pieces, query_grad_ref):
    low, place = lane_parts()
    query, grad = query_ref[...], grad_ref[...]
    count = query.shape[0]
    product = grad.astype(F32) * wide(context_ref)
    logsum = logsum_ref[...]
    ones_key = jnp.where(place < 3, 1.0, 0.0).astype(BF16)
    zero = jnp.zeros_like(query)
    heads = []
    for head in range(2):
        own = low if head == 0 else ~low
        inner = jnp.sum(jnp.where(own, product, 0.0), -1, keepdims=True)
        heads.append(
            (
                own,
                with_offset(own, place, query, -logsum),
                with_offset(own, place, grad, jnp.broadcast_to(-inner, logsum.shape)),
                jnp.where(own, query, zero),
                jnp.where(own, grad, zero),
            )
        )
    length = sum(piece[0].shape[0] for piece in pieces)
    query_grads = [0.0, 0.0]
    key_mean = 0.0
    for key_ref, value_ref, key_grad_ref, value_grad_ref, before in pieces:
        if before is not None:
            before()
        key, value = key_ref[...], value_ref[...]
        key_turned = key.T
        key_mean = key_mean + jnp.sum(key_turned.astype(F32), 1, keepdims=True) / length
        ones = jnp.ones((16, key.shape[0]), BF16)
        key_grad, value_grad = 0.0, 0.0
        for head, (own, query_off, grad_off, query_own, grad_own) in enumerate(heads):
            scores = dot(jnp.where(own, key, ones_key), query_off, NT)
            probs = jnp.exp(scores)
            prob_grad = dot(jnp.where(own, value, ones_key), grad_off, NT)
            score_grad = (probs * prob_grad).astype(BF16)
            value_grad = value_grad + dot(probs.astype(BF16), grad_own, NN)
            key_grad = key_grad + dot(score_grad, query_own, NN)
            lanes = slice(head * HEAD_DIM, (head + 1) * HEAD_DIM)
            turned = jnp.concatenate([key_turned[lanes], ones], 0)
            query_grads[head] = query_grads[head] + dot(turned, score_grad, NN)
        key_grad_ref[...] = key_grad.astype(BF16)
        value_grad_ref[...] = value_grad.astype(BF16)
    parts = [
        made[:HEAD_DIM]
        - key_mean[head * HEAD_DIM : (head + 1) * HEAD_DIM]
        * jnp.broadcast_to(made[HEAD_DIM : HEAD_DIM + 1], (HEAD_DIM, count))
        for head, made in enumerate(query_grads)
    ]
    query_grad_ref[...] = (jnp.concatenate(parts, 0) * HEAD_DIM ** (-0.5)).T.astype(BF16)


def attend_back_kernel(query_ref, grad_ref, context_ref, logsum_ref, *refs, pieces):
    key_refs, value_refs = refs[:pieces], refs[pieces : 2 * pieces]
    query_grad_ref = refs[2 * pieces]
    key_grad_refs = refs[2 * pieces + 1 : 3 * pieces + 1]
    value_grad_refs = refs[3 * pieces + 1 :]
    steps = list(zip(key_refs, value_refs, key_grad_refs, value_grad_refs, [None] * pieces))
    attend_back_step(query_ref, grad_ref, context_ref, logsum_ref, steps, query_grad_ref)


def attend_back(query, grad, context, logsum, kvs):
    count, width = query.shape
    pairs, pieces, length = width // LANES, len(kvs), kvs[0].shape[0]
    row = pl.BlockSpec((count, LANES), lambda p: (0, p))
    piece = pl.BlockSpec((length, LANES), lambda p: (0, p))
    return pl.pallas_call(
        functools.partial(attend_back_kernel, pieces=pieces),
        grid=(pairs,),
        in_specs=[row] * 4
        + [piece] * pieces
        + [pl.BlockSpec((length, LANES), lambda p: (0, pairs + p))] * pieces,
        out_specs=[row] + [piece] * (2 * pieces),
        out_shape=[shape_of((count, width))] + [shape_of((length, width))] * (2 * pieces),
        compiler_params=params(),
        cost_estimate=cost(75),
        name="attend_back",
    )(query, grad, context, logsum, *kvs, *kvs)


def here():
    d, z = lax.axis_index("dp"), lax.axis_index("seq")
    return d, z, d // 4, (d // 2) % 2, d % 2


def partners():
    d, z, y, x, core = here()
    return {
        "core": (d + 1 - 2 * core, z),
        "x": (d + 2 - 4 * x, z),
        "y": (d + 4 - 8 * y, z),
        "near": (d, z + 1 - 2 * (z % 2)),
        "far": (d, (z + 2) % 4),
    }


def remote(source, target, sends, receives, send_index, receive_index, device):
    return pltpu.make_async_remote_copy(
        src_ref=source,
        dst_ref=target,
        send_sem=sends.at[send_index],
        recv_sem=receives.at[receive_index],
        device_id=device,
        device_id_type=pl.DeviceIdType.MESH,
    )


class Reduction:
    def __init__(self, source, out, scratch):
        self.source, self.out = source, out
        self.own = source.at[:, :, :, here()[4]]
        self.from_core, self.first, self.second, self.near, self.far, self.other = scratch[:6]
        self.sends, self.receives, self.local = scratch[6:9]
        self.parts, _, _, self.rows, self.width = self.from_core.shape
        self.half, self.top = self.width // 2, self.rows // 2

    @staticmethod
    def scratch(parts, block, width):
        half, top = width // 2, block // 2
        return [
            pltpu.VMEM((parts, 2, 2, block, width), BF16),
            pltpu.VMEM((2, parts, 2, block, half), BF16),
            pltpu.VMEM((2, parts, block, half), BF16),
            pltpu.VMEM((parts, top, width), BF16),
            pltpu.VMEM((parts, top, width), BF16),
            pltpu.VMEM((parts, top, width), BF16),
            pltpu.SemaphoreType.DMA((8,)),
            pltpu.SemaphoreType.DMA((8,)),
            pltpu.SemaphoreType.DMA((2,)),
        ]

    def copy(self, number):
        d, z, y, x, core = here()
        to = partners()
        left, right = pl.ds(0, self.half), pl.ds(self.half, self.half)
        kept = pl.ds(pl.multiple_of((z % 2) * self.top, self.top), self.top)
        given = pl.ds(pl.multiple_of((1 - z % 2) * self.top, self.top), self.top)
        source, target, device = (
            lambda: (self.source.at[:, :, :, 1 - core], self.from_core, to["core"]),
            lambda: (self.own.at[:, :, 1 - x, :, left], self.first.at[0], to["x"]),
            lambda: (self.own.at[:, 1 - y, :, :, right], self.first.at[1], to["y"]),
            lambda: (self.own.at[:, 1 - y, x, :, left], self.second.at[0], to["y"]),
            lambda: (self.own.at[:, y, 1 - x, :, right], self.second.at[1], to["x"]),
            lambda: (self.own.at[:, y, x, given], self.near, to["near"]),
            lambda: (self.own.at[:, y, x, kept], self.far, to["far"]),
            lambda: (self.own.at[:, y, x, kept], self.other, to["near"]),
        )[number]()
        return remote(source, target, self.sends, self.receives, number, number, device)

    def to_cores(self):
        self.copy(0).start()

    def to_first(self):
        self.copy(0).wait()
        for part in range(self.parts):
            for i in range(2):
                for j in range(2):
                    self.own[part, i, j] = self.own[part, i, j] + self.from_core[part, i, j]
        self.copy(1).start()
        self.copy(2).start()

    def to_second(self):
        _, _, y, x, _ = here()
        self.copy(1).wait()
        self.copy(2).wait()
        left, right = slice(0, self.half), slice(self.half, self.width)
        for part in range(self.parts):
            for i in range(2):
                self.own[part, i, x, :, left] = self.own[part, i, x, :, left] + self.first[0, part, i]
                self.own[part, y, i, :, right] = self.own[part, y, i, :, right] + self.first[1, part, i]
        self.copy(3).start()
        self.copy(4).start()

    def to_near(self):
        _, _, y, x, _ = here()
        self.copy(3).wait()
        self.copy(4).wait()
        left, right = slice(0, self.half), slice(self.half, self.width)
        for part in range(self.parts):
            self.own[part, y, x, :, left] = self.own[part, y, x, :, left] + self.second[0, part]
            self.own[part, y, x, :, right] = self.own[part, y, x, :, right] + self.second[1, part]
        self.copy(5).start()

    def add_rows(self, received):
        _, z, y, x, _ = here()
        kept = pl.ds(pl.multiple_of((z % 2) * self.top, self.top), self.top)
        for part in range(self.parts):
            self.own[part, y, x, kept] = self.own[part, y, x, kept] + received[part]

    def to_far(self):
        self.copy(5).wait()
        self.add_rows(self.near)
        self.copy(6).start()

    def to_other(self):
        self.copy(6).wait()
        self.add_rows(self.far)
        self.copy(7).start()

    def stores(self):
        _, z, y, x, _ = here()
        kept = pl.ds(pl.multiple_of((z % 2) * self.top, self.top), self.top)
        given = pl.ds(pl.multiple_of((1 - z % 2) * self.top, self.top), self.top)
        return (
            pltpu.make_async_copy(self.own.at[:, y, x, kept], self.out.at[:, kept], self.local.at[0]),
            pltpu.make_async_copy(self.other, self.out.at[:, given], self.local.at[1]),
        )

    def to_out(self):
        self.copy(7).wait()
        for copy in self.stores():
            copy.start()

    def finish(self):
        for copy in self.stores():
            copy.wait()


class Return:
    def __init__(self, out, sends, receives, local):
        self.out, self.sends, self.receives, self.local = out, sends, receives, local

    def targets(self):
        d, z, _, _, core = here()
        return [(d - core + z // 2, 2 * core + (z + p) % 2) for p in range(2)]

    def sources(self):
        d, z, _, _, core = here()
        return [(d - core + z // 2, 2 * core + j) for j in range(2)]

    def stays(self):
        _, z, _, _, core = here()
        return z // 2 == core

    def greet(self, barrier):
        _, z, _, _, _ = here()
        for j, source in enumerate(self.sources()):

            @pl.when(jnp.logical_not(self.stays() & (z % 2 == j)))
            def _():
                pl.semaphore_signal(barrier, inc=1, device_id=source, device_id_type=pl.DeviceIdType.MESH)

        return jnp.where(self.stays(), 1, 2)

    def keep(self, block):
        z = lax.axis_index("seq")
        return pltpu.make_async_copy(block, self.out.at[z % 2], self.local.at[0])

    def copy(self, p, block):
        z = lax.axis_index("seq")
        return remote(block, self.out.at[z % 2], self.sends, self.receives, p, z % 2, self.targets()[p])

    def begin(self, p, block):
        if p == 1:
            self.copy(1, block).start()
            return

        @pl.when(self.stays())
        def _():
            self.keep(block).start()

        @pl.when(jnp.logical_not(self.stays()))
        def _():
            self.copy(0, block).start()

    def finish(self, blocks):
        z = lax.axis_index("seq")
        self.copy(1, blocks[1]).wait_send()

        @pl.when(self.stays())
        def _():
            self.keep(blocks[0]).wait()

        @pl.when(jnp.logical_not(self.stays()))
        def _():
            self.copy(0, blocks[0]).wait_send()

        for j in range(2):

            @pl.when(jnp.logical_not(self.stays() & (z % 2 == j)))
            def _():
                remote(
                    blocks[0], self.out.at[j], self.sends, self.receives, 0, j, self.sources()[j]
                ).wait_recv()


def meet(names, *returns):
    barrier = pltpu.get_barrier_semaphore()
    to = partners()
    for name in names:
        pl.semaphore_signal(barrier, inc=1, device_id=to[name], device_id_type=pl.DeviceIdType.MESH)
    expected = len(names)
    for one in returns:
        expected = expected + one.greet(barrier)
    pl.semaphore_wait(barrier, expected)


def fixed_any():
    return pl.BlockSpec(memory_space=pl.ANY)


def back_kernel(
    query_ref, grad_ref, context_ref, logsum_ref, *refs, pieces, parts
):
    key_refs, value_refs = refs[:pieces], refs[pieces : 2 * pieces]
    refs = refs[2 * pieces :]
    normed_ref, hidden_grad_ref, whole_context_ref, branch_ref, active_ref, cot0_ref, cot1_ref, layer_ref = refs[:8]
    refs = refs[8:]
    near = pieces // 2
    query_grad_ref = refs[0]
    key_grad_refs, value_grad_refs = refs[1 : 1 + near], refs[1 + near : 1 + 2 * near]
    far_out, layer_out, down_out, up_out = refs[1 + 2 * near : 5 + 2 * near]
    refs = refs[5 + 2 * near :]
    down_parts, up_parts = refs[:2]
    chunks = []
    for number, (which, at, many) in enumerate(back_chunks(down_parts.shape, up_parts.shape)):
        scratch = refs[2 + 9 * number : 11 + 9 * number]
        if which == "down":
            here_rows = pl.ds(at, many)
            chunks.append(
                Reduction(down_parts.at[:, :, :, :, here_rows], down_out.at[:, here_rows], scratch)
            )
        else:
            here_parts = pl.ds(at, many)
            chunks.append(Reduction(up_parts.at[here_parts], up_out.at[here_parts], scratch))
    one, two, three, four = chunks
    far_grads, far_sends, far_receives, layer_sends, layer_receives, layer_local = refs[38:]
    back = Return(layer_out, layer_sends, layer_receives, layer_local)
    block = key_refs[0].shape[0]
    layer_blocks = [layer_ref.at[pl.ds(p * block, block)] for p in range(2)]
    step = pl.program_id(0)
    made = 2 * parts + 1
    pair, last = step - made, pl.num_programs(0) - 1

    def far_copy(which):
        return remote(
            far_grads, far_out.at[which], far_sends, far_receives, 0, which, partners()["core"]
        )

    def begin():
        meet(("core", "x", "y", "near", "far"), back)
        back.begin(0, layer_blocks[0])
        back.begin(1, layer_blocks[1])

    plan = {
        (0, 0): [begin],
        (2, 0): [one.to_cores],
        (4, 0): [one.to_first],
        (5, 0): [two.to_cores],
        (8, 0): [one.to_second, two.to_first],
        (9, 0): [three.to_cores, four.to_cores],
        (10, 0): [one.to_near],
        (10, 1): [two.to_second, three.to_first],
        (10, 3): [one.to_far],
        (11, 0): [four.to_first],
        (11, 2): [one.to_other, two.to_near, three.to_second],
        (12, 0): [one.to_out, two.to_far],
        (12, 1): [three.to_near],
        (12, 2): [four.to_second],
        (12, 3): [three.to_far],
        (13, 0): [two.to_other],
        (13, 1): [four.to_near],
        (13, 2): [three.to_other],
        (13, 3): [two.to_out, four.to_far],
        (14, 0): [three.to_out],
        (14, 1): [four.to_other],
        (14, 3): [four.to_out],
    }

    def run_plan(place, steps):
        for (at, where), actions in plan.items():
            if where == place and at in steps:

                @pl.when(step == at)
                def _():
                    for action in actions:
                        action()

    run_plan(0, range(made))

    @pl.when(step < parts)
    def _():
        part = dot(normed_ref[...], hidden_grad_ref[...], TN).astype(BF16)
        up_parts[step] = part.reshape(up_parts.shape[1:])

    @pl.when(step == parts)
    def _():
        part = dot(whole_context_ref[...], branch_ref[...], TN).astype(BF16)
        up_parts[parts] = part.reshape(up_parts.shape[1:])

    @pl.when((step > parts) & (step < made))
    def _():
        part = dot(active_ref[:block], cot0_ref[...], TN) + dot(active_ref[block:], cot1_ref[...], TN)
        part = part.astype(BF16).reshape(down_parts.shape[3:])
        at = step - parts - 1
        down_parts[0, at // 2, at % 2] = part

    def before(place):
        def run():
            run_plan(place, range(made, 100))
            if place == 0:

                @pl.when(pair > 0)
                def _():
                    far_copy(pair - 1).wait_send()

            if place == near:
                far_copy(pair).start()

        return run

    @pl.when(step >= made)
    def _():
        order = []
        for i in range(near):
            far_rows = pl.ds(i * block, block)
            order.append(
                (key_refs[near + i], value_refs[near + i], far_grads.at[0, far_rows], far_grads.at[1, far_rows])
            )
        for i in range(near):
            order.append((key_refs[i], value_refs[i], key_grad_refs[i], value_grad_refs[i]))
        steps = [one_piece + (before(place),) for place, one_piece in enumerate(order)]
        attend_back_step(query_ref, grad_ref, context_ref, logsum_ref, steps, query_grad_ref)

    @pl.when(step == last)
    def _():
        far_copy(pair).wait_send()

        def received(which, carry):
            far_copy(which).wait_recv()
            return carry

        lax.fori_loop(0, last + 1 - made, received, 0)
        back.finish(layer_blocks)
        for chunk in chunks:
            chunk.finish()


def back_chunks(down_shape, up_shape):
    block, parts = down_shape[-2], up_shape[0]
    return [
        ("up", 0, parts // 2),
        ("up", parts // 2, parts - parts // 2),
        ("down", 0, block // 2),
        ("down", block // 2, block // 2),
    ]


def back(query, grad, context, logsum, kvs, normed, hidden_grad, branch, active, cots, layer_out):
    count, width = query.shape
    pairs, pieces, length = width // LANES, len(kvs), kvs[0].shape[0]
    near = pieces // 2
    parts = hidden_grad.shape[1] // width
    made = 2 * parts + 1
    pair = lambda i: jnp.maximum(i - made, 0)
    row = pl.BlockSpec((count, LANES), lambda i: (0, pair(i)))
    piece = pl.BlockSpec((length, LANES), lambda i: (0, pair(i)))
    value = pl.BlockSpec((length, LANES), lambda i: (0, pairs + pair(i)))
    whole = fixed((count, width))
    up_rows, down_rows = width // 8, hidden_grad.shape[1] // 8
    down_shape, up_shape = (1, 2, 2, 2, down_rows, width), (parts + 1, 2, 2, 2, up_rows, width)
    return pl.pallas_call(
        functools.partial(back_kernel, pieces=pieces, parts=parts),
        grid=(made + pairs,),
        in_specs=[row] * 4
        + [piece] * pieces
        + [value] * pieces
        + [
            whole,
            pl.BlockSpec((count, width), lambda i: (0, jnp.minimum(i, parts - 1))),
            whole,
            whole,
            pl.BlockSpec((count, width), lambda i: (0, jnp.clip(i - parts - 1, 0, parts - 1))),
            fixed((length, width)),
            fixed((length, width)),
            fixed_any(),
        ],
        out_specs=[row] + [piece] * (2 * near) + [fixed_any()] * 4,
        out_shape=[shape_of((count, width))]
        + [shape_of((length, width))] * (2 * near)
        + [shape_of((pairs, 2, near * length, LANES)), shape_of((2, length, width))]
        + [shape_of((1, down_rows, width)), shape_of((parts + 1, up_rows, width))],
        scratch_shapes=[pltpu.VMEM(down_shape, BF16), pltpu.VMEM(up_shape, BF16)]
        + [
            shape
            for which, _, many in back_chunks(down_shape, up_shape)
            for shape in Reduction.scratch(*((1, many) if which == "down" else (many, up_rows)), width)
        ]
        + [
            pltpu.VMEM((2, near * length, LANES), BF16),
            pltpu.SemaphoreType.DMA((1,)),
            pltpu.SemaphoreType.DMA((pairs,)),
            pltpu.SemaphoreType.DMA((2,)),
            pltpu.SemaphoreType.DMA((2,)),
            pltpu.SemaphoreType.DMA((1,)),
        ],
        compiler_params=pltpu.CompilerParams(
            vmem_limit_bytes=VMEM_BYTES, collective_id=0, has_side_effects=True
        ),
        cost_estimate=cost(100),
        name="back",
    )(
        query, grad, context, logsum, *kvs, *kvs, normed, hidden_grad, context, branch, active, *cots, layer_out
    )


def tail_kernel(
    query_grad, key0, key1, value0, value1, far, normed, x0, x1, middle_grad, weight,
    time_ref, gain_ref, feed_ref, marks_ref,
    tokens_out, qkv_out, sums_ref,
    query_v, near_v, far_v, normed_v, x_v, middle_v, weight_v, key_v, value_v, token_v,
    query_parts, key_parts, value_parts, *refs, total_tokens, parts,
):
    reductions = []
    for number, made in enumerate((query_parts, key_parts, value_parts)):
        reductions.append(Reduction(made, qkv_out.at[pl.ds(number, 1)], refs[9 * number : 9 * number + 9]))
    of_query, of_key, of_value = reductions
    sums_in, sums_sends, sums_receives, loads, back_sends, back_receives, back_local = refs[27:]
    back = Return(tokens_out, back_sends, back_receives, back_local)
    block, width = x0.shape
    pairs = width // LANES
    d, z, _, _, core = here()
    copies = [
        pltpu.make_async_copy(source, target, loads.at[number])
        for number, (source, target) in enumerate(
            (
                (normed, normed_v), (query_grad, query_v), (key0, near_v.at[0, 0]), (value0, near_v.at[1, 0]),
                (far, far_v), (weight, weight_v), (x0, x_v.at[0]), (middle_grad, middle_v),
                (key1, near_v.at[0, 1]), (value1, near_v.at[1, 1]), (x1, x_v.at[1]),
            )
        )
    ]
    for copy in copies:
        copy.start()
    meet(("core", "x", "y", "near", "far"), back)

    def product(grads, out):
        out[0] = dot(normed_v[...], grads[...], TN).astype(BF16).reshape(out.shape[1:])

    def start_block(p):
        held = pl.ds(p * block, block)
        for pair in range(pairs):
            lanes = slice(pair * LANES, (pair + 1) * LANES)
            key_v[held, lanes] = near_v[0, p, :, lanes] + far_v[pair, 0, held]
            value_v[held, lanes] = near_v[1, p, :, lanes] + far_v[pair, 1, held]
        normed_grad = 0.0
        for part, grads in enumerate((query_v, key_v, value_v)):
            columns = slice(part * width, (part + 1) * width)
            normed_grad = normed_grad + dot(grads[held], weight_v[:, columns], NT)
        unit, scale = norm_parts(x_v[p].astype(F32) + wide(time_ref))
        token_grad = middle_v[held] + norm_backward(normed_grad, wide(gain_ref), unit, scale)
        token_v[p] = token_grad.astype(BF16)
        back.begin(p, token_v.at[p])
        return [
            column_sum(normed_grad * unit),
            column_sum(normed_grad),
            column_sum(query_v[held].astype(F32)),
            column_sum(value_v[held].astype(F32)),
            column_sum(token_grad),
        ]

    def sums_copy(number):
        to = partners()[("core", "x", "y", "near", "far")[number]]
        return remote(sums_ref, sums_in.at[number], sums_sends, sums_receives, number, number, to)

    def sums_next(number):
        sums_copy(number).wait()
        sums_ref[...] = sums_ref[...] + sums_in[number]
        if number < 4:
            sums_copy(number + 1).start()

    copies[0].wait()
    copies[1].wait()
    product(query_v, query_parts)
    of_query.to_cores()
    for copy in copies[2:8]:
        copy.wait()
    first = start_block(0)
    of_query.to_first()
    for copy in copies[8:]:
        copy.wait()
    second = start_block(1)
    of_query.to_second()
    sums = [a + b for a, b in zip(first, second)]
    sums_ref[...] = jnp.zeros_like(sums_ref)
    sums_ref[0:4] = feed_ref[0:4]
    sums_ref[4 : 4 + parts] = feed_ref[8 : 8 + parts]
    for number in range(4):
        sums_ref[4 + parts + number : 5 + parts + number] = sums[number]
    energy = jnp.sum(feed_ref[4:5], keepdims=True) / (width * total_tokens)
    sums_ref[8 + parts : 9 + parts] = marks_ref[0:1] * energy + marks_ref[1:2]
    sums_ref[9 + parts : 10 + parts] = marks_ref[2:3]
    sequence = (d - core + z // 2) * 2 + z % 2
    sums_ref[pl.ds(16 + sequence, 1)] = sums[4]
    sums_copy(0).start()
    product(key_v, key_parts)
    of_key.to_cores()
    sums_next(0)
    product(value_v, value_parts)
    of_value.to_cores()
    of_query.to_near()
    of_key.to_first()
    sums_next(1)
    of_query.to_far()
    of_value.to_first()
    sums_next(2)
    of_key.to_second()
    sums_next(3)
    of_value.to_second()
    of_query.to_other()
    of_key.to_near()
    sums_next(4)
    of_value.to_near()
    of_key.to_far()
    of_query.to_out()
    of_value.to_far()
    of_key.to_other()
    of_value.to_other()
    of_key.to_out()
    of_value.to_out()
    back.finish([token_v.at[0], token_v.at[1]])
    for one in reductions:
        one.finish()


def tail(query_grad, key_grads, value_grads, far, normed, xs, middle_grad, weight, time_row, gain, feed_sums, marks, total_tokens, hidden_parts):
    block, width = xs[0].shape
    count, total_seqs = 2 * block, 16
    any_spec = fixed_any()
    inside = pl.BlockSpec(memory_space=pltpu.VMEM)
    up_rows = width // 8
    parts = pltpu.VMEM((1, 2, 2, 2, up_rows, width), BF16)
    held = lambda *shape, dtype=BF16: pltpu.VMEM(shape, dtype)
    sums_shape = (16 + total_seqs, width)
    return pl.pallas_call(
        functools.partial(tail_kernel, total_tokens=total_tokens, parts=hidden_parts),
        in_specs=[any_spec] * 11 + [inside] * 4,
        out_specs=[any_spec, any_spec, inside],
        out_shape=[
            shape_of((2, block, width)), shape_of((3, up_rows, width)), shape_of(sums_shape, F32),
        ],
        scratch_shapes=[
            held(count, width), held(2, 2, block, width), held(*far.shape), held(count, width),
            held(2, block, width), held(count, width, dtype=F32), held(*weight.shape), held(count, width),
            held(count, width), held(2, block, width), parts, parts, parts,
        ]
        + Reduction.scratch(1, up_rows, width) * 3
        + [
            held(5, *sums_shape, dtype=F32),
            pltpu.SemaphoreType.DMA((5,)),
            pltpu.SemaphoreType.DMA((5,)),
            pltpu.SemaphoreType.DMA((11,)),
            pltpu.SemaphoreType.DMA((2,)),
            pltpu.SemaphoreType.DMA((2,)),
            pltpu.SemaphoreType.DMA((1,)),
        ],
        compiler_params=pltpu.CompilerParams(
            vmem_limit_bytes=VMEM_BYTES, collective_id=1, has_side_effects=True
        ),
        cost_estimate=cost(60),
        name="tail",
    )(
        query_grad, *key_grads, *value_grads, far, normed, *xs, middle_grad, weight, time_row, gain, feed_sums, marks
    )


def gelu_parts(hidden):
    share = 0.5 + 0.5 * lax.erf(hidden * 2**-0.5)
    bell = jnp.exp(-0.5 * hidden * hidden) * 0.3989422804014327
    return hidden * share, share + hidden * bell


def feed_kernel(
    context_ref, x0_ref, x1_ref, time_ref, cot0_ref, cot1_ref, out_weight_ref, out_bias_ref,
    gain_ref, shift_ref, up_ref, up_bias_ref, down_ref, down_bias_ref,
    out_ref, active_ref, hidden_grad_ref, normed_ref, middle_grad_ref, branch_ref, context_grad_ref, sums_ref,
):
    step = pl.program_id(0)
    width, hidden_width = x0_ref.shape[1], up_ref.shape[1]

    @pl.when(step == 0)
    def _():
        sums_ref[...] = jnp.zeros_like(sums_ref)

    x = jnp.where(step == 0, x0_ref[...], x1_ref[...])
    cot = jnp.where(step == 0, cot0_ref[...], cot1_ref[...])
    middle = x.astype(F32) + wide(time_ref) + dot(context_ref[...], out_weight_ref[...], NN) + wide(out_bias_ref)
    unit, scale = norm_parts(middle)
    gain = wide(gain_ref)
    normed = (unit * gain + wide(shift_ref)).astype(BF16)
    normed_ref[...] = normed
    out = middle + wide(down_bias_ref)
    normed_grad = jnp.zeros_like(out)
    for part in range(hidden_width // width):
        columns = slice(part * width, (part + 1) * width)
        hidden = dot(normed, up_ref[:, columns], NN) + up_bias_ref[:, columns].astype(F32)
        active, slope = gelu_parts(hidden)
        active = active.astype(BF16)
        active_ref[:, columns] = active
        out = out + dot(active, down_ref[columns, :], NN)
        hidden_grad = (dot(cot, down_ref[columns, :], NT) * slope).astype(BF16)
        hidden_grad_ref[:, columns] = hidden_grad
        sums_ref[8 + part : 9 + part] += column_sum(hidden_grad.astype(F32))
        normed_grad = normed_grad + dot(hidden_grad, up_ref[:, columns], NT)
    out_ref[...] = out.astype(BF16)
    cot = cot.astype(F32)
    middle_grad = cot + norm_backward(normed_grad, gain, unit, scale)
    middle_grad_ref[...] = middle_grad
    branch = middle_grad.astype(BF16)
    branch_ref[...] = branch
    context_grad_ref[...] = dot(branch, out_weight_ref[...], NT).astype(BF16)
    sums_ref[0:1] += column_sum(cot)
    sums_ref[1:2] += column_sum(normed_grad * unit)
    sums_ref[2:3] += column_sum(normed_grad)
    sums_ref[3:4] += column_sum(branch.astype(F32))
    sums_ref[4:5] += column_sum(out * out)


def feed(context, xs, time_row, cots, out_weight, out_bias, gain, shift, up, up_bias, down, down_bias):
    block, width = xs[0].shape
    count, hidden_width = 2 * block, up.shape[1]
    sums_rows = 8 + hidden_width // width + (-(hidden_width // width)) % 8
    row = fixed((1, width))
    whole = fixed((block, width))
    return pl.pallas_call(
        feed_kernel,
        grid=(2,),
        in_specs=[
            rows(block, width), whole, whole, row, whole, whole, fixed(out_weight.shape), row, row, row,
            fixed(up.shape), fixed((1, hidden_width)), fixed(down.shape), row,
        ],
        out_specs=[
            rows(block, width), rows(block, hidden_width), rows(block, hidden_width), rows(block, width),
            rows(block, width), rows(block, width), rows(block, width),
            pl.BlockSpec((sums_rows, width), lambda i: (0, 0)),
        ],
        out_shape=[
            shape_of((count, width)), shape_of((count, hidden_width)), shape_of((count, hidden_width)),
            shape_of((count, width)), shape_of((count, width), F32), shape_of((count, width)),
            shape_of((count, width)), shape_of((sums_rows, width), F32),
        ],
        compiler_params=params(),
        cost_estimate=cost(34),
        name="feed",
    )(context, *xs, time_row, *cots, out_weight, out_bias, gain, shift, up, up_bias, down, down_bias)


def down_grad_kernel(active_ref, cot0_ref, cot1_ref, out_ref):
    block = cot0_ref.shape[0]
    out_ref[...] = (
        dot(active_ref[:block], cot0_ref[...], TN) + dot(active_ref[block:], cot1_ref[...], TN)
    ).astype(BF16)


def down_grad(active, cots):
    block, width = cots[0].shape
    count, hidden_width = active.shape
    return pl.pallas_call(
        down_grad_kernel,
        grid=(hidden_width // width,),
        in_specs=[pl.BlockSpec((count, width), lambda i: (0, i))] + [fixed((block, width))] * 2,
        out_specs=rows(width, width),
        out_shape=shape_of((hidden_width, width)),
        compiler_params=params(),
        cost_estimate=cost(8),
        name="down_grad",
    )(active, *cots)


def up_out_grad_kernel(normed_ref, hidden_grad_ref, context_ref, branch_ref, out_ref):
    last = pl.num_programs(0) - 1

    @pl.when(pl.program_id(0) < last)
    def _():
        out_ref[0] = dot(normed_ref[...], hidden_grad_ref[...], TN).astype(BF16)

    @pl.when(pl.program_id(0) == last)
    def _():
        out_ref[0] = dot(context_ref[...], branch_ref[...], TN).astype(BF16)


def up_out_grad(normed, hidden_grad, context, branch):
    count, width = normed.shape
    parts = hidden_grad.shape[1] // width
    whole = fixed((count, width))
    return pl.pallas_call(
        up_out_grad_kernel,
        grid=(parts + 1,),
        in_specs=[
            whole,
            pl.BlockSpec((count, width), lambda i: (0, jnp.minimum(i, parts - 1))),
            whole,
            whole,
        ],
        out_specs=pl.BlockSpec((1, width, width), lambda i: (i, 0, 0)),
        out_shape=shape_of((parts + 1, width, width)),
        compiler_params=params(),
        cost_estimate=cost(10),
        name="up_out_grad",
    )(normed, hidden_grad, context, branch)


def qkv_grad_kernel(normed_ref, grad_ref, out_ref):
    out_ref[0] = dot(normed_ref[...], grad_ref[...], TN).astype(BF16)


def qkv_grad(normed, grads):
    count, width = normed.shape
    parts = grads.shape[1] // width
    return pl.pallas_call(
        qkv_grad_kernel,
        grid=(parts,),
        in_specs=[fixed((count, width)), pl.BlockSpec((count, width), lambda i: (0, i))],
        out_specs=pl.BlockSpec((1, width, width), lambda i: (i, 0, 0)),
        out_shape=shape_of((parts, width, width)),
        compiler_params=params(),
        cost_estimate=cost(7),
        name="qkv_grad",
    )(normed, grads)


def start_kernel(
    query_grad_ref, key0_ref, key1_ref, far_key0_ref, far_key1_ref, value0_ref, value1_ref, far_value0_ref,
    far_value1_ref, x0_ref, x1_ref, time_ref, middle_grad_ref, gain_ref, weight_ref,
    token0_ref, token1_ref, grads_ref, sums_ref,
):
    step = pl.program_id(0)
    width = x0_ref.shape[1]

    @pl.when(step == 0)
    def _():
        sums_ref[...] = jnp.zeros_like(sums_ref)

    def pick(first, second):
        return jnp.where(step == 0, first[...], second[...])

    query_grad = query_grad_ref[...]
    key_grad = (pick(key0_ref, key1_ref).astype(F32) + pick(far_key0_ref, far_key1_ref).astype(F32)).astype(BF16)
    value_grad = (
        pick(value0_ref, value1_ref).astype(F32) + pick(far_value0_ref, far_value1_ref).astype(F32)
    ).astype(BF16)
    normed_grad = 0.0
    for part, grad in enumerate((query_grad, key_grad, value_grad)):
        columns = slice(part * width, (part + 1) * width)
        grads_ref[:, columns] = grad
        normed_grad = normed_grad + dot(grad, weight_ref[:, columns], NT)
    unit, scale = norm_parts(pick(x0_ref, x1_ref).astype(F32) + wide(time_ref))
    token_grad = middle_grad_ref[...] + norm_backward(normed_grad, wide(gain_ref), unit, scale)

    @pl.when(step == 0)
    def _():
        token0_ref[...] = token_grad.astype(BF16)

    @pl.when(step == 1)
    def _():
        token1_ref[...] = token_grad.astype(BF16)

    sums_ref[0:1] += column_sum(normed_grad * unit)
    sums_ref[1:2] += column_sum(normed_grad)
    sums_ref[2:3] += column_sum(query_grad.astype(F32))
    sums_ref[3:4] += column_sum(value_grad.astype(F32))
    sums_ref[4:5] += column_sum(token_grad)


def start_back(query_grad, key_grads, value_grads, xs, time_row, middle_grad, gain, weight):
    block, width = xs[0].shape
    count = 2 * block
    whole = fixed((block, width))
    row = fixed((1, width))
    kept = pl.BlockSpec((block, width), lambda i: (0, 0))
    return pl.pallas_call(
        start_kernel,
        grid=(2,),
        in_specs=[rows(block, width)]
        + [whole] * 10
        + [row, rows(block, width), row, fixed(weight.shape)],
        out_specs=[kept, kept, rows(block, 3 * width), pl.BlockSpec((8, width), lambda i: (0, 0))],
        out_shape=[
            shape_of((block, width)), shape_of((block, width)), shape_of((count, 3 * width)),
            shape_of((8, width), F32),
        ],
        compiler_params=params(),
        cost_estimate=cost(10),
        name="start_back",
    )(query_grad, *key_grads, *value_grads, *xs, time_row, middle_grad, gain, weight)


class Places:
    def __init__(self, dp, seq):
        self.dp, self.seq = dp, seq
        self.bits = dp.bit_length() - 1

    def flat(self, d, z):
        return d * self.seq + z

    def pairs(self, to):
        return [
            (self.flat(d, z), self.flat(*to(d, z))) for d in range(self.dp) for z in range(self.seq)
        ]

    def gather_order(self, turn):
        def to(d, z):
            core, j = d % 2, (z + turn) % 2
            return d - core + z // 2, 2 * core + j

        return self.pairs(to)

    def scatter_order(self, turn):
        return [(b, a) for a, b in self.gather_order(turn)]

    def swap(self, bit):
        return self.pairs(lambda d, z: (d ^ (1 << bit), z))

    def swap_seq(self, step):
        return self.pairs(lambda d, z: (d, z ^ step))


def send(x, order):
    return lax.ppermute(x, BOTH, order)


def add(a, b):
    return (a.astype(F32) + b.astype(F32)).astype(BF16)


def reduce_parts(parts, places):
    d, z = lax.axis_index("dp"), lax.axis_index("seq")
    count, height, width = parts.shape
    block = height // places.dp
    grid = parts.reshape((count,) + (2,) * places.bits + (block, width))

    def halve(value, bit, axes):
        axis = 1 + axes.index(bit)
        mine = (d >> bit) & 1
        kept = lax.dynamic_index_in_dim(value, mine, axis, keepdims=False)
        sent = lax.dynamic_index_in_dim(value, 1 - mine, axis, keepdims=False)
        axes.remove(bit)
        return add(kept, send(sent, places.swap(bit)))

    axes = list(range(places.bits - 1, -1, -1))
    grid = halve(grid, 0, axes)
    halves = []
    for number, order in enumerate((range(1, places.bits), range(places.bits - 1, 0, -1))):
        at = block // 2
        value = lax.slice_in_dim(grid, number * at, (number + 1) * at, axis=grid.ndim - 2)
        left = list(axes)
        for bit in order:
            value = halve(value, bit, left)
        halves.append(sum_along_seq(value, z, places))
    return jnp.concatenate(halves, 1)


def sum_along_seq(value, z, places):
    count, block, width = value.shape
    mine = z % 2
    grid = value.reshape(count, block, 2, width // 2)
    kept = lax.dynamic_index_in_dim(grid, mine, 2, keepdims=False)
    sent = lax.dynamic_index_in_dim(grid, 1 - mine, 2, keepdims=False)
    half = add(kept, send(sent, places.swap_seq(1)))
    half = add(half, send(half, places.swap_seq(2)))
    other = send(half, places.swap_seq(1))
    first = jnp.where(mine == 0, half, other)
    second = jnp.where(mine == 0, other, half)
    return jnp.concatenate([first, second], 2).astype(F32)


def sum_everywhere(value, places):
    for bit in range(places.bits):
        value = value + send(value, places.swap(bit))
    for step in (1, 2):
        value = value + send(value, places.swap_seq(step))
    return value


def per_device(
    tokens, timesteps, time_table, ln1_gain, ln1_bias, qkv_weight, q_bias, v_bias, out_weight, out_bias,
    ln2_gain, ln2_bias, up_weight, up_bias, down_weight, down_bias, cotangent,
):
    places = Places(lax.axis_size("dp"), lax.axis_size("seq"))
    seq_count, local_len, width = tokens.shape
    hidden_width = up_weight.shape[1]
    assert places.seq == 4 and seq_count == 2 and places.dp == 1 << places.bits
    d, z = lax.axis_index("dp"), lax.axis_index("seq")
    core = d % 2
    total_seqs = seq_count * places.dp
    total_tokens = total_seqs * local_len * places.seq

    def gathered(array):
        blocks = []
        for turn in range(2):
            mine = lax.dynamic_index_in_dim(array, (z + turn) % 2, 0, keepdims=False)
            blocks.append(send(mine, places.gather_order(turn)))
        return blocks

    far_steps = send(timesteps, places.swap(0))
    xs = gathered(tokens)
    cots = gathered(cotangent)
    here = z // 2 == core
    step_value = lax.dynamic_index_in_dim(jnp.where(here, timesteps, far_steps), z % 2, 0, keepdims=False)
    sequence = (d - core + z // 2) * seq_count + z % 2
    time_row = lax.dynamic_slice_in_dim(time_table, step_value, 1, 0)

    def row(v):
        return v.reshape(1, -1)

    bias_all = jnp.concatenate(
        [q_bias.astype(F32), jnp.zeros((width,), F32), v_bias.astype(F32)]
    ).reshape(1, -1)
    count = 2 * local_len
    normed, query, kv0 = project(xs[0], time_row, row(ln1_gain), row(ln1_bias), qkv_weight, bias_all, count)
    far0 = send(kv0, places.swap(0))
    normed, query, kv1 = project(
        xs[1], time_row, row(ln1_gain), row(ln1_bias), qkv_weight, bias_all, count, (normed, query)
    )
    far1 = send(kv1, places.swap(0))
    kvs = [kv0, kv1, far0, far1]
    context, logsum = attend(query, kvs)
    out, active, hidden_grad, normed_two, middle_grad, branch, context_grad, feed_sums = feed(
        context, xs, time_row, cots, out_weight, row(out_bias), row(ln2_gain), row(ln2_bias),
        up_weight, row(up_bias), down_weight, row(down_bias),
    )

    def scattered(blocks, dtype):
        back = [send(block, places.scatter_order(turn)) for turn, block in enumerate(blocks)]
        even = z % 2 == 0
        return jnp.stack(
            [jnp.where(even, back[0], back[1]), jnp.where(even, back[1], back[0])]
        ).astype(dtype)

    parts = hidden_width // width
    bucket = step_value * BUCKETS // TSTEPS
    lane = jnp.arange(width)
    step_row = jnp.where((lane == sequence) & (core == 0), step_value, 0).astype(F32)
    mark = (lane == bucket).astype(F32)
    count_row = jnp.where(lane == BUCKETS + bucket, count / total_tokens, 0.0)
    if places.dp == 8:
        made = back(
            query, context_grad, context, logsum, kvs, normed_two, hidden_grad, branch, active, cots, out
        )
        layer_out = made[6]
        down_sum, up_out_sum = made[7][0].astype(F32), made[8].astype(F32)
        marks = jnp.concatenate([jnp.stack([mark, count_row, step_row]), jnp.zeros((5, width), F32)])
        tokens_grad, qkv_sum, packed = tail(
            made[0], made[1:3], made[3:5], made[5], normed, xs, middle_grad, qkv_weight, time_row, row(ln1_gain),
            feed_sums, marks, total_tokens, parts,
        )
        tokens_grad, qkv_sum = tokens_grad.astype(F32), qkv_sum.astype(F32)
        sums = packed[16:]
    else:
        layer_out = scattered([out[:local_len], out[local_len:]], BF16)
        down_sum = reduce_parts(down_grad(active, cots)[None], places)[0]
        up_out_sum = reduce_parts(up_out_grad(normed_two, hidden_grad, context, branch), places)
        made = attend_back(query, context_grad, context, logsum, kvs)
        token0, token1, projected_grad, start_sums = start_back(
            made[0],
            list(made[1:3]) + [send(g, places.swap(0)) for g in made[3:5]],
            list(made[5:7]) + [send(g, places.swap(0)) for g in made[7:9]],
            xs, time_row, middle_grad, row(ln1_gain), qkv_weight,
        )
        tokens_grad = scattered([token0, token1], F32)
        qkv_sum = reduce_parts(qkv_grad(normed, projected_grad), places)
        energy = jnp.sum(feed_sums[4]) / (width * total_tokens)
        sequence_rows = jnp.where(jnp.arange(total_seqs)[:, None] == sequence, start_sums[4][None], 0.0)
        packed = jnp.concatenate(
            [
                feed_sums[0:4], feed_sums[8 : 8 + parts], start_sums[0:4],
                jnp.stack([mark * energy + count_row, step_row]), sequence_rows,
            ]
        )
        packed = sum_everywhere(packed, places)
        sums = packed[10 + parts :]
    piece = width // places.dp
    mine = lax.dynamic_slice_in_dim(packed[: 8 + parts], d * piece, piece, 1)
    up_piece = hidden_width // places.dp
    up_bias_sum = lax.dynamic_slice_in_dim(packed[4 : 4 + parts].reshape(-1), d * up_piece, up_piece, 0)
    stats = packed[8 + parts]
    steps = packed[9 + parts, :total_seqs].astype(jnp.int32)
    table_rows = time_table.shape[0] // places.dp
    chosen = (steps[None, :] == (jnp.arange(table_rows) + d * table_rows)[:, None]).astype(F32)
    table_grad = jnp.dot(chosen, sums, precision=lax.Precision.HIGHEST)

    def side_by_side(stacked):
        return jnp.moveaxis(stacked, 0, 1).reshape(stacked.shape[1], -1)

    return (
        layer_out,
        tokens_grad,
        table_grad,
        mine[4 + parts],
        mine[5 + parts],
        side_by_side(qkv_sum),
        mine[6 + parts],
        mine[7 + parts],
        up_out_sum[parts],
        mine[3],
        mine[1],
        mine[2],
        side_by_side(up_out_sum[:parts]),
        up_bias_sum,
        down_sum,
        mine[0],
        stats[:BUCKETS],
        stats[BUCKETS : 2 * BUCKETS],
    )


def solution(mesh):
    split = P("dp", "seq", None)
    return jax.shard_map(
        per_device,
        mesh=mesh,
        in_specs=(split, P("dp")) + (P(),) * 14 + (split,),
        out_specs=(
            split, split, P("dp", None), P("dp"), P("dp"), P("dp", None), P("dp"), P("dp"), P("dp", None),
            P("dp"), P("dp"), P("dp"), P("dp", None), P("dp"), P("dp", None), P("dp"), P(), P(),
        ),
        check_vma=False,
    )
```

```python
import functools

import jax
import jax.numpy as jnp
from jax import lax
from jax.experimental import pallas as pl
from jax.experimental.pallas import tpu as pltpu
from jax.sharding import PartitionSpec as P

HEAD_DIM = 64
TSTEPS = 2048
BUCKETS = 4
EPS = 1e-05
LANES = 128
VMEM_BYTES = 56 * 1024 * 1024
BOTH = ("dp", "seq")
TOKEN_PARTS = 8
TOKENS_AHEAD = 6
F32 = jnp.float32
BF16 = jnp.bfloat16
NN = (((1,), (0,)), ((), ()))
NT = (((1,), (1,)), ((), ()))
TN = (((0,), (0,)), ((), ()))


def dot(a, b, dims):
    return lax.dot_general(a, b, dims, preferred_element_type=F32)


def wide(ref):
    return ref[...].astype(F32)


def column_sum(v):
    return jnp.sum(v, 0, keepdims=True)


def fixed(shape):
    return pl.BlockSpec(shape, lambda *i: (0,) * len(shape), pipeline_mode=pl.Buffered(1))


def rows(block, width):
    return pl.BlockSpec((block, width), lambda i: (i, 0))


def shape_of(shape, dtype=BF16):
    return jax.ShapeDtypeStruct(shape, dtype)


def cost(us):
    return pl.CostEstimate(flops=int(us * 1.15e9), bytes_accessed=0, transcendentals=0)


def params():
    return pltpu.CompilerParams(vmem_limit_bytes=VMEM_BYTES)


def norm_parts(v):
    centered = v - jnp.mean(v, -1, keepdims=True)
    scale = lax.rsqrt(jnp.mean(centered * centered, -1, keepdims=True) + EPS)
    return centered * scale, scale


def norm_backward(grad, gain, unit, scale):
    scaled = grad * gain
    return scale * (
        scaled
        - jnp.mean(scaled, -1, keepdims=True)
        - unit * jnp.mean(scaled * unit, -1, keepdims=True)
    )


TIME, MARK, SHARE, STEP = range(4)


def one_row(ref, at):
    return ref[at : at + 1].astype(F32)


def vector(ref):
    return ref[...].astype(F32).reshape(1, -1)


def whole_vector(v):
    return pl.BlockSpec(v.shape, lambda *i: (0,), pipeline_mode=pl.Buffered(1))


def known_rows(step, sequence, share, time_row):
    lane = lax.broadcasted_iota(jnp.int32, time_row.shape, 1)
    bucket = step * BUCKETS // TSTEPS
    return jnp.concatenate(
        [
            time_row,
            jnp.where(lane == bucket, 1.0, 0.0),
            jnp.where(lane == BUCKETS + bucket, share, 0.0),
            jnp.where(lane == sequence, step.astype(F32), 0.0),
        ],
        0,
    )


def project_rows(x, info_ref, small, weight_ref):
    width = x.shape[1]
    gain, shift, query_bias, value_bias = small
    unit, _ = norm_parts(x.astype(F32) + one_row(info_ref, TIME))
    normed = (unit * vector(gain) + vector(shift)).astype(BF16)

    def part(number):
        made = dot(normed, weight_ref[:, number * width : (number + 1) * width], NN)
        if number != 1:
            made = made + vector(query_bias if number == 0 else value_bias)
        made = made.astype(BF16)
        return made * jnp.asarray(HEAD_DIM ** (-0.5), BF16) if number == 0 else made

    return normed, part


def project_kernel(x_ref, info_ref, weight_ref, *refs):
    normed_ref, query_ref, kv_ref = refs[-3:]
    width = x_ref.shape[1]
    normed, part = project_rows(x_ref[...], info_ref, refs[:4], weight_ref)
    normed_ref[...] = normed
    query_ref[...] = part(0)
    kv_ref[:, :width] = part(1)
    kv_ref[:, width:] = part(2)


def project(x, info, small, weight, total, begun=None, block=256):
    count, width = x.shape
    first = 0 if begun is None else total // block - count // block
    later = pl.BlockSpec((block, width), lambda i: (i + first, 0))
    extra = [] if begun is None else list(begun)
    return pl.pallas_call(
        project_kernel,
        grid=(count // block,),
        in_specs=[rows(block, width), fixed(info.shape), fixed(weight.shape)]
        + [whole_vector(v) for v in small]
        + [pl.BlockSpec(memory_space=pl.ANY)] * len(extra),
        out_specs=[later, later, rows(block, 2 * width)],
        out_shape=[
            shape_of((total, width)),
            shape_of((total, width)),
            shape_of((count, 2 * width)),
        ],
        input_output_aliases={7: 0, 8: 1} if extra else {},
        compiler_params=params(),
        cost_estimate=cost(5),
        name="project",
    )(x, info, weight, *small, *extra)


def lane_parts():
    lane = lax.broadcasted_iota(jnp.int32, (1, LANES), 1)
    return lane < HEAD_DIM, lane % HEAD_DIM


def with_offset(own, place, base, offset):
    high = offset.astype(BF16)
    left = offset - high.astype(F32)
    mid = left.astype(BF16)
    low = (left - mid.astype(F32)).astype(BF16)
    zero = jnp.zeros_like(low)
    parts = jnp.where(place == 0, high, jnp.where(place == 1, mid, jnp.where(place == 2, low, zero)))
    return jnp.where(own, base, parts)


def attend_kernel(query_ref, *refs, pieces):
    key_refs, value_refs = refs[:pieces], refs[pieces : 2 * pieces]
    context_ref, logsum_ref = refs[2 * pieces :]
    count = query_ref.shape[0]
    low, place = lane_parts()
    row_half = lax.broadcasted_iota(jnp.int32, (LANES, LANES), 0) // HEAD_DIM
    lane_half = lax.broadcasted_iota(jnp.int32, (LANES, LANES), 1) // HEAD_DIM
    swapped = jnp.where(row_half != lane_half, 1.0, 0.0).astype(BF16)
    query = query_ref[...]

    def norms(v):
        v = v.astype(F32)
        return dot((v * v).astype(BF16), swapped, NN)

    key_norm = functools.reduce(
        jnp.maximum, [jnp.max(norms(ref[...]), 0, keepdims=True) for ref in key_refs]
    )
    bound = jnp.sqrt(norms(query) * key_norm) * 1.01
    ones_key = jnp.where(place < 3, 1.0, 0.0).astype(BF16)
    values = [ref[...].T for ref in value_refs]
    ones = jnp.ones((16, value_refs[0].shape[0]), BF16)

    def value_of(piece, head):
        return jnp.concatenate([values[piece][head * HEAD_DIM : (head + 1) * HEAD_DIM], ones], 0)

    def finish(mixed, offset):
        totals = [m[HEAD_DIM : HEAD_DIM + 1] for m in mixed]
        context = jnp.concatenate([m[:HEAD_DIM] / t for m, t in zip(mixed, totals)], 0)
        context_ref[...] = context.T.astype(BF16)
        logs = [jnp.broadcast_to(jnp.log(t), (HEAD_DIM, count)) for t in reversed(totals)]
        logsum_ref[...] = jnp.concatenate(logs, 0).T + offset

    mixed = []
    for head in range(2):
        own = low if head == 0 else ~low
        query_own = with_offset(own, place, query, -bound)
        out = 0.0
        for piece in range(pieces):
            key_own = jnp.where(own, key_refs[piece][...], ones_key)
            weights = jnp.exp(dot(key_own, query_own, NT)).astype(BF16)
            out = out + dot(value_of(piece, head), weights, NN)
        mixed.append(out)
    finish(mixed, bound)
    smallest = jnp.min(jnp.minimum(mixed[0][HEAD_DIM], mixed[1][HEAD_DIM]))

    @pl.when(smallest < 1e-25)
    def _():
        again, tops = [], []
        for head in range(2):
            own = low if head == 0 else ~low
            query_own = jnp.where(own, query, jnp.zeros_like(query))
            top = jnp.full((1, count), -jnp.inf, F32)
            for piece in range(pieces):
                scores = dot(key_refs[piece][...], query_own, NT)
                top = jnp.maximum(top, jnp.max(scores, 0, keepdims=True))
            out = 0.0
            for piece in range(pieces):
                scores = dot(key_refs[piece][...], query_own, NT)
                out = out + dot(value_of(piece, head), jnp.exp(scores - top).astype(BF16), NN)
            again.append(out)
            tops.append(jnp.broadcast_to(top, (HEAD_DIM, count)))
        finish(again, jnp.concatenate(tops[::-1], 0).T)


def attend(query, kvs):
    count, width = query.shape
    pairs, pieces, length = width // LANES, len(kvs), kvs[0].shape[0]
    row = pl.BlockSpec((count, LANES), lambda p: (0, p))
    return pl.pallas_call(
        functools.partial(attend_kernel, pieces=pieces),
        grid=(pairs,),
        in_specs=[row]
        + [pl.BlockSpec((length, LANES), lambda p: (0, p))] * pieces
        + [pl.BlockSpec((length, LANES), lambda p: (0, pairs + p))] * pieces,
        out_specs=[row, row],
        out_shape=[shape_of((count, width)), shape_of((count, width), F32)],
        compiler_params=params(),
        cost_estimate=cost(32),
        name="attend",
    )(query, *kvs, *kvs)


def attend_back_step(query_ref, grad_ref, context_ref, logsum_ref, pieces, query_grad_ref):
    low, place = lane_parts()
    query, grad = query_ref[...], grad_ref[...]
    count = query.shape[0]
    product = grad.astype(F32) * wide(context_ref)
    logsum = logsum_ref[...]
    ones_key = jnp.where(place < 3, 1.0, 0.0).astype(BF16)
    zero = jnp.zeros_like(query)
    heads = []
    for head in range(2):
        own = low if head == 0 else ~low
        inner = jnp.sum(jnp.where(own, product, 0.0), -1, keepdims=True)
        heads.append(
            (
                own,
                with_offset(own, place, query, -logsum),
                with_offset(own, place, grad, jnp.broadcast_to(-inner, logsum.shape)),
                jnp.where(own, query, zero),
                jnp.where(own, grad, zero),
            )
        )
    length = sum(piece[0].shape[0] for piece in pieces)
    query_grads = [0.0, 0.0]
    key_mean = 0.0
    for key_ref, value_ref, key_grad_ref, value_grad_ref, before in pieces:
        if before is not None:
            before()
        key, value = key_ref[...], value_ref[...]
        key_turned = key.T
        key_mean = key_mean + jnp.sum(key_turned.astype(F32), 1, keepdims=True) / length
        ones = jnp.ones((16, key.shape[0]), BF16)
        key_grad, value_grad = 0.0, 0.0
        for head, (own, query_off, grad_off, query_own, grad_own) in enumerate(heads):
            scores = dot(jnp.where(own, key, ones_key), query_off, NT)
            probs = jnp.exp(scores)
            prob_grad = dot(jnp.where(own, value, ones_key), grad_off, NT)
            score_grad = (probs * prob_grad).astype(BF16)
            value_grad = value_grad + dot(probs.astype(BF16), grad_own, NN)
            key_grad = key_grad + dot(score_grad, query_own, NN)
            lanes = slice(head * HEAD_DIM, (head + 1) * HEAD_DIM)
            turned = jnp.concatenate([key_turned[lanes], ones], 0)
            query_grads[head] = query_grads[head] + dot(turned, score_grad, NN)
        key_grad_ref[...] = key_grad.astype(BF16)
        value_grad_ref[...] = value_grad.astype(BF16)
    parts = [
        made[:HEAD_DIM]
        - key_mean[head * HEAD_DIM : (head + 1) * HEAD_DIM]
        * jnp.broadcast_to(made[HEAD_DIM : HEAD_DIM + 1], (HEAD_DIM, count))
        for head, made in enumerate(query_grads)
    ]
    query_grad_ref[...] = (jnp.concatenate(parts, 0) * HEAD_DIM ** (-0.5)).T.astype(BF16)


def attend_back_kernel(query_ref, grad_ref, context_ref, logsum_ref, *refs, pieces):
    key_refs, value_refs = refs[:pieces], refs[pieces : 2 * pieces]
    query_grad_ref = refs[2 * pieces]
    key_grad_refs = refs[2 * pieces + 1 : 3 * pieces + 1]
    value_grad_refs = refs[3 * pieces + 1 :]
    steps = list(zip(key_refs, value_refs, key_grad_refs, value_grad_refs, [None] * pieces))
    attend_back_step(query_ref, grad_ref, context_ref, logsum_ref, steps, query_grad_ref)


def attend_back(query, grad, context, logsum, kvs):
    count, width = query.shape
    pairs, pieces, length = width // LANES, len(kvs), kvs[0].shape[0]
    row = pl.BlockSpec((count, LANES), lambda p: (0, p))
    piece = pl.BlockSpec((length, LANES), lambda p: (0, p))
    return pl.pallas_call(
        functools.partial(attend_back_kernel, pieces=pieces),
        grid=(pairs,),
        in_specs=[row] * 4
        + [piece] * pieces
        + [pl.BlockSpec((length, LANES), lambda p: (0, pairs + p))] * pieces,
        out_specs=[row] + [piece] * (2 * pieces),
        out_shape=[shape_of((count, width))] + [shape_of((length, width))] * (2 * pieces),
        compiler_params=params(),
        cost_estimate=cost(75),
        name="attend_back",
    )(query, grad, context, logsum, *kvs, *kvs)


def here():
    d, z = lax.axis_index("dp"), lax.axis_index("seq")
    return d, z, d // 4, (d // 2) % 2, d % 2


def partners():
    d, z, y, x, core = here()
    return {
        "core": (d + 1 - 2 * core, z),
        "x": (d + 2 - 4 * x, z),
        "y": (d + 4 - 8 * y, z),
        "near": (d, z + 1 - 2 * (z % 2)),
        "far": (d, (z + 2) % 4),
    }


def remote(source, target, sends, receives, send_index, receive_index, device):
    return pltpu.make_async_remote_copy(
        src_ref=source,
        dst_ref=target,
        send_sem=sends.at[send_index],
        recv_sem=receives.at[receive_index],
        device_id=device,
        device_id_type=pl.DeviceIdType.MESH,
    )


class Reduction:
    def __init__(self, source, out, scratch):
        self.source, self.out = source, out
        self.own = source.at[:, :, :, here()[4]]
        self.from_core, self.first, self.second, self.near, self.far, self.other = scratch[:6]
        self.sends, self.receives, self.local = scratch[6:9]
        self.parts, _, _, self.rows, self.width = self.from_core.shape
        self.half, self.top = self.width // 2, self.rows // 2

    @staticmethod
    def scratch(parts, block, width):
        half, top = width // 2, block // 2
        return [
            pltpu.VMEM((parts, 2, 2, block, width), BF16),
            pltpu.VMEM((2, parts, 2, block, half), BF16),
            pltpu.VMEM((2, parts, block, half), BF16),
            pltpu.VMEM((parts, top, width), BF16),
            pltpu.VMEM((parts, top, width), BF16),
            pltpu.VMEM((parts, top, width), BF16),
            pltpu.SemaphoreType.DMA((8,)),
            pltpu.SemaphoreType.DMA((8,)),
            pltpu.SemaphoreType.DMA((2,)),
        ]

    def copy(self, number):
        d, z, y, x, core = here()
        to = partners()
        left, right = pl.ds(0, self.half), pl.ds(self.half, self.half)
        kept = pl.ds(pl.multiple_of((z % 2) * self.top, self.top), self.top)
        given = pl.ds(pl.multiple_of((1 - z % 2) * self.top, self.top), self.top)
        source, target, device = (
            lambda: (self.source.at[:, :, :, 1 - core], self.from_core, to["core"]),
            lambda: (self.own.at[:, :, 1 - x, :, left], self.first.at[0], to["x"]),
            lambda: (self.own.at[:, 1 - y, :, :, right], self.first.at[1], to["y"]),
            lambda: (self.own.at[:, 1 - y, x, :, left], self.second.at[0], to["y"]),
            lambda: (self.own.at[:, y, 1 - x, :, right], self.second.at[1], to["x"]),
            lambda: (self.own.at[:, y, x, given], self.near, to["near"]),
            lambda: (self.own.at[:, y, x, kept], self.far, to["far"]),
            lambda: (self.own.at[:, y, x, kept], self.other, to["near"]),
        )[number]()
        return remote(source, target, self.sends, self.receives, number, number, device)

    def to_cores(self):
        self.copy(0).start()

    def to_first(self):
        self.copy(0).wait()
        for part in range(self.parts):
            for i in range(2):
                for j in range(2):
                    self.own[part, i, j] = self.own[part, i, j] + self.from_core[part, i, j]
        self.copy(1).start()
        self.copy(2).start()

    def to_second(self):
        _, _, y, x, _ = here()
        self.copy(1).wait()
        self.copy(2).wait()
        left, right = slice(0, self.half), slice(self.half, self.width)
        for part in range(self.parts):
            for i in range(2):
                self.own[part, i, x, :, left] = self.own[part, i, x, :, left] + self.first[0, part, i]
                self.own[part, y, i, :, right] = self.own[part, y, i, :, right] + self.first[1, part, i]
        self.copy(3).start()
        self.copy(4).start()

    def to_near(self):
        _, _, y, x, _ = here()
        self.copy(3).wait()
        self.copy(4).wait()
        left, right = slice(0, self.half), slice(self.half, self.width)
        for part in range(self.parts):
            self.own[part, y, x, :, left] = self.own[part, y, x, :, left] + self.second[0, part]
            self.own[part, y, x, :, right] = self.own[part, y, x, :, right] + self.second[1, part]
        self.copy(5).start()

    def add_rows(self, received):
        _, z, y, x, _ = here()
        kept = pl.ds(pl.multiple_of((z % 2) * self.top, self.top), self.top)
        for part in range(self.parts):
            self.own[part, y, x, kept] = self.own[part, y, x, kept] + received[part]

    def to_far(self):
        self.copy(5).wait()
        self.add_rows(self.near)
        self.copy(6).start()

    def to_other(self):
        self.copy(6).wait()
        self.add_rows(self.far)
        self.copy(7).start()

    def stores(self):
        _, z, y, x, _ = here()
        kept = pl.ds(pl.multiple_of((z % 2) * self.top, self.top), self.top)
        given = pl.ds(pl.multiple_of((1 - z % 2) * self.top, self.top), self.top)
        return (
            pltpu.make_async_copy(self.own.at[:, y, x, kept], self.out.at[:, kept], self.local.at[0]),
            pltpu.make_async_copy(self.other, self.out.at[:, given], self.local.at[1]),
        )

    def to_out(self):
        self.copy(7).wait()
        for copy in self.stores():
            copy.start()

    def finish(self):
        for copy in self.stores():
            copy.wait()


class Trade:
    def __init__(self, out, sends, receives, local, gather=False, parts=1):
        self.out, self.sends, self.receives, self.local = out, sends, receives, local
        self.gather, self.parts = gather, parts

    @staticmethod
    def semaphores(parts=1):
        return [pltpu.SemaphoreType.DMA((2, parts)), pltpu.SemaphoreType.DMA((2, parts)), pltpu.SemaphoreType.DMA((parts,))]

    def device(self, p):
        d, z, _, _, core = here()
        return (d - core + z // 2, 2 * core + (z + p) % 2)

    def stays(self):
        _, z, _, _, core = here()
        return z // 2 == core

    def slot(self, p):
        return p if self.gather else lax.axis_index("seq") % 2

    def own_slot(self, p):
        return p if self.gather else (lax.axis_index("seq") + p) % 2

    def greet(self, barrier):
        @pl.when(jnp.logical_not(self.stays()))
        def _():
            pl.semaphore_signal(barrier, inc=1, device_id=self.device(0), device_id_type=pl.DeviceIdType.MESH)

        pl.semaphore_signal(barrier, inc=1, device_id=self.device(1), device_id_type=pl.DeviceIdType.MESH)
        return jnp.where(self.stays(), 1, 2)

    def rows(self, ref, part):
        many = ref.shape[0] // self.parts
        return ref.at[pl.ds(part * many, many)]

    def keep(self, block, part):
        return pltpu.make_async_copy(
            self.rows(block, part), self.rows(self.out.at[self.own_slot(0)], part), self.local.at[part]
        )

    def copy(self, p, block, part):
        slot = self.slot(p)
        return pltpu.make_async_remote_copy(
            src_ref=self.rows(block, part),
            dst_ref=self.rows(self.out.at[slot], part),
            send_sem=self.sends.at[p, part],
            recv_sem=self.receives.at[slot, part],
            device_id=self.device(p),
            device_id_type=pl.DeviceIdType.MESH,
        )

    def each(self, p, far, near):
        if p == 1:
            far()
            return
        pl.when(jnp.logical_not(self.stays()))(far)
        pl.when(self.stays())(near)

    def begin(self, p, block, part=0):
        self.each(p, lambda: self.copy(p, block, part).start(), lambda: self.keep(block, part).start())

    def sent(self, p, block, part=0):
        self.each(p, lambda: self.copy(p, block, part).wait_send(), lambda: None)

    def arrived(self, p, block, part=0):
        slot = self.own_slot(p)
        target = self.rows(self.out.at[slot], part)

        def far():
            pltpu.make_async_remote_copy(
                src_ref=target,
                dst_ref=target,
                send_sem=self.sends.at[p, part],
                recv_sem=self.receives.at[slot, part],
                device_id=self.device(p),
                device_id_type=pl.DeviceIdType.MESH,
            ).wait_recv()

        self.each(p, far, lambda: self.keep(block, part).wait())


def meet(names, *trades):
    barrier = pltpu.get_barrier_semaphore()
    to = partners()
    for name in names:
        pl.semaphore_signal(barrier, inc=1, device_id=to[name], device_id_type=pl.DeviceIdType.MESH)
    expected = len(names)
    for one in trades:
        expected = expected + one.greet(barrier)
    pl.semaphore_wait(barrier, expected)


def front_kernel(
    tokens, weight, table, steps_ref, gain, shift, query_bias, value_bias,
    x0_out, x1_out, normed_out, query_out, near0_out, near1_out, far0_out, far1_out, info_out,
    x_v, weight_v, table_v, info_here, info_in, normed_v, query_v, near_v, far_v,
    load, stores, info_sends, info_receives, sends, receives, *trade, share,
):
    d, z, _, _, core = here()
    block, width = x_v.shape[1:]
    small = (gain, shift, query_bias, value_bias)
    trade = Trade(x_v, *trade, gather=True)
    loaded = pltpu.make_async_copy(weight, weight_v, load.at[0])
    looked_up = pltpu.make_async_copy(table, table_v, load.at[1])
    meet(("core",), trade)
    held = [tokens.at[(z + p) % 2] for p in range(2)]
    for p in range(2):
        trade.begin(p, held[p])
    looked_up.start()
    loaded.start()
    steps = [steps_ref[j] for j in range(2)]
    row = lax.broadcasted_iota(jnp.int32, (16, table.shape[0]), 0)
    place = lax.broadcasted_iota(jnp.int32, (16, table.shape[0]), 1)
    wanted = jnp.where(row == 0, steps[0], jnp.where(row == 1, steps[1], -1))
    chosen = jnp.where(place == wanted, 1.0, 0.0).astype(BF16)
    looked_up.wait()
    time_rows = dot(chosen, table_v[...], NN)
    for j in range(2):
        info_here[4 * j : 4 * j + 4] = known_rows(steps[j], 2 * d + j, share, time_rows[j : j + 1])
    known = remote(info_here, info_in, info_sends, info_receives, 0, 0, partners()["core"])
    known.start()
    known.wait()
    mine = jnp.where(z // 2 == core, info_here[...], info_in[...])
    info_out[0:4] = jnp.where(z % 2 == 0, mine[0:4], mine[4:8])
    info_out[4:8] = jnp.zeros_like(info_in[4:8])
    loaded.wait()
    copies, moved = [], []
    for p in range(2):
        trade.arrived(p, held[p])
        normed, part = project_rows(x_v[p], info_out, small, weight_v)
        near_v[p, :, :width] = part(1)
        near_v[p, :, width:] = part(2)
        moved.append(remote(near_v.at[p], far_v.at[p], sends, receives, p, p, partners()["core"]))
        moved[p].start()
        normed_v[p] = normed
        query_v[p] = part(0)
        outs = (x0_out, x1_out)[p], (near0_out, near1_out)[p]
        here_rows = pl.ds(p * block, block)
        for number, (source, target) in enumerate(
            (
                (x_v.at[p], outs[0]), (normed_v.at[p], normed_out.at[here_rows]),
                (query_v.at[p], query_out.at[here_rows]), (near_v.at[p], outs[1]),
            )
        ):
            copies.append(pltpu.make_async_copy(source, target, stores.at[p, number]))
            copies[-1].start()
    for p in range(2):
        moved[p].wait()
        copies.append(pltpu.make_async_copy(far_v.at[p], (far0_out, far1_out)[p], stores.at[p, 4]))
        copies[-1].start()
    for p in range(2):
        trade.sent(p, held[p])
    for copy in copies:
        copy.wait()


def front(tokens, weight, table, steps, small, share):
    _, block, width = tokens.shape
    info_shape = (8, width)
    any_spec = pl.BlockSpec(memory_space=pl.ANY)
    inside = pl.BlockSpec(memory_space=pltpu.VMEM)
    pair = pltpu.VMEM((2, block, width), BF16)
    wide_pair = pltpu.VMEM((2, block, 2 * width), BF16)
    one = pltpu.SemaphoreType.DMA((1,))
    two = pltpu.SemaphoreType.DMA((2,))
    return pl.pallas_call(
        functools.partial(front_kernel, share=share),
        in_specs=[any_spec] * 3 + [pl.BlockSpec(memory_space=pltpu.SMEM)] + [inside] * 4,
        out_specs=[any_spec] * 8 + [inside],
        out_shape=[shape_of((block, width))] * 2
        + [shape_of((2 * block, width))] * 2
        + [shape_of((block, 2 * width))] * 4
        + [shape_of(info_shape, F32)],
        scratch_shapes=[
            pair, pltpu.VMEM(weight.shape, BF16), pltpu.VMEM(table.shape, BF16), pltpu.VMEM(info_shape, F32),
            pltpu.VMEM(info_shape, F32), pair, pair, wide_pair, wide_pair,
            two, pltpu.SemaphoreType.DMA((2, 5)), one, one, two, two,
        ]
        + Trade.semaphores(),
        compiler_params=pltpu.CompilerParams(
            vmem_limit_bytes=VMEM_BYTES, collective_id=2, has_side_effects=True
        ),
        cost_estimate=cost(48),
        name="front",
    )(tokens, weight, table, steps, *small)


def fixed_any():
    return pl.BlockSpec(memory_space=pl.ANY)


def back_kernel(
    query_ref, grad_ref, context_ref, logsum_ref, *refs, pieces, parts
):
    key_refs, value_refs = refs[:pieces], refs[pieces : 2 * pieces]
    refs = refs[2 * pieces :]
    normed_ref, hidden_grad_ref, whole_context_ref, branch_ref, active_ref, cot0_ref, cot1_ref, layer_ref = refs[:8]
    refs = refs[8:]
    near = pieces // 2
    query_grad_ref = refs[0]
    key_grad_refs, value_grad_refs = refs[1 : 1 + near], refs[1 + near : 1 + 2 * near]
    far_out, layer_out, down_out, up_out = refs[1 + 2 * near : 5 + 2 * near]
    refs = refs[5 + 2 * near :]
    down_parts, up_parts = refs[:2]
    chunks = []
    for number, (which, at, many) in enumerate(back_chunks(down_parts.shape, up_parts.shape)):
        scratch = refs[2 + 9 * number : 11 + 9 * number]
        if which == "down":
            here_rows = pl.ds(at, many)
            chunks.append(
                Reduction(down_parts.at[:, :, :, :, here_rows], down_out.at[:, here_rows], scratch)
            )
        else:
            here_parts = pl.ds(at, many)
            chunks.append(Reduction(up_parts.at[here_parts], up_out.at[here_parts], scratch))
    one, two, three, four = chunks
    far_grads, far_sends, far_receives = refs[38:41]
    back = Trade(layer_out, *refs[41:])
    block = key_refs[0].shape[0]
    layer_blocks = [layer_ref.at[pl.ds(p * block, block)] for p in range(2)]
    step = pl.program_id(0)
    made = 2 * parts + 1
    pair, last = step - made, pl.num_programs(0) - 1

    def far_copy(which):
        return remote(
            far_grads, far_out.at[which], far_sends, far_receives, 0, which, partners()["core"]
        )

    def begin():
        meet(("core", "x", "y", "near", "far"), back)
        back.begin(0, layer_blocks[0])
        back.begin(1, layer_blocks[1])

    plan = {
        (0, 0): [begin],
        (2, 0): [one.to_cores],
        (4, 0): [one.to_first],
        (5, 0): [two.to_cores],
        (8, 0): [one.to_second, two.to_first],
        (9, 0): [three.to_cores, four.to_cores],
        (10, 0): [one.to_near],
        (10, 1): [two.to_second, three.to_first],
        (10, 3): [one.to_far],
        (11, 0): [four.to_first],
        (11, 2): [one.to_other, two.to_near, three.to_second],
        (12, 0): [one.to_out, two.to_far],
        (12, 1): [three.to_near],
        (12, 2): [four.to_second],
        (12, 3): [three.to_far],
        (13, 0): [two.to_other],
        (13, 1): [four.to_near],
        (13, 2): [three.to_other],
        (13, 3): [two.to_out, four.to_far],
        (14, 0): [three.to_out],
        (14, 1): [four.to_other],
        (14, 3): [four.to_out],
    }

    def run_plan(place, steps):
        for (at, where), actions in plan.items():
            if where == place and at in steps:

                @pl.when(step == at)
                def _():
                    for action in actions:
                        action()

    run_plan(0, range(made))

    @pl.when(step < parts)
    def _():
        part = dot(normed_ref[...], hidden_grad_ref[...], TN).astype(BF16)
        up_parts[step] = part.reshape(up_parts.shape[1:])

    @pl.when(step == parts)
    def _():
        part = dot(whole_context_ref[...], branch_ref[...], TN).astype(BF16)
        up_parts[parts] = part.reshape(up_parts.shape[1:])

    @pl.when((step > parts) & (step < made))
    def _():
        part = dot(active_ref[:block], cot0_ref[...], TN) + dot(active_ref[block:], cot1_ref[...], TN)
        part = part.astype(BF16).reshape(down_parts.shape[3:])
        at = step - parts - 1
        down_parts[0, at // 2, at % 2] = part

    def before(place):
        def run():
            run_plan(place, range(made, 100))
            if place == 0:

                @pl.when(pair > 0)
                def _():
                    far_copy(pair - 1).wait_send()

            if place == near:
                far_copy(pair).start()

        return run

    @pl.when(step >= made)
    def _():
        order = []
        for i in range(near):
            far_rows = pl.ds(i * block, block)
            order.append(
                (key_refs[near + i], value_refs[near + i], far_grads.at[0, far_rows], far_grads.at[1, far_rows])
            )
        for i in range(near):
            order.append((key_refs[i], value_refs[i], key_grad_refs[i], value_grad_refs[i]))
        steps = [one_piece + (before(place),) for place, one_piece in enumerate(order)]
        attend_back_step(query_ref, grad_ref, context_ref, logsum_ref, steps, query_grad_ref)

    @pl.when(step == last)
    def _():
        far_copy(pair).wait_send()

        def received(which, carry):
            far_copy(which).wait_recv()
            return carry

        lax.fori_loop(0, last + 1 - made, received, 0)
        for p in range(2):
            back.sent(p, layer_blocks[p])
            back.arrived(p, layer_blocks[p])
        for chunk in chunks:
            chunk.finish()


def back_chunks(down_shape, up_shape):
    block, parts = down_shape[-2], up_shape[0]
    return [
        ("up", 0, parts // 2),
        ("up", parts // 2, parts - parts // 2),
        ("down", 0, block // 2),
        ("down", block // 2, block // 2),
    ]


def back(query, grad, context, logsum, kvs, normed, hidden_grad, branch, active, cots, layer_out):
    count, width = query.shape
    pairs, pieces, length = width // LANES, len(kvs), kvs[0].shape[0]
    near = pieces // 2
    parts = hidden_grad.shape[1] // width
    made = 2 * parts + 1
    pair = lambda i: jnp.maximum(i - made, 0)
    row = pl.BlockSpec((count, LANES), lambda i: (0, pair(i)))
    piece = pl.BlockSpec((length, LANES), lambda i: (0, pair(i)))
    value = pl.BlockSpec((length, LANES), lambda i: (0, pairs + pair(i)))
    whole = fixed((count, width))
    up_rows, down_rows = width // 8, hidden_grad.shape[1] // 8
    down_shape, up_shape = (1, 2, 2, 2, down_rows, width), (parts + 1, 2, 2, 2, up_rows, width)
    return pl.pallas_call(
        functools.partial(back_kernel, pieces=pieces, parts=parts),
        grid=(made + pairs,),
        in_specs=[row] * 4
        + [piece] * pieces
        + [value] * pieces
        + [
            whole,
            pl.BlockSpec((count, width), lambda i: (0, jnp.minimum(i, parts - 1))),
            whole,
            whole,
            pl.BlockSpec((count, width), lambda i: (0, jnp.clip(i - parts - 1, 0, parts - 1))),
            fixed((length, width)),
            fixed((length, width)),
            fixed_any(),
        ],
        out_specs=[row] + [piece] * (2 * near) + [fixed_any()] * 4,
        out_shape=[shape_of((count, width))]
        + [shape_of((length, width))] * (2 * near)
        + [shape_of((pairs, 2, near * length, LANES)), shape_of((2, length, width))]
        + [shape_of((1, down_rows, width)), shape_of((parts + 1, up_rows, width))],
        scratch_shapes=[pltpu.VMEM(down_shape, BF16), pltpu.VMEM(up_shape, BF16)]
        + [
            shape
            for which, _, many in back_chunks(down_shape, up_shape)
            for shape in Reduction.scratch(*((1, many) if which == "down" else (many, up_rows)), width)
        ]
        + [
            pltpu.VMEM((2, near * length, LANES), BF16),
            pltpu.SemaphoreType.DMA((1,)),
            pltpu.SemaphoreType.DMA((pairs,)),
        ]
        + Trade.semaphores(),
        compiler_params=pltpu.CompilerParams(
            vmem_limit_bytes=VMEM_BYTES, collective_id=0, has_side_effects=True
        ),
        cost_estimate=cost(100),
        name="back",
    )(
        query, grad, context, logsum, *kvs, *kvs, normed, hidden_grad, context, branch, active, *cots, layer_out
    )


def tail_kernel(
    query_grad, key0, key1, value0, value1, far, normed, x0, x1, middle_grad, weight,
    info_ref, gain_ref, feed_ref,
    tokens_out, qkv_out, sums_ref,
    query_v, near_v, far_v, normed_v, x_v, middle_v, weight_v, key_v, value_v, token_v,
    query_parts, key_parts, value_parts, *refs, total_tokens, parts,
):
    reductions = []
    for number, made in enumerate((query_parts, key_parts, value_parts)):
        reductions.append(Reduction(made, qkv_out.at[pl.ds(number, 1)], refs[9 * number : 9 * number + 9]))
    of_query, of_key, of_value = reductions
    sums_in, sums_sends, sums_receives, loads = refs[27:31]
    back = Trade(tokens_out, *refs[31:], parts=TOKEN_PARTS)
    block, width = x0.shape
    pairs = width // LANES
    d, z, _, _, core = here()
    copies = [
        pltpu.make_async_copy(source, target, loads.at[number])
        for number, (source, target) in enumerate(
            (
                (normed, normed_v), (query_grad, query_v), (key0, near_v.at[0, 0]), (value0, near_v.at[1, 0]),
                (far, far_v), (weight, weight_v), (x0, x_v.at[0]), (middle_grad, middle_v),
                (key1, near_v.at[0, 1]), (value1, near_v.at[1, 1]), (x1, x_v.at[1]),
            )
        )
    ]
    for copy in copies:
        copy.start()
    meet(("core", "x", "y", "near", "far"), back)

    def product(grads, out):
        out[0] = dot(normed_v[...], grads[...], TN).astype(BF16).reshape(out.shape[1:])

    def start_block(p):
        held = pl.ds(p * block, block)
        for pair in range(pairs):
            lanes = slice(pair * LANES, (pair + 1) * LANES)
            key_v[held, lanes] = near_v[0, p, :, lanes] + far_v[pair, 0, held]
            value_v[held, lanes] = near_v[1, p, :, lanes] + far_v[pair, 1, held]
        normed_grad = 0.0
        for part, grads in enumerate((query_v, key_v, value_v)):
            columns = slice(part * width, (part + 1) * width)
            normed_grad = normed_grad + dot(grads[held], weight_v[:, columns], NT)
        unit, scale = norm_parts(x_v[p].astype(F32) + one_row(info_ref, TIME))
        token_grad = middle_v[held] + norm_backward(normed_grad, vector(gain_ref), unit, scale)
        token_v[p] = token_grad.astype(BF16)
        return [
            column_sum(normed_grad * unit),
            column_sum(normed_grad),
            column_sum(query_v[held].astype(F32)),
            column_sum(value_v[held].astype(F32)),
            column_sum(token_grad),
        ]

    def sums_copy(number):
        to = partners()[("core", "x", "y", "near", "far")[number]]
        return remote(sums_ref, sums_in.at[number], sums_sends, sums_receives, number, number, to)

    def sums_next(number):
        sums_copy(number).wait()
        sums_ref[...] = sums_ref[...] + sums_in[number]
        if number < 4:
            sums_copy(number + 1).start()

    def move(number):
        if number >= TOKENS_AHEAD:
            p, part = divmod(number - TOKENS_AHEAD, TOKEN_PARTS)
            back.sent(p, token_v.at[p], part)
        p, part = divmod(number, TOKEN_PARTS)
        back.begin(p, token_v.at[p], part)

    for copy in copies[1:8]:
        copy.wait()
    first = start_block(0)
    for number in range(4):
        move(number)
    for copy in copies[8:]:
        copy.wait()
    second = start_block(1)
    sums = [a + b for a, b in zip(first, second)]
    sums_ref[...] = jnp.zeros_like(sums_ref)
    sums_ref[0:4] = feed_ref[0:4]
    sums_ref[4 : 4 + parts] = feed_ref[8 : 8 + parts]
    for number in range(4):
        sums_ref[4 + parts + number : 5 + parts + number] = sums[number]
    energy = jnp.sum(feed_ref[4:5], keepdims=True) / (width * total_tokens)
    sums_ref[8 + parts : 9 + parts] = info_ref[MARK : MARK + 1] * energy + info_ref[SHARE : SHARE + 1]
    sums_ref[9 + parts : 10 + parts] = info_ref[STEP : STEP + 1] * jnp.where(core == 0, 1.0, 0.0)
    sequence = (d - core + z // 2) * 2 + z % 2
    sums_ref[pl.ds(16 + sequence, 1)] = sums[4]
    sums_copy(0).start()
    move(4)
    move(5)
    copies[0].wait()
    product(query_v, query_parts)
    of_query.to_cores()
    move(6)
    product(key_v, key_parts)
    of_key.to_cores()
    sums_next(0)
    move(7)
    of_query.to_first()
    product(value_v, value_parts)
    of_value.to_cores()
    sums_next(1)
    move(8)
    of_key.to_first()
    move(9)
    of_query.to_second()
    sums_next(2)
    move(10)
    of_value.to_first()
    move(11)
    of_key.to_second()
    of_query.to_near()
    sums_next(3)
    move(12)
    of_query.to_far()
    of_value.to_second()
    sums_next(4)
    of_key.to_near()
    move(13)
    of_key.to_far()
    of_value.to_near()
    move(14)
    of_query.to_other()
    of_value.to_far()
    move(15)
    of_key.to_other()
    of_query.to_out()
    of_value.to_other()
    of_key.to_out()
    of_value.to_out()
    total = 2 * TOKEN_PARTS
    for number in range(total - TOKENS_AHEAD, total):
        p, part = divmod(number, TOKEN_PARTS)
        back.sent(p, token_v.at[p], part)
    for number in range(total):
        p, part = divmod(number, TOKEN_PARTS)
        back.arrived(p, token_v.at[p], part)
    for one in reductions:
        one.finish()


def tail(query_grad, key_grads, value_grads, far, normed, xs, middle_grad, weight, info, gain, feed_sums, total_tokens, hidden_parts):
    block, width = xs[0].shape
    count, total_seqs = 2 * block, 16
    any_spec = fixed_any()
    inside = pl.BlockSpec(memory_space=pltpu.VMEM)
    up_rows = width // 8
    parts = pltpu.VMEM((1, 2, 2, 2, up_rows, width), BF16)
    held = lambda *shape, dtype=BF16: pltpu.VMEM(shape, dtype)
    sums_shape = (16 + total_seqs, width)
    return pl.pallas_call(
        functools.partial(tail_kernel, total_tokens=total_tokens, parts=hidden_parts),
        in_specs=[any_spec] * 11 + [inside] * 3,
        out_specs=[any_spec, any_spec, inside],
        out_shape=[
            shape_of((2, block, width)), shape_of((3, up_rows, width)), shape_of(sums_shape, F32),
        ],
        scratch_shapes=[
            held(count, width), held(2, 2, block, width), held(*far.shape), held(count, width),
            held(2, block, width), held(count, width, dtype=F32), held(*weight.shape), held(count, width),
            held(count, width), held(2, block, width), parts, parts, parts,
        ]
        + Reduction.scratch(1, up_rows, width) * 3
        + [
            held(5, *sums_shape, dtype=F32),
            pltpu.SemaphoreType.DMA((5,)),
            pltpu.SemaphoreType.DMA((5,)),
            pltpu.SemaphoreType.DMA((11,)),
        ]
        + Trade.semaphores(TOKEN_PARTS),
        compiler_params=pltpu.CompilerParams(
            vmem_limit_bytes=VMEM_BYTES, collective_id=1, has_side_effects=True
        ),
        cost_estimate=cost(60),
        name="tail",
    )(
        query_grad, *key_grads, *value_grads, far, normed, *xs, middle_grad, weight, info, gain, feed_sums
    )


def finish_kernel(
    token_ref, layer_ref, qkv_ref, up_out_ref, out_part_ref, down_ref, sums_ref,
    token_out, layer_out, qkv_out, up_out, out_out, down_out, table_out, *, total_seqs, steps_row, table_rows,
):
    token_out[...] = wide(token_ref)
    layer_out[...] = layer_ref[...]
    qkv_out[...] = qkv_ref[0].astype(F32)
    up_out[...] = up_out_ref[0].astype(F32)
    out_out[...] = out_part_ref[0].astype(F32)
    down_out[...] = wide(down_ref)
    block = table_out.shape[0]
    first = lax.axis_index("dp") * table_rows + pl.program_id(0) * block
    place = (lax.broadcasted_iota(jnp.int32, (block, 1), 0) + first).astype(F32)
    total = jnp.zeros_like(table_out)
    for s in range(total_seqs):
        chosen = place == sums_ref[steps_row : steps_row + 1, s : s + 1]
        total = total + jnp.where(chosen, sums_ref[16 + s : 17 + s], 0.0)
    table_out[...] = total


def finish(token, layer, qkv, up_out, down, sums, table_rows, steps_row):
    seqs, length, width = token.shape
    parts, block = up_out.shape[0] - 1, up_out.shape[1]
    steps = parts
    rows_at = lambda many: pl.BlockSpec((many // steps, width), lambda i: (i, 0))
    count = seqs * length
    wide_rows = rows_at(count)
    made = pl.pallas_call(
        functools.partial(
            finish_kernel, total_seqs=sums.shape[0] - 16, steps_row=steps_row, table_rows=table_rows
        ),
        grid=(steps,),
        in_specs=[
            wide_rows, wide_rows,
            pl.BlockSpec((1, block, width), lambda i: (jnp.minimum(i, 2), 0, 0)),
            pl.BlockSpec((1, block, width), lambda i: (i, 0, 0)),
            pl.BlockSpec((1, block, width), lambda i: (parts, 0, 0)),
            rows_at(down.shape[0]),
            fixed(sums.shape),
        ],
        out_specs=[
            wide_rows, wide_rows,
            pl.BlockSpec((block, width), lambda i: (0, jnp.minimum(i, 2))),
            pl.BlockSpec((block, width), lambda i: (0, i)),
            pl.BlockSpec((block, width), lambda i: (0, 0)),
            rows_at(down.shape[0]), rows_at(table_rows),
        ],
        out_shape=[
            shape_of((count, width), F32), shape_of((count, width)), shape_of((block, 3 * width), F32),
            shape_of((block, parts * width), F32), shape_of((block, width), F32), shape_of(down.shape, F32),
            shape_of((table_rows, width), F32),
        ],
        compiler_params=params(),
        cost_estimate=cost(6),
        name="finish",
    )(token.reshape(count, width), layer.reshape(count, width), qkv, up_out, up_out, down, sums)
    shape = (seqs, length, width)
    return [made[0].reshape(shape), made[1].reshape(shape)] + list(made[2:])


def gelu_parts(hidden):
    share = 0.5 + 0.5 * lax.erf(hidden * 2**-0.5)
    bell = jnp.exp(-0.5 * hidden * hidden) * 0.3989422804014327
    return hidden * share, share + hidden * bell


def feed_kernel(
    context_ref, x0_ref, x1_ref, info_ref, cot0_ref, cot1_ref, out_weight_ref, up_ref, down_ref,
    out_bias_ref, gain_ref, shift_ref, down_bias_ref, up_bias_ref,
    out_ref, active_ref, hidden_grad_ref, normed_ref, middle_grad_ref, branch_ref, context_grad_ref, sums_ref,
):
    step = pl.program_id(0)
    width, hidden_width = x0_ref.shape[1], up_ref.shape[1]

    @pl.when(step == 0)
    def _():
        sums_ref[...] = jnp.zeros_like(sums_ref)

    x = jnp.where(step == 0, x0_ref[...], x1_ref[...])
    cot = jnp.where(step == 0, cot0_ref[...], cot1_ref[...])
    middle = (
        x.astype(F32)
        + one_row(info_ref, TIME)
        + dot(context_ref[...], out_weight_ref[...], NN)
        + vector(out_bias_ref)
    )
    unit, scale = norm_parts(middle)
    gain = vector(gain_ref)
    normed = (unit * gain + vector(shift_ref)).astype(BF16)
    normed_ref[...] = normed
    out = middle + vector(down_bias_ref)
    normed_grad = jnp.zeros_like(out)
    up_bias = vector(up_bias_ref)
    for part in range(hidden_width // width):
        columns = slice(part * width, (part + 1) * width)
        hidden = dot(normed, up_ref[:, columns], NN) + up_bias[:, columns]
        active, slope = gelu_parts(hidden)
        active = active.astype(BF16)
        active_ref[:, columns] = active
        out = out + dot(active, down_ref[columns, :], NN)
        hidden_grad = (dot(cot, down_ref[columns, :], NT) * slope).astype(BF16)
        hidden_grad_ref[:, columns] = hidden_grad
        sums_ref[8 + part : 9 + part] += column_sum(hidden_grad.astype(F32))
        normed_grad = normed_grad + dot(hidden_grad, up_ref[:, columns], NT)
    out_ref[...] = out.astype(BF16)
    cot = cot.astype(F32)
    middle_grad = cot + norm_backward(normed_grad, gain, unit, scale)
    middle_grad_ref[...] = middle_grad
    branch = middle_grad.astype(BF16)
    branch_ref[...] = branch
    context_grad_ref[...] = dot(branch, out_weight_ref[...], NT).astype(BF16)
    sums_ref[0:1] += column_sum(cot)
    sums_ref[1:2] += column_sum(normed_grad * unit)
    sums_ref[2:3] += column_sum(normed_grad)
    sums_ref[3:4] += column_sum(branch.astype(F32))
    sums_ref[4:5] += column_sum(out * out)


def feed(context, xs, info, small, cots, out_weight, up, down):
    block, width = xs[0].shape
    count, hidden_width = 2 * block, up.shape[1]
    sums_rows = 8 + hidden_width // width + (-(hidden_width // width)) % 8
    whole = fixed((block, width))
    return pl.pallas_call(
        feed_kernel,
        grid=(2,),
        in_specs=[
            rows(block, width), whole, whole, fixed(info.shape), whole, whole,
            fixed(out_weight.shape), fixed(up.shape), fixed(down.shape),
        ]
        + [whole_vector(v) for v in small],
        out_specs=[
            rows(block, width), rows(block, hidden_width), rows(block, hidden_width), rows(block, width),
            rows(block, width), rows(block, width), rows(block, width),
            pl.BlockSpec((sums_rows, width), lambda i: (0, 0)),
        ],
        out_shape=[
            shape_of((count, width)), shape_of((count, hidden_width)), shape_of((count, hidden_width)),
            shape_of((count, width)), shape_of((count, width), F32), shape_of((count, width)),
            shape_of((count, width)), shape_of((sums_rows, width), F32),
        ],
        compiler_params=params(),
        cost_estimate=cost(34),
        name="feed",
    )(context, *xs, info, *cots, out_weight, up, down, *small)


def down_grad_kernel(active_ref, cot0_ref, cot1_ref, out_ref):
    block = cot0_ref.shape[0]
    out_ref[...] = (
        dot(active_ref[:block], cot0_ref[...], TN) + dot(active_ref[block:], cot1_ref[...], TN)
    ).astype(BF16)


def down_grad(active, cots):
    block, width = cots[0].shape
    count, hidden_width = active.shape
    return pl.pallas_call(
        down_grad_kernel,
        grid=(hidden_width // width,),
        in_specs=[pl.BlockSpec((count, width), lambda i: (0, i))] + [fixed((block, width))] * 2,
        out_specs=rows(width, width),
        out_shape=shape_of((hidden_width, width)),
        compiler_params=params(),
        cost_estimate=cost(8),
        name="down_grad",
    )(active, *cots)


def up_out_grad_kernel(normed_ref, hidden_grad_ref, context_ref, branch_ref, out_ref):
    last = pl.num_programs(0) - 1

    @pl.when(pl.program_id(0) < last)
    def _():
        out_ref[0] = dot(normed_ref[...], hidden_grad_ref[...], TN).astype(BF16)

    @pl.when(pl.program_id(0) == last)
    def _():
        out_ref[0] = dot(context_ref[...], branch_ref[...], TN).astype(BF16)


def up_out_grad(normed, hidden_grad, context, branch):
    count, width = normed.shape
    parts = hidden_grad.shape[1] // width
    whole = fixed((count, width))
    return pl.pallas_call(
        up_out_grad_kernel,
        grid=(parts + 1,),
        in_specs=[
            whole,
            pl.BlockSpec((count, width), lambda i: (0, jnp.minimum(i, parts - 1))),
            whole,
            whole,
        ],
        out_specs=pl.BlockSpec((1, width, width), lambda i: (i, 0, 0)),
        out_shape=shape_of((parts + 1, width, width)),
        compiler_params=params(),
        cost_estimate=cost(10),
        name="up_out_grad",
    )(normed, hidden_grad, context, branch)


def qkv_grad_kernel(normed_ref, grad_ref, out_ref):
    out_ref[0] = dot(normed_ref[...], grad_ref[...], TN).astype(BF16)


def qkv_grad(normed, grads):
    count, width = normed.shape
    parts = grads.shape[1] // width
    return pl.pallas_call(
        qkv_grad_kernel,
        grid=(parts,),
        in_specs=[fixed((count, width)), pl.BlockSpec((count, width), lambda i: (0, i))],
        out_specs=pl.BlockSpec((1, width, width), lambda i: (i, 0, 0)),
        out_shape=shape_of((parts, width, width)),
        compiler_params=params(),
        cost_estimate=cost(7),
        name="qkv_grad",
    )(normed, grads)


def start_kernel(
    query_grad_ref, key0_ref, key1_ref, far_key0_ref, far_key1_ref, value0_ref, value1_ref, far_value0_ref,
    far_value1_ref, x0_ref, x1_ref, info_ref, middle_grad_ref, gain_ref, weight_ref,
    token0_ref, token1_ref, grads_ref, sums_ref,
):
    step = pl.program_id(0)
    width = x0_ref.shape[1]

    @pl.when(step == 0)
    def _():
        sums_ref[...] = jnp.zeros_like(sums_ref)

    def pick(first, second):
        return jnp.where(step == 0, first[...], second[...])

    query_grad = query_grad_ref[...]
    key_grad = (pick(key0_ref, key1_ref).astype(F32) + pick(far_key0_ref, far_key1_ref).astype(F32)).astype(BF16)
    value_grad = (
        pick(value0_ref, value1_ref).astype(F32) + pick(far_value0_ref, far_value1_ref).astype(F32)
    ).astype(BF16)
    normed_grad = 0.0
    for part, grad in enumerate((query_grad, key_grad, value_grad)):
        columns = slice(part * width, (part + 1) * width)
        grads_ref[:, columns] = grad
        normed_grad = normed_grad + dot(grad, weight_ref[:, columns], NT)
    unit, scale = norm_parts(pick(x0_ref, x1_ref).astype(F32) + one_row(info_ref, TIME))
    token_grad = middle_grad_ref[...] + norm_backward(normed_grad, vector(gain_ref), unit, scale)

    @pl.when(step == 0)
    def _():
        token0_ref[...] = token_grad.astype(BF16)

    @pl.when(step == 1)
    def _():
        token1_ref[...] = token_grad.astype(BF16)

    sums_ref[0:1] += column_sum(normed_grad * unit)
    sums_ref[1:2] += column_sum(normed_grad)
    sums_ref[2:3] += column_sum(query_grad.astype(F32))
    sums_ref[3:4] += column_sum(value_grad.astype(F32))
    sums_ref[4:5] += column_sum(token_grad)


def start_back(query_grad, key_grads, value_grads, xs, info, middle_grad, gain, weight):
    block, width = xs[0].shape
    count = 2 * block
    whole = fixed((block, width))
    kept = pl.BlockSpec((block, width), lambda i: (0, 0))
    return pl.pallas_call(
        start_kernel,
        grid=(2,),
        in_specs=[rows(block, width)]
        + [whole] * 10
        + [fixed(info.shape), rows(block, width), whole_vector(gain), fixed(weight.shape)],
        out_specs=[kept, kept, rows(block, 3 * width), pl.BlockSpec((8, width), lambda i: (0, 0))],
        out_shape=[
            shape_of((block, width)), shape_of((block, width)), shape_of((count, 3 * width)),
            shape_of((8, width), F32),
        ],
        compiler_params=params(),
        cost_estimate=cost(10),
        name="start_back",
    )(query_grad, *key_grads, *value_grads, *xs, info, middle_grad, gain, weight)


class Places:
    def __init__(self, dp, seq):
        self.dp, self.seq = dp, seq
        self.bits = dp.bit_length() - 1

    def flat(self, d, z):
        return d * self.seq + z

    def pairs(self, to):
        return [
            (self.flat(d, z), self.flat(*to(d, z))) for d in range(self.dp) for z in range(self.seq)
        ]

    def gather_order(self, turn):
        def to(d, z):
            core, j = d % 2, (z + turn) % 2
            return d - core + z // 2, 2 * core + j

        return self.pairs(to)

    def scatter_order(self, turn):
        return [(b, a) for a, b in self.gather_order(turn)]

    def swap(self, bit):
        return self.pairs(lambda d, z: (d ^ (1 << bit), z))

    def swap_seq(self, step):
        return self.pairs(lambda d, z: (d, z ^ step))


def send(x, order):
    return lax.ppermute(x, BOTH, order)


def add(a, b):
    return (a.astype(F32) + b.astype(F32)).astype(BF16)


def reduce_parts(parts, places):
    d, z = lax.axis_index("dp"), lax.axis_index("seq")
    count, height, width = parts.shape
    block = height // places.dp
    grid = parts.reshape((count,) + (2,) * places.bits + (block, width))

    def halve(value, bit, axes):
        axis = 1 + axes.index(bit)
        mine = (d >> bit) & 1
        kept = lax.dynamic_index_in_dim(value, mine, axis, keepdims=False)
        sent = lax.dynamic_index_in_dim(value, 1 - mine, axis, keepdims=False)
        axes.remove(bit)
        return add(kept, send(sent, places.swap(bit)))

    axes = list(range(places.bits - 1, -1, -1))
    grid = halve(grid, 0, axes)
    halves = []
    for number, order in enumerate((range(1, places.bits), range(places.bits - 1, 0, -1))):
        at = block // 2
        value = lax.slice_in_dim(grid, number * at, (number + 1) * at, axis=grid.ndim - 2)
        left = list(axes)
        for bit in order:
            value = halve(value, bit, left)
        halves.append(sum_along_seq(value, z, places))
    return jnp.concatenate(halves, 1)


def sum_along_seq(value, z, places):
    count, block, width = value.shape
    mine = z % 2
    grid = value.reshape(count, block, 2, width // 2)
    kept = lax.dynamic_index_in_dim(grid, mine, 2, keepdims=False)
    sent = lax.dynamic_index_in_dim(grid, 1 - mine, 2, keepdims=False)
    half = add(kept, send(sent, places.swap_seq(1)))
    half = add(half, send(half, places.swap_seq(2)))
    other = send(half, places.swap_seq(1))
    first = jnp.where(mine == 0, half, other)
    second = jnp.where(mine == 0, other, half)
    return jnp.concatenate([first, second], 2).astype(F32)


def sum_everywhere(value, places):
    for bit in range(places.bits):
        value = value + send(value, places.swap(bit))
    for step in (1, 2):
        value = value + send(value, places.swap_seq(step))
    return value


def per_device(
    tokens, timesteps, time_table, ln1_gain, ln1_bias, qkv_weight, q_bias, v_bias, out_weight, out_bias,
    ln2_gain, ln2_bias, up_weight, up_bias, down_weight, down_bias, cotangent,
):
    places = Places(lax.axis_size("dp"), lax.axis_size("seq"))
    seq_count, local_len, width = tokens.shape
    hidden_width = up_weight.shape[1]
    assert places.seq == 4 and seq_count == 2 and places.dp == 1 << places.bits
    d, z = lax.axis_index("dp"), lax.axis_index("seq")
    core = d % 2
    total_seqs = seq_count * places.dp
    total_tokens = total_seqs * local_len * places.seq

    def gathered(array):
        blocks = []
        for turn in range(2):
            mine = lax.dynamic_index_in_dim(array, (z + turn) % 2, 0, keepdims=False)
            blocks.append(send(mine, places.gather_order(turn)))
        return blocks

    count = 2 * local_len
    parts = hidden_width // width
    first_small = (ln1_gain, ln1_bias, q_bias, v_bias)
    second_small = (out_bias, ln2_gain, ln2_bias, down_bias, up_bias)
    sequence = (d - core + z // 2) * seq_count + z % 2
    if places.dp == 8:
        made = front(tokens, qkv_weight, time_table, timesteps, first_small, count / total_tokens)
        xs, (normed, query), kvs, info = made[:2], made[2:4], list(made[4:8]), made[8]
        cotangent, query = lax.optimization_barrier((cotangent, query))
        cots = gathered(cotangent)
    else:
        info = jnp.concatenate(
            [
                known_rows(
                    timesteps[j], seq_count * d + j, count / total_tokens,
                    lax.dynamic_slice_in_dim(time_table, timesteps[j], 1, 0).astype(F32),
                )
                for j in range(2)
            ]
        )
        far_info = send(info, places.swap(0))
        xs = gathered(tokens)
        cots = gathered(cotangent)
        info = jnp.where(z // 2 == core, info, far_info)
        info = jnp.pad(jnp.where(z % 2 == 0, info[:4], info[4:]), ((0, 4), (0, 0)))
        normed, query, kv0 = project(xs[0], info, first_small, qkv_weight, count)
        far0 = send(kv0, places.swap(0))
        normed, query, kv1 = project(xs[1], info, first_small, qkv_weight, count, (normed, query))
        kvs = [kv0, kv1, far0, send(kv1, places.swap(0))]
    context, logsum = attend(query, kvs)
    out, active, hidden_grad, normed_two, middle_grad, branch, context_grad, feed_sums = feed(
        context, xs, info, second_small, cots, out_weight, up_weight, down_weight
    )

    def scattered(blocks, dtype):
        back = [send(block, places.scatter_order(turn)) for turn, block in enumerate(blocks)]
        even = z % 2 == 0
        return jnp.stack(
            [jnp.where(even, back[0], back[1]), jnp.where(even, back[1], back[0])]
        ).astype(dtype)


    if places.dp == 8:
        made = back(
            query, context_grad, context, logsum, kvs, normed_two, hidden_grad, branch, active, cots, out
        )
        tokens_grad, qkv_sum, packed = tail(
            made[0], made[1:3], made[3:5], made[5], normed, xs, middle_grad, qkv_weight, info, ln1_gain,
            feed_sums, total_tokens, parts,
        )
        tokens_grad, layer_out, qkv_sum, up_sum, out_sum, down_sum, table_grad = finish(
            tokens_grad, made[6], qkv_sum, made[8], made[7][0], packed, time_table.shape[0] // places.dp, 9 + parts
        )
    else:
        layer_out = scattered([out[:local_len], out[local_len:]], BF16)
        down_sum = reduce_parts(down_grad(active, cots)[None], places)[0]
        up_out_sum = reduce_parts(up_out_grad(normed_two, hidden_grad, context, branch), places)
        made = attend_back(query, context_grad, context, logsum, kvs)
        token0, token1, projected_grad, start_sums = start_back(
            made[0],
            list(made[1:3]) + [send(g, places.swap(0)) for g in made[3:5]],
            list(made[5:7]) + [send(g, places.swap(0)) for g in made[7:9]],
            xs, info, middle_grad, ln1_gain, qkv_weight,
        )
        tokens_grad = scattered([token0, token1], F32)
        qkv_sum = reduce_parts(qkv_grad(normed, projected_grad), places)
        energy = jnp.sum(feed_sums[4]) / (width * total_tokens)
        sequence_rows = jnp.where(jnp.arange(total_seqs)[:, None] == sequence, start_sums[4][None], 0.0)
        packed = jnp.concatenate(
            [
                feed_sums[0:4], feed_sums[8 : 8 + parts], start_sums[0:4],
                jnp.stack(
                    [info[MARK] * energy + info[SHARE], info[STEP] * jnp.where(core == 0, 1.0, 0.0)]
                ),
                sequence_rows,
            ]
        )
        packed = sum_everywhere(packed, places)
        steps = packed[9 + parts, :total_seqs].astype(jnp.int32)
        table_rows = time_table.shape[0] // places.dp
        chosen = (steps[None, :] == (jnp.arange(table_rows) + d * table_rows)[:, None]).astype(F32)
        table_grad = jnp.dot(chosen, packed[10 + parts :], precision=lax.Precision.HIGHEST)

        def side_by_side(stacked):
            return jnp.moveaxis(stacked, 0, 1).reshape(stacked.shape[1], -1)

        qkv_sum, out_sum = side_by_side(qkv_sum), up_out_sum[parts]
        up_sum = side_by_side(up_out_sum[:parts])
    piece = width // places.dp
    mine = lax.dynamic_slice_in_dim(packed[: 8 + parts], d * piece, piece, 1)
    up_piece = hidden_width // places.dp
    up_bias_sum = lax.dynamic_slice_in_dim(packed[4 : 4 + parts].reshape(-1), d * up_piece, up_piece, 0)
    stats = packed[8 + parts]

    return (
        layer_out,
        tokens_grad,
        table_grad,
        mine[4 + parts],
        mine[5 + parts],
        qkv_sum,
        mine[6 + parts],
        mine[7 + parts],
        out_sum,
        mine[3],
        mine[1],
        mine[2],
        up_sum,
        up_bias_sum,
        down_sum,
        mine[0],
        stats[:BUCKETS],
        stats[BUCKETS : 2 * BUCKETS],
    )


def solution(mesh):
    split = P("dp", "seq", None)
    return jax.shard_map(
        per_device,
        mesh=mesh,
        in_specs=(split, P("dp")) + (P(),) * 14 + (split,),
        out_specs=(
            split, split, P("dp", None), P("dp"), P("dp"), P("dp", None), P("dp"), P("dp"), P("dp", None),
            P("dp"), P("dp"), P("dp"), P("dp", None), P("dp"), P("dp", None), P("dp"), P(), P(),
        ),
        check_vma=False,
    )
```

```python
import functools

import jax
import jax.numpy as jnp
from jax import lax
from jax.experimental import pallas as pl
from jax.experimental.pallas import tpu as pltpu
from jax.sharding import PartitionSpec as P

HEAD_DIM = 64
TSTEPS = 2048
BUCKETS = 4
EPS = 1e-05
LANES = 128
VMEM_BYTES = 60 * 1024 * 1024
BOTH = ("dp", "seq")
TOKEN_PARTS = 8
TOKENS_AHEAD = 6
F32 = jnp.float32
BF16 = jnp.bfloat16
NN = (((1,), (0,)), ((), ()))
NT = (((1,), (1,)), ((), ()))
TN = (((0,), (0,)), ((), ()))


def dot(a, b, dims):
    return lax.dot_general(a, b, dims, preferred_element_type=F32)


def wide(ref):
    return ref[...].astype(F32)


def column_sum(v):
    return jnp.sum(v, 0, keepdims=True)


def fixed(shape):
    return pl.BlockSpec(shape, lambda *i: (0,) * len(shape), pipeline_mode=pl.Buffered(1))


def rows(block, width):
    return pl.BlockSpec((block, width), lambda i: (i, 0))


def shape_of(shape, dtype=BF16):
    return jax.ShapeDtypeStruct(shape, dtype)


def cost(us):
    return pl.CostEstimate(flops=int(us * 1.15e9), bytes_accessed=0, transcendentals=0)


def params():
    return pltpu.CompilerParams(vmem_limit_bytes=VMEM_BYTES)


def norm_parts(v):
    centered = v - jnp.mean(v, -1, keepdims=True)
    scale = lax.rsqrt(jnp.mean(centered * centered, -1, keepdims=True) + EPS)
    return centered * scale, scale


def norm_backward(grad, gain, unit, scale):
    scaled = grad * gain
    return scale * (
        scaled
        - jnp.mean(scaled, -1, keepdims=True)
        - unit * jnp.mean(scaled * unit, -1, keepdims=True)
    )


TIME, MARK, SHARE, STEP = range(4)


def one_row(ref, at):
    return ref[at : at + 1].astype(F32)


def vector(ref):
    return ref[...].astype(F32).reshape(1, -1)


def whole_vector(v):
    return pl.BlockSpec(v.shape, lambda *i: (0,), pipeline_mode=pl.Buffered(1))


def known_rows(step, sequence, share, time_row):
    lane = lax.broadcasted_iota(jnp.int32, time_row.shape, 1)
    bucket = step * BUCKETS // TSTEPS
    return jnp.concatenate(
        [
            time_row,
            jnp.where(lane == bucket, 1.0, 0.0),
            jnp.where(lane == BUCKETS + bucket, share, 0.0),
            jnp.where(lane == sequence, step.astype(F32), 0.0),
        ],
        0,
    )


def project_rows(x, info_ref, small, weight_ref):
    width = x.shape[1]
    gain, shift, query_bias, value_bias = small
    unit, _ = norm_parts(x.astype(F32) + one_row(info_ref, TIME))
    normed = (unit * vector(gain) + vector(shift)).astype(BF16)

    def part(number):
        made = dot(normed, weight_ref[:, number * width : (number + 1) * width], NN)
        if number != 1:
            made = made + vector(query_bias if number == 0 else value_bias)
        made = made.astype(BF16)
        return made * jnp.asarray(HEAD_DIM ** (-0.5), BF16) if number == 0 else made

    return normed, part


def project_kernel(x_ref, info_ref, weight_ref, *refs):
    normed_ref, query_ref, kv_ref = refs[-3:]
    width = x_ref.shape[1]
    normed, part = project_rows(x_ref[...], info_ref, refs[:4], weight_ref)
    normed_ref[...] = normed
    query_ref[...] = part(0)
    kv_ref[:, :width] = part(1)
    kv_ref[:, width:] = part(2)


def project(x, info, small, weight, total, begun=None, block=256):
    count, width = x.shape
    first = 0 if begun is None else total // block - count // block
    later = pl.BlockSpec((block, width), lambda i: (i + first, 0))
    extra = [] if begun is None else list(begun)
    return pl.pallas_call(
        project_kernel,
        grid=(count // block,),
        in_specs=[rows(block, width), fixed(info.shape), fixed(weight.shape)]
        + [whole_vector(v) for v in small]
        + [pl.BlockSpec(memory_space=pl.ANY)] * len(extra),
        out_specs=[later, later, rows(block, 2 * width)],
        out_shape=[
            shape_of((total, width)),
            shape_of((total, width)),
            shape_of((count, 2 * width)),
        ],
        input_output_aliases={7: 0, 8: 1} if extra else {},
        compiler_params=params(),
        cost_estimate=cost(5),
        name="project",
    )(x, info, weight, *small, *extra)


def lane_parts():
    lane = lax.broadcasted_iota(jnp.int32, (1, LANES), 1)
    return lane < HEAD_DIM, lane % HEAD_DIM


def with_offset(own, place, base, offset):
    high = offset.astype(BF16)
    left = offset - high.astype(F32)
    mid = left.astype(BF16)
    low = (left - mid.astype(F32)).astype(BF16)
    zero = jnp.zeros_like(low)
    parts = jnp.where(place == 0, high, jnp.where(place == 1, mid, jnp.where(place == 2, low, zero)))
    return jnp.where(own, base, parts)


def attend_kernel(query_ref, *refs, pieces):
    key_refs, value_refs = refs[:pieces], refs[pieces : 2 * pieces]
    context_ref, logsum_ref = refs[2 * pieces :]
    count = query_ref.shape[0]
    low, place = lane_parts()
    row_half = lax.broadcasted_iota(jnp.int32, (LANES, LANES), 0) // HEAD_DIM
    lane_half = lax.broadcasted_iota(jnp.int32, (LANES, LANES), 1) // HEAD_DIM
    swapped = jnp.where(row_half != lane_half, 1.0, 0.0).astype(BF16)
    query = query_ref[...]

    def norms(v):
        v = v.astype(F32)
        return dot((v * v).astype(BF16), swapped, NN)

    key_norm = functools.reduce(
        jnp.maximum, [jnp.max(norms(ref[...]), 0, keepdims=True) for ref in key_refs]
    )
    bound = jnp.sqrt(norms(query) * key_norm) * 1.01
    ones_key = jnp.where(place < 3, 1.0, 0.0).astype(BF16)
    values = [ref[...].T for ref in value_refs]
    ones = jnp.ones((16, value_refs[0].shape[0]), BF16)

    def value_of(piece, head):
        return jnp.concatenate([values[piece][head * HEAD_DIM : (head + 1) * HEAD_DIM], ones], 0)

    def finish(mixed, offset):
        totals = [m[HEAD_DIM : HEAD_DIM + 1] for m in mixed]
        context = jnp.concatenate([m[:HEAD_DIM] / t for m, t in zip(mixed, totals)], 0)
        context_ref[...] = context.T.astype(BF16)
        logs = [jnp.broadcast_to(jnp.log(t), (HEAD_DIM, count)) for t in reversed(totals)]
        logsum_ref[...] = jnp.concatenate(logs, 0).T + offset

    mixed = []
    for head in range(2):
        own = low if head == 0 else ~low
        query_own = with_offset(own, place, query, -bound)
        out = 0.0
        for piece in range(pieces):
            key_own = jnp.where(own, key_refs[piece][...], ones_key)
            weights = jnp.exp(dot(key_own, query_own, NT)).astype(BF16)
            out = out + dot(value_of(piece, head), weights, NN)
        mixed.append(out)
    finish(mixed, bound)
    smallest = jnp.min(jnp.minimum(mixed[0][HEAD_DIM], mixed[1][HEAD_DIM]))

    @pl.when(smallest < 1e-25)
    def _():
        again, tops = [], []
        for head in range(2):
            own = low if head == 0 else ~low
            query_own = jnp.where(own, query, jnp.zeros_like(query))
            top = jnp.full((1, count), -jnp.inf, F32)
            for piece in range(pieces):
                scores = dot(key_refs[piece][...], query_own, NT)
                top = jnp.maximum(top, jnp.max(scores, 0, keepdims=True))
            out = 0.0
            for piece in range(pieces):
                scores = dot(key_refs[piece][...], query_own, NT)
                out = out + dot(value_of(piece, head), jnp.exp(scores - top).astype(BF16), NN)
            again.append(out)
            tops.append(jnp.broadcast_to(top, (HEAD_DIM, count)))
        finish(again, jnp.concatenate(tops[::-1], 0).T)


def attend(query, kvs):
    count, width = query.shape
    pairs, pieces, length = width // LANES, len(kvs), kvs[0].shape[0]
    row = pl.BlockSpec((count, LANES), lambda p: (0, p))
    return pl.pallas_call(
        functools.partial(attend_kernel, pieces=pieces),
        grid=(pairs,),
        in_specs=[row]
        + [pl.BlockSpec((length, LANES), lambda p: (0, p))] * pieces
        + [pl.BlockSpec((length, LANES), lambda p: (0, pairs + p))] * pieces,
        out_specs=[row, row],
        out_shape=[shape_of((count, width)), shape_of((count, width), F32)],
        compiler_params=params(),
        cost_estimate=cost(32),
        name="attend",
    )(query, *kvs, *kvs)


def attend_back_step(query_ref, grad_ref, context_ref, logsum_ref, pieces, query_grad_ref):
    low, place = lane_parts()
    query, grad = query_ref[...], grad_ref[...]
    count = query.shape[0]
    product = grad.astype(F32) * wide(context_ref)
    logsum = logsum_ref[...]
    ones_key = jnp.where(place < 3, 1.0, 0.0).astype(BF16)
    zero = jnp.zeros_like(query)
    heads = []
    for head in range(2):
        own = low if head == 0 else ~low
        inner = jnp.sum(jnp.where(own, product, 0.0), -1, keepdims=True)
        heads.append(
            (
                own,
                with_offset(own, place, query, -logsum),
                with_offset(own, place, grad, jnp.broadcast_to(-inner, logsum.shape)),
                jnp.where(own, query, zero),
                jnp.where(own, grad, zero),
            )
        )
    length = sum(piece[0].shape[0] for piece in pieces)
    query_grads = [0.0, 0.0]
    key_mean = 0.0
    for key_ref, value_ref, key_grad_ref, value_grad_ref, before in pieces:
        if before is not None:
            before()
        key, value = key_ref[...], value_ref[...]
        key_turned = key.T
        key_mean = key_mean + jnp.sum(key_turned.astype(F32), 1, keepdims=True) / length
        ones = jnp.ones((16, key.shape[0]), BF16)
        key_grad, value_grad = 0.0, 0.0
        for head, (own, query_off, grad_off, query_own, grad_own) in enumerate(heads):
            scores = dot(jnp.where(own, key, ones_key), query_off, NT)
            probs = jnp.exp(scores)
            prob_grad = dot(jnp.where(own, value, ones_key), grad_off, NT)
            score_grad = (probs * prob_grad).astype(BF16)
            value_grad = value_grad + dot(probs.astype(BF16), grad_own, NN)
            key_grad = key_grad + dot(score_grad, query_own, NN)
            lanes = slice(head * HEAD_DIM, (head + 1) * HEAD_DIM)
            turned = jnp.concatenate([key_turned[lanes], ones], 0)
            query_grads[head] = query_grads[head] + dot(turned, score_grad, NN)
        key_grad_ref[...] = key_grad.astype(BF16)
        value_grad_ref[...] = value_grad.astype(BF16)
    parts = [
        made[:HEAD_DIM]
        - key_mean[head * HEAD_DIM : (head + 1) * HEAD_DIM]
        * jnp.broadcast_to(made[HEAD_DIM : HEAD_DIM + 1], (HEAD_DIM, count))
        for head, made in enumerate(query_grads)
    ]
    query_grad_ref[...] = (jnp.concatenate(parts, 0) * HEAD_DIM ** (-0.5)).T.astype(BF16)


def attend_back_kernel(query_ref, grad_ref, context_ref, logsum_ref, *refs, pieces):
    key_refs, value_refs = refs[:pieces], refs[pieces : 2 * pieces]
    query_grad_ref = refs[2 * pieces]
    key_grad_refs = refs[2 * pieces + 1 : 3 * pieces + 1]
    value_grad_refs = refs[3 * pieces + 1 :]
    steps = list(zip(key_refs, value_refs, key_grad_refs, value_grad_refs, [None] * pieces))
    attend_back_step(query_ref, grad_ref, context_ref, logsum_ref, steps, query_grad_ref)


def attend_back(query, grad, context, logsum, kvs):
    count, width = query.shape
    pairs, pieces, length = width // LANES, len(kvs), kvs[0].shape[0]
    row = pl.BlockSpec((count, LANES), lambda p: (0, p))
    piece = pl.BlockSpec((length, LANES), lambda p: (0, p))
    return pl.pallas_call(
        functools.partial(attend_back_kernel, pieces=pieces),
        grid=(pairs,),
        in_specs=[row] * 4
        + [piece] * pieces
        + [pl.BlockSpec((length, LANES), lambda p: (0, pairs + p))] * pieces,
        out_specs=[row] + [piece] * (2 * pieces),
        out_shape=[shape_of((count, width))] + [shape_of((length, width))] * (2 * pieces),
        compiler_params=params(),
        cost_estimate=cost(75),
        name="attend_back",
    )(query, grad, context, logsum, *kvs, *kvs)


def here():
    d, z = lax.axis_index("dp"), lax.axis_index("seq")
    return d, z, d // 4, (d // 2) % 2, d % 2


def partners():
    d, z, y, x, core = here()
    return {
        "core": (d + 1 - 2 * core, z),
        "x": (d + 2 - 4 * x, z),
        "y": (d + 4 - 8 * y, z),
        "near": (d, z + 1 - 2 * (z % 2)),
        "far": (d, (z + 2) % 4),
    }


def remote(source, target, sends, receives, send_index, receive_index, device):
    return pltpu.make_async_remote_copy(
        src_ref=source,
        dst_ref=target,
        send_sem=sends.at[send_index],
        recv_sem=receives.at[receive_index],
        device_id=device,
        device_id_type=pl.DeviceIdType.MESH,
    )


class Reduction:
    def __init__(self, source, out, scratch):
        self.source, self.out = source, out
        self.own = source.at[:, :, :, here()[4]]
        self.from_core, self.first, self.second, self.near, self.far, self.other = scratch[:6]
        self.sends, self.receives, self.local = scratch[6:9]
        self.parts, _, _, self.rows, self.width = self.from_core.shape
        self.half, self.top = self.width // 2, self.rows // 2

    @staticmethod
    def scratch(parts, block, width):
        half, top = width // 2, block // 2
        return [
            pltpu.VMEM((parts, 2, 2, block, width), BF16),
            pltpu.VMEM((2, parts, 2, block, half), BF16),
            pltpu.VMEM((2, parts, block, half), BF16),
            pltpu.VMEM((parts, top, width), BF16),
            pltpu.VMEM((parts, top, width), BF16),
            pltpu.VMEM((parts, top, width), BF16),
            pltpu.SemaphoreType.DMA((8,)),
            pltpu.SemaphoreType.DMA((8,)),
            pltpu.SemaphoreType.DMA((2,)),
        ]

    def copy(self, number):
        d, z, y, x, core = here()
        to = partners()
        left, right = pl.ds(0, self.half), pl.ds(self.half, self.half)
        kept = pl.ds(pl.multiple_of((z % 2) * self.top, self.top), self.top)
        given = pl.ds(pl.multiple_of((1 - z % 2) * self.top, self.top), self.top)
        source, target, device = (
            lambda: (self.source.at[:, :, :, 1 - core], self.from_core, to["core"]),
            lambda: (self.own.at[:, :, 1 - x, :, left], self.first.at[0], to["x"]),
            lambda: (self.own.at[:, 1 - y, :, :, right], self.first.at[1], to["y"]),
            lambda: (self.own.at[:, 1 - y, x, :, left], self.second.at[0], to["y"]),
            lambda: (self.own.at[:, y, 1 - x, :, right], self.second.at[1], to["x"]),
            lambda: (self.own.at[:, y, x, given], self.near, to["near"]),
            lambda: (self.own.at[:, y, x, kept], self.far, to["far"]),
            lambda: (self.own.at[:, y, x, kept], self.other, to["near"]),
        )[number]()
        return remote(source, target, self.sends, self.receives, number, number, device)

    def to_cores(self):
        self.copy(0).start()

    def to_first(self):
        self.copy(0).wait()
        for part in range(self.parts):
            for i in range(2):
                for j in range(2):
                    self.own[part, i, j] = self.own[part, i, j] + self.from_core[part, i, j]
        self.copy(1).start()
        self.copy(2).start()

    def to_second(self):
        _, _, y, x, _ = here()
        self.copy(1).wait()
        self.copy(2).wait()
        left, right = slice(0, self.half), slice(self.half, self.width)
        for part in range(self.parts):
            for i in range(2):
                self.own[part, i, x, :, left] = self.own[part, i, x, :, left] + self.first[0, part, i]
                self.own[part, y, i, :, right] = self.own[part, y, i, :, right] + self.first[1, part, i]
        self.copy(3).start()
        self.copy(4).start()

    def to_near(self):
        _, _, y, x, _ = here()
        self.copy(3).wait()
        self.copy(4).wait()
        left, right = slice(0, self.half), slice(self.half, self.width)
        for part in range(self.parts):
            self.own[part, y, x, :, left] = self.own[part, y, x, :, left] + self.second[0, part]
            self.own[part, y, x, :, right] = self.own[part, y, x, :, right] + self.second[1, part]
        self.copy(5).start()

    def add_rows(self, received):
        _, z, y, x, _ = here()
        kept = pl.ds(pl.multiple_of((z % 2) * self.top, self.top), self.top)
        for part in range(self.parts):
            self.own[part, y, x, kept] = self.own[part, y, x, kept] + received[part]

    def to_far(self):
        self.copy(5).wait()
        self.add_rows(self.near)
        self.copy(6).start()

    def to_other(self):
        self.copy(6).wait()
        self.add_rows(self.far)
        self.copy(7).start()

    def stores(self):
        _, z, y, x, _ = here()
        kept = pl.ds(pl.multiple_of((z % 2) * self.top, self.top), self.top)
        given = pl.ds(pl.multiple_of((1 - z % 2) * self.top, self.top), self.top)
        return (
            pltpu.make_async_copy(self.own.at[:, y, x, kept], self.out.at[:, kept], self.local.at[0]),
            pltpu.make_async_copy(self.other, self.out.at[:, given], self.local.at[1]),
        )

    def to_out(self):
        self.copy(7).wait()
        for copy in self.stores():
            copy.start()

    def finish(self):
        for copy in self.stores():
            copy.wait()


class Trade:
    def __init__(self, out, sends, receives, local, gather=False, parts=1):
        self.out, self.sends, self.receives, self.local = out, sends, receives, local
        self.gather, self.parts = gather, parts

    @staticmethod
    def semaphores(parts=1):
        return [pltpu.SemaphoreType.DMA((2, parts)), pltpu.SemaphoreType.DMA((2, parts)), pltpu.SemaphoreType.DMA((parts,))]

    def device(self, p):
        d, z, _, _, core = here()
        return (d - core + z // 2, 2 * core + (z + p) % 2)

    def stays(self):
        _, z, _, _, core = here()
        return z // 2 == core

    def slot(self, p):
        return p if self.gather else lax.axis_index("seq") % 2

    def own_slot(self, p):
        return p if self.gather else (lax.axis_index("seq") + p) % 2

    def greet(self, barrier):
        @pl.when(jnp.logical_not(self.stays()))
        def _():
            pl.semaphore_signal(barrier, inc=1, device_id=self.device(0), device_id_type=pl.DeviceIdType.MESH)

        pl.semaphore_signal(barrier, inc=1, device_id=self.device(1), device_id_type=pl.DeviceIdType.MESH)
        return jnp.where(self.stays(), 1, 2)

    def rows(self, ref, part):
        many = ref.shape[0] // self.parts
        return ref.at[pl.ds(part * many, many)]

    def keep(self, block, part):
        return pltpu.make_async_copy(
            self.rows(block, part), self.rows(self.out.at[self.own_slot(0)], part), self.local.at[part]
        )

    def copy(self, p, block, part):
        slot = self.slot(p)
        return pltpu.make_async_remote_copy(
            src_ref=self.rows(block, part),
            dst_ref=self.rows(self.out.at[slot], part),
            send_sem=self.sends.at[p, part],
            recv_sem=self.receives.at[slot, part],
            device_id=self.device(p),
            device_id_type=pl.DeviceIdType.MESH,
        )

    def each(self, p, far, near):
        if p == 1:
            far()
            return
        pl.when(jnp.logical_not(self.stays()))(far)
        pl.when(self.stays())(near)

    def begin(self, p, block, part=0):
        self.each(p, lambda: self.copy(p, block, part).start(), lambda: self.keep(block, part).start())

    def sent(self, p, block, part=0):
        self.each(p, lambda: self.copy(p, block, part).wait_send(), lambda: None)

    def arrived(self, p, block, part=0):
        slot = self.own_slot(p)
        target = self.rows(self.out.at[slot], part)

        def far():
            pltpu.make_async_remote_copy(
                src_ref=target,
                dst_ref=target,
                send_sem=self.sends.at[p, part],
                recv_sem=self.receives.at[slot, part],
                device_id=self.device(p),
                device_id_type=pl.DeviceIdType.MESH,
            ).wait_recv()

        self.each(p, far, lambda: self.keep(block, part).wait())


def meet(names, *trades):
    barrier = pltpu.get_barrier_semaphore()
    to = partners()
    for name in names:
        pl.semaphore_signal(barrier, inc=1, device_id=to[name], device_id_type=pl.DeviceIdType.MESH)
    expected = len(names)
    for one in trades:
        expected = expected + one.greet(barrier)
    pl.semaphore_wait(barrier, expected)


def front_kernel(
    tokens, weight, table, steps_ref, gain, shift, query_bias, value_bias,
    x0_out, x1_out, normed_out, query_out, near0_out, near1_out, far0_out, far1_out, info_out,
    x_v, weight_v, table_v, info_here, info_in, normed_v, query_v, near_v, far_v,
    load, stores, info_sends, info_receives, sends, receives, *trade, share,
):
    d, z, _, _, core = here()
    block, width = x_v.shape[1:]
    small = (gain, shift, query_bias, value_bias)
    trade = Trade(x_v, *trade, gather=True)
    loaded = pltpu.make_async_copy(weight, weight_v, load.at[0])
    looked_up = pltpu.make_async_copy(table, table_v, load.at[1])
    meet(("core",), trade)
    held = [tokens.at[(z + p) % 2] for p in range(2)]
    for p in range(2):
        trade.begin(p, held[p])
    looked_up.start()
    loaded.start()
    steps = [steps_ref[j] for j in range(2)]
    row = lax.broadcasted_iota(jnp.int32, (16, table.shape[0]), 0)
    place = lax.broadcasted_iota(jnp.int32, (16, table.shape[0]), 1)
    wanted = jnp.where(row == 0, steps[0], jnp.where(row == 1, steps[1], -1))
    chosen = jnp.where(place == wanted, 1.0, 0.0).astype(BF16)
    looked_up.wait()
    time_rows = dot(chosen, table_v[...], NN)
    for j in range(2):
        info_here[4 * j : 4 * j + 4] = known_rows(steps[j], 2 * d + j, share, time_rows[j : j + 1])
    known = remote(info_here, info_in, info_sends, info_receives, 0, 0, partners()["core"])
    known.start()
    known.wait()
    mine = jnp.where(z // 2 == core, info_here[...], info_in[...])
    info_out[0:4] = jnp.where(z % 2 == 0, mine[0:4], mine[4:8])
    info_out[4:8] = jnp.zeros_like(info_in[4:8])
    loaded.wait()
    copies, moved = [], []
    for p in range(2):
        trade.arrived(p, held[p])
        normed, part = project_rows(x_v[p], info_out, small, weight_v)
        near_v[p, :, :width] = part(1)
        near_v[p, :, width:] = part(2)
        moved.append(remote(near_v.at[p], far_v.at[p], sends, receives, p, p, partners()["core"]))
        moved[p].start()
        normed_v[p] = normed
        query_v[p] = part(0)
        outs = (x0_out, x1_out)[p], (near0_out, near1_out)[p]
        here_rows = pl.ds(p * block, block)
        for number, (source, target) in enumerate(
            (
                (x_v.at[p], outs[0]), (normed_v.at[p], normed_out.at[here_rows]),
                (query_v.at[p], query_out.at[here_rows]), (near_v.at[p], outs[1]),
            )
        ):
            copies.append(pltpu.make_async_copy(source, target, stores.at[p, number]))
            copies[-1].start()
    for p in range(2):
        moved[p].wait()
        copies.append(pltpu.make_async_copy(far_v.at[p], (far0_out, far1_out)[p], stores.at[p, 4]))
        copies[-1].start()
    for p in range(2):
        trade.sent(p, held[p])
    for copy in copies:
        copy.wait()


def front(tokens, weight, table, steps, small, share):
    _, block, width = tokens.shape
    info_shape = (8, width)
    any_spec = pl.BlockSpec(memory_space=pl.ANY)
    inside = pl.BlockSpec(memory_space=pltpu.VMEM)
    pair = pltpu.VMEM((2, block, width), BF16)
    wide_pair = pltpu.VMEM((2, block, 2 * width), BF16)
    one = pltpu.SemaphoreType.DMA((1,))
    two = pltpu.SemaphoreType.DMA((2,))
    return pl.pallas_call(
        functools.partial(front_kernel, share=share),
        in_specs=[any_spec] * 3 + [pl.BlockSpec(memory_space=pltpu.SMEM)] + [inside] * 4,
        out_specs=[any_spec] * 8 + [inside],
        out_shape=[shape_of((block, width))] * 2
        + [shape_of((2 * block, width))] * 2
        + [shape_of((block, 2 * width))] * 4
        + [shape_of(info_shape, F32)],
        scratch_shapes=[
            pair, pltpu.VMEM(weight.shape, BF16), pltpu.VMEM(table.shape, BF16), pltpu.VMEM(info_shape, F32),
            pltpu.VMEM(info_shape, F32), pair, pair, wide_pair, wide_pair,
            two, pltpu.SemaphoreType.DMA((2, 5)), one, one, two, two,
        ]
        + Trade.semaphores(),
        compiler_params=pltpu.CompilerParams(
            vmem_limit_bytes=VMEM_BYTES, collective_id=2, has_side_effects=True
        ),
        cost_estimate=cost(48),
        name="front",
    )(tokens, weight, table, steps, *small)


def fixed_any():
    return pl.BlockSpec(memory_space=pl.ANY)


def back_kernel(
    query_ref, grad_ref, context_ref, logsum_ref, *refs, pieces, parts, pairs
):
    key_refs, value_refs = refs[:pieces], refs[pieces : 2 * pieces]
    refs = refs[2 * pieces :]
    normed_ref, hidden_grad_ref, whole_context, branch, active_ref, cot0, cot1 = refs[:7]
    first_normed, layer_ref, query_grad_ref, key_out, value_out, layer_out, down_out, up_out, qkv_out = refs[7:16]
    refs = refs[16:]
    near = pieces // 2
    down_parts, up_parts = refs[:2]
    chunks = []
    for number, (which, at, many) in enumerate(back_chunks(down_parts.shape, up_parts.shape)):
        scratch = refs[2 + 9 * number : 11 + 9 * number]
        if which == "down":
            here_rows = pl.ds(at, many)
            chunks.append(
                Reduction(down_parts.at[:, :, :, :, here_rows], down_out.at[:, here_rows], scratch)
            )
        else:
            here_parts = pl.ds(at, many)
            chunks.append(Reduction(up_parts.at[here_parts], up_out.at[here_parts], scratch))
    qkv_parts = refs[38]
    for group in range(2):
        lanes = pl.ds(2 * group * LANES, 2 * LANES)
        scratch = refs[39 + 9 * group : 48 + 9 * group]
        chunks.append(Reduction(qkv_parts.at[group], qkv_out.at[:, :, lanes], scratch))
    one, two, three, four, five, six = chunks
    query_held, near_grads, far_grads, far_in, far_sends, far_receives = refs[57:63]
    whole_context_ref, branch_ref, cots_ref, first_normed_ref, loads = refs[63:68]
    back = Trade(layer_out, *refs[68:])
    block = key_refs[0].shape[0]
    layer_blocks = [layer_ref.at[pl.ds(p * block, block)] for p in range(2)]
    step = pl.program_id(0)
    made = 2 * parts + 1
    pair, last = step - made, pl.num_programs(0) - 1

    def far_copy(which):
        return remote(
            far_grads, far_in.at[which % 2], far_sends, far_receives, 0, which, partners()["core"]
        )

    loaded = [
        pltpu.make_async_copy(source, target, loads.at[number])
        for number, (source, target) in enumerate(
            (
                (whole_context, whole_context_ref), (branch, branch_ref), (cot0, cots_ref.at[pl.ds(0, block)]),
                (cot1, cots_ref.at[pl.ds(block, block)]), (first_normed, first_normed_ref),
            )
        )
    ]

    def begin():
        for copy in loaded:
            copy.start()
        meet(("core", "x", "y", "near", "far"), back)
        back.begin(0, layer_blocks[0])
        back.begin(1, layer_blocks[1])

    def settle():
        which = pair - 1
        slot = which % 2
        far_copy(which).wait()
        key_grad = near_grads[slot, 0] + far_in[slot, 0]
        value_grad = near_grads[slot, 1] + far_in[slot, 1]
        key_out[...] = key_grad
        value_out[...] = value_grad

        @pl.when(which < 4)
        def _():
            grads = jnp.concatenate([query_held[slot], key_grad, value_grad], 1)
            product = dot(first_normed_ref[...], grads, TN).astype(BF16)
            lanes = pl.ds(pl.multiple_of(slot * LANES, LANES), LANES)
            for part in range(3):
                block_of = product[:, part * LANES : (part + 1) * LANES]
                qkv_parts[which // 2, part, :, :, :, :, lanes] = block_of.reshape(qkv_parts.shape[2:6] + (LANES,))

    plan = {
        (0, 0): [begin],
        (2, 0): [one.to_cores],
        (4, 0): [one.to_first],
        (5, 0): [two.to_cores],
        (8, 0): [two.to_first],
        (9, 0): [three.to_cores, one.to_second],
        (9, 1): [four.to_cores],
        (10, 0): [three.to_first, one.to_near],
        (10, 1): [two.to_second],
        (10, 2): [four.to_first],
        (10, 3): [one.to_far],
        (11, 0): [five.to_cores],
        (11, 1): [two.to_near],
        (11, 2): [three.to_second, one.to_other],
        (11, 3): [five.to_first, four.to_second],
        (12, 0): [two.to_far, one.to_out],
        (12, 1): [three.to_near],
        (12, 2): [five.to_second, four.to_near],
        (12, 3): [three.to_far],
        (13, 0): [six.to_cores, five.to_near, four.to_far, two.to_other],
        (13, 1): [six.to_first],
        (13, 2): [five.to_far],
        (13, 3): [six.to_second, three.to_other, two.to_out],
        (14, 1): [six.to_near, four.to_other, five.to_other, three.to_out],
        (14, 2): [six.to_far],
        (14, 3): [four.to_out, five.to_out],
        (15, 0): [six.to_other, six.to_out],
    }

    def run_plan(place, steps):
        for (at, where), actions in plan.items():
            if where == place and at in steps:

                @pl.when(step == at)
                def _():
                    for action in actions:
                        action()

    run_plan(0, range(made))

    @pl.when(step < parts)
    def _():
        part = dot(normed_ref[...], hidden_grad_ref[...], TN).astype(BF16)
        up_parts[step] = part.reshape(up_parts.shape[1:])

    @pl.when(step == parts)
    def _():
        for copy in loaded:
            copy.wait()
        part = dot(whole_context_ref[...], branch_ref[...], TN).astype(BF16)
        up_parts[parts] = part.reshape(up_parts.shape[1:])

    @pl.when((step > parts) & (step < made))
    def _():
        part = dot(active_ref[...], cots_ref[...], TN).astype(BF16).reshape(down_parts.shape[3:])
        at = step - parts - 1
        down_parts[0, at // 2, at % 2] = part

    def before(place):
        def run():
            run_plan(place, range(made, made + pairs))
            if place == near:
                far_copy(pair).start()

        return run

    pl.when(pair >= 1)(settle)

    @pl.when((step >= made) & (pair < pairs))
    def _():
        order = []
        slot = pair % 2
        for i in range(near):
            far_rows = pl.ds(i * block, block)
            order.append(
                (key_refs[near + i], value_refs[near + i], far_grads.at[0, far_rows], far_grads.at[1, far_rows])
            )
        for i in range(near):
            near_rows = pl.ds(i * block, block)
            order.append(
                (key_refs[i], value_refs[i], near_grads.at[slot, 0, near_rows], near_grads.at[slot, 1, near_rows])
            )
        steps = [one_piece + (before(place),) for place, one_piece in enumerate(order)]
        attend_back_step(query_ref, grad_ref, context_ref, logsum_ref, steps, query_grad_ref)
        query_held[slot] = query_grad_ref[...]

    @pl.when(step == last)
    def _():
        run_plan(0, [made + pairs])
        for p in range(2):
            back.sent(p, layer_blocks[p])
            back.arrived(p, layer_blocks[p])
        for chunk in chunks:
            chunk.finish()


def back_chunks(down_shape, up_shape):
    block, parts = down_shape[-2], up_shape[0]
    return [
        ("up", 0, parts // 2),
        ("up", parts // 2, parts - parts // 2),
        ("down", 0, block // 2),
        ("down", block // 2, block // 2),
    ]


def back(query, grad, context, logsum, kvs, normed, hidden_grad, branch, active, cots, first_normed, layer_out):
    count, width = query.shape
    pairs, pieces, length = width // LANES, len(kvs), kvs[0].shape[0]
    near = pieces // 2
    parts = hidden_grad.shape[1] // width
    made = 2 * parts + 1
    pair = lambda i: jnp.clip(i - made, 0, pairs - 1)
    row = pl.BlockSpec((count, LANES), lambda i: (0, pair(i)))
    settled = pl.BlockSpec((count, LANES), lambda i: (0, jnp.clip(i - made - 1, 0, pairs - 1)))
    piece = pl.BlockSpec((length, LANES), lambda i: (0, pair(i)))
    value = pl.BlockSpec((length, LANES), lambda i: (0, pairs + pair(i)))
    whole = fixed((count, width))
    up_rows, down_rows = width // 8, hidden_grad.shape[1] // 8
    down_shape, up_shape = (1, 2, 2, 2, down_rows, width), (parts + 1, 2, 2, 2, up_rows, width)
    return pl.pallas_call(
        functools.partial(back_kernel, pieces=pieces, parts=parts, pairs=pairs),
        grid=(made + pairs + 1,),
        in_specs=[row] * 4
        + [piece] * pieces
        + [value] * pieces
        + [
            whole,
            pl.BlockSpec((count, width), lambda i: (0, jnp.minimum(i, parts - 1))),
            fixed_any(),
            fixed_any(),
            pl.BlockSpec((count, width), lambda i: (0, jnp.clip(i - parts - 1, 0, parts - 1))),
        ]
        + [fixed_any()] * 4,
        out_specs=[row, settled, settled] + [fixed_any()] * 4,
        out_shape=[shape_of((count, width))] * 3
        + [
            shape_of((2, length, width)), shape_of((1, down_rows, width)), shape_of((parts + 1, up_rows, width)),
            shape_of((3, up_rows, 4 * LANES)),
        ],
        scratch_shapes=[pltpu.VMEM(down_shape, BF16), pltpu.VMEM(up_shape, BF16)]
        + [
            shape
            for which, _, many in back_chunks(down_shape, up_shape)
            for shape in Reduction.scratch(*((1, many) if which == "down" else (many, up_rows)), width)
        ]
        + [pltpu.VMEM((2, 3, 2, 2, 2, up_rows, 2 * LANES), BF16)]
        + Reduction.scratch(3, up_rows, 2 * LANES) * 2
        + [
            pltpu.VMEM((2, count, LANES), BF16),
            pltpu.VMEM((2, 2, count, LANES), BF16),
            pltpu.VMEM((2, count, LANES), BF16),
            pltpu.VMEM((2, 2, count, LANES), BF16),
            pltpu.SemaphoreType.DMA((1,)),
            pltpu.SemaphoreType.DMA((pairs,)),
        ]
        + [pltpu.VMEM((count, width), BF16)] * 4
        + [pltpu.SemaphoreType.DMA((5,))]
        + Trade.semaphores(),
        compiler_params=pltpu.CompilerParams(
            vmem_limit_bytes=VMEM_BYTES, collective_id=0, has_side_effects=True
        ),
        cost_estimate=cost(100),
        name="back",
    )(
        query, grad, context, logsum, *kvs, *kvs, normed, hidden_grad, context, branch, active, *cots,
        first_normed, layer_out
    )


def tail_kernel(
    query_grad, key_grad, value_grad, normed, x0, x1, middle_grad, weight,
    info_ref, gain_ref, feed_ref,
    tokens_out, qkv_out, sums_ref,
    query_v, key_v, value_v, normed_v, x_v, middle_v, weight_v, token_v, last_parts, *refs, total_tokens, parts,
):
    one = Reduction(last_parts, qkv_out, refs[:9])
    sums_in, sums_sends, sums_receives, loads = refs[9:13]
    back = Trade(tokens_out, *refs[13:], parts=TOKEN_PARTS)
    block, width = x0.shape
    d, z, _, _, core = here()
    total = 2 * TOKEN_PARTS
    top, bottom = pl.ds(0, block), pl.ds(block, block)
    later = ((query_grad, query_v), (key_grad, key_v), (value_grad, value_v), (middle_grad, middle_v))
    copies = [
        pltpu.make_async_copy(source, target, loads.at[number])
        for number, (source, target) in enumerate(
            (
                (weight, weight_v), (x0, x_v.at[0]),
                *((ref.at[top], held.at[top]) for ref, held in later),
                (normed, normed_v), (x1, x_v.at[1]),
                *((ref.at[bottom], held.at[bottom]) for ref, held in later),
            )
        )
    ]
    for copy in copies:
        copy.start()
    meet(("core", "x", "y", "near", "far"), back)

    def start_block(p):
        held = pl.ds(p * block, block)
        normed_grad = 0.0
        for part, grads in enumerate((query_v, key_v, value_v)):
            columns = slice(part * width, (part + 1) * width)
            normed_grad = normed_grad + dot(grads[held], weight_v[:, columns], NT)
        unit, scale = norm_parts(x_v[p].astype(F32) + one_row(info_ref, TIME))
        token_grad = middle_v[held] + norm_backward(normed_grad, vector(gain_ref), unit, scale)
        token_v[p] = token_grad.astype(BF16)
        return [
            column_sum(normed_grad * unit),
            column_sum(normed_grad),
            column_sum(query_v[held].astype(F32)),
            column_sum(value_v[held].astype(F32)),
            column_sum(token_grad),
        ]

    def sums_copy(number):
        to = partners()[("core", "x", "y", "near", "far")[number]]
        return remote(sums_ref, sums_in.at[number], sums_sends, sums_receives, number, number, to)

    def sums_next(number):
        sums_copy(number).wait()
        sums_ref[...] = sums_ref[...] + sums_in[number]
        if number < 4:
            sums_copy(number + 1).start()

    def move(number):
        if number >= TOKENS_AHEAD:
            p, part = divmod(number - TOKENS_AHEAD, TOKEN_PARTS)
            back.sent(p, token_v.at[p], part)
        p, part = divmod(number, TOKEN_PARTS)
        back.begin(p, token_v.at[p], part)

    for copy in copies[:6]:
        copy.wait()
    first = start_block(0)
    for number in range(TOKENS_AHEAD):
        move(number)
    for copy in copies[6:]:
        copy.wait()
    lanes = slice(width - 2 * LANES, width)
    for part, grads in enumerate((query_v, key_v, value_v)):
        made = dot(normed_v[...], grads[:, lanes], TN).astype(BF16)
        last_parts[part] = made.reshape(last_parts.shape[1:])
    one.to_cores()
    second = start_block(1)
    one.to_first()
    sums = [a + b for a, b in zip(first, second)]
    sums_ref[...] = jnp.zeros_like(sums_ref)
    sums_ref[0:4] = feed_ref[0:4]
    sums_ref[4 : 4 + parts] = feed_ref[8 : 8 + parts]
    for number in range(4):
        sums_ref[4 + parts + number : 5 + parts + number] = sums[number]
    energy = jnp.sum(feed_ref[4:5], keepdims=True) / (width * total_tokens)
    sums_ref[8 + parts : 9 + parts] = info_ref[MARK : MARK + 1] * energy + info_ref[SHARE : SHARE + 1]
    sums_ref[9 + parts : 10 + parts] = info_ref[STEP : STEP + 1] * jnp.where(core == 0, 1.0, 0.0)
    sequence = (d - core + z // 2) * 2 + z % 2
    sums_ref[pl.ds(16 + sequence, 1)] = sums[4]
    sums_copy(0).start()
    for number in range(TOKENS_AHEAD, TOKENS_AHEAD + 2):
        move(number)
    sums_next(0)
    one.to_second()
    sums_next(1)
    one.to_near()
    sums_next(2)
    for number in range(TOKENS_AHEAD + 2, TOKENS_AHEAD + 4):
        move(number)
    one.to_far()
    sums_next(3)
    for number in range(TOKENS_AHEAD + 4, TOKENS_AHEAD + 6):
        move(number)
    one.to_other()
    sums_next(4)
    for number in range(TOKENS_AHEAD + 6, total):
        move(number)
    one.to_out()
    for number in range(total - TOKENS_AHEAD, total):
        p, part = divmod(number, TOKEN_PARTS)
        back.sent(p, token_v.at[p], part)
    for number in range(total):
        p, part = divmod(number, TOKEN_PARTS)
        back.arrived(p, token_v.at[p], part)
    one.finish()


def tail(grads, normed, xs, middle_grad, weight, info, gain, feed_sums, total_tokens, hidden_parts):
    block, width = xs[0].shape
    count, total_seqs = 2 * block, 16
    any_spec = fixed_any()
    inside = pl.BlockSpec(memory_space=pltpu.VMEM)
    up_rows = width // 8
    held = lambda *shape, dtype=BF16: pltpu.VMEM(shape, dtype)
    sums_shape = (16 + total_seqs, width)
    return pl.pallas_call(
        functools.partial(tail_kernel, total_tokens=total_tokens, parts=hidden_parts),
        in_specs=[any_spec] * 8 + [inside] * 3,
        out_specs=[any_spec, any_spec, inside],
        out_shape=[
            shape_of((2, block, width)), shape_of((3, up_rows, 2 * LANES)), shape_of(sums_shape, F32),
        ],
        scratch_shapes=[
            held(count, width), held(count, width), held(count, width), held(count, width),
            held(2, block, width), held(count, width, dtype=F32), held(*weight.shape), held(2, block, width),
            held(3, 2, 2, 2, up_rows, 2 * LANES),
        ]
        + Reduction.scratch(3, up_rows, 2 * LANES)
        + [
            held(5, *sums_shape, dtype=F32),
            pltpu.SemaphoreType.DMA((5,)),
            pltpu.SemaphoreType.DMA((5,)),
            pltpu.SemaphoreType.DMA((12,)),
        ]
        + Trade.semaphores(TOKEN_PARTS),
        compiler_params=pltpu.CompilerParams(
            vmem_limit_bytes=VMEM_BYTES, collective_id=1, has_side_effects=True
        ),
        cost_estimate=cost(60),
        name="tail",
    )(*grads, normed, *xs, middle_grad, weight, info, gain, feed_sums)


def finish_kernel(
    token_ref, layer_ref, qkv_ref, last_qkv_ref, up_out_ref, out_part_ref, down_ref, sums_ref,
    token_out, layer_out, qkv_out, up_out, out_out, down_out, table_out, *small_outs, total_seqs, parts, table_rows,
):
    token_out[...] = wide(token_ref)
    layer_out[...] = layer_ref[...]
    qkv_out[...] = jnp.concatenate([qkv_ref[0], last_qkv_ref[0]], 1).astype(F32)
    up_out[...] = up_out_ref[0].astype(F32)
    out_out[...] = out_part_ref[0].astype(F32)
    down_out[...] = wide(down_ref)
    block, width = table_out.shape
    steps_row = 9 + parts
    first = lax.axis_index("dp") * table_rows + pl.program_id(0) * block
    place = (lax.broadcasted_iota(jnp.int32, (block, 1), 0) + first).astype(F32)
    total = jnp.zeros_like(table_out)
    for s in range(total_seqs):
        chosen = place == sums_ref[steps_row : steps_row + 1, s : s + 1]
        total = total + jnp.where(chosen, sums_ref[16 + s : 17 + s], 0.0)
    table_out[...] = total

    @pl.when(pl.program_id(0) == 0)
    def _():
        d = lax.axis_index("dp")
        piece = small_outs[0].shape[0]
        turned = pltpu.roll(sums_ref[0:16], lax.rem(width - d * piece, width), 1)
        order = [row for row in range(8 + parts) if not 4 <= row < 4 + parts]
        for row, out in zip(order, small_outs):
            out[...] = turned[row, :piece]
        up_piece = small_outs[8].shape[0]
        share = width // up_piece
        mine = sums_ref[pl.ds(4 + d // share, 1)]
        mine = pltpu.roll(mine, lax.rem(width - d % share * up_piece, width), 1)
        small_outs[8][...] = mine[0, :up_piece]
        small_outs[9][...] = sums_ref[8 + parts, :BUCKETS]
        small_outs[10][...] = sums_ref[8 + parts, BUCKETS : 2 * BUCKETS]


def finish(token, layer, qkv, last_qkv, up_out, down, sums, table_rows, dp):
    seqs, length, width = token.shape
    parts, block = up_out.shape[0] - 1, up_out.shape[1]
    steps = parts
    small = [width // dp] * 8 + [parts * width // dp] + [BUCKETS] * 2
    rows_at = lambda many: pl.BlockSpec((many // steps, width), lambda i: (i, 0))
    count = seqs * length
    wide_rows = rows_at(count)
    made = pl.pallas_call(
        functools.partial(
            finish_kernel, total_seqs=sums.shape[0] - 16, parts=parts, table_rows=table_rows
        ),
        grid=(steps,),
        in_specs=[
            wide_rows, wide_rows,
            pl.BlockSpec((1, block, qkv.shape[2]), lambda i: (jnp.minimum(i, 2), 0, 0)),
            pl.BlockSpec((1, block, last_qkv.shape[2]), lambda i: (jnp.minimum(i, 2), 0, 0)),
            pl.BlockSpec((1, block, width), lambda i: (i, 0, 0)),
            pl.BlockSpec((1, block, width), lambda i: (parts, 0, 0)),
            rows_at(down.shape[0]),
            fixed(sums.shape),
        ],
        out_specs=[
            wide_rows, wide_rows,
            pl.BlockSpec((block, width), lambda i: (0, jnp.minimum(i, 2))),
            pl.BlockSpec((block, width), lambda i: (0, i)),
            pl.BlockSpec((block, width), lambda i: (0, 0)),
            rows_at(down.shape[0]), rows_at(table_rows),
        ]
        + [pl.BlockSpec((many,), lambda i: (0,)) for many in small],
        out_shape=[
            shape_of((count, width), F32), shape_of((count, width)), shape_of((block, 3 * width), F32),
            shape_of((block, parts * width), F32), shape_of((block, width), F32), shape_of(down.shape, F32),
            shape_of((table_rows, width), F32),
        ]
        + [shape_of((many,), F32) for many in small],
        compiler_params=params(),
        cost_estimate=cost(6),
        name="finish",
    )(token.reshape(count, width), layer.reshape(count, width), qkv, last_qkv, up_out, up_out, down, sums)
    shape = (seqs, length, width)
    return [made[0].reshape(shape), made[1].reshape(shape)] + list(made[2:])


def gelu_parts(hidden):
    share = 0.5 + 0.5 * lax.erf(hidden * 2**-0.5)
    bell = jnp.exp(-0.5 * hidden * hidden) * 0.3989422804014327
    return hidden * share, share + hidden * bell


def feed_kernel(
    context_ref, x0_ref, x1_ref, info_ref, cot0_ref, cot1_ref, out_weight_ref, up_ref, down_ref,
    out_bias_ref, gain_ref, shift_ref, down_bias_ref, up_bias_ref,
    out_ref, active_ref, hidden_grad_ref, normed_ref, middle_grad_ref, branch_ref, context_grad_ref, sums_ref,
    out_weight_v, up_v, down_v, loads,
):
    step = pl.program_id(0)
    width, hidden_width = x0_ref.shape[1], up_ref.shape[1]

    parts = hidden_width // width
    out_copy = pltpu.make_async_copy(out_weight_ref, out_weight_v, loads.at[0, parts])
    copies = []
    for part in range(parts):
        columns = pl.ds(part * width, width)
        copies.append(
            (
                pltpu.make_async_copy(up_ref.at[:, columns], up_v.at[:, columns], loads.at[0, part]),
                pltpu.make_async_copy(down_ref.at[columns], down_v.at[columns], loads.at[1, part]),
            )
        )

    @pl.when(step == 0)
    def _():
        out_copy.start()
        for one, two in copies:
            one.start()
            two.start()
        sums_ref[...] = jnp.zeros_like(sums_ref)
        out_copy.wait()

    x = jnp.where(step == 0, x0_ref[...], x1_ref[...])
    cot = jnp.where(step == 0, cot0_ref[...], cot1_ref[...])
    middle = (
        x.astype(F32)
        + one_row(info_ref, TIME)
        + dot(context_ref[...], out_weight_v[...], NN)
        + vector(out_bias_ref)
    )
    unit, scale = norm_parts(middle)
    gain = vector(gain_ref)
    normed = (unit * gain + vector(shift_ref)).astype(BF16)
    normed_ref[...] = normed
    out = middle + vector(down_bias_ref)
    normed_grad = jnp.zeros_like(out)
    up_bias = vector(up_bias_ref)
    for part in range(parts):
        columns = slice(part * width, (part + 1) * width)

        @pl.when(step == 0)
        def _():
            for copy in copies[part]:
                copy.wait()

        hidden = dot(normed, up_v[:, columns], NN) + up_bias[:, columns]
        active, slope = gelu_parts(hidden)
        active = active.astype(BF16)
        active_ref[:, columns] = active
        out = out + dot(active, down_v[columns, :], NN)
        hidden_grad = (dot(cot, down_v[columns, :], NT) * slope).astype(BF16)
        hidden_grad_ref[:, columns] = hidden_grad
        sums_ref[8 + part : 9 + part] += column_sum(hidden_grad.astype(F32))
        normed_grad = normed_grad + dot(hidden_grad, up_v[:, columns], NT)
    out_ref[...] = out.astype(BF16)
    cot = cot.astype(F32)
    middle_grad = cot + norm_backward(normed_grad, gain, unit, scale)
    middle_grad_ref[...] = middle_grad
    branch = middle_grad.astype(BF16)
    branch_ref[...] = branch
    context_grad_ref[...] = dot(branch, out_weight_v[...], NT).astype(BF16)
    sums_ref[0:1] += column_sum(cot)
    sums_ref[1:2] += column_sum(normed_grad * unit)
    sums_ref[2:3] += column_sum(normed_grad)
    sums_ref[3:4] += column_sum(branch.astype(F32))
    sums_ref[4:5] += column_sum(out * out)


def feed(context, xs, info, small, cots, out_weight, up, down):
    block, width = xs[0].shape
    count, hidden_width = 2 * block, up.shape[1]
    sums_rows = 8 + hidden_width // width + (-(hidden_width // width)) % 8
    whole = fixed((block, width))
    return pl.pallas_call(
        feed_kernel,
        grid=(2,),
        in_specs=[
            rows(block, width), whole, whole, fixed(info.shape), whole, whole,
        ]
        + [pl.BlockSpec(memory_space=pl.ANY)] * 3
        + [whole_vector(v) for v in small],
        out_specs=[
            rows(block, width), rows(block, hidden_width), rows(block, hidden_width), rows(block, width),
            rows(block, width), rows(block, width), rows(block, width),
            pl.BlockSpec((sums_rows, width), lambda i: (0, 0)),
        ],
        out_shape=[
            shape_of((count, width)), shape_of((count, hidden_width)), shape_of((count, hidden_width)),
            shape_of((count, width)), shape_of((count, width), F32), shape_of((count, width)),
            shape_of((count, width)), shape_of((sums_rows, width), F32),
        ],
        scratch_shapes=[
            pltpu.VMEM(out_weight.shape, BF16), pltpu.VMEM(up.shape, BF16), pltpu.VMEM(down.shape, BF16),
            pltpu.SemaphoreType.DMA((2, hidden_width // width + 1)),
        ],
        compiler_params=params(),
        cost_estimate=cost(34),
        name="feed",
    )(context, *xs, info, *cots, out_weight, up, down, *small)


def down_grad_kernel(active_ref, cot0_ref, cot1_ref, out_ref):
    block = cot0_ref.shape[0]
    out_ref[...] = (
        dot(active_ref[:block], cot0_ref[...], TN) + dot(active_ref[block:], cot1_ref[...], TN)
    ).astype(BF16)


def down_grad(active, cots):
    block, width = cots[0].shape
    count, hidden_width = active.shape
    return pl.pallas_call(
        down_grad_kernel,
        grid=(hidden_width // width,),
        in_specs=[pl.BlockSpec((count, width), lambda i: (0, i))] + [fixed((block, width))] * 2,
        out_specs=rows(width, width),
        out_shape=shape_of((hidden_width, width)),
        compiler_params=params(),
        cost_estimate=cost(8),
        name="down_grad",
    )(active, *cots)


def up_out_grad_kernel(normed_ref, hidden_grad_ref, context_ref, branch_ref, out_ref):
    last = pl.num_programs(0) - 1

    @pl.when(pl.program_id(0) < last)
    def _():
        out_ref[0] = dot(normed_ref[...], hidden_grad_ref[...], TN).astype(BF16)

    @pl.when(pl.program_id(0) == last)
    def _():
        out_ref[0] = dot(context_ref[...], branch_ref[...], TN).astype(BF16)


def up_out_grad(normed, hidden_grad, context, branch):
    count, width = normed.shape
    parts = hidden_grad.shape[1] // width
    whole = fixed((count, width))
    return pl.pallas_call(
        up_out_grad_kernel,
        grid=(parts + 1,),
        in_specs=[
            whole,
            pl.BlockSpec((count, width), lambda i: (0, jnp.minimum(i, parts - 1))),
            whole,
            whole,
        ],
        out_specs=pl.BlockSpec((1, width, width), lambda i: (i, 0, 0)),
        out_shape=shape_of((parts + 1, width, width)),
        compiler_params=params(),
        cost_estimate=cost(10),
        name="up_out_grad",
    )(normed, hidden_grad, context, branch)


def qkv_grad_kernel(normed_ref, grad_ref, out_ref):
    out_ref[0] = dot(normed_ref[...], grad_ref[...], TN).astype(BF16)


def qkv_grad(normed, grads):
    count, width = normed.shape
    parts = grads.shape[1] // width
    return pl.pallas_call(
        qkv_grad_kernel,
        grid=(parts,),
        in_specs=[fixed((count, width)), pl.BlockSpec((count, width), lambda i: (0, i))],
        out_specs=pl.BlockSpec((1, width, width), lambda i: (i, 0, 0)),
        out_shape=shape_of((parts, width, width)),
        compiler_params=params(),
        cost_estimate=cost(7),
        name="qkv_grad",
    )(normed, grads)


def start_kernel(
    query_grad_ref, key0_ref, key1_ref, far_key0_ref, far_key1_ref, value0_ref, value1_ref, far_value0_ref,
    far_value1_ref, x0_ref, x1_ref, info_ref, middle_grad_ref, gain_ref, weight_ref,
    token0_ref, token1_ref, grads_ref, sums_ref,
):
    step = pl.program_id(0)
    width = x0_ref.shape[1]

    @pl.when(step == 0)
    def _():
        sums_ref[...] = jnp.zeros_like(sums_ref)

    def pick(first, second):
        return jnp.where(step == 0, first[...], second[...])

    query_grad = query_grad_ref[...]
    key_grad = (pick(key0_ref, key1_ref).astype(F32) + pick(far_key0_ref, far_key1_ref).astype(F32)).astype(BF16)
    value_grad = (
        pick(value0_ref, value1_ref).astype(F32) + pick(far_value0_ref, far_value1_ref).astype(F32)
    ).astype(BF16)
    normed_grad = 0.0
    for part, grad in enumerate((query_grad, key_grad, value_grad)):
        columns = slice(part * width, (part + 1) * width)
        grads_ref[:, columns] = grad
        normed_grad = normed_grad + dot(grad, weight_ref[:, columns], NT)
    unit, scale = norm_parts(pick(x0_ref, x1_ref).astype(F32) + one_row(info_ref, TIME))
    token_grad = middle_grad_ref[...] + norm_backward(normed_grad, vector(gain_ref), unit, scale)

    @pl.when(step == 0)
    def _():
        token0_ref[...] = token_grad.astype(BF16)

    @pl.when(step == 1)
    def _():
        token1_ref[...] = token_grad.astype(BF16)

    sums_ref[0:1] += column_sum(normed_grad * unit)
    sums_ref[1:2] += column_sum(normed_grad)
    sums_ref[2:3] += column_sum(query_grad.astype(F32))
    sums_ref[3:4] += column_sum(value_grad.astype(F32))
    sums_ref[4:5] += column_sum(token_grad)


def start_back(query_grad, key_grads, value_grads, xs, info, middle_grad, gain, weight):
    block, width = xs[0].shape
    count = 2 * block
    whole = fixed((block, width))
    kept = pl.BlockSpec((block, width), lambda i: (0, 0))
    return pl.pallas_call(
        start_kernel,
        grid=(2,),
        in_specs=[rows(block, width)]
        + [whole] * 10
        + [fixed(info.shape), rows(block, width), whole_vector(gain), fixed(weight.shape)],
        out_specs=[kept, kept, rows(block, 3 * width), pl.BlockSpec((8, width), lambda i: (0, 0))],
        out_shape=[
            shape_of((block, width)), shape_of((block, width)), shape_of((count, 3 * width)),
            shape_of((8, width), F32),
        ],
        compiler_params=params(),
        cost_estimate=cost(10),
        name="start_back",
    )(query_grad, *key_grads, *value_grads, *xs, info, middle_grad, gain, weight)


class Places:
    def __init__(self, dp, seq):
        self.dp, self.seq = dp, seq
        self.bits = dp.bit_length() - 1

    def flat(self, d, z):
        return d * self.seq + z

    def pairs(self, to):
        return [
            (self.flat(d, z), self.flat(*to(d, z))) for d in range(self.dp) for z in range(self.seq)
        ]

    def gather_order(self, turn):
        def to(d, z):
            core, j = d % 2, (z + turn) % 2
            return d - core + z // 2, 2 * core + j

        return self.pairs(to)

    def scatter_order(self, turn):
        return [(b, a) for a, b in self.gather_order(turn)]

    def swap(self, bit):
        return self.pairs(lambda d, z: (d ^ (1 << bit), z))

    def swap_seq(self, step):
        return self.pairs(lambda d, z: (d, z ^ step))


def send(x, order):
    return lax.ppermute(x, BOTH, order)


def add(a, b):
    return (a.astype(F32) + b.astype(F32)).astype(BF16)


def reduce_parts(parts, places):
    d, z = lax.axis_index("dp"), lax.axis_index("seq")
    count, height, width = parts.shape
    block = height // places.dp
    grid = parts.reshape((count,) + (2,) * places.bits + (block, width))

    def halve(value, bit, axes):
        axis = 1 + axes.index(bit)
        mine = (d >> bit) & 1
        kept = lax.dynamic_index_in_dim(value, mine, axis, keepdims=False)
        sent = lax.dynamic_index_in_dim(value, 1 - mine, axis, keepdims=False)
        axes.remove(bit)
        return add(kept, send(sent, places.swap(bit)))

    axes = list(range(places.bits - 1, -1, -1))
    grid = halve(grid, 0, axes)
    halves = []
    for number, order in enumerate((range(1, places.bits), range(places.bits - 1, 0, -1))):
        at = block // 2
        value = lax.slice_in_dim(grid, number * at, (number + 1) * at, axis=grid.ndim - 2)
        left = list(axes)
        for bit in order:
            value = halve(value, bit, left)
        halves.append(sum_along_seq(value, z, places))
    return jnp.concatenate(halves, 1)


def sum_along_seq(value, z, places):
    count, block, width = value.shape
    mine = z % 2
    grid = value.reshape(count, block, 2, width // 2)
    kept = lax.dynamic_index_in_dim(grid, mine, 2, keepdims=False)
    sent = lax.dynamic_index_in_dim(grid, 1 - mine, 2, keepdims=False)
    half = add(kept, send(sent, places.swap_seq(1)))
    half = add(half, send(half, places.swap_seq(2)))
    other = send(half, places.swap_seq(1))
    first = jnp.where(mine == 0, half, other)
    second = jnp.where(mine == 0, other, half)
    return jnp.concatenate([first, second], 2).astype(F32)


def sum_everywhere(value, places):
    for bit in range(places.bits):
        value = value + send(value, places.swap(bit))
    for step in (1, 2):
        value = value + send(value, places.swap_seq(step))
    return value


def per_device(
    tokens, timesteps, time_table, ln1_gain, ln1_bias, qkv_weight, q_bias, v_bias, out_weight, out_bias,
    ln2_gain, ln2_bias, up_weight, up_bias, down_weight, down_bias, cotangent,
):
    places = Places(lax.axis_size("dp"), lax.axis_size("seq"))
    seq_count, local_len, width = tokens.shape
    hidden_width = up_weight.shape[1]
    assert places.seq == 4 and seq_count == 2 and places.dp == 1 << places.bits
    d, z = lax.axis_index("dp"), lax.axis_index("seq")
    core = d % 2
    total_seqs = seq_count * places.dp
    total_tokens = total_seqs * local_len * places.seq

    def gathered(array):
        blocks = []
        for turn in range(2):
            mine = lax.dynamic_index_in_dim(array, (z + turn) % 2, 0, keepdims=False)
            blocks.append(send(mine, places.gather_order(turn)))
        return blocks

    count = 2 * local_len
    parts = hidden_width // width
    first_small = (ln1_gain, ln1_bias, q_bias, v_bias)
    second_small = (out_bias, ln2_gain, ln2_bias, down_bias, up_bias)
    sequence = (d - core + z // 2) * seq_count + z % 2
    if places.dp == 8:
        made = front(tokens, qkv_weight, time_table, timesteps, first_small, count / total_tokens)
        xs, (normed, query), kvs, info = made[:2], made[2:4], list(made[4:8]), made[8]
        cotangent, query = lax.optimization_barrier((cotangent, query))
        cots = gathered(cotangent)
    else:
        info = jnp.concatenate(
            [
                known_rows(
                    timesteps[j], seq_count * d + j, count / total_tokens,
                    lax.dynamic_slice_in_dim(time_table, timesteps[j], 1, 0).astype(F32),
                )
                for j in range(2)
            ]
        )
        far_info = send(info, places.swap(0))
        xs = gathered(tokens)
        cots = gathered(cotangent)
        info = jnp.where(z // 2 == core, info, far_info)
        info = jnp.pad(jnp.where(z % 2 == 0, info[:4], info[4:]), ((0, 4), (0, 0)))
        normed, query, kv0 = project(xs[0], info, first_small, qkv_weight, count)
        far0 = send(kv0, places.swap(0))
        normed, query, kv1 = project(xs[1], info, first_small, qkv_weight, count, (normed, query))
        kvs = [kv0, kv1, far0, send(kv1, places.swap(0))]
    context, logsum = attend(query, kvs)
    out, active, hidden_grad, normed_two, middle_grad, branch, context_grad, feed_sums = feed(
        context, xs, info, second_small, cots, out_weight, up_weight, down_weight
    )

    def scattered(blocks, dtype):
        back = [send(block, places.scatter_order(turn)) for turn, block in enumerate(blocks)]
        even = z % 2 == 0
        return jnp.stack(
            [jnp.where(even, back[0], back[1]), jnp.where(even, back[1], back[0])]
        ).astype(dtype)


    if places.dp == 8:
        made = back(
            query, context_grad, context, logsum, kvs, normed_two, hidden_grad, branch, active, cots,
            normed, out
        )
        tokens_grad, last_qkv, packed = tail(
            made[:3], normed, xs, middle_grad, qkv_weight, info, ln1_gain, feed_sums, total_tokens, parts
        )
        tokens_grad, layer_out, qkv_sum, up_sum, out_sum, down_sum, table_grad, *small = finish(
            tokens_grad, made[3], made[6], last_qkv, made[5], made[4][0], packed,
            time_table.shape[0] // places.dp, places.dp,
        )
    else:
        layer_out = scattered([out[:local_len], out[local_len:]], BF16)
        down_sum = reduce_parts(down_grad(active, cots)[None], places)[0]
        up_out_sum = reduce_parts(up_out_grad(normed_two, hidden_grad, context, branch), places)
        made = attend_back(query, context_grad, context, logsum, kvs)
        token0, token1, projected_grad, start_sums = start_back(
            made[0],
            list(made[1:3]) + [send(g, places.swap(0)) for g in made[3:5]],
            list(made[5:7]) + [send(g, places.swap(0)) for g in made[7:9]],
            xs, info, middle_grad, ln1_gain, qkv_weight,
        )
        tokens_grad = scattered([token0, token1], F32)
        qkv_sum = reduce_parts(qkv_grad(normed, projected_grad), places)
        energy = jnp.sum(feed_sums[4]) / (width * total_tokens)
        sequence_rows = jnp.where(jnp.arange(total_seqs)[:, None] == sequence, start_sums[4][None], 0.0)
        packed = jnp.concatenate(
            [
                feed_sums[0:4], feed_sums[8 : 8 + parts], start_sums[0:4],
                jnp.stack(
                    [info[MARK] * energy + info[SHARE], info[STEP] * jnp.where(core == 0, 1.0, 0.0)]
                ),
                sequence_rows,
            ]
        )
        packed = sum_everywhere(packed, places)
        steps = packed[9 + parts, :total_seqs].astype(jnp.int32)
        table_rows = time_table.shape[0] // places.dp
        chosen = (steps[None, :] == (jnp.arange(table_rows) + d * table_rows)[:, None]).astype(F32)
        table_grad = jnp.dot(chosen, packed[10 + parts :], precision=lax.Precision.HIGHEST)

        def side_by_side(stacked):
            return jnp.moveaxis(stacked, 0, 1).reshape(stacked.shape[1], -1)

        qkv_sum, out_sum = side_by_side(qkv_sum), up_out_sum[parts]
        up_sum = side_by_side(up_out_sum[:parts])
        piece = width // places.dp
        mine = lax.dynamic_slice_in_dim(packed[: 8 + parts], d * piece, piece, 1)
        up_piece = hidden_width // places.dp
        up_bias_sum = lax.dynamic_slice_in_dim(packed[4 : 4 + parts].reshape(-1), d * up_piece, up_piece, 0)
        stats = packed[8 + parts]
        small = [mine[row] for row in (0, 1, 2, 3, 4 + parts, 5 + parts, 6 + parts, 7 + parts)]
        small += [up_bias_sum, stats[:BUCKETS], stats[BUCKETS : 2 * BUCKETS]]
    down_bias_sum, gain_two, shift_two, out_bias_sum, gain_one, shift_one, q_sum, v_sum = small[:8]
    return (
        layer_out, tokens_grad, table_grad, gain_one, shift_one, qkv_sum, q_sum, v_sum, out_sum, out_bias_sum,
        gain_two, shift_two, up_sum, small[8], down_sum, down_bias_sum, small[9], small[10],
    )


def solution(mesh):
    split = P("dp", "seq", None)
    return jax.shard_map(
        per_device,
        mesh=mesh,
        in_specs=(split, P("dp")) + (P(),) * 14 + (split,),
        out_specs=(
            split, split, P("dp", None), P("dp"), P("dp"), P("dp", None), P("dp"), P("dp"), P("dp", None),
            P("dp"), P("dp"), P("dp"), P("dp", None), P("dp"), P("dp", None), P("dp"), P(), P(),
        ),
        check_vma=False,
    )
```

```python
import functools

import jax
import jax.numpy as jnp
from jax import lax
from jax.experimental import pallas as pl
from jax.experimental.pallas import tpu as pltpu
from jax.sharding import PartitionSpec as P

HEAD_DIM = 64
TSTEPS = 2048
BUCKETS = 4
EPS = 1e-05
LANES = 128
VMEM_BYTES = 60 * 1024 * 1024
BOTH = ("dp", "seq")
TOKEN_PARTS = 8
F32 = jnp.float32
BF16 = jnp.bfloat16
NN = (((1,), (0,)), ((), ()))
NT = (((1,), (1,)), ((), ()))
TN = (((0,), (0,)), ((), ()))


def dot(a, b, dims):
    return lax.dot_general(a, b, dims, preferred_element_type=F32)


def wide(ref):
    return ref[...].astype(F32)


def column_sum(v):
    return jnp.sum(v, 0, keepdims=True)


def fixed(shape):
    return pl.BlockSpec(shape, lambda *i: (0,) * len(shape), pipeline_mode=pl.Buffered(1))


def rows(block, width):
    return pl.BlockSpec((block, width), lambda i: (i, 0))


def shape_of(shape, dtype=BF16):
    return jax.ShapeDtypeStruct(shape, dtype)


def cost(us):
    return pl.CostEstimate(flops=int(us * 1.15e9), bytes_accessed=0, transcendentals=0)


def params():
    return pltpu.CompilerParams(vmem_limit_bytes=VMEM_BYTES)


def norm_parts(v):
    centered = v - jnp.mean(v, -1, keepdims=True)
    scale = lax.rsqrt(jnp.mean(centered * centered, -1, keepdims=True) + EPS)
    return centered * scale, scale


def norm_backward(grad, gain, unit, scale):
    scaled = grad * gain
    return scale * (
        scaled
        - jnp.mean(scaled, -1, keepdims=True)
        - unit * jnp.mean(scaled * unit, -1, keepdims=True)
    )


TIME, MARK, SHARE, STEP = range(4)


def one_row(ref, at):
    return ref[at : at + 1].astype(F32)


def vector(ref):
    return ref[...].astype(F32).reshape(1, -1)


def whole_vector(v):
    return pl.BlockSpec(v.shape, lambda *i: (0,), pipeline_mode=pl.Buffered(1))


def known_rows(step, sequence, share, time_row):
    lane = lax.broadcasted_iota(jnp.int32, time_row.shape, 1)
    bucket = step * BUCKETS // TSTEPS
    return jnp.concatenate(
        [
            time_row,
            jnp.where(lane == bucket, 1.0, 0.0),
            jnp.where(lane == BUCKETS + bucket, share, 0.0),
            jnp.where(lane == sequence, step.astype(F32), 0.0),
        ],
        0,
    )


def project_rows(x, info_ref, small, weight_ref):
    width = x.shape[1]
    gain, shift, query_bias, value_bias = small
    unit, _ = norm_parts(x.astype(F32) + one_row(info_ref, TIME))
    normed = (unit * vector(gain) + vector(shift)).astype(BF16)

    def part(number):
        made = dot(normed, weight_ref[:, number * width : (number + 1) * width], NN)
        if number != 1:
            made = made + vector(query_bias if number == 0 else value_bias)
        made = made.astype(BF16)
        return made * jnp.asarray(HEAD_DIM ** (-0.5), BF16) if number == 0 else made

    return normed, part


def project_kernel(x_ref, info_ref, weight_ref, *refs):
    normed_ref, query_ref, kv_ref = refs[-3:]
    width = x_ref.shape[1]
    normed, part = project_rows(x_ref[...], info_ref, refs[:4], weight_ref)
    normed_ref[...] = normed
    query_ref[...] = part(0)
    kv_ref[:, :width] = part(1)
    kv_ref[:, width:] = part(2)


def project(x, info, small, weight, total, begun=None, block=256):
    count, width = x.shape
    first = 0 if begun is None else total // block - count // block
    later = pl.BlockSpec((block, width), lambda i: (i + first, 0))
    extra = [] if begun is None else list(begun)
    return pl.pallas_call(
        project_kernel,
        grid=(count // block,),
        in_specs=[rows(block, width), fixed(info.shape), fixed(weight.shape)]
        + [whole_vector(v) for v in small]
        + [pl.BlockSpec(memory_space=pl.ANY)] * len(extra),
        out_specs=[later, later, rows(block, 2 * width)],
        out_shape=[
            shape_of((total, width)),
            shape_of((total, width)),
            shape_of((count, 2 * width)),
        ],
        input_output_aliases={7: 0, 8: 1} if extra else {},
        compiler_params=params(),
        cost_estimate=cost(5),
        name="project",
    )(x, info, weight, *small, *extra)


def lane_parts():
    lane = lax.broadcasted_iota(jnp.int32, (1, LANES), 1)
    return lane < HEAD_DIM, lane % HEAD_DIM


def with_offset(own, place, base, offset):
    high = offset.astype(BF16)
    left = offset - high.astype(F32)
    mid = left.astype(BF16)
    low = (left - mid.astype(F32)).astype(BF16)
    zero = jnp.zeros_like(low)
    parts = jnp.where(place == 0, high, jnp.where(place == 1, mid, jnp.where(place == 2, low, zero)))
    return jnp.where(own, base, parts)


def attend_kernel(query_ref, *refs, pieces):
    key_refs, value_refs = refs[:pieces], refs[pieces : 2 * pieces]
    context_ref, logsum_ref = refs[2 * pieces :]
    count = query_ref.shape[0]
    low, place = lane_parts()
    row_half = lax.broadcasted_iota(jnp.int32, (LANES, LANES), 0) // HEAD_DIM
    lane_half = lax.broadcasted_iota(jnp.int32, (LANES, LANES), 1) // HEAD_DIM
    swapped = jnp.where(row_half != lane_half, 1.0, 0.0).astype(BF16)
    query = query_ref[...]

    def norms(v):
        v = v.astype(F32)
        return dot((v * v).astype(BF16), swapped, NN)

    key_norm = functools.reduce(
        jnp.maximum, [jnp.max(norms(ref[...]), 0, keepdims=True) for ref in key_refs]
    )
    bound = jnp.sqrt(norms(query) * key_norm) * 1.01
    ones_key = jnp.where(place < 3, 1.0, 0.0).astype(BF16)
    values = [ref[...].T for ref in value_refs]
    ones = jnp.ones((16, value_refs[0].shape[0]), BF16)

    def value_of(piece, head):
        return jnp.concatenate([values[piece][head * HEAD_DIM : (head + 1) * HEAD_DIM], ones], 0)

    def finish(mixed, offset):
        totals = [m[HEAD_DIM : HEAD_DIM + 1] for m in mixed]
        context = jnp.concatenate([m[:HEAD_DIM] / t for m, t in zip(mixed, totals)], 0)
        context_ref[...] = context.T.astype(BF16)
        logs = [jnp.broadcast_to(jnp.log(t), (HEAD_DIM, count)) for t in reversed(totals)]
        logsum_ref[...] = jnp.concatenate(logs, 0).T + offset

    mixed = []
    for head in range(2):
        own = low if head == 0 else ~low
        query_own = with_offset(own, place, query, -bound)
        out = 0.0
        for piece in range(pieces):
            key_own = jnp.where(own, key_refs[piece][...], ones_key)
            weights = jnp.exp(dot(key_own, query_own, NT)).astype(BF16)
            out = out + dot(value_of(piece, head), weights, NN)
        mixed.append(out)
    finish(mixed, bound)
    smallest = jnp.min(jnp.minimum(mixed[0][HEAD_DIM], mixed[1][HEAD_DIM]))

    @pl.when(smallest < 1e-25)
    def _():
        again, tops = [], []
        for head in range(2):
            own = low if head == 0 else ~low
            query_own = jnp.where(own, query, jnp.zeros_like(query))
            top = jnp.full((1, count), -jnp.inf, F32)
            for piece in range(pieces):
                scores = dot(key_refs[piece][...], query_own, NT)
                top = jnp.maximum(top, jnp.max(scores, 0, keepdims=True))
            out = 0.0
            for piece in range(pieces):
                scores = dot(key_refs[piece][...], query_own, NT)
                out = out + dot(value_of(piece, head), jnp.exp(scores - top).astype(BF16), NN)
            again.append(out)
            tops.append(jnp.broadcast_to(top, (HEAD_DIM, count)))
        finish(again, jnp.concatenate(tops[::-1], 0).T)


def attend(query, kvs):
    count, width = query.shape
    pairs, pieces, length = width // LANES, len(kvs), kvs[0].shape[0]
    row = pl.BlockSpec((count, LANES), lambda p: (0, p))
    return pl.pallas_call(
        functools.partial(attend_kernel, pieces=pieces),
        grid=(pairs,),
        in_specs=[row]
        + [pl.BlockSpec((length, LANES), lambda p: (0, p))] * pieces
        + [pl.BlockSpec((length, LANES), lambda p: (0, pairs + p))] * pieces,
        out_specs=[row, row],
        out_shape=[shape_of((count, width)), shape_of((count, width), F32)],
        compiler_params=params(),
        cost_estimate=cost(32),
        name="attend",
    )(query, *kvs, *kvs)


def attend_back_step(query_ref, grad_ref, context_ref, logsum_ref, pieces, query_grad_ref):
    low, place = lane_parts()
    query, grad = query_ref[...], grad_ref[...]
    count = query.shape[0]
    product = grad.astype(F32) * wide(context_ref)
    logsum = logsum_ref[...]
    ones_key = jnp.where(place < 3, 1.0, 0.0).astype(BF16)
    zero = jnp.zeros_like(query)
    heads = []
    for head in range(2):
        own = low if head == 0 else ~low
        inner = jnp.sum(jnp.where(own, product, 0.0), -1, keepdims=True)
        heads.append(
            (
                own,
                with_offset(own, place, query, -logsum),
                with_offset(own, place, grad, jnp.broadcast_to(-inner, logsum.shape)),
                jnp.where(own, query, zero),
                jnp.where(own, grad, zero),
            )
        )
    length = sum(piece[0].shape[0] for piece in pieces)
    query_grads = [0.0, 0.0]
    key_mean = 0.0
    for key_ref, value_ref, key_grad_ref, value_grad_ref, before in pieces:
        if before is not None:
            before()
        key, value = key_ref[...], value_ref[...]
        key_turned = key.T
        key_mean = key_mean + jnp.sum(key_turned.astype(F32), 1, keepdims=True) / length
        ones = jnp.ones((16, key.shape[0]), BF16)
        key_grad, value_grad = 0.0, 0.0
        for head, (own, query_off, grad_off, query_own, grad_own) in enumerate(heads):
            scores = dot(jnp.where(own, key, ones_key), query_off, NT)
            probs = jnp.exp(scores)
            prob_grad = dot(jnp.where(own, value, ones_key), grad_off, NT)
            score_grad = (probs * prob_grad).astype(BF16)
            value_grad = value_grad + dot(probs.astype(BF16), grad_own, NN)
            key_grad = key_grad + dot(score_grad, query_own, NN)
            lanes = slice(head * HEAD_DIM, (head + 1) * HEAD_DIM)
            turned = jnp.concatenate([key_turned[lanes], ones], 0)
            query_grads[head] = query_grads[head] + dot(turned, score_grad, NN)
        key_grad_ref[...] = key_grad.astype(BF16)
        value_grad_ref[...] = value_grad.astype(BF16)
    parts = [
        made[:HEAD_DIM]
        - key_mean[head * HEAD_DIM : (head + 1) * HEAD_DIM]
        * jnp.broadcast_to(made[HEAD_DIM : HEAD_DIM + 1], (HEAD_DIM, count))
        for head, made in enumerate(query_grads)
    ]
    query_grad_ref[...] = (jnp.concatenate(parts, 0) * HEAD_DIM ** (-0.5)).T.astype(BF16)


def attend_back_kernel(query_ref, grad_ref, context_ref, logsum_ref, *refs, pieces):
    key_refs, value_refs = refs[:pieces], refs[pieces : 2 * pieces]
    query_grad_ref = refs[2 * pieces]
    key_grad_refs = refs[2 * pieces + 1 : 3 * pieces + 1]
    value_grad_refs = refs[3 * pieces + 1 :]
    steps = list(zip(key_refs, value_refs, key_grad_refs, value_grad_refs, [None] * pieces))
    attend_back_step(query_ref, grad_ref, context_ref, logsum_ref, steps, query_grad_ref)


def attend_back(query, grad, context, logsum, kvs):
    count, width = query.shape
    pairs, pieces, length = width // LANES, len(kvs), kvs[0].shape[0]
    row = pl.BlockSpec((count, LANES), lambda p: (0, p))
    piece = pl.BlockSpec((length, LANES), lambda p: (0, p))
    return pl.pallas_call(
        functools.partial(attend_back_kernel, pieces=pieces),
        grid=(pairs,),
        in_specs=[row] * 4
        + [piece] * pieces
        + [pl.BlockSpec((length, LANES), lambda p: (0, pairs + p))] * pieces,
        out_specs=[row] + [piece] * (2 * pieces),
        out_shape=[shape_of((count, width))] + [shape_of((length, width))] * (2 * pieces),
        compiler_params=params(),
        cost_estimate=cost(75),
        name="attend_back",
    )(query, grad, context, logsum, *kvs, *kvs)


def here():
    d, z = lax.axis_index("dp"), lax.axis_index("seq")
    return d, z, d // 4, (d // 2) % 2, d % 2


def partners():
    d, z, y, x, core = here()
    return {
        "core": (d + 1 - 2 * core, z),
        "x": (d + 2 - 4 * x, z),
        "y": (d + 4 - 8 * y, z),
        "near": (d, z + 1 - 2 * (z % 2)),
        "across": (d, (z + 2) % 4),
        "inner": (d, 3 - z),
    }


def outer():
    z = lax.axis_index("seq")
    return (z == 0) | (z == 3)


def remote(source, target, sends, receives, send_index, receive_index, device):
    return pltpu.make_async_remote_copy(
        src_ref=source,
        dst_ref=target,
        send_sem=sends.at[send_index],
        recv_sem=receives.at[receive_index],
        device_id=device,
        device_id_type=pl.DeviceIdType.MESH,
    )


class Reduction:
    def __init__(self, source, out, scratch):
        self.source, self.out = source, out
        self.own = source.at[:, :, :, here()[4]]
        self.from_core, self.first, self.second, self.near, self.far = scratch[:5]
        self.sends, self.receives, self.local = scratch[5:8]
        self.parts, _, _, self.rows, self.width = self.from_core.shape
        self.half = self.width // 2

    @staticmethod
    def scratch(parts, block, width):
        half = width // 2
        return [
            pltpu.VMEM((parts, 2, 2, block, width), BF16),
            pltpu.VMEM((2, parts, 2, block, half), BF16),
            pltpu.VMEM((2, parts, block, half), BF16),
            pltpu.VMEM((parts, block, width), BF16),
            pltpu.VMEM((parts, block, width), BF16),
            pltpu.SemaphoreType.DMA((8,)),
            pltpu.SemaphoreType.DMA((8,)),
            pltpu.SemaphoreType.DMA((1,)),
        ]

    def copy(self, number):
        d, z, y, x, core = here()
        to = partners()
        left, right = pl.ds(0, self.half), pl.ds(self.half, self.half)
        source, target, device = (
            lambda: (self.source.at[:, :, :, 1 - core], self.from_core, to["core"]),
            lambda: (self.own.at[:, :, 1 - x, :, left], self.first.at[0], to["x"]),
            lambda: (self.own.at[:, 1 - y, :, :, right], self.first.at[1], to["y"]),
            lambda: (self.own.at[:, 1 - y, x, :, left], self.second.at[0], to["y"]),
            lambda: (self.own.at[:, y, 1 - x, :, right], self.second.at[1], to["x"]),
            lambda: (self.own.at[:, y, x], self.near, to["near"]),
            lambda: (self.own.at[:, y, x], self.far, to["inner"]),
            lambda: (self.own.at[:, y, x], self.near, to["near"]),
        )[number]()
        return remote(source, target, self.sends, self.receives, number, number, device)

    def to_cores(self):
        self.copy(0).start()

    def to_first(self):
        self.copy(0).wait()
        for part in range(self.parts):
            for i in range(2):
                for j in range(2):
                    self.own[part, i, j] = self.own[part, i, j] + self.from_core[part, i, j]
        self.copy(1).start()
        self.copy(2).start()

    def to_second(self):
        _, _, y, x, _ = here()
        self.copy(1).wait()
        self.copy(2).wait()
        left, right = slice(0, self.half), slice(self.half, self.width)
        for part in range(self.parts):
            for i in range(2):
                self.own[part, i, x, :, left] = self.own[part, i, x, :, left] + self.first[0, part, i]
                self.own[part, y, i, :, right] = self.own[part, y, i, :, right] + self.first[1, part, i]
        self.copy(3).start()
        self.copy(4).start()

    def to_near(self):
        _, _, y, x, _ = here()
        self.copy(3).wait()
        self.copy(4).wait()
        left, right = slice(0, self.half), slice(self.half, self.width)
        for part in range(self.parts):
            self.own[part, y, x, :, left] = self.own[part, y, x, :, left] + self.second[0, part]
            self.own[part, y, x, :, right] = self.own[part, y, x, :, right] + self.second[1, part]

        @pl.when(outer())
        def _():
            self.copy(5).start()

    def add_whole(self, received):
        _, _, y, x, _ = here()
        for part in range(self.parts):
            self.own[part, y, x] = self.own[part, y, x] + received[part]

    def to_far(self):
        @pl.when(jnp.logical_not(outer()))
        def _():
            self.copy(5).wait_recv()
            self.add_whole(self.near)
            self.copy(6).start()

    def to_other(self):
        @pl.when(jnp.logical_not(outer()))
        def _():
            self.copy(6).wait()
            self.add_whole(self.far)
            self.copy(7).start()

    def to_out(self):
        _, _, y, x, _ = here()

        @pl.when(outer())
        def _():
            self.copy(5).wait_send()
            self.copy(7).wait_recv()
            pltpu.make_async_copy(self.near, self.out, self.local.at[0]).start()

        @pl.when(jnp.logical_not(outer()))
        def _():
            pltpu.make_async_copy(self.own.at[:, y, x], self.out, self.local.at[0]).start()

    def finish(self):
        _, _, y, x, _ = here()

        @pl.when(outer())
        def _():
            pltpu.make_async_copy(self.near, self.out, self.local.at[0]).wait()

        @pl.when(jnp.logical_not(outer()))
        def _():
            self.copy(7).wait_send()
            pltpu.make_async_copy(self.own.at[:, y, x], self.out, self.local.at[0]).wait()


class Trade:
    def __init__(self, out, sends, receives, local, gather=False, parts=1):
        self.out, self.sends, self.receives, self.local = out, sends, receives, local
        self.gather, self.parts = gather, parts

    @staticmethod
    def semaphores(parts=1):
        return [pltpu.SemaphoreType.DMA((2, parts)), pltpu.SemaphoreType.DMA((2, parts)), pltpu.SemaphoreType.DMA((parts,))]

    def device(self, p):
        d, z, _, _, core = here()
        return (d - core + z // 2, 2 * core + (z + p) % 2)

    def stays(self):
        _, z, _, _, core = here()
        return z // 2 == core

    def slot(self, p):
        return p if self.gather else lax.axis_index("seq") % 2

    def own_slot(self, p):
        return p if self.gather else (lax.axis_index("seq") + p) % 2

    def greet(self, barrier):
        @pl.when(jnp.logical_not(self.stays()))
        def _():
            pl.semaphore_signal(barrier, inc=1, device_id=self.device(0), device_id_type=pl.DeviceIdType.MESH)

        pl.semaphore_signal(barrier, inc=1, device_id=self.device(1), device_id_type=pl.DeviceIdType.MESH)
        return jnp.where(self.stays(), 1, 2)

    def rows(self, ref, part):
        many = ref.shape[0] // self.parts
        return ref.at[pl.ds(part * many, many)]

    def keep(self, block, part):
        return pltpu.make_async_copy(
            self.rows(block, part), self.rows(self.out.at[self.own_slot(0)], part), self.local.at[part]
        )

    def copy(self, p, block, part):
        slot = self.slot(p)
        return pltpu.make_async_remote_copy(
            src_ref=self.rows(block, part),
            dst_ref=self.rows(self.out.at[slot], part),
            send_sem=self.sends.at[p, part],
            recv_sem=self.receives.at[slot, part],
            device_id=self.device(p),
            device_id_type=pl.DeviceIdType.MESH,
        )

    def each(self, p, far, near):
        if p == 1:
            far()
            return
        pl.when(jnp.logical_not(self.stays()))(far)
        pl.when(self.stays())(near)

    def begin(self, p, block, part=0):
        self.each(p, lambda: self.copy(p, block, part).start(), lambda: self.keep(block, part).start())

    def sent(self, p, block, part=0):
        self.each(p, lambda: self.copy(p, block, part).wait_send(), lambda: None)

    def arrived(self, p, block, part=0):
        slot = self.own_slot(p)
        target = self.rows(self.out.at[slot], part)

        def far():
            pltpu.make_async_remote_copy(
                src_ref=target,
                dst_ref=target,
                send_sem=self.sends.at[p, part],
                recv_sem=self.receives.at[slot, part],
                device_id=self.device(p),
                device_id_type=pl.DeviceIdType.MESH,
            ).wait_recv()

        self.each(p, far, lambda: self.keep(block, part).wait())


def meet(names, *trades):
    barrier = pltpu.get_barrier_semaphore()
    to = partners()
    for name in names:
        pl.semaphore_signal(barrier, inc=1, device_id=to[name], device_id_type=pl.DeviceIdType.MESH)
    expected = len(names)
    for one in trades:
        expected = expected + one.greet(barrier)
    pl.semaphore_wait(barrier, expected)


def front_kernel(
    tokens, weight, table, steps_ref, gain, shift, query_bias, value_bias,
    x0_out, x1_out, normed_out, query_out, near0_out, near1_out, far0_out, far1_out, info_out,
    x_v, weight_v, table_v, info_here, info_in, normed_v, query_v, near_v, far_v,
    load, stores, info_sends, info_receives, sends, receives, *trade, share,
):
    d, z, _, _, core = here()
    block, width = x_v.shape[1:]
    small = (gain, shift, query_bias, value_bias)
    trade = Trade(x_v, *trade, gather=True)
    loaded = pltpu.make_async_copy(weight, weight_v, load.at[0])
    looked_up = pltpu.make_async_copy(table, table_v, load.at[1])
    meet(("core",), trade)
    held = [tokens.at[(z + p) % 2] for p in range(2)]
    for p in range(2):
        trade.begin(p, held[p])
    looked_up.start()
    loaded.start()
    steps = [steps_ref[j] for j in range(2)]
    row = lax.broadcasted_iota(jnp.int32, (16, table.shape[0]), 0)
    place = lax.broadcasted_iota(jnp.int32, (16, table.shape[0]), 1)
    wanted = jnp.where(row == 0, steps[0], jnp.where(row == 1, steps[1], -1))
    chosen = jnp.where(place == wanted, 1.0, 0.0).astype(BF16)
    looked_up.wait()
    time_rows = dot(chosen, table_v[...], NN)
    for j in range(2):
        info_here[4 * j : 4 * j + 4] = known_rows(steps[j], 2 * d + j, share, time_rows[j : j + 1])
    known = remote(info_here, info_in, info_sends, info_receives, 0, 0, partners()["core"])
    known.start()
    known.wait()
    mine = jnp.where(z // 2 == core, info_here[...], info_in[...])
    info_out[0:4] = jnp.where(z % 2 == 0, mine[0:4], mine[4:8])
    info_out[4:8] = jnp.zeros_like(info_in[4:8])
    loaded.wait()
    copies, moved = [], []
    for p in range(2):
        trade.arrived(p, held[p])
        normed, part = project_rows(x_v[p], info_out, small, weight_v)
        near_v[p, :, :width] = part(1)
        near_v[p, :, width:] = part(2)
        moved.append(remote(near_v.at[p], far_v.at[p], sends, receives, p, p, partners()["core"]))
        moved[p].start()
        normed_v[p] = normed
        query_v[p] = part(0)
        outs = (x0_out, x1_out)[p], (near0_out, near1_out)[p]
        here_rows = pl.ds(p * block, block)
        for number, (source, target) in enumerate(
            (
                (x_v.at[p], outs[0]), (normed_v.at[p], normed_out.at[here_rows]),
                (query_v.at[p], query_out.at[here_rows]), (near_v.at[p], outs[1]),
            )
        ):
            copies.append(pltpu.make_async_copy(source, target, stores.at[p, number]))
            copies[-1].start()
    for p in range(2):
        moved[p].wait()
        copies.append(pltpu.make_async_copy(far_v.at[p], (far0_out, far1_out)[p], stores.at[p, 4]))
        copies[-1].start()
    for p in range(2):
        trade.sent(p, held[p])
    for copy in copies:
        copy.wait()


def front(tokens, weight, table, steps, small, share):
    _, block, width = tokens.shape
    info_shape = (8, width)
    any_spec = pl.BlockSpec(memory_space=pl.ANY)
    inside = pl.BlockSpec(memory_space=pltpu.VMEM)
    pair = pltpu.VMEM((2, block, width), BF16)
    wide_pair = pltpu.VMEM((2, block, 2 * width), BF16)
    one = pltpu.SemaphoreType.DMA((1,))
    two = pltpu.SemaphoreType.DMA((2,))
    return pl.pallas_call(
        functools.partial(front_kernel, share=share),
        in_specs=[any_spec] * 3 + [pl.BlockSpec(memory_space=pltpu.SMEM)] + [inside] * 4,
        out_specs=[any_spec] * 8 + [inside],
        out_shape=[shape_of((block, width))] * 2
        + [shape_of((2 * block, width))] * 2
        + [shape_of((block, 2 * width))] * 4
        + [shape_of(info_shape, F32)],
        scratch_shapes=[
            pair, pltpu.VMEM(weight.shape, BF16), pltpu.VMEM(table.shape, BF16), pltpu.VMEM(info_shape, F32),
            pltpu.VMEM(info_shape, F32), pair, pair, wide_pair, wide_pair,
            two, pltpu.SemaphoreType.DMA((2, 5)), one, one, two, two,
        ]
        + Trade.semaphores(),
        compiler_params=pltpu.CompilerParams(
            vmem_limit_bytes=VMEM_BYTES, collective_id=2, has_side_effects=True
        ),
        cost_estimate=cost(48),
        name="front",
    )(tokens, weight, table, steps, *small)


def fixed_any():
    return pl.BlockSpec(memory_space=pl.ANY)


def back_kernel(
    query_ref, grad_ref, context_ref, logsum_ref, *refs, pieces, parts, pairs
):
    key_refs, value_refs = refs[:pieces], refs[pieces : 2 * pieces]
    refs = refs[2 * pieces :]
    normed_ref, hidden_grad_ref, whole_context, branch, active_ref, cot0, cot1 = refs[:7]
    first_normed, layer_ref, query_grad_ref, key_out, value_out, layer_out, down_out, up_out, qkv_out = refs[7:16]
    refs = refs[16:]
    near = pieces // 2
    down_parts, up_parts = refs[:2]
    chunks = []
    for number, (which, at, many) in enumerate(back_chunks(down_parts.shape, up_parts.shape)):
        scratch = refs[2 + 8 * number : 10 + 8 * number]
        if which == "down":
            here_rows = pl.ds(at, many)
            chunks.append(
                Reduction(down_parts.at[:, :, :, :, here_rows], down_out.at[:, here_rows], scratch)
            )
        else:
            here_parts = pl.ds(at, many)
            chunks.append(Reduction(up_parts.at[here_parts], up_out.at[here_parts], scratch))
    qkv_parts = refs[34]
    for group in range(2):
        lanes = pl.ds(2 * group * LANES, 2 * LANES)
        scratch = refs[35 + 8 * group : 43 + 8 * group]
        chunks.append(Reduction(qkv_parts.at[group], qkv_out.at[:, :, lanes], scratch))
    one, two, three, four, five, six = chunks
    query_held, near_grads, far_grads, far_in, far_sends, far_receives = refs[51:57]
    whole_context_ref, branch_ref, cots_ref, first_normed_ref, loads = refs[57:62]
    back = Trade(layer_out, *refs[62:])
    block = key_refs[0].shape[0]
    layer_blocks = [layer_ref.at[pl.ds(p * block, block)] for p in range(2)]
    step = pl.program_id(0)
    made = 2 * parts + 1
    pair, last = step - made, pl.num_programs(0) - 1

    def far_copy(which):
        return remote(
            far_grads, far_in.at[which % 2], far_sends, far_receives, 0, which, partners()["core"]
        )

    loaded = [
        pltpu.make_async_copy(source, target, loads.at[number])
        for number, (source, target) in enumerate(
            (
                (whole_context, whole_context_ref), (branch, branch_ref), (cot0, cots_ref.at[pl.ds(0, block)]),
                (cot1, cots_ref.at[pl.ds(block, block)]), (first_normed, first_normed_ref),
            )
        )
    ]

    def begin():
        for copy in loaded:
            copy.start()
        meet(("core", "x", "y", "near", "inner"), back)
        back.begin(0, layer_blocks[0])
        back.begin(1, layer_blocks[1])

    def settle():
        which = pair - 1
        slot = which % 2
        far_copy(which).wait()
        key_grad = near_grads[slot, 0] + far_in[slot, 0]
        value_grad = near_grads[slot, 1] + far_in[slot, 1]
        key_out[...] = key_grad
        value_out[...] = value_grad

        @pl.when(which < 4)
        def _():
            grads = jnp.concatenate([query_held[slot], key_grad, value_grad], 1)
            product = dot(first_normed_ref[...], grads, TN).astype(BF16)
            lanes = pl.ds(pl.multiple_of(slot * LANES, LANES), LANES)
            for part in range(3):
                block_of = product[:, part * LANES : (part + 1) * LANES]
                qkv_parts[which // 2, part, :, :, :, :, lanes] = block_of.reshape(qkv_parts.shape[2:6] + (LANES,))

    plan = {
        (0, 0): [begin],
        (2, 0): [one.to_cores],
        (4, 0): [one.to_first],
        (5, 0): [two.to_cores],
        (8, 0): [two.to_first],
        (9, 0): [three.to_cores, one.to_second],
        (9, 1): [four.to_cores],
        (10, 0): [three.to_first, one.to_near],
        (10, 1): [two.to_second],
        (10, 2): [four.to_first],
        (10, 3): [one.to_far],
        (11, 0): [five.to_cores],
        (11, 1): [two.to_near],
        (11, 2): [three.to_second, one.to_other],
        (11, 3): [five.to_first, four.to_second],
        (12, 1): [three.to_near, two.to_far, one.to_out],
        (12, 2): [five.to_second, four.to_near],
        (13, 0): [six.to_cores, five.to_near, three.to_far],
        (13, 1): [six.to_first, four.to_far, two.to_other],
        (13, 2): [five.to_far],
        (13, 3): [six.to_second, three.to_other],
        (14, 1): [six.to_near, four.to_other, five.to_other, two.to_out],
        (14, 2): [three.to_out],
        (14, 3): [six.to_far, five.to_out],
        (15, 0): [six.to_other, four.to_out, six.to_out],
    }

    def run_plan(place, steps):
        for (at, where), actions in plan.items():
            if where == place and at in steps:

                @pl.when(step == at)
                def _():
                    for action in actions:
                        action()

    run_plan(0, range(made))

    @pl.when(step < parts)
    def _():
        part = dot(normed_ref[...], hidden_grad_ref[...], TN).astype(BF16)
        up_parts[step] = part.reshape(up_parts.shape[1:])

    @pl.when(step == parts)
    def _():
        for copy in loaded:
            copy.wait()
        part = dot(whole_context_ref[...], branch_ref[...], TN).astype(BF16)
        up_parts[parts] = part.reshape(up_parts.shape[1:])

    @pl.when((step > parts) & (step < made))
    def _():
        part = dot(active_ref[...], cots_ref[...], TN).astype(BF16).reshape(down_parts.shape[3:])
        at = step - parts - 1
        down_parts[0, at // 2, at % 2] = part

    def before(place):
        def run():
            run_plan(place, range(made, made + pairs))
            if place == near:
                far_copy(pair).start()

        return run

    pl.when(pair >= 1)(settle)

    @pl.when((step >= made) & (pair < pairs))
    def _():
        order = []
        slot = pair % 2
        for i in range(near):
            far_rows = pl.ds(i * block, block)
            order.append(
                (key_refs[near + i], value_refs[near + i], far_grads.at[0, far_rows], far_grads.at[1, far_rows])
            )
        for i in range(near):
            near_rows = pl.ds(i * block, block)
            order.append(
                (key_refs[i], value_refs[i], near_grads.at[slot, 0, near_rows], near_grads.at[slot, 1, near_rows])
            )
        steps = [one_piece + (before(place),) for place, one_piece in enumerate(order)]
        attend_back_step(query_ref, grad_ref, context_ref, logsum_ref, steps, query_grad_ref)
        query_held[slot] = query_grad_ref[...]

    @pl.when(step == last)
    def _():
        run_plan(0, [made + pairs])
        for p in range(2):
            back.sent(p, layer_blocks[p])
            back.arrived(p, layer_blocks[p])
        for chunk in chunks:
            chunk.finish()


def back_chunks(down_shape, up_shape):
    block, parts = down_shape[-2], up_shape[0]
    return [
        ("up", 0, parts // 2),
        ("up", parts // 2, parts - parts // 2),
        ("down", 0, block // 2),
        ("down", block // 2, block // 2),
    ]


def back(query, grad, context, logsum, kvs, normed, hidden_grad, branch, active, cots, first_normed, layer_out):
    count, width = query.shape
    pairs, pieces, length = width // LANES, len(kvs), kvs[0].shape[0]
    near = pieces // 2
    parts = hidden_grad.shape[1] // width
    made = 2 * parts + 1
    pair = lambda i: jnp.clip(i - made, 0, pairs - 1)
    row = pl.BlockSpec((count, LANES), lambda i: (0, pair(i)))
    settled = pl.BlockSpec((count, LANES), lambda i: (0, jnp.clip(i - made - 1, 0, pairs - 1)))
    piece = pl.BlockSpec((length, LANES), lambda i: (0, pair(i)))
    value = pl.BlockSpec((length, LANES), lambda i: (0, pairs + pair(i)))
    whole = fixed((count, width))
    up_rows, down_rows = width // 8, hidden_grad.shape[1] // 8
    down_shape, up_shape = (1, 2, 2, 2, down_rows, width), (parts + 1, 2, 2, 2, up_rows, width)
    return pl.pallas_call(
        functools.partial(back_kernel, pieces=pieces, parts=parts, pairs=pairs),
        grid=(made + pairs + 1,),
        in_specs=[row] * 4
        + [piece] * pieces
        + [value] * pieces
        + [
            whole,
            pl.BlockSpec((count, width), lambda i: (0, jnp.minimum(i, parts - 1))),
            fixed_any(),
            fixed_any(),
            pl.BlockSpec((count, width), lambda i: (0, jnp.clip(i - parts - 1, 0, parts - 1))),
        ]
        + [fixed_any()] * 4,
        out_specs=[row, settled, settled] + [fixed_any()] * 4,
        out_shape=[shape_of((count, width))] * 3
        + [
            shape_of((2, length, width)), shape_of((1, down_rows, width)), shape_of((parts + 1, up_rows, width)),
            shape_of((3, up_rows, 4 * LANES)),
        ],
        scratch_shapes=[pltpu.VMEM(down_shape, BF16), pltpu.VMEM(up_shape, BF16)]
        + [
            shape
            for which, _, many in back_chunks(down_shape, up_shape)
            for shape in Reduction.scratch(*((1, many) if which == "down" else (many, up_rows)), width)
        ]
        + [pltpu.VMEM((2, 3, 2, 2, 2, up_rows, 2 * LANES), BF16)]
        + Reduction.scratch(3, up_rows, 2 * LANES) * 2
        + [
            pltpu.VMEM((2, count, LANES), BF16),
            pltpu.VMEM((2, 2, count, LANES), BF16),
            pltpu.VMEM((2, count, LANES), BF16),
            pltpu.VMEM((2, 2, count, LANES), BF16),
            pltpu.SemaphoreType.DMA((1,)),
            pltpu.SemaphoreType.DMA((pairs,)),
        ]
        + [pltpu.VMEM((count, width), BF16)] * 4
        + [pltpu.SemaphoreType.DMA((5,))]
        + Trade.semaphores(),
        compiler_params=pltpu.CompilerParams(
            vmem_limit_bytes=VMEM_BYTES, collective_id=0, has_side_effects=True
        ),
        cost_estimate=cost(100),
        name="back",
    )(
        query, grad, context, logsum, *kvs, *kvs, normed, hidden_grad, context, branch, active, *cots,
        first_normed, layer_out
    )


def tail_kernel(
    query_grad, key_grad, value_grad, normed, x0, x1, middle_grad, weight,
    info_ref, gain_ref, feed_ref,
    tokens_out, qkv_out, sums_ref,
    query_v, key_v, value_v, normed_v, x_v, middle_v, weight_v, token_v, last_parts, *refs, total_tokens, parts,
):
    one = Reduction(last_parts, qkv_out, refs[:8])
    sums_in, sums_sends, sums_receives, loads = refs[8:12]
    back = Trade(tokens_out, *refs[12:], parts=TOKEN_PARTS)
    block, width = x0.shape
    d, z, _, _, core = here()
    total, ahead, many = 2 * TOKEN_PARTS, TOKEN_PARTS, block // 2
    top, bottom = pl.ds(0, block), pl.ds(block, block)
    later = ((query_grad, query_v), (key_grad, key_v), (value_grad, value_v), (middle_grad, middle_v))
    copies = [
        pltpu.make_async_copy(source, target, loads.at[number])
        for number, (source, target) in enumerate(
            (
                (weight, weight_v), (x0, x_v.at[0]),
                *((ref.at[top], held.at[top]) for ref, held in later),
                (normed, normed_v), (x1, x_v.at[1]),
                *((ref.at[bottom], held.at[bottom]) for ref, held in later),
            )
        )
    ]
    for copy in copies:
        copy.start()
    meet(("core", "x", "y", "near", "inner", "across"), back)

    def start_block(number):
        p, at = divmod(number * many, block)
        held = pl.ds(number * many, many)
        inner = pl.ds(at, many)
        normed_grad = 0.0
        for part, grads in enumerate((query_v, key_v, value_v)):
            columns = slice(part * width, (part + 1) * width)
            normed_grad = normed_grad + dot(grads[held], weight_v[:, columns], NT)
        unit, scale = norm_parts(x_v[p, inner].astype(F32) + one_row(info_ref, TIME))
        token_grad = middle_v[held] + norm_backward(normed_grad, vector(gain_ref), unit, scale)
        token_v[p, inner] = token_grad.astype(BF16)
        return [
            column_sum(normed_grad * unit),
            column_sum(normed_grad),
            column_sum(query_v[held].astype(F32)),
            column_sum(value_v[held].astype(F32)),
            column_sum(token_grad),
        ]

    def sums_copy(number):
        to = partners()[("core", "x", "y", "near", "across")[number]]
        return remote(sums_ref, sums_in.at[number], sums_sends, sums_receives, number, number, to)

    def sums_next(number):
        sums_copy(number).wait()
        sums_ref[...] = sums_ref[...] + sums_in[number]
        if number < 4:
            sums_copy(number + 1).start()

    def move(number):
        if number >= ahead:
            p, part = divmod(number - ahead, TOKEN_PARTS)
            back.sent(p, token_v.at[p], part)
        p, part = divmod(number, TOKEN_PARTS)
        back.begin(p, token_v.at[p], part)

    for copy in copies[:6]:
        copy.wait()
    sums = start_block(0)
    for number in range(ahead // 2):
        move(number)
    sums = [a + b for a, b in zip(sums, start_block(1))]
    for number in range(ahead // 2, ahead):
        move(number)
    for copy in copies[6:]:
        copy.wait()
    lanes = slice(width - 2 * LANES, width)
    for part, grads in enumerate((query_v, key_v, value_v)):
        made = dot(normed_v[...], grads[:, lanes], TN).astype(BF16)
        last_parts[part] = made.reshape(last_parts.shape[1:])
    one.to_cores()
    sums = [a + b for a, b in zip(sums, start_block(2))]
    one.to_first()
    sums = [a + b for a, b in zip(sums, start_block(3))]
    sums_ref[...] = jnp.zeros_like(sums_ref)
    sums_ref[0:4] = feed_ref[0:4]
    sums_ref[4 : 4 + parts] = feed_ref[8 : 8 + parts]
    for number in range(4):
        sums_ref[4 + parts + number : 5 + parts + number] = sums[number]
    energy = jnp.sum(feed_ref[4:5], keepdims=True) / (width * total_tokens)
    sums_ref[8 + parts : 9 + parts] = info_ref[MARK : MARK + 1] * energy + info_ref[SHARE : SHARE + 1]
    sums_ref[9 + parts : 10 + parts] = info_ref[STEP : STEP + 1] * jnp.where(core == 0, 1.0, 0.0)
    sequence = (d - core + z // 2) * 2 + z % 2
    sums_ref[pl.ds(16 + sequence, 1)] = sums[4]
    sums_copy(0).start()
    for number in range(ahead, ahead + 2):
        move(number)
    sums_next(0)
    one.to_second()
    sums_next(1)
    one.to_near()
    sums_next(2)
    for number in range(ahead + 2, ahead + 4):
        move(number)
    one.to_far()
    sums_next(3)
    for number in range(ahead + 4, ahead + 6):
        move(number)
    one.to_other()
    sums_next(4)
    for number in range(ahead + 6, total):
        move(number)
    one.to_out()
    for number in range(total - ahead, total):
        p, part = divmod(number, TOKEN_PARTS)
        back.sent(p, token_v.at[p], part)
    for number in range(total):
        p, part = divmod(number, TOKEN_PARTS)
        back.arrived(p, token_v.at[p], part)
    one.finish()


def tail(grads, normed, xs, middle_grad, weight, info, gain, feed_sums, total_tokens, hidden_parts):
    block, width = xs[0].shape
    count, total_seqs = 2 * block, 16
    any_spec = fixed_any()
    inside = pl.BlockSpec(memory_space=pltpu.VMEM)
    up_rows = width // 8
    held = lambda *shape, dtype=BF16: pltpu.VMEM(shape, dtype)
    sums_shape = (16 + total_seqs, width)
    return pl.pallas_call(
        functools.partial(tail_kernel, total_tokens=total_tokens, parts=hidden_parts),
        in_specs=[any_spec] * 8 + [inside] * 3,
        out_specs=[any_spec, any_spec, inside],
        out_shape=[
            shape_of((2, block, width)), shape_of((3, up_rows, 2 * LANES)), shape_of(sums_shape, F32),
        ],
        scratch_shapes=[
            held(count, width), held(count, width), held(count, width), held(count, width),
            held(2, block, width), held(count, width, dtype=F32), held(*weight.shape), held(2, block, width),
            held(3, 2, 2, 2, up_rows, 2 * LANES),
        ]
        + Reduction.scratch(3, up_rows, 2 * LANES)
        + [
            held(5, *sums_shape, dtype=F32),
            pltpu.SemaphoreType.DMA((5,)),
            pltpu.SemaphoreType.DMA((5,)),
            pltpu.SemaphoreType.DMA((12,)),
        ]
        + Trade.semaphores(TOKEN_PARTS),
        compiler_params=pltpu.CompilerParams(
            vmem_limit_bytes=VMEM_BYTES, collective_id=1, has_side_effects=True
        ),
        cost_estimate=cost(60),
        name="tail",
    )(*grads, normed, *xs, middle_grad, weight, info, gain, feed_sums)


def finish_kernel(
    token_ref, layer_ref, qkv_ref, last_qkv_ref, up_out_ref, out_part_ref, down_ref, sums_ref,
    token_out, layer_out, qkv_out, up_out, out_out, down_out, table_out, *small_outs, total_seqs, parts, table_rows,
):
    token_out[...] = wide(token_ref)
    layer_out[...] = layer_ref[...]
    qkv_out[...] = jnp.concatenate([qkv_ref[0], last_qkv_ref[0]], 1).astype(F32)
    up_out[...] = up_out_ref[0].astype(F32)
    out_out[...] = out_part_ref[0].astype(F32)
    down_out[...] = wide(down_ref)
    block, width = table_out.shape
    steps_row = 9 + parts
    first = lax.axis_index("dp") * table_rows + pl.program_id(0) * block
    place = (lax.broadcasted_iota(jnp.int32, (block, 1), 0) + first).astype(F32)
    total = jnp.zeros_like(table_out)
    for s in range(total_seqs):
        chosen = place == sums_ref[steps_row : steps_row + 1, s : s + 1]
        total = total + jnp.where(chosen, sums_ref[16 + s : 17 + s], 0.0)
    table_out[...] = total

    @pl.when(pl.program_id(0) == 0)
    def _():
        d = lax.axis_index("dp")
        piece = small_outs[0].shape[0]
        turned = pltpu.roll(sums_ref[0:16], lax.rem(width - d * piece, width), 1)
        order = [row for row in range(8 + parts) if not 4 <= row < 4 + parts]
        for row, out in zip(order, small_outs):
            out[...] = turned[row, :piece]
        up_piece = small_outs[8].shape[0]
        share = width // up_piece
        mine = sums_ref[pl.ds(4 + d // share, 1)]
        mine = pltpu.roll(mine, lax.rem(width - d % share * up_piece, width), 1)
        small_outs[8][...] = mine[0, :up_piece]
        small_outs[9][...] = sums_ref[8 + parts, :BUCKETS]
        small_outs[10][...] = sums_ref[8 + parts, BUCKETS : 2 * BUCKETS]


def finish(token, layer, qkv, last_qkv, up_out, down, sums, table_rows, dp):
    seqs, length, width = token.shape
    parts, block = up_out.shape[0] - 1, up_out.shape[1]
    steps = parts
    small = [width // dp] * 8 + [parts * width // dp] + [BUCKETS] * 2
    rows_at = lambda many: pl.BlockSpec((many // steps, width), lambda i: (i, 0))
    count = seqs * length
    wide_rows = rows_at(count)
    made = pl.pallas_call(
        functools.partial(
            finish_kernel, total_seqs=sums.shape[0] - 16, parts=parts, table_rows=table_rows
        ),
        grid=(steps,),
        in_specs=[
            wide_rows, wide_rows,
            pl.BlockSpec((1, block, qkv.shape[2]), lambda i: (jnp.minimum(i, 2), 0, 0)),
            pl.BlockSpec((1, block, last_qkv.shape[2]), lambda i: (jnp.minimum(i, 2), 0, 0)),
            pl.BlockSpec((1, block, width), lambda i: (i, 0, 0)),
            pl.BlockSpec((1, block, width), lambda i: (parts, 0, 0)),
            rows_at(down.shape[0]),
            fixed(sums.shape),
        ],
        out_specs=[
            wide_rows, wide_rows,
            pl.BlockSpec((block, width), lambda i: (0, jnp.minimum(i, 2))),
            pl.BlockSpec((block, width), lambda i: (0, i)),
            pl.BlockSpec((block, width), lambda i: (0, 0)),
            rows_at(down.shape[0]), rows_at(table_rows),
        ]
        + [pl.BlockSpec((many,), lambda i: (0,)) for many in small],
        out_shape=[
            shape_of((count, width), F32), shape_of((count, width)), shape_of((block, 3 * width), F32),
            shape_of((block, parts * width), F32), shape_of((block, width), F32), shape_of(down.shape, F32),
            shape_of((table_rows, width), F32),
        ]
        + [shape_of((many,), F32) for many in small],
        compiler_params=params(),
        cost_estimate=cost(6),
        name="finish",
    )(token.reshape(count, width), layer.reshape(count, width), qkv, last_qkv, up_out, up_out, down, sums)
    shape = (seqs, length, width)
    return [made[0].reshape(shape), made[1].reshape(shape)] + list(made[2:])


def gelu_parts(hidden):
    share = 0.5 + 0.5 * lax.erf(hidden * 2**-0.5)
    bell = jnp.exp(-0.5 * hidden * hidden) * 0.3989422804014327
    return hidden * share, share + hidden * bell


def feed_kernel(
    context_ref, x0_ref, x1_ref, info_ref, cot0_ref, cot1_ref, out_weight_ref, up_ref, down_ref,
    out_bias_ref, gain_ref, shift_ref, down_bias_ref, up_bias_ref,
    out_ref, active_ref, hidden_grad_ref, normed_ref, middle_grad_ref, branch_ref, context_grad_ref, sums_ref,
    out_weight_v, up_v, down_v, loads,
):
    step = pl.program_id(0)
    width, hidden_width = x0_ref.shape[1], up_ref.shape[1]

    parts = hidden_width // width
    out_copy = pltpu.make_async_copy(out_weight_ref, out_weight_v, loads.at[0, parts])
    copies = []
    for part in range(parts):
        columns = pl.ds(part * width, width)
        copies.append(
            (
                pltpu.make_async_copy(up_ref.at[:, columns], up_v.at[:, columns], loads.at[0, part]),
                pltpu.make_async_copy(down_ref.at[columns], down_v.at[columns], loads.at[1, part]),
            )
        )

    @pl.when(step == 0)
    def _():
        out_copy.start()
        for one, two in copies:
            one.start()
            two.start()
        sums_ref[...] = jnp.zeros_like(sums_ref)
        out_copy.wait()

    x = jnp.where(step == 0, x0_ref[...], x1_ref[...])
    cot = jnp.where(step == 0, cot0_ref[...], cot1_ref[...])
    middle = (
        x.astype(F32)
        + one_row(info_ref, TIME)
        + dot(context_ref[...], out_weight_v[...], NN)
        + vector(out_bias_ref)
    )
    unit, scale = norm_parts(middle)
    gain = vector(gain_ref)
    normed = (unit * gain + vector(shift_ref)).astype(BF16)
    normed_ref[...] = normed
    out = middle + vector(down_bias_ref)
    normed_grad = jnp.zeros_like(out)
    up_bias = vector(up_bias_ref)
    for part in range(parts):
        columns = slice(part * width, (part + 1) * width)

        @pl.when(step == 0)
        def _():
            for copy in copies[part]:
                copy.wait()

        hidden = dot(normed, up_v[:, columns], NN) + up_bias[:, columns]
        active, slope = gelu_parts(hidden)
        active = active.astype(BF16)
        active_ref[:, columns] = active
        out = out + dot(active, down_v[columns, :], NN)
        hidden_grad = (dot(cot, down_v[columns, :], NT) * slope).astype(BF16)
        hidden_grad_ref[:, columns] = hidden_grad
        sums_ref[8 + part : 9 + part] += column_sum(hidden_grad.astype(F32))
        normed_grad = normed_grad + dot(hidden_grad, up_v[:, columns], NT)
    out_ref[...] = out.astype(BF16)
    cot = cot.astype(F32)
    middle_grad = cot + norm_backward(normed_grad, gain, unit, scale)
    middle_grad_ref[...] = middle_grad
    branch = middle_grad.astype(BF16)
    branch_ref[...] = branch
    context_grad_ref[...] = dot(branch, out_weight_v[...], NT).astype(BF16)
    sums_ref[0:1] += column_sum(cot)
    sums_ref[1:2] += column_sum(normed_grad * unit)
    sums_ref[2:3] += column_sum(normed_grad)
    sums_ref[3:4] += column_sum(branch.astype(F32))
    sums_ref[4:5] += column_sum(out * out)


def feed(context, xs, info, small, cots, out_weight, up, down):
    block, width = xs[0].shape
    count, hidden_width = 2 * block, up.shape[1]
    sums_rows = 8 + hidden_width // width + (-(hidden_width // width)) % 8
    whole = fixed((block, width))
    return pl.pallas_call(
        feed_kernel,
        grid=(2,),
        in_specs=[
            rows(block, width), whole, whole, fixed(info.shape), whole, whole,
        ]
        + [pl.BlockSpec(memory_space=pl.ANY)] * 3
        + [whole_vector(v) for v in small],
        out_specs=[
            rows(block, width), rows(block, hidden_width), rows(block, hidden_width), rows(block, width),
            rows(block, width), rows(block, width), rows(block, width),
            pl.BlockSpec((sums_rows, width), lambda i: (0, 0)),
        ],
        out_shape=[
            shape_of((count, width)), shape_of((count, hidden_width)), shape_of((count, hidden_width)),
            shape_of((count, width)), shape_of((count, width), F32), shape_of((count, width)),
            shape_of((count, width)), shape_of((sums_rows, width), F32),
        ],
        scratch_shapes=[
            pltpu.VMEM(out_weight.shape, BF16), pltpu.VMEM(up.shape, BF16), pltpu.VMEM(down.shape, BF16),
            pltpu.SemaphoreType.DMA((2, hidden_width // width + 1)),
        ],
        compiler_params=params(),
        cost_estimate=cost(34),
        name="feed",
    )(context, *xs, info, *cots, out_weight, up, down, *small)


def down_grad_kernel(active_ref, cot0_ref, cot1_ref, out_ref):
    block = cot0_ref.shape[0]
    out_ref[...] = (
        dot(active_ref[:block], cot0_ref[...], TN) + dot(active_ref[block:], cot1_ref[...], TN)
    ).astype(BF16)


def down_grad(active, cots):
    block, width = cots[0].shape
    count, hidden_width = active.shape
    return pl.pallas_call(
        down_grad_kernel,
        grid=(hidden_width // width,),
        in_specs=[pl.BlockSpec((count, width), lambda i: (0, i))] + [fixed((block, width))] * 2,
        out_specs=rows(width, width),
        out_shape=shape_of((hidden_width, width)),
        compiler_params=params(),
        cost_estimate=cost(8),
        name="down_grad",
    )(active, *cots)


def up_out_grad_kernel(normed_ref, hidden_grad_ref, context_ref, branch_ref, out_ref):
    last = pl.num_programs(0) - 1

    @pl.when(pl.program_id(0) < last)
    def _():
        out_ref[0] = dot(normed_ref[...], hidden_grad_ref[...], TN).astype(BF16)

    @pl.when(pl.program_id(0) == last)
    def _():
        out_ref[0] = dot(context_ref[...], branch_ref[...], TN).astype(BF16)


def up_out_grad(normed, hidden_grad, context, branch):
    count, width = normed.shape
    parts = hidden_grad.shape[1] // width
    whole = fixed((count, width))
    return pl.pallas_call(
        up_out_grad_kernel,
        grid=(parts + 1,),
        in_specs=[
            whole,
            pl.BlockSpec((count, width), lambda i: (0, jnp.minimum(i, parts - 1))),
            whole,
            whole,
        ],
        out_specs=pl.BlockSpec((1, width, width), lambda i: (i, 0, 0)),
        out_shape=shape_of((parts + 1, width, width)),
        compiler_params=params(),
        cost_estimate=cost(10),
        name="up_out_grad",
    )(normed, hidden_grad, context, branch)


def qkv_grad_kernel(normed_ref, grad_ref, out_ref):
    out_ref[0] = dot(normed_ref[...], grad_ref[...], TN).astype(BF16)


def qkv_grad(normed, grads):
    count, width = normed.shape
    parts = grads.shape[1] // width
    return pl.pallas_call(
        qkv_grad_kernel,
        grid=(parts,),
        in_specs=[fixed((count, width)), pl.BlockSpec((count, width), lambda i: (0, i))],
        out_specs=pl.BlockSpec((1, width, width), lambda i: (i, 0, 0)),
        out_shape=shape_of((parts, width, width)),
        compiler_params=params(),
        cost_estimate=cost(7),
        name="qkv_grad",
    )(normed, grads)


def start_kernel(
    query_grad_ref, key0_ref, key1_ref, far_key0_ref, far_key1_ref, value0_ref, value1_ref, far_value0_ref,
    far_value1_ref, x0_ref, x1_ref, info_ref, middle_grad_ref, gain_ref, weight_ref,
    token0_ref, token1_ref, grads_ref, sums_ref,
):
    step = pl.program_id(0)
    width = x0_ref.shape[1]

    @pl.when(step == 0)
    def _():
        sums_ref[...] = jnp.zeros_like(sums_ref)

    def pick(first, second):
        return jnp.where(step == 0, first[...], second[...])

    query_grad = query_grad_ref[...]
    key_grad = (pick(key0_ref, key1_ref).astype(F32) + pick(far_key0_ref, far_key1_ref).astype(F32)).astype(BF16)
    value_grad = (
        pick(value0_ref, value1_ref).astype(F32) + pick(far_value0_ref, far_value1_ref).astype(F32)
    ).astype(BF16)
    normed_grad = 0.0
    for part, grad in enumerate((query_grad, key_grad, value_grad)):
        columns = slice(part * width, (part + 1) * width)
        grads_ref[:, columns] = grad
        normed_grad = normed_grad + dot(grad, weight_ref[:, columns], NT)
    unit, scale = norm_parts(pick(x0_ref, x1_ref).astype(F32) + one_row(info_ref, TIME))
    token_grad = middle_grad_ref[...] + norm_backward(normed_grad, vector(gain_ref), unit, scale)

    @pl.when(step == 0)
    def _():
        token0_ref[...] = token_grad.astype(BF16)

    @pl.when(step == 1)
    def _():
        token1_ref[...] = token_grad.astype(BF16)

    sums_ref[0:1] += column_sum(normed_grad * unit)
    sums_ref[1:2] += column_sum(normed_grad)
    sums_ref[2:3] += column_sum(query_grad.astype(F32))
    sums_ref[3:4] += column_sum(value_grad.astype(F32))
    sums_ref[4:5] += column_sum(token_grad)


def start_back(query_grad, key_grads, value_grads, xs, info, middle_grad, gain, weight):
    block, width = xs[0].shape
    count = 2 * block
    whole = fixed((block, width))
    kept = pl.BlockSpec((block, width), lambda i: (0, 0))
    return pl.pallas_call(
        start_kernel,
        grid=(2,),
        in_specs=[rows(block, width)]
        + [whole] * 10
        + [fixed(info.shape), rows(block, width), whole_vector(gain), fixed(weight.shape)],
        out_specs=[kept, kept, rows(block, 3 * width), pl.BlockSpec((8, width), lambda i: (0, 0))],
        out_shape=[
            shape_of((block, width)), shape_of((block, width)), shape_of((count, 3 * width)),
            shape_of((8, width), F32),
        ],
        compiler_params=params(),
        cost_estimate=cost(10),
        name="start_back",
    )(query_grad, *key_grads, *value_grads, *xs, info, middle_grad, gain, weight)


class Places:
    def __init__(self, dp, seq):
        self.dp, self.seq = dp, seq
        self.bits = dp.bit_length() - 1

    def flat(self, d, z):
        return d * self.seq + z

    def pairs(self, to):
        return [
            (self.flat(d, z), self.flat(*to(d, z))) for d in range(self.dp) for z in range(self.seq)
        ]

    def gather_order(self, turn):
        def to(d, z):
            core, j = d % 2, (z + turn) % 2
            return d - core + z // 2, 2 * core + j

        return self.pairs(to)

    def scatter_order(self, turn):
        return [(b, a) for a, b in self.gather_order(turn)]

    def swap(self, bit):
        return self.pairs(lambda d, z: (d ^ (1 << bit), z))

    def swap_seq(self, step):
        return self.pairs(lambda d, z: (d, z ^ step))


def send(x, order):
    return lax.ppermute(x, BOTH, order)


def add(a, b):
    return (a.astype(F32) + b.astype(F32)).astype(BF16)


def reduce_parts(parts, places):
    d, z = lax.axis_index("dp"), lax.axis_index("seq")
    count, height, width = parts.shape
    block = height // places.dp
    grid = parts.reshape((count,) + (2,) * places.bits + (block, width))

    def halve(value, bit, axes):
        axis = 1 + axes.index(bit)
        mine = (d >> bit) & 1
        kept = lax.dynamic_index_in_dim(value, mine, axis, keepdims=False)
        sent = lax.dynamic_index_in_dim(value, 1 - mine, axis, keepdims=False)
        axes.remove(bit)
        return add(kept, send(sent, places.swap(bit)))

    axes = list(range(places.bits - 1, -1, -1))
    grid = halve(grid, 0, axes)
    halves = []
    for number, order in enumerate((range(1, places.bits), range(places.bits - 1, 0, -1))):
        at = block // 2
        value = lax.slice_in_dim(grid, number * at, (number + 1) * at, axis=grid.ndim - 2)
        left = list(axes)
        for bit in order:
            value = halve(value, bit, left)
        halves.append(sum_along_seq(value, z, places))
    return jnp.concatenate(halves, 1)


def sum_along_seq(value, z, places):
    count, block, width = value.shape
    mine = z % 2
    grid = value.reshape(count, block, 2, width // 2)
    kept = lax.dynamic_index_in_dim(grid, mine, 2, keepdims=False)
    sent = lax.dynamic_index_in_dim(grid, 1 - mine, 2, keepdims=False)
    half = add(kept, send(sent, places.swap_seq(1)))
    half = add(half, send(half, places.swap_seq(2)))
    other = send(half, places.swap_seq(1))
    first = jnp.where(mine == 0, half, other)
    second = jnp.where(mine == 0, other, half)
    return jnp.concatenate([first, second], 2).astype(F32)


def sum_everywhere(value, places):
    for bit in range(places.bits):
        value = value + send(value, places.swap(bit))
    for step in (1, 2):
        value = value + send(value, places.swap_seq(step))
    return value


def per_device(
    tokens, timesteps, time_table, ln1_gain, ln1_bias, qkv_weight, q_bias, v_bias, out_weight, out_bias,
    ln2_gain, ln2_bias, up_weight, up_bias, down_weight, down_bias, cotangent,
):
    places = Places(lax.axis_size("dp"), lax.axis_size("seq"))
    seq_count, local_len, width = tokens.shape
    hidden_width = up_weight.shape[1]
    assert places.seq == 4 and seq_count == 2 and places.dp == 1 << places.bits
    d, z = lax.axis_index("dp"), lax.axis_index("seq")
    core = d % 2
    total_seqs = seq_count * places.dp
    total_tokens = total_seqs * local_len * places.seq

    def gathered(array):
        blocks = []
        for turn in range(2):
            mine = lax.dynamic_index_in_dim(array, (z + turn) % 2, 0, keepdims=False)
            blocks.append(send(mine, places.gather_order(turn)))
        return blocks

    count = 2 * local_len
    parts = hidden_width // width
    first_small = (ln1_gain, ln1_bias, q_bias, v_bias)
    second_small = (out_bias, ln2_gain, ln2_bias, down_bias, up_bias)
    sequence = (d - core + z // 2) * seq_count + z % 2
    if places.dp == 8:
        made = front(tokens, qkv_weight, time_table, timesteps, first_small, count / total_tokens)
        xs, (normed, query), kvs, info = made[:2], made[2:4], list(made[4:8]), made[8]
        cotangent, query = lax.optimization_barrier((cotangent, query))
        cots = gathered(cotangent)
    else:
        info = jnp.concatenate(
            [
                known_rows(
                    timesteps[j], seq_count * d + j, count / total_tokens,
                    lax.dynamic_slice_in_dim(time_table, timesteps[j], 1, 0).astype(F32),
                )
                for j in range(2)
            ]
        )
        far_info = send(info, places.swap(0))
        xs = gathered(tokens)
        cots = gathered(cotangent)
        info = jnp.where(z // 2 == core, info, far_info)
        info = jnp.pad(jnp.where(z % 2 == 0, info[:4], info[4:]), ((0, 4), (0, 0)))
        normed, query, kv0 = project(xs[0], info, first_small, qkv_weight, count)
        far0 = send(kv0, places.swap(0))
        normed, query, kv1 = project(xs[1], info, first_small, qkv_weight, count, (normed, query))
        kvs = [kv0, kv1, far0, send(kv1, places.swap(0))]
    context, logsum = attend(query, kvs)
    out, active, hidden_grad, normed_two, middle_grad, branch, context_grad, feed_sums = feed(
        context, xs, info, second_small, cots, out_weight, up_weight, down_weight
    )

    def scattered(blocks, dtype):
        back = [send(block, places.scatter_order(turn)) for turn, block in enumerate(blocks)]
        even = z % 2 == 0
        return jnp.stack(
            [jnp.where(even, back[0], back[1]), jnp.where(even, back[1], back[0])]
        ).astype(dtype)


    if places.dp == 8:
        made = back(
            query, context_grad, context, logsum, kvs, normed_two, hidden_grad, branch, active, cots,
            normed, out
        )
        tokens_grad, last_qkv, packed = tail(
            made[:3], normed, xs, middle_grad, qkv_weight, info, ln1_gain, feed_sums, total_tokens, parts
        )
        tokens_grad, layer_out, qkv_sum, up_sum, out_sum, down_sum, table_grad, *small = finish(
            tokens_grad, made[3], made[6], last_qkv, made[5], made[4][0], packed,
            time_table.shape[0] // places.dp, places.dp,
        )
    else:
        layer_out = scattered([out[:local_len], out[local_len:]], BF16)
        down_sum = reduce_parts(down_grad(active, cots)[None], places)[0]
        up_out_sum = reduce_parts(up_out_grad(normed_two, hidden_grad, context, branch), places)
        made = attend_back(query, context_grad, context, logsum, kvs)
        token0, token1, projected_grad, start_sums = start_back(
            made[0],
            list(made[1:3]) + [send(g, places.swap(0)) for g in made[3:5]],
            list(made[5:7]) + [send(g, places.swap(0)) for g in made[7:9]],
            xs, info, middle_grad, ln1_gain, qkv_weight,
        )
        tokens_grad = scattered([token0, token1], F32)
        qkv_sum = reduce_parts(qkv_grad(normed, projected_grad), places)
        energy = jnp.sum(feed_sums[4]) / (width * total_tokens)
        sequence_rows = jnp.where(jnp.arange(total_seqs)[:, None] == sequence, start_sums[4][None], 0.0)
        packed = jnp.concatenate(
            [
                feed_sums[0:4], feed_sums[8 : 8 + parts], start_sums[0:4],
                jnp.stack(
                    [info[MARK] * energy + info[SHARE], info[STEP] * jnp.where(core == 0, 1.0, 0.0)]
                ),
                sequence_rows,
            ]
        )
        packed = sum_everywhere(packed, places)
        steps = packed[9 + parts, :total_seqs].astype(jnp.int32)
        table_rows = time_table.shape[0] // places.dp
        chosen = (steps[None, :] == (jnp.arange(table_rows) + d * table_rows)[:, None]).astype(F32)
        table_grad = jnp.dot(chosen, packed[10 + parts :], precision=lax.Precision.HIGHEST)

        def side_by_side(stacked):
            return jnp.moveaxis(stacked, 0, 1).reshape(stacked.shape[1], -1)

        qkv_sum, out_sum = side_by_side(qkv_sum), up_out_sum[parts]
        up_sum = side_by_side(up_out_sum[:parts])
        piece = width // places.dp
        mine = lax.dynamic_slice_in_dim(packed[: 8 + parts], d * piece, piece, 1)
        up_piece = hidden_width // places.dp
        up_bias_sum = lax.dynamic_slice_in_dim(packed[4 : 4 + parts].reshape(-1), d * up_piece, up_piece, 0)
        stats = packed[8 + parts]
        small = [mine[row] for row in (0, 1, 2, 3, 4 + parts, 5 + parts, 6 + parts, 7 + parts)]
        small += [up_bias_sum, stats[:BUCKETS], stats[BUCKETS : 2 * BUCKETS]]
    down_bias_sum, gain_two, shift_two, out_bias_sum, gain_one, shift_one, q_sum, v_sum = small[:8]
    return (
        layer_out, tokens_grad, table_grad, gain_one, shift_one, qkv_sum, q_sum, v_sum, out_sum, out_bias_sum,
        gain_two, shift_two, up_sum, small[8], down_sum, down_bias_sum, small[9], small[10],
    )


def solution(mesh):
    split = P("dp", "seq", None)
    return jax.shard_map(
        per_device,
        mesh=mesh,
        in_specs=(split, P("dp")) + (P(),) * 14 + (split,),
        out_specs=(
            split, split, P("dp", None), P("dp"), P("dp"), P("dp", None), P("dp"), P("dp"), P("dp", None),
            P("dp"), P("dp"), P("dp"), P("dp", None), P("dp"), P("dp", None), P("dp"), P(), P(),
        ),
        check_vma=False,
    )
```

```python
import functools

import jax
import jax.numpy as jnp
from jax import lax
from jax.experimental import pallas as pl
from jax.experimental.pallas import tpu as pltpu
from jax.sharding import PartitionSpec as P

HEAD_DIM = 64
TSTEPS = 2048
BUCKETS = 4
EPS = 1e-05
LANES = 128
VMEM_BYTES = 60 * 1024 * 1024
BOTH = ("dp", "seq")
TOKEN_PARTS = 8
F32 = jnp.float32
BF16 = jnp.bfloat16
NN = (((1,), (0,)), ((), ()))
NT = (((1,), (1,)), ((), ()))
TN = (((0,), (0,)), ((), ()))


def dot(a, b, dims):
    return lax.dot_general(a, b, dims, preferred_element_type=F32)


def wide(ref):
    return ref[...].astype(F32)


def column_sum(v):
    return jnp.sum(v, 0, keepdims=True)


def fixed(shape):
    return pl.BlockSpec(shape, lambda *i: (0,) * len(shape), pipeline_mode=pl.Buffered(1))


def rows(block, width):
    return pl.BlockSpec((block, width), lambda i: (i, 0))


def shape_of(shape, dtype=BF16):
    return jax.ShapeDtypeStruct(shape, dtype)


def cost(us):
    return pl.CostEstimate(flops=int(us * 1.15e9), bytes_accessed=0, transcendentals=0)


def params():
    return pltpu.CompilerParams(vmem_limit_bytes=VMEM_BYTES)


def norm_parts(v):
    centered = v - jnp.mean(v, -1, keepdims=True)
    scale = lax.rsqrt(jnp.mean(centered * centered, -1, keepdims=True) + EPS)
    return centered * scale, scale


def norm_backward(grad, gain, unit, scale):
    scaled = grad * gain
    return scale * (
        scaled
        - jnp.mean(scaled, -1, keepdims=True)
        - unit * jnp.mean(scaled * unit, -1, keepdims=True)
    )


TIME, MARK, SHARE, STEP = range(4)


def one_row(ref, at):
    return ref[at : at + 1].astype(F32)


def vector(ref):
    return ref[...].astype(F32).reshape(1, -1)


def whole_vector(v):
    return pl.BlockSpec(v.shape, lambda *i: (0,), pipeline_mode=pl.Buffered(1))


def known_rows(step, sequence, share, time_row):
    lane = lax.broadcasted_iota(jnp.int32, time_row.shape, 1)
    bucket = step * BUCKETS // TSTEPS
    return jnp.concatenate(
        [
            time_row,
            jnp.where(lane == bucket, 1.0, 0.0),
            jnp.where(lane == BUCKETS + bucket, share, 0.0),
            jnp.where(lane == sequence, step.astype(F32), 0.0),
        ],
        0,
    )


def project_rows(x, info_ref, small, weight_ref):
    width = x.shape[1]
    gain, shift, query_bias, value_bias = small
    unit, _ = norm_parts(x.astype(F32) + one_row(info_ref, TIME))
    normed = (unit * vector(gain) + vector(shift)).astype(BF16)

    def part(number):
        made = dot(normed, weight_ref[:, number * width : (number + 1) * width], NN)
        if number != 1:
            made = made + vector(query_bias if number == 0 else value_bias)
        made = made.astype(BF16)
        return made * jnp.asarray(HEAD_DIM ** (-0.5), BF16) if number == 0 else made

    return normed, part


def project_kernel(x_ref, info_ref, weight_ref, *refs):
    normed_ref, query_ref, kv_ref = refs[-3:]
    width = x_ref.shape[1]
    normed, part = project_rows(x_ref[...], info_ref, refs[:4], weight_ref)
    normed_ref[...] = normed
    query_ref[...] = part(0)
    kv_ref[:, :width] = part(1)
    kv_ref[:, width:] = part(2)


def project(x, info, small, weight, total, begun=None, block=256):
    count, width = x.shape
    first = 0 if begun is None else total // block - count // block
    later = pl.BlockSpec((block, width), lambda i: (i + first, 0))
    extra = [] if begun is None else list(begun)
    return pl.pallas_call(
        project_kernel,
        grid=(count // block,),
        in_specs=[rows(block, width), fixed(info.shape), fixed(weight.shape)]
        + [whole_vector(v) for v in small]
        + [pl.BlockSpec(memory_space=pl.ANY)] * len(extra),
        out_specs=[later, later, rows(block, 2 * width)],
        out_shape=[
            shape_of((total, width)),
            shape_of((total, width)),
            shape_of((count, 2 * width)),
        ],
        input_output_aliases={7: 0, 8: 1} if extra else {},
        compiler_params=params(),
        cost_estimate=cost(5),
        name="project",
    )(x, info, weight, *small, *extra)


def lane_parts():
    lane = lax.broadcasted_iota(jnp.int32, (1, LANES), 1)
    return lane < HEAD_DIM, lane % HEAD_DIM


def with_offset(own, place, base, offset):
    high = offset.astype(BF16)
    left = offset - high.astype(F32)
    mid = left.astype(BF16)
    low = (left - mid.astype(F32)).astype(BF16)
    zero = jnp.zeros_like(low)
    parts = jnp.where(place == 0, high, jnp.where(place == 1, mid, jnp.where(place == 2, low, zero)))
    return jnp.where(own, base, parts)


def attend_kernel(query_ref, *refs, pieces):
    key_refs, value_refs = refs[:pieces], refs[pieces : 2 * pieces]
    context_ref, logsum_ref = refs[2 * pieces :]
    count = query_ref.shape[0]
    low, place = lane_parts()
    row_half = lax.broadcasted_iota(jnp.int32, (LANES, LANES), 0) // HEAD_DIM
    lane_half = lax.broadcasted_iota(jnp.int32, (LANES, LANES), 1) // HEAD_DIM
    swapped = jnp.where(row_half != lane_half, 1.0, 0.0).astype(BF16)
    query = query_ref[...]

    def norms(v):
        v = v.astype(F32)
        return dot((v * v).astype(BF16), swapped, NN)

    key_norm = functools.reduce(
        jnp.maximum, [jnp.max(norms(ref[...]), 0, keepdims=True) for ref in key_refs]
    )
    bound = jnp.sqrt(norms(query) * key_norm) * 1.01
    ones_key = jnp.where(place < 3, 1.0, 0.0).astype(BF16)
    values = [ref[...].T for ref in value_refs]
    ones = jnp.ones((16, value_refs[0].shape[0]), BF16)

    def value_of(piece, head):
        return jnp.concatenate([values[piece][head * HEAD_DIM : (head + 1) * HEAD_DIM], ones], 0)

    def finish(mixed, offset):
        totals = [m[HEAD_DIM : HEAD_DIM + 1] for m in mixed]
        context = jnp.concatenate([m[:HEAD_DIM] / t for m, t in zip(mixed, totals)], 0)
        context_ref[...] = context.T.astype(BF16)
        logs = [jnp.broadcast_to(jnp.log(t), (HEAD_DIM, count)) for t in reversed(totals)]
        logsum_ref[...] = jnp.concatenate(logs, 0).T + offset

    mixed = []
    for head in range(2):
        own = low if head == 0 else ~low
        query_own = with_offset(own, place, query, -bound)
        out = 0.0
        for piece in range(pieces):
            key_own = jnp.where(own, key_refs[piece][...], ones_key)
            weights = jnp.exp(dot(key_own, query_own, NT)).astype(BF16)
            out = out + dot(value_of(piece, head), weights, NN)
        mixed.append(out)
    finish(mixed, bound)
    smallest = jnp.min(jnp.minimum(mixed[0][HEAD_DIM], mixed[1][HEAD_DIM]))

    @pl.when(smallest < 1e-25)
    def _():
        again, tops = [], []
        for head in range(2):
            own = low if head == 0 else ~low
            query_own = jnp.where(own, query, jnp.zeros_like(query))
            top = jnp.full((1, count), -jnp.inf, F32)
            for piece in range(pieces):
                scores = dot(key_refs[piece][...], query_own, NT)
                top = jnp.maximum(top, jnp.max(scores, 0, keepdims=True))
            out = 0.0
            for piece in range(pieces):
                scores = dot(key_refs[piece][...], query_own, NT)
                out = out + dot(value_of(piece, head), jnp.exp(scores - top).astype(BF16), NN)
            again.append(out)
            tops.append(jnp.broadcast_to(top, (HEAD_DIM, count)))
        finish(again, jnp.concatenate(tops[::-1], 0).T)


def attend(query, kvs):
    count, width = query.shape
    pairs, pieces, length = width // LANES, len(kvs), kvs[0].shape[0]
    row = pl.BlockSpec((count, LANES), lambda p: (0, p))
    return pl.pallas_call(
        functools.partial(attend_kernel, pieces=pieces),
        grid=(pairs,),
        in_specs=[row]
        + [pl.BlockSpec((length, LANES), lambda p: (0, p))] * pieces
        + [pl.BlockSpec((length, LANES), lambda p: (0, pairs + p))] * pieces,
        out_specs=[row, row],
        out_shape=[shape_of((count, width)), shape_of((count, width), F32)],
        compiler_params=params(),
        cost_estimate=cost(32),
        name="attend",
    )(query, *kvs, *kvs)


def attend_back_step(query_ref, grad_ref, context_ref, logsum_ref, pieces, query_grad_ref):
    low, place = lane_parts()
    query, grad = query_ref[...], grad_ref[...]
    count = query.shape[0]
    product = grad.astype(F32) * wide(context_ref)
    logsum = logsum_ref[...]
    ones_key = jnp.where(place < 3, 1.0, 0.0).astype(BF16)
    zero = jnp.zeros_like(query)
    heads = []
    for head in range(2):
        own = low if head == 0 else ~low
        inner = jnp.sum(jnp.where(own, product, 0.0), -1, keepdims=True)
        heads.append(
            (
                own,
                with_offset(own, place, query, -logsum),
                with_offset(own, place, grad, jnp.broadcast_to(-inner, logsum.shape)),
                jnp.where(own, query, zero),
                jnp.where(own, grad, zero),
            )
        )
    length = sum(piece[0].shape[0] for piece in pieces)
    query_grads = [0.0, 0.0]
    key_mean = 0.0
    for key_ref, value_ref, key_grad_ref, value_grad_ref, before in pieces:
        if before is not None:
            before()
        key, value = key_ref[...], value_ref[...]
        key_turned = key.T
        key_mean = key_mean + jnp.sum(key_turned.astype(F32), 1, keepdims=True) / length
        ones = jnp.ones((16, key.shape[0]), BF16)
        key_grad, value_grad = 0.0, 0.0
        for head, (own, query_off, grad_off, query_own, grad_own) in enumerate(heads):
            scores = dot(jnp.where(own, key, ones_key), query_off, NT)
            probs = jnp.exp(scores)
            prob_grad = dot(jnp.where(own, value, ones_key), grad_off, NT)
            score_grad = (probs * prob_grad).astype(BF16)
            value_grad = value_grad + dot(probs.astype(BF16), grad_own, NN)
            key_grad = key_grad + dot(score_grad, query_own, NN)
            lanes = slice(head * HEAD_DIM, (head + 1) * HEAD_DIM)
            turned = jnp.concatenate([key_turned[lanes], ones], 0)
            query_grads[head] = query_grads[head] + dot(turned, score_grad, NN)
        key_grad_ref[...] = key_grad.astype(BF16)
        value_grad_ref[...] = value_grad.astype(BF16)
    parts = [
        made[:HEAD_DIM]
        - key_mean[head * HEAD_DIM : (head + 1) * HEAD_DIM]
        * jnp.broadcast_to(made[HEAD_DIM : HEAD_DIM + 1], (HEAD_DIM, count))
        for head, made in enumerate(query_grads)
    ]
    query_grad_ref[...] = (jnp.concatenate(parts, 0) * HEAD_DIM ** (-0.5)).T.astype(BF16)


def attend_back_kernel(query_ref, grad_ref, context_ref, logsum_ref, *refs, pieces):
    key_refs, value_refs = refs[:pieces], refs[pieces : 2 * pieces]
    query_grad_ref = refs[2 * pieces]
    key_grad_refs = refs[2 * pieces + 1 : 3 * pieces + 1]
    value_grad_refs = refs[3 * pieces + 1 :]
    steps = list(zip(key_refs, value_refs, key_grad_refs, value_grad_refs, [None] * pieces))
    attend_back_step(query_ref, grad_ref, context_ref, logsum_ref, steps, query_grad_ref)


def attend_back(query, grad, context, logsum, kvs):
    count, width = query.shape
    pairs, pieces, length = width // LANES, len(kvs), kvs[0].shape[0]
    row = pl.BlockSpec((count, LANES), lambda p: (0, p))
    piece = pl.BlockSpec((length, LANES), lambda p: (0, p))
    return pl.pallas_call(
        functools.partial(attend_back_kernel, pieces=pieces),
        grid=(pairs,),
        in_specs=[row] * 4
        + [piece] * pieces
        + [pl.BlockSpec((length, LANES), lambda p: (0, pairs + p))] * pieces,
        out_specs=[row] + [piece] * (2 * pieces),
        out_shape=[shape_of((count, width))] + [shape_of((length, width))] * (2 * pieces),
        compiler_params=params(),
        cost_estimate=cost(75),
        name="attend_back",
    )(query, grad, context, logsum, *kvs, *kvs)


def here():
    d, z = lax.axis_index("dp"), lax.axis_index("seq")
    return d, z, d // 4, (d // 2) % 2, d % 2


def partners():
    d, z, y, x, core = here()
    return {
        "core": (d + 1 - 2 * core, z),
        "x": (d + 2 - 4 * x, z),
        "y": (d + 4 - 8 * y, z),
        "near": (d, z + 1 - 2 * (z % 2)),
        "inner": (d, 3 - z),
    }


def outer():
    z = lax.axis_index("seq")
    return (z == 0) | (z == 3)


def remote(source, target, sends, receives, send_index, receive_index, device):
    return pltpu.make_async_remote_copy(
        src_ref=source,
        dst_ref=target,
        send_sem=sends.at[send_index],
        recv_sem=receives.at[receive_index],
        device_id=device,
        device_id_type=pl.DeviceIdType.MESH,
    )


class Reduction:
    def __init__(self, source, out, scratch):
        self.source, self.out = source, out
        self.own = source.at[:, :, :, here()[4]]
        self.from_core, self.first, self.second, self.near, self.far = scratch[:5]
        self.sends, self.receives, self.local = scratch[5:8]
        self.parts, _, _, self.rows, self.width = self.from_core.shape
        self.half = self.width // 2

    @staticmethod
    def scratch(parts, block, width):
        half = width // 2
        return [
            pltpu.VMEM((parts, 2, 2, block, width), BF16),
            pltpu.VMEM((2, parts, 2, block, half), BF16),
            pltpu.VMEM((2, parts, block, half), BF16),
            pltpu.VMEM((parts, block, width), BF16),
            pltpu.VMEM((parts, block, width), BF16),
            pltpu.SemaphoreType.DMA((8,)),
            pltpu.SemaphoreType.DMA((8,)),
            pltpu.SemaphoreType.DMA((1,)),
        ]

    def copy(self, number):
        d, z, y, x, core = here()
        to = partners()
        left, right = pl.ds(0, self.half), pl.ds(self.half, self.half)
        source, target, device = (
            lambda: (self.source.at[:, :, :, 1 - core], self.from_core, to["core"]),
            lambda: (self.own.at[:, :, 1 - x, :, left], self.first.at[0], to["x"]),
            lambda: (self.own.at[:, 1 - y, :, :, right], self.first.at[1], to["y"]),
            lambda: (self.own.at[:, 1 - y, x, :, left], self.second.at[0], to["y"]),
            lambda: (self.own.at[:, y, 1 - x, :, right], self.second.at[1], to["x"]),
            lambda: (self.own.at[:, y, x], self.near, to["near"]),
            lambda: (self.own.at[:, y, x], self.far, to["inner"]),
            lambda: (self.own.at[:, y, x], self.near, to["near"]),
        )[number]()
        return remote(source, target, self.sends, self.receives, number, number, device)

    def to_cores(self):
        self.copy(0).start()

    def to_first(self):
        self.copy(0).wait()
        for part in range(self.parts):
            for i in range(2):
                for j in range(2):
                    self.own[part, i, j] = self.own[part, i, j] + self.from_core[part, i, j]
        self.copy(1).start()
        self.copy(2).start()

    def to_second(self):
        _, _, y, x, _ = here()
        self.copy(1).wait()
        self.copy(2).wait()
        left, right = slice(0, self.half), slice(self.half, self.width)
        for part in range(self.parts):
            for i in range(2):
                self.own[part, i, x, :, left] = self.own[part, i, x, :, left] + self.first[0, part, i]
                self.own[part, y, i, :, right] = self.own[part, y, i, :, right] + self.first[1, part, i]
        self.copy(3).start()
        self.copy(4).start()

    def to_near(self):
        _, _, y, x, _ = here()
        self.copy(3).wait()
        self.copy(4).wait()
        left, right = slice(0, self.half), slice(self.half, self.width)
        for part in range(self.parts):
            self.own[part, y, x, :, left] = self.own[part, y, x, :, left] + self.second[0, part]
            self.own[part, y, x, :, right] = self.own[part, y, x, :, right] + self.second[1, part]

        @pl.when(outer())
        def _():
            self.copy(5).start()

    def add_whole(self, received):
        _, _, y, x, _ = here()
        for part in range(self.parts):
            self.own[part, y, x] = self.own[part, y, x] + received[part]

    def to_far(self):
        @pl.when(jnp.logical_not(outer()))
        def _():
            self.copy(5).wait_recv()
            self.add_whole(self.near)
            self.copy(6).start()

    def to_other(self):
        @pl.when(jnp.logical_not(outer()))
        def _():
            self.copy(6).wait()
            self.add_whole(self.far)
            self.copy(7).start()

    def to_out(self):
        _, _, y, x, _ = here()

        @pl.when(outer())
        def _():
            self.copy(5).wait_send()
            self.copy(7).wait_recv()
            pltpu.make_async_copy(self.near, self.out, self.local.at[0]).start()

        @pl.when(jnp.logical_not(outer()))
        def _():
            pltpu.make_async_copy(self.own.at[:, y, x], self.out, self.local.at[0]).start()

    def finish(self):
        _, _, y, x, _ = here()

        @pl.when(outer())
        def _():
            pltpu.make_async_copy(self.near, self.out, self.local.at[0]).wait()

        @pl.when(jnp.logical_not(outer()))
        def _():
            self.copy(7).wait_send()
            pltpu.make_async_copy(self.own.at[:, y, x], self.out, self.local.at[0]).wait()


class Trade:
    def __init__(self, out, sends, receives, local, gather=False, parts=1):
        self.out, self.sends, self.receives, self.local = out, sends, receives, local
        self.gather, self.parts = gather, parts

    @staticmethod
    def semaphores(parts=1):
        return [pltpu.SemaphoreType.DMA((2, parts)), pltpu.SemaphoreType.DMA((2, parts)), pltpu.SemaphoreType.DMA((parts,))]

    def device(self, p):
        d, z, _, _, core = here()
        return (d - core + z // 2, 2 * core + (z + p) % 2)

    def stays(self):
        _, z, _, _, core = here()
        return z // 2 == core

    def slot(self, p):
        return p if self.gather else lax.axis_index("seq") % 2

    def own_slot(self, p):
        return p if self.gather else (lax.axis_index("seq") + p) % 2

    def greet(self, barrier):
        @pl.when(jnp.logical_not(self.stays()))
        def _():
            pl.semaphore_signal(barrier, inc=1, device_id=self.device(0), device_id_type=pl.DeviceIdType.MESH)

        pl.semaphore_signal(barrier, inc=1, device_id=self.device(1), device_id_type=pl.DeviceIdType.MESH)
        return jnp.where(self.stays(), 1, 2)

    def rows(self, ref, part):
        many = ref.shape[0] // self.parts
        return ref.at[pl.ds(part * many, many)]

    def keep(self, block, part):
        return pltpu.make_async_copy(
            self.rows(block, part), self.rows(self.out.at[self.own_slot(0)], part), self.local.at[part]
        )

    def copy(self, p, block, part):
        slot = self.slot(p)
        return pltpu.make_async_remote_copy(
            src_ref=self.rows(block, part),
            dst_ref=self.rows(self.out.at[slot], part),
            send_sem=self.sends.at[p, part],
            recv_sem=self.receives.at[slot, part],
            device_id=self.device(p),
            device_id_type=pl.DeviceIdType.MESH,
        )

    def each(self, p, far, near):
        if p == 1:
            far()
            return
        pl.when(jnp.logical_not(self.stays()))(far)
        pl.when(self.stays())(near)

    def begin(self, p, block, part=0):
        self.each(p, lambda: self.copy(p, block, part).start(), lambda: self.keep(block, part).start())

    def sent(self, p, block, part=0):
        self.each(p, lambda: self.copy(p, block, part).wait_send(), lambda: None)

    def arrived(self, p, block, part=0):
        slot = self.own_slot(p)
        target = self.rows(self.out.at[slot], part)

        def far():
            pltpu.make_async_remote_copy(
                src_ref=target,
                dst_ref=target,
                send_sem=self.sends.at[p, part],
                recv_sem=self.receives.at[slot, part],
                device_id=self.device(p),
                device_id_type=pl.DeviceIdType.MESH,
            ).wait_recv()

        self.each(p, far, lambda: self.keep(block, part).wait())


def meet(names, *trades):
    barrier = pltpu.get_barrier_semaphore()
    to = partners()
    for name in names:
        pl.semaphore_signal(barrier, inc=1, device_id=to[name], device_id_type=pl.DeviceIdType.MESH)
    expected = len(names)
    for one in trades:
        expected = expected + one.greet(barrier)
    pl.semaphore_wait(barrier, expected)


def front_kernel(
    tokens, weight, table, steps_ref, gain, shift, query_bias, value_bias,
    x0_out, x1_out, normed_out, query_out, near0_out, near1_out, far0_out, far1_out, info_out,
    x_v, weight_v, table_v, info_here, info_in, normed_v, query_v, near_v, far_v,
    load, stores, info_sends, info_receives, sends, receives, *trade, share,
):
    d, z, _, _, core = here()
    block, width = x_v.shape[1:]
    small = (gain, shift, query_bias, value_bias)
    trade = Trade(x_v, *trade, gather=True, parts=2)
    loaded = pltpu.make_async_copy(weight, weight_v, load.at[0])
    looked_up = pltpu.make_async_copy(table, table_v, load.at[1])
    meet(("core",), trade)
    held = [tokens.at[(z + p) % 2] for p in range(2)]
    pieces = [(p, part) for p in range(2) for part in range(2)]
    many = block // 2
    for p, part in pieces:
        trade.begin(p, held[p], part)
    looked_up.start()
    loaded.start()
    steps = [steps_ref[j] for j in range(2)]
    row = lax.broadcasted_iota(jnp.int32, (16, table.shape[0]), 0)
    place = lax.broadcasted_iota(jnp.int32, (16, table.shape[0]), 1)
    wanted = jnp.where(row == 0, steps[0], jnp.where(row == 1, steps[1], -1))
    chosen = jnp.where(place == wanted, 1.0, 0.0).astype(BF16)
    looked_up.wait()
    time_rows = dot(chosen, table_v[...], NN)
    for j in range(2):
        info_here[4 * j : 4 * j + 4] = known_rows(steps[j], 2 * d + j, share, time_rows[j : j + 1])
    known = remote(info_here, info_in, info_sends, info_receives, 0, 0, partners()["core"])
    known.start()
    known.wait()
    mine = jnp.where(z // 2 == core, info_here[...], info_in[...])
    info_out[0:4] = jnp.where(z % 2 == 0, mine[0:4], mine[4:8])
    info_out[4:8] = jnp.zeros_like(info_in[4:8])
    loaded.wait()
    copies, moved = [], []
    for number, (p, part) in enumerate(pieces):
        trade.arrived(p, held[p], part)
        inner = pl.ds(part * many, many)
        normed, made = project_rows(x_v[p, inner], info_out, small, weight_v)
        near_v[p, inner, :width] = made(1)
        near_v[p, inner, width:] = made(2)
        moved.append(
            remote(near_v.at[p, inner], far_v.at[p, inner], sends, receives, number, number, partners()["core"])
        )
        moved[number].start()
        normed_v[p, inner] = normed
        query_v[p, inner] = made(0)
        whole = pl.ds(number * many, many)
        for at, (source, target) in enumerate(
            (
                (x_v.at[p, inner], (x0_out, x1_out)[p].at[inner]), (normed_v.at[p, inner], normed_out.at[whole]),
                (query_v.at[p, inner], query_out.at[whole]), (near_v.at[p, inner], (near0_out, near1_out)[p].at[inner]),
            )
        ):
            copies.append(pltpu.make_async_copy(source, target, stores.at[number, at]))
            copies[-1].start()
    for number, (p, part) in enumerate(pieces):
        inner = pl.ds(part * many, many)
        moved[number].wait()
        copies.append(
            pltpu.make_async_copy(far_v.at[p, inner], (far0_out, far1_out)[p].at[inner], stores.at[number, 4])
        )
        copies[-1].start()
    for p, part in pieces:
        trade.sent(p, held[p], part)
    for copy in copies:
        copy.wait()


def front(tokens, weight, table, steps, small, share):
    _, block, width = tokens.shape
    info_shape = (8, width)
    any_spec = pl.BlockSpec(memory_space=pl.ANY)
    inside = pl.BlockSpec(memory_space=pltpu.VMEM)
    pair = pltpu.VMEM((2, block, width), BF16)
    wide_pair = pltpu.VMEM((2, block, 2 * width), BF16)
    one = pltpu.SemaphoreType.DMA((1,))
    two, four = pltpu.SemaphoreType.DMA((2,)), pltpu.SemaphoreType.DMA((4,))
    return pl.pallas_call(
        functools.partial(front_kernel, share=share),
        in_specs=[any_spec] * 3 + [pl.BlockSpec(memory_space=pltpu.SMEM)] + [inside] * 4,
        out_specs=[any_spec] * 8 + [inside],
        out_shape=[shape_of((block, width))] * 2
        + [shape_of((2 * block, width))] * 2
        + [shape_of((block, 2 * width))] * 4
        + [shape_of(info_shape, F32)],
        scratch_shapes=[
            pair, pltpu.VMEM(weight.shape, BF16), pltpu.VMEM(table.shape, BF16), pltpu.VMEM(info_shape, F32),
            pltpu.VMEM(info_shape, F32), pair, pair, wide_pair, wide_pair,
            two, pltpu.SemaphoreType.DMA((4, 5)), one, one, four, four,
        ]
        + Trade.semaphores(2),
        compiler_params=pltpu.CompilerParams(
            vmem_limit_bytes=VMEM_BYTES, collective_id=2, has_side_effects=True
        ),
        cost_estimate=cost(48),
        name="front",
    )(tokens, weight, table, steps, *small)


def fixed_any():
    return pl.BlockSpec(memory_space=pl.ANY)


def back_kernel(
    query_ref, grad_ref, context_ref, logsum_ref, *refs, pieces, parts, pairs
):
    key_refs, value_refs = refs[:pieces], refs[pieces : 2 * pieces]
    refs = refs[2 * pieces :]
    normed_ref, hidden_grad_ref, whole_context, branch, active_ref, cot0, cot1 = refs[:7]
    first_normed, layer_ref, query_grad_ref, key_out, value_out, layer_out, down_out, up_out, qkv_out = refs[7:16]
    refs = refs[16:]
    near = pieces // 2
    down_parts, up_parts = refs[:2]
    chunks = []
    for number, (which, at, many) in enumerate(back_chunks(down_parts.shape, up_parts.shape)):
        scratch = refs[2 + 8 * number : 10 + 8 * number]
        if which == "down":
            here_rows = pl.ds(at, many)
            chunks.append(
                Reduction(down_parts.at[:, :, :, :, here_rows], down_out.at[:, here_rows], scratch)
            )
        else:
            here_parts = pl.ds(at, many)
            chunks.append(Reduction(up_parts.at[here_parts], up_out.at[here_parts], scratch))
    qkv_parts = refs[34]
    for group in range(2):
        lanes = pl.ds(2 * group * LANES, 2 * LANES)
        scratch = refs[35 + 8 * group : 43 + 8 * group]
        chunks.append(Reduction(qkv_parts.at[group], qkv_out.at[:, :, lanes], scratch))
    one, two, three, four, five, six = chunks
    query_held, near_grads, far_grads, far_in, far_sends, far_receives = refs[51:57]
    whole_context_ref, branch_ref, cots_ref, first_normed_ref, loads = refs[57:62]
    back = Trade(layer_out, *refs[62:])
    block = key_refs[0].shape[0]
    layer_blocks = [layer_ref.at[pl.ds(p * block, block)] for p in range(2)]
    step = pl.program_id(0)
    made = 2 * parts + 1
    pair, last = step - made, pl.num_programs(0) - 1

    def far_copy(which):
        return remote(
            far_grads, far_in.at[which % 2], far_sends, far_receives, 0, which, partners()["core"]
        )

    loaded = [
        pltpu.make_async_copy(source, target, loads.at[number])
        for number, (source, target) in enumerate(
            (
                (whole_context, whole_context_ref), (branch, branch_ref), (cot0, cots_ref.at[pl.ds(0, block)]),
                (cot1, cots_ref.at[pl.ds(block, block)]), (first_normed, first_normed_ref),
            )
        )
    ]

    def begin():
        for copy in loaded:
            copy.start()
        meet(("core", "x", "y", "near", "inner"), back)
        back.begin(0, layer_blocks[0])
        back.begin(1, layer_blocks[1])

    def settle():
        which = pair - 1
        slot = which % 2
        far_copy(which).wait()
        key_grad = near_grads[slot, 0] + far_in[slot, 0]
        value_grad = near_grads[slot, 1] + far_in[slot, 1]
        key_out[...] = key_grad
        value_out[...] = value_grad

        @pl.when(which < 4)
        def _():
            grads = jnp.concatenate([query_held[slot], key_grad, value_grad], 1)
            product = dot(first_normed_ref[...], grads, TN).astype(BF16)
            lanes = pl.ds(pl.multiple_of(slot * LANES, LANES), LANES)
            for part in range(3):
                block_of = product[:, part * LANES : (part + 1) * LANES]
                qkv_parts[which // 2, part, :, :, :, :, lanes] = block_of.reshape(qkv_parts.shape[2:6] + (LANES,))

    plan = {
        (0, 0): [begin],
        (2, 0): [one.to_cores],
        (4, 0): [one.to_first],
        (5, 0): [two.to_cores],
        (8, 0): [two.to_first],
        (9, 0): [three.to_cores, one.to_second],
        (9, 1): [four.to_cores],
        (10, 0): [three.to_first, one.to_near],
        (10, 1): [two.to_second],
        (10, 2): [four.to_first],
        (10, 3): [one.to_far],
        (11, 0): [five.to_cores],
        (11, 1): [two.to_near],
        (11, 2): [three.to_second, one.to_other],
        (11, 3): [five.to_first, four.to_second],
        (12, 1): [three.to_near, two.to_far, one.to_out],
        (12, 2): [five.to_second, four.to_near],
        (13, 0): [six.to_cores, five.to_near, three.to_far],
        (13, 1): [six.to_first, four.to_far, two.to_other],
        (13, 2): [five.to_far],
        (13, 3): [six.to_second, three.to_other],
        (14, 1): [six.to_near, four.to_other, five.to_other, two.to_out],
        (14, 2): [three.to_out],
        (14, 3): [six.to_far, five.to_out],
        (15, 0): [six.to_other, four.to_out, six.to_out],
    }

    def run_plan(place, steps):
        for (at, where), actions in plan.items():
            if where == place and at in steps:

                @pl.when(step == at)
                def _():
                    for action in actions:
                        action()

    run_plan(0, range(made))

    @pl.when(step < parts)
    def _():
        part = dot(normed_ref[...], hidden_grad_ref[...], TN).astype(BF16)
        up_parts[step] = part.reshape(up_parts.shape[1:])

    @pl.when(step == parts)
    def _():
        for copy in loaded:
            copy.wait()
        part = dot(whole_context_ref[...], branch_ref[...], TN).astype(BF16)
        up_parts[parts] = part.reshape(up_parts.shape[1:])

    @pl.when((step > parts) & (step < made))
    def _():
        part = dot(active_ref[...], cots_ref[...], TN).astype(BF16).reshape(down_parts.shape[3:])
        at = step - parts - 1
        down_parts[0, at // 2, at % 2] = part

    def before(place):
        def run():
            run_plan(place, range(made, made + pairs))
            if place == near:
                far_copy(pair).start()

        return run

    pl.when(pair >= 1)(settle)

    @pl.when((step >= made) & (pair < pairs))
    def _():
        order = []
        slot = pair % 2
        for i in range(near):
            far_rows = pl.ds(i * block, block)
            order.append(
                (key_refs[near + i], value_refs[near + i], far_grads.at[0, far_rows], far_grads.at[1, far_rows])
            )
        for i in range(near):
            near_rows = pl.ds(i * block, block)
            order.append(
                (key_refs[i], value_refs[i], near_grads.at[slot, 0, near_rows], near_grads.at[slot, 1, near_rows])
            )
        steps = [one_piece + (before(place),) for place, one_piece in enumerate(order)]
        attend_back_step(query_ref, grad_ref, context_ref, logsum_ref, steps, query_grad_ref)
        query_held[slot] = query_grad_ref[...]

    @pl.when(step == last)
    def _():
        run_plan(0, [made + pairs])
        for p in range(2):
            back.sent(p, layer_blocks[p])
            back.arrived(p, layer_blocks[p])
        for chunk in chunks:
            chunk.finish()


def back_chunks(down_shape, up_shape):
    block, parts = down_shape[-2], up_shape[0]
    return [
        ("up", 0, parts // 2),
        ("up", parts // 2, parts - parts // 2),
        ("down", 0, block // 2),
        ("down", block // 2, block // 2),
    ]


def back(query, grad, context, logsum, kvs, normed, hidden_grad, branch, active, cots, first_normed, layer_out):
    count, width = query.shape
    pairs, pieces, length = width // LANES, len(kvs), kvs[0].shape[0]
    near = pieces // 2
    parts = hidden_grad.shape[1] // width
    made = 2 * parts + 1
    pair = lambda i: jnp.clip(i - made, 0, pairs - 1)
    row = pl.BlockSpec((count, LANES), lambda i: (0, pair(i)))
    settled = pl.BlockSpec((count, LANES), lambda i: (0, jnp.clip(i - made - 1, 0, pairs - 1)))
    piece = pl.BlockSpec((length, LANES), lambda i: (0, pair(i)))
    value = pl.BlockSpec((length, LANES), lambda i: (0, pairs + pair(i)))
    whole = fixed((count, width))
    up_rows, down_rows = width // 8, hidden_grad.shape[1] // 8
    down_shape, up_shape = (1, 2, 2, 2, down_rows, width), (parts + 1, 2, 2, 2, up_rows, width)
    return pl.pallas_call(
        functools.partial(back_kernel, pieces=pieces, parts=parts, pairs=pairs),
        grid=(made + pairs + 1,),
        in_specs=[row] * 4
        + [piece] * pieces
        + [value] * pieces
        + [
            whole,
            pl.BlockSpec((count, width), lambda i: (0, jnp.minimum(i, parts - 1))),
            fixed_any(),
            fixed_any(),
            pl.BlockSpec((count, width), lambda i: (0, jnp.clip(i - parts - 1, 0, parts - 1))),
        ]
        + [fixed_any()] * 4,
        out_specs=[row, settled, settled] + [fixed_any()] * 4,
        out_shape=[shape_of((count, width))] * 3
        + [
            shape_of((2, length, width)), shape_of((1, down_rows, width)), shape_of((parts + 1, up_rows, width)),
            shape_of((3, up_rows, 4 * LANES)),
        ],
        scratch_shapes=[pltpu.VMEM(down_shape, BF16), pltpu.VMEM(up_shape, BF16)]
        + [
            shape
            for which, _, many in back_chunks(down_shape, up_shape)
            for shape in Reduction.scratch(*((1, many) if which == "down" else (many, up_rows)), width)
        ]
        + [pltpu.VMEM((2, 3, 2, 2, 2, up_rows, 2 * LANES), BF16)]
        + Reduction.scratch(3, up_rows, 2 * LANES) * 2
        + [
            pltpu.VMEM((2, count, LANES), BF16),
            pltpu.VMEM((2, 2, count, LANES), BF16),
            pltpu.VMEM((2, count, LANES), BF16),
            pltpu.VMEM((2, 2, count, LANES), BF16),
            pltpu.SemaphoreType.DMA((1,)),
            pltpu.SemaphoreType.DMA((pairs,)),
        ]
        + [pltpu.VMEM((count, width), BF16)] * 4
        + [pltpu.SemaphoreType.DMA((5,))]
        + Trade.semaphores(),
        compiler_params=pltpu.CompilerParams(
            vmem_limit_bytes=VMEM_BYTES, collective_id=0, has_side_effects=True
        ),
        cost_estimate=cost(100),
        name="back",
    )(
        query, grad, context, logsum, *kvs, *kvs, normed, hidden_grad, context, branch, active, *cots,
        first_normed, layer_out
    )


def tail_kernel(
    query_grad, key_grad, value_grad, normed, x0, x1, middle_grad, weight,
    info_ref, gain_ref, feed_ref,
    tokens_out, qkv_out, sums_ref,
    query_v, key_v, value_v, normed_v, x_v, middle_v, weight_v, token_v, last_parts, *refs, total_tokens, parts,
):
    one = Reduction(last_parts, qkv_out, refs[:8])
    sums_in, sums_sends, sums_receives, loads = refs[8:12]
    back = Trade(tokens_out, *refs[12:], parts=TOKEN_PARTS)
    block, width = x0.shape
    d, z, _, _, core = here()
    total, ahead, many = 2 * TOKEN_PARTS, TOKEN_PARTS, block // 2
    top, bottom = pl.ds(0, block), pl.ds(block, block)
    later = ((query_grad, query_v), (key_grad, key_v), (value_grad, value_v), (middle_grad, middle_v))
    copies = [
        pltpu.make_async_copy(source, target, loads.at[number])
        for number, (source, target) in enumerate(
            (
                (weight, weight_v), (x0, x_v.at[0]),
                *((ref.at[top], held.at[top]) for ref, held in later),
                (normed, normed_v), (x1, x_v.at[1]),
                *((ref.at[bottom], held.at[bottom]) for ref, held in later),
            )
        )
    ]
    for copy in copies:
        copy.start()
    meet(("core", "x", "y", "near", "inner"), back)

    def start_block(number):
        p, at = divmod(number * many, block)
        held = pl.ds(number * many, many)
        inner = pl.ds(at, many)
        normed_grad = 0.0
        for part, grads in enumerate((query_v, key_v, value_v)):
            columns = slice(part * width, (part + 1) * width)
            normed_grad = normed_grad + dot(grads[held], weight_v[:, columns], NT)
        unit, scale = norm_parts(x_v[p, inner].astype(F32) + one_row(info_ref, TIME))
        token_grad = middle_v[held] + norm_backward(normed_grad, vector(gain_ref), unit, scale)
        token_v[p, inner] = token_grad.astype(BF16)
        return [
            column_sum(normed_grad * unit),
            column_sum(normed_grad),
            column_sum(query_v[held].astype(F32)),
            column_sum(value_v[held].astype(F32)),
            column_sum(token_grad),
        ]

    def sums_copy(number):
        to = partners()[("core", "x", "y", "near", "inner", "near")[number]]
        return remote(sums_ref, sums_in.at[number], sums_sends, sums_receives, number, number, to)

    def sums_next(number):
        def add_up():
            sums_ref[...] = sums_ref[...] + sums_in[number]

        if number < 3:
            sums_copy(number).wait()
            add_up()
            if number < 2:
                sums_copy(number + 1).start()
            else:
                pl.when(outer())(sums_copy(3).start)
            return

        @pl.when(outer())
        def _():
            if number == 3:
                sums_copy(3).wait_send()
            if number == 5:
                sums_copy(5).wait_recv()
                sums_ref[...] = sums_in[5]

        @pl.when(jnp.logical_not(outer()))
        def _():
            if number == 3:
                sums_copy(3).wait_recv()
                add_up()
                sums_copy(4).start()
            if number == 4:
                sums_copy(4).wait()
                add_up()
                sums_copy(5).start()
            if number == 5:
                sums_copy(5).wait_send()

    def move(number):
        if number >= ahead:
            p, part = divmod(number - ahead, TOKEN_PARTS)
            back.sent(p, token_v.at[p], part)
        p, part = divmod(number, TOKEN_PARTS)
        back.begin(p, token_v.at[p], part)

    for copy in copies[:6]:
        copy.wait()
    sums = start_block(0)
    for number in range(ahead // 2):
        move(number)
    sums = [a + b for a, b in zip(sums, start_block(1))]
    for number in range(ahead // 2, ahead):
        move(number)
    for copy in copies[6:]:
        copy.wait()
    lanes = slice(width - 2 * LANES, width)
    for part, grads in enumerate((query_v, key_v, value_v)):
        made = dot(normed_v[...], grads[:, lanes], TN).astype(BF16)
        last_parts[part] = made.reshape(last_parts.shape[1:])
    one.to_cores()
    sums = [a + b for a, b in zip(sums, start_block(2))]
    one.to_first()
    sums = [a + b for a, b in zip(sums, start_block(3))]
    sums_ref[...] = jnp.zeros_like(sums_ref)
    sums_ref[0:4] = feed_ref[0:4]
    sums_ref[4 : 4 + parts] = feed_ref[8 : 8 + parts]
    for number in range(4):
        sums_ref[4 + parts + number : 5 + parts + number] = sums[number]
    energy = jnp.sum(feed_ref[4:5], keepdims=True) / (width * total_tokens)
    sums_ref[8 + parts : 9 + parts] = info_ref[MARK : MARK + 1] * energy + info_ref[SHARE : SHARE + 1]
    sums_ref[9 + parts : 10 + parts] = info_ref[STEP : STEP + 1] * jnp.where(core == 0, 1.0, 0.0)
    sequence = (d - core + z // 2) * 2 + z % 2
    sums_ref[pl.ds(16 + sequence, 1)] = sums[4]
    sums_copy(0).start()
    for number in range(ahead, ahead + 2):
        move(number)
    sums_next(0)
    one.to_second()
    sums_next(1)
    one.to_near()
    sums_next(2)
    for number in range(ahead + 2, ahead + 4):
        move(number)
    one.to_far()
    sums_next(3)
    for number in range(ahead + 4, ahead + 6):
        move(number)
    one.to_other()
    sums_next(4)
    for number in range(ahead + 6, total):
        move(number)
    one.to_out()
    sums_next(5)
    for number in range(total - ahead, total):
        p, part = divmod(number, TOKEN_PARTS)
        back.sent(p, token_v.at[p], part)
    for number in range(total):
        p, part = divmod(number, TOKEN_PARTS)
        back.arrived(p, token_v.at[p], part)
    one.finish()


def tail(grads, normed, xs, middle_grad, weight, info, gain, feed_sums, total_tokens, hidden_parts):
    block, width = xs[0].shape
    count, total_seqs = 2 * block, 16
    any_spec = fixed_any()
    inside = pl.BlockSpec(memory_space=pltpu.VMEM)
    up_rows = width // 8
    held = lambda *shape, dtype=BF16: pltpu.VMEM(shape, dtype)
    sums_shape = (16 + total_seqs, width)
    return pl.pallas_call(
        functools.partial(tail_kernel, total_tokens=total_tokens, parts=hidden_parts),
        in_specs=[any_spec] * 8 + [inside] * 3,
        out_specs=[any_spec, any_spec, inside],
        out_shape=[
            shape_of((2, block, width)), shape_of((3, up_rows, 2 * LANES)), shape_of(sums_shape, F32),
        ],
        scratch_shapes=[
            held(count, width), held(count, width), held(count, width), held(count, width),
            held(2, block, width), held(count, width, dtype=F32), held(*weight.shape), held(2, block, width),
            held(3, 2, 2, 2, up_rows, 2 * LANES),
        ]
        + Reduction.scratch(3, up_rows, 2 * LANES)
        + [
            held(6, *sums_shape, dtype=F32),
            pltpu.SemaphoreType.DMA((6,)),
            pltpu.SemaphoreType.DMA((6,)),
            pltpu.SemaphoreType.DMA((12,)),
        ]
        + Trade.semaphores(TOKEN_PARTS),
        compiler_params=pltpu.CompilerParams(
            vmem_limit_bytes=VMEM_BYTES, collective_id=1, has_side_effects=True
        ),
        cost_estimate=cost(60),
        name="tail",
    )(*grads, normed, *xs, middle_grad, weight, info, gain, feed_sums)


def finish_kernel(
    token_ref, layer_ref, qkv_ref, last_qkv_ref, up_out_ref, out_part_ref, down_ref, sums_ref,
    token_out, layer_out, qkv_out, up_out, out_out, down_out, table_out, *small_outs, total_seqs, parts, table_rows,
):
    token_out[...] = wide(token_ref)
    layer_out[...] = layer_ref[...]
    qkv_out[...] = jnp.concatenate([qkv_ref[0], last_qkv_ref[0]], 1).astype(F32)
    up_out[...] = up_out_ref[0].astype(F32)
    out_out[...] = out_part_ref[0].astype(F32)
    down_out[...] = wide(down_ref)
    block, width = table_out.shape
    steps_row = 9 + parts
    first = lax.axis_index("dp") * table_rows + pl.program_id(0) * block
    place = (lax.broadcasted_iota(jnp.int32, (block, 1), 0) + first).astype(F32)
    total = jnp.zeros_like(table_out)
    for s in range(total_seqs):
        chosen = place == sums_ref[steps_row : steps_row + 1, s : s + 1]
        total = total + jnp.where(chosen, sums_ref[16 + s : 17 + s], 0.0)
    table_out[...] = total

    @pl.when(pl.program_id(0) == 0)
    def _():
        d = lax.axis_index("dp")
        piece = small_outs[0].shape[0]
        turned = pltpu.roll(sums_ref[0:16], lax.rem(width - d * piece, width), 1)
        order = [row for row in range(8 + parts) if not 4 <= row < 4 + parts]
        for row, out in zip(order, small_outs):
            out[...] = turned[row, :piece]
        up_piece = small_outs[8].shape[0]
        share = width // up_piece
        mine = sums_ref[pl.ds(4 + d // share, 1)]
        mine = pltpu.roll(mine, lax.rem(width - d % share * up_piece, width), 1)
        small_outs[8][...] = mine[0, :up_piece]
        small_outs[9][...] = sums_ref[8 + parts, :BUCKETS]
        small_outs[10][...] = sums_ref[8 + parts, BUCKETS : 2 * BUCKETS]


def finish(token, layer, qkv, last_qkv, up_out, down, sums, table_rows, dp):
    seqs, length, width = token.shape
    parts, block = up_out.shape[0] - 1, up_out.shape[1]
    steps = parts
    small = [width // dp] * 8 + [parts * width // dp] + [BUCKETS] * 2
    rows_at = lambda many: pl.BlockSpec((many // steps, width), lambda i: (i, 0))
    count = seqs * length
    wide_rows = rows_at(count)
    made = pl.pallas_call(
        functools.partial(
            finish_kernel, total_seqs=sums.shape[0] - 16, parts=parts, table_rows=table_rows
        ),
        grid=(steps,),
        in_specs=[
            wide_rows, wide_rows,
            pl.BlockSpec((1, block, qkv.shape[2]), lambda i: (jnp.minimum(i, 2), 0, 0)),
            pl.BlockSpec((1, block, last_qkv.shape[2]), lambda i: (jnp.minimum(i, 2), 0, 0)),
            pl.BlockSpec((1, block, width), lambda i: (i, 0, 0)),
            pl.BlockSpec((1, block, width), lambda i: (parts, 0, 0)),
            rows_at(down.shape[0]),
            fixed(sums.shape),
        ],
        out_specs=[
            wide_rows, wide_rows,
            pl.BlockSpec((block, width), lambda i: (0, jnp.minimum(i, 2))),
            pl.BlockSpec((block, width), lambda i: (0, i)),
            pl.BlockSpec((block, width), lambda i: (0, 0)),
            rows_at(down.shape[0]), rows_at(table_rows),
        ]
        + [pl.BlockSpec((many,), lambda i: (0,)) for many in small],
        out_shape=[
            shape_of((count, width), F32), shape_of((count, width)), shape_of((block, 3 * width), F32),
            shape_of((block, parts * width), F32), shape_of((block, width), F32), shape_of(down.shape, F32),
            shape_of((table_rows, width), F32),
        ]
        + [shape_of((many,), F32) for many in small],
        compiler_params=params(),
        cost_estimate=cost(6),
        name="finish",
    )(token.reshape(count, width), layer.reshape(count, width), qkv, last_qkv, up_out, up_out, down, sums)
    shape = (seqs, length, width)
    return [made[0].reshape(shape), made[1].reshape(shape)] + list(made[2:])


def gelu_parts(hidden):
    share = 0.5 + 0.5 * lax.erf(hidden * 2**-0.5)
    bell = jnp.exp(-0.5 * hidden * hidden) * 0.3989422804014327
    return hidden * share, share + hidden * bell


def feed_kernel(
    context_ref, x0_ref, x1_ref, info_ref, cot0_ref, cot1_ref, out_weight_ref, up_ref, down_ref,
    out_bias_ref, gain_ref, shift_ref, down_bias_ref, up_bias_ref,
    out_ref, active_ref, hidden_grad_ref, normed_ref, middle_grad_ref, branch_ref, context_grad_ref, sums_ref,
    out_weight_v, up_v, down_v, loads,
):
    step = pl.program_id(0)
    width, hidden_width = x0_ref.shape[1], up_ref.shape[1]

    parts = hidden_width // width
    out_copy = pltpu.make_async_copy(out_weight_ref, out_weight_v, loads.at[0, parts])
    copies = []
    for part in range(parts):
        columns = pl.ds(part * width, width)
        copies.append(
            (
                pltpu.make_async_copy(up_ref.at[:, columns], up_v.at[:, columns], loads.at[0, part]),
                pltpu.make_async_copy(down_ref.at[columns], down_v.at[columns], loads.at[1, part]),
            )
        )

    @pl.when(step == 0)
    def _():
        out_copy.start()
        for one, two in copies:
            one.start()
            two.start()
        sums_ref[...] = jnp.zeros_like(sums_ref)
        out_copy.wait()

    x = jnp.where(step == 0, x0_ref[...], x1_ref[...])
    cot = jnp.where(step == 0, cot0_ref[...], cot1_ref[...])
    middle = (
        x.astype(F32)
        + one_row(info_ref, TIME)
        + dot(context_ref[...], out_weight_v[...], NN)
        + vector(out_bias_ref)
    )
    unit, scale = norm_parts(middle)
    gain = vector(gain_ref)
    normed = (unit * gain + vector(shift_ref)).astype(BF16)
    normed_ref[...] = normed
    out = middle + vector(down_bias_ref)
    normed_grad = jnp.zeros_like(out)
    up_bias = vector(up_bias_ref)
    for part in range(parts):
        columns = slice(part * width, (part + 1) * width)

        @pl.when(step == 0)
        def _():
            for copy in copies[part]:
                copy.wait()

        hidden = dot(normed, up_v[:, columns], NN) + up_bias[:, columns]
        active, slope = gelu_parts(hidden)
        active = active.astype(BF16)
        active_ref[:, columns] = active
        out = out + dot(active, down_v[columns, :], NN)
        hidden_grad = (dot(cot, down_v[columns, :], NT) * slope).astype(BF16)
        hidden_grad_ref[:, columns] = hidden_grad
        sums_ref[8 + part : 9 + part] += column_sum(hidden_grad.astype(F32))
        normed_grad = normed_grad + dot(hidden_grad, up_v[:, columns], NT)
    out_ref[...] = out.astype(BF16)
    cot = cot.astype(F32)
    middle_grad = cot + norm_backward(normed_grad, gain, unit, scale)
    middle_grad_ref[...] = middle_grad
    branch = middle_grad.astype(BF16)
    branch_ref[...] = branch
    context_grad_ref[...] = dot(branch, out_weight_v[...], NT).astype(BF16)
    sums_ref[0:1] += column_sum(cot)
    sums_ref[1:2] += column_sum(normed_grad * unit)
    sums_ref[2:3] += column_sum(normed_grad)
    sums_ref[3:4] += column_sum(branch.astype(F32))
    sums_ref[4:5] += column_sum(out * out)


def feed(context, xs, info, small, cots, out_weight, up, down):
    block, width = xs[0].shape
    count, hidden_width = 2 * block, up.shape[1]
    sums_rows = 8 + hidden_width // width + (-(hidden_width // width)) % 8
    whole = fixed((block, width))
    return pl.pallas_call(
        feed_kernel,
        grid=(2,),
        in_specs=[
            rows(block, width), whole, whole, fixed(info.shape), whole, whole,
        ]
        + [pl.BlockSpec(memory_space=pl.ANY)] * 3
        + [whole_vector(v) for v in small],
        out_specs=[
            rows(block, width), rows(block, hidden_width), rows(block, hidden_width), rows(block, width),
            rows(block, width), rows(block, width), rows(block, width),
            pl.BlockSpec((sums_rows, width), lambda i: (0, 0)),
        ],
        out_shape=[
            shape_of((count, width)), shape_of((count, hidden_width)), shape_of((count, hidden_width)),
            shape_of((count, width)), shape_of((count, width), F32), shape_of((count, width)),
            shape_of((count, width)), shape_of((sums_rows, width), F32),
        ],
        scratch_shapes=[
            pltpu.VMEM(out_weight.shape, BF16), pltpu.VMEM(up.shape, BF16), pltpu.VMEM(down.shape, BF16),
            pltpu.SemaphoreType.DMA((2, hidden_width // width + 1)),
        ],
        compiler_params=params(),
        cost_estimate=cost(34),
        name="feed",
    )(context, *xs, info, *cots, out_weight, up, down, *small)


def down_grad_kernel(active_ref, cot0_ref, cot1_ref, out_ref):
    block = cot0_ref.shape[0]
    out_ref[...] = (
        dot(active_ref[:block], cot0_ref[...], TN) + dot(active_ref[block:], cot1_ref[...], TN)
    ).astype(BF16)


def down_grad(active, cots):
    block, width = cots[0].shape
    count, hidden_width = active.shape
    return pl.pallas_call(
        down_grad_kernel,
        grid=(hidden_width // width,),
        in_specs=[pl.BlockSpec((count, width), lambda i: (0, i))] + [fixed((block, width))] * 2,
        out_specs=rows(width, width),
        out_shape=shape_of((hidden_width, width)),
        compiler_params=params(),
        cost_estimate=cost(8),
        name="down_grad",
    )(active, *cots)


def up_out_grad_kernel(normed_ref, hidden_grad_ref, context_ref, branch_ref, out_ref):
    last = pl.num_programs(0) - 1

    @pl.when(pl.program_id(0) < last)
    def _():
        out_ref[0] = dot(normed_ref[...], hidden_grad_ref[...], TN).astype(BF16)

    @pl.when(pl.program_id(0) == last)
    def _():
        out_ref[0] = dot(context_ref[...], branch_ref[...], TN).astype(BF16)


def up_out_grad(normed, hidden_grad, context, branch):
    count, width = normed.shape
    parts = hidden_grad.shape[1] // width
    whole = fixed((count, width))
    return pl.pallas_call(
        up_out_grad_kernel,
        grid=(parts + 1,),
        in_specs=[
            whole,
            pl.BlockSpec((count, width), lambda i: (0, jnp.minimum(i, parts - 1))),
            whole,
            whole,
        ],
        out_specs=pl.BlockSpec((1, width, width), lambda i: (i, 0, 0)),
        out_shape=shape_of((parts + 1, width, width)),
        compiler_params=params(),
        cost_estimate=cost(10),
        name="up_out_grad",
    )(normed, hidden_grad, context, branch)


def qkv_grad_kernel(normed_ref, grad_ref, out_ref):
    out_ref[0] = dot(normed_ref[...], grad_ref[...], TN).astype(BF16)


def qkv_grad(normed, grads):
    count, width = normed.shape
    parts = grads.shape[1] // width
    return pl.pallas_call(
        qkv_grad_kernel,
        grid=(parts,),
        in_specs=[fixed((count, width)), pl.BlockSpec((count, width), lambda i: (0, i))],
        out_specs=pl.BlockSpec((1, width, width), lambda i: (i, 0, 0)),
        out_shape=shape_of((parts, width, width)),
        compiler_params=params(),
        cost_estimate=cost(7),
        name="qkv_grad",
    )(normed, grads)


def start_kernel(
    query_grad_ref, key0_ref, key1_ref, far_key0_ref, far_key1_ref, value0_ref, value1_ref, far_value0_ref,
    far_value1_ref, x0_ref, x1_ref, info_ref, middle_grad_ref, gain_ref, weight_ref,
    token0_ref, token1_ref, grads_ref, sums_ref,
):
    step = pl.program_id(0)
    width = x0_ref.shape[1]

    @pl.when(step == 0)
    def _():
        sums_ref[...] = jnp.zeros_like(sums_ref)

    def pick(first, second):
        return jnp.where(step == 0, first[...], second[...])

    query_grad = query_grad_ref[...]
    key_grad = (pick(key0_ref, key1_ref).astype(F32) + pick(far_key0_ref, far_key1_ref).astype(F32)).astype(BF16)
    value_grad = (
        pick(value0_ref, value1_ref).astype(F32) + pick(far_value0_ref, far_value1_ref).astype(F32)
    ).astype(BF16)
    normed_grad = 0.0
    for part, grad in enumerate((query_grad, key_grad, value_grad)):
        columns = slice(part * width, (part + 1) * width)
        grads_ref[:, columns] = grad
        normed_grad = normed_grad + dot(grad, weight_ref[:, columns], NT)
    unit, scale = norm_parts(pick(x0_ref, x1_ref).astype(F32) + one_row(info_ref, TIME))
    token_grad = middle_grad_ref[...] + norm_backward(normed_grad, vector(gain_ref), unit, scale)

    @pl.when(step == 0)
    def _():
        token0_ref[...] = token_grad.astype(BF16)

    @pl.when(step == 1)
    def _():
        token1_ref[...] = token_grad.astype(BF16)

    sums_ref[0:1] += column_sum(normed_grad * unit)
    sums_ref[1:2] += column_sum(normed_grad)
    sums_ref[2:3] += column_sum(query_grad.astype(F32))
    sums_ref[3:4] += column_sum(value_grad.astype(F32))
    sums_ref[4:5] += column_sum(token_grad)


def start_back(query_grad, key_grads, value_grads, xs, info, middle_grad, gain, weight):
    block, width = xs[0].shape
    count = 2 * block
    whole = fixed((block, width))
    kept = pl.BlockSpec((block, width), lambda i: (0, 0))
    return pl.pallas_call(
        start_kernel,
        grid=(2,),
        in_specs=[rows(block, width)]
        + [whole] * 10
        + [fixed(info.shape), rows(block, width), whole_vector(gain), fixed(weight.shape)],
        out_specs=[kept, kept, rows(block, 3 * width), pl.BlockSpec((8, width), lambda i: (0, 0))],
        out_shape=[
            shape_of((block, width)), shape_of((block, width)), shape_of((count, 3 * width)),
            shape_of((8, width), F32),
        ],
        compiler_params=params(),
        cost_estimate=cost(10),
        name="start_back",
    )(query_grad, *key_grads, *value_grads, *xs, info, middle_grad, gain, weight)


class Places:
    def __init__(self, dp, seq):
        self.dp, self.seq = dp, seq
        self.bits = dp.bit_length() - 1

    def flat(self, d, z):
        return d * self.seq + z

    def pairs(self, to):
        return [
            (self.flat(d, z), self.flat(*to(d, z))) for d in range(self.dp) for z in range(self.seq)
        ]

    def gather_order(self, turn):
        def to(d, z):
            core, j = d % 2, (z + turn) % 2
            return d - core + z // 2, 2 * core + j

        return self.pairs(to)

    def scatter_order(self, turn):
        return [(b, a) for a, b in self.gather_order(turn)]

    def swap(self, bit):
        return self.pairs(lambda d, z: (d ^ (1 << bit), z))

    def swap_seq(self, step):
        return self.pairs(lambda d, z: (d, z ^ step))


def send(x, order):
    return lax.ppermute(x, BOTH, order)


def add(a, b):
    return (a.astype(F32) + b.astype(F32)).astype(BF16)


def reduce_parts(parts, places):
    d, z = lax.axis_index("dp"), lax.axis_index("seq")
    count, height, width = parts.shape
    block = height // places.dp
    grid = parts.reshape((count,) + (2,) * places.bits + (block, width))

    def halve(value, bit, axes):
        axis = 1 + axes.index(bit)
        mine = (d >> bit) & 1
        kept = lax.dynamic_index_in_dim(value, mine, axis, keepdims=False)
        sent = lax.dynamic_index_in_dim(value, 1 - mine, axis, keepdims=False)
        axes.remove(bit)
        return add(kept, send(sent, places.swap(bit)))

    axes = list(range(places.bits - 1, -1, -1))
    grid = halve(grid, 0, axes)
    halves = []
    for number, order in enumerate((range(1, places.bits), range(places.bits - 1, 0, -1))):
        at = block // 2
        value = lax.slice_in_dim(grid, number * at, (number + 1) * at, axis=grid.ndim - 2)
        left = list(axes)
        for bit in order:
            value = halve(value, bit, left)
        halves.append(sum_along_seq(value, z, places))
    return jnp.concatenate(halves, 1)


def sum_along_seq(value, z, places):
    count, block, width = value.shape
    mine = z % 2
    grid = value.reshape(count, block, 2, width // 2)
    kept = lax.dynamic_index_in_dim(grid, mine, 2, keepdims=False)
    sent = lax.dynamic_index_in_dim(grid, 1 - mine, 2, keepdims=False)
    half = add(kept, send(sent, places.swap_seq(1)))
    half = add(half, send(half, places.swap_seq(2)))
    other = send(half, places.swap_seq(1))
    first = jnp.where(mine == 0, half, other)
    second = jnp.where(mine == 0, other, half)
    return jnp.concatenate([first, second], 2).astype(F32)


def sum_everywhere(value, places):
    for bit in range(places.bits):
        value = value + send(value, places.swap(bit))
    for step in (1, 2):
        value = value + send(value, places.swap_seq(step))
    return value


def per_device(
    tokens, timesteps, time_table, ln1_gain, ln1_bias, qkv_weight, q_bias, v_bias, out_weight, out_bias,
    ln2_gain, ln2_bias, up_weight, up_bias, down_weight, down_bias, cotangent,
):
    places = Places(lax.axis_size("dp"), lax.axis_size("seq"))
    seq_count, local_len, width = tokens.shape
    hidden_width = up_weight.shape[1]
    assert places.seq == 4 and seq_count == 2 and places.dp == 1 << places.bits
    d, z = lax.axis_index("dp"), lax.axis_index("seq")
    core = d % 2
    total_seqs = seq_count * places.dp
    total_tokens = total_seqs * local_len * places.seq

    def gathered(array):
        blocks = []
        for turn in range(2):
            mine = lax.dynamic_index_in_dim(array, (z + turn) % 2, 0, keepdims=False)
            blocks.append(send(mine, places.gather_order(turn)))
        return blocks

    count = 2 * local_len
    parts = hidden_width // width
    first_small = (ln1_gain, ln1_bias, q_bias, v_bias)
    second_small = (out_bias, ln2_gain, ln2_bias, down_bias, up_bias)
    sequence = (d - core + z // 2) * seq_count + z % 2
    if places.dp == 8:
        made = front(tokens, qkv_weight, time_table, timesteps, first_small, count / total_tokens)
        xs, (normed, query), kvs, info = made[:2], made[2:4], list(made[4:8]), made[8]
        cotangent, query = lax.optimization_barrier((cotangent, query))
        cots = gathered(cotangent)
    else:
        info = jnp.concatenate(
            [
                known_rows(
                    timesteps[j], seq_count * d + j, count / total_tokens,
                    lax.dynamic_slice_in_dim(time_table, timesteps[j], 1, 0).astype(F32),
                )
                for j in range(2)
            ]
        )
        far_info = send(info, places.swap(0))
        xs = gathered(tokens)
        cots = gathered(cotangent)
        info = jnp.where(z // 2 == core, info, far_info)
        info = jnp.pad(jnp.where(z % 2 == 0, info[:4], info[4:]), ((0, 4), (0, 0)))
        normed, query, kv0 = project(xs[0], info, first_small, qkv_weight, count)
        far0 = send(kv0, places.swap(0))
        normed, query, kv1 = project(xs[1], info, first_small, qkv_weight, count, (normed, query))
        kvs = [kv0, kv1, far0, send(kv1, places.swap(0))]
    context, logsum = attend(query, kvs)
    out, active, hidden_grad, normed_two, middle_grad, branch, context_grad, feed_sums = feed(
        context, xs, info, second_small, cots, out_weight, up_weight, down_weight
    )

    def scattered(blocks, dtype):
        back = [send(block, places.scatter_order(turn)) for turn, block in enumerate(blocks)]
        even = z % 2 == 0
        return jnp.stack(
            [jnp.where(even, back[0], back[1]), jnp.where(even, back[1], back[0])]
        ).astype(dtype)


    if places.dp == 8:
        made = back(
            query, context_grad, context, logsum, kvs, normed_two, hidden_grad, branch, active, cots,
            normed, out
        )
        tokens_grad, last_qkv, packed = tail(
            made[:3], normed, xs, middle_grad, qkv_weight, info, ln1_gain, feed_sums, total_tokens, parts
        )
        tokens_grad, layer_out, qkv_sum, up_sum, out_sum, down_sum, table_grad, *small = finish(
            tokens_grad, made[3], made[6], last_qkv, made[5], made[4][0], packed,
            time_table.shape[0] // places.dp, places.dp,
        )
    else:
        layer_out = scattered([out[:local_len], out[local_len:]], BF16)
        down_sum = reduce_parts(down_grad(active, cots)[None], places)[0]
        up_out_sum = reduce_parts(up_out_grad(normed_two, hidden_grad, context, branch), places)
        made = attend_back(query, context_grad, context, logsum, kvs)
        token0, token1, projected_grad, start_sums = start_back(
            made[0],
            list(made[1:3]) + [send(g, places.swap(0)) for g in made[3:5]],
            list(made[5:7]) + [send(g, places.swap(0)) for g in made[7:9]],
            xs, info, middle_grad, ln1_gain, qkv_weight,
        )
        tokens_grad = scattered([token0, token1], F32)
        qkv_sum = reduce_parts(qkv_grad(normed, projected_grad), places)
        energy = jnp.sum(feed_sums[4]) / (width * total_tokens)
        sequence_rows = jnp.where(jnp.arange(total_seqs)[:, None] == sequence, start_sums[4][None], 0.0)
        packed = jnp.concatenate(
            [
                feed_sums[0:4], feed_sums[8 : 8 + parts], start_sums[0:4],
                jnp.stack(
                    [info[MARK] * energy + info[SHARE], info[STEP] * jnp.where(core == 0, 1.0, 0.0)]
                ),
                sequence_rows,
            ]
        )
        packed = sum_everywhere(packed, places)
        steps = packed[9 + parts, :total_seqs].astype(jnp.int32)
        table_rows = time_table.shape[0] // places.dp
        chosen = (steps[None, :] == (jnp.arange(table_rows) + d * table_rows)[:, None]).astype(F32)
        table_grad = jnp.dot(chosen, packed[10 + parts :], precision=lax.Precision.HIGHEST)

        def side_by_side(stacked):
            return jnp.moveaxis(stacked, 0, 1).reshape(stacked.shape[1], -1)

        qkv_sum, out_sum = side_by_side(qkv_sum), up_out_sum[parts]
        up_sum = side_by_side(up_out_sum[:parts])
        piece = width // places.dp
        mine = lax.dynamic_slice_in_dim(packed[: 8 + parts], d * piece, piece, 1)
        up_piece = hidden_width // places.dp
        up_bias_sum = lax.dynamic_slice_in_dim(packed[4 : 4 + parts].reshape(-1), d * up_piece, up_piece, 0)
        stats = packed[8 + parts]
        small = [mine[row] for row in (0, 1, 2, 3, 4 + parts, 5 + parts, 6 + parts, 7 + parts)]
        small += [up_bias_sum, stats[:BUCKETS], stats[BUCKETS : 2 * BUCKETS]]
    down_bias_sum, gain_two, shift_two, out_bias_sum, gain_one, shift_one, q_sum, v_sum = small[:8]
    return (
        layer_out, tokens_grad, table_grad, gain_one, shift_one, qkv_sum, q_sum, v_sum, out_sum, out_bias_sum,
        gain_two, shift_two, up_sum, small[8], down_sum, down_bias_sum, small[9], small[10],
    )


def solution(mesh):
    split = P("dp", "seq", None)
    return jax.shard_map(
        per_device,
        mesh=mesh,
        in_specs=(split, P("dp")) + (P(),) * 14 + (split,),
        out_specs=(
            split, split, P("dp", None), P("dp"), P("dp"), P("dp", None), P("dp"), P("dp"), P("dp", None),
            P("dp"), P("dp"), P("dp"), P("dp", None), P("dp"), P("dp", None), P("dp"), P(), P(),
        ),
        check_vma=False,
    )
```

```python
import functools

import jax
import jax.numpy as jnp
from jax import lax
from jax.experimental import pallas as pl
from jax.experimental.pallas import tpu as pltpu
from jax.sharding import PartitionSpec as P

HEAD_DIM = 64
TSTEPS = 2048
BUCKETS = 4
EPS = 1e-05
LANES = 128
VMEM_BYTES = 60 * 1024 * 1024
BOTH = ("dp", "seq")
TOKEN_PARTS = 8
F32 = jnp.float32
BF16 = jnp.bfloat16
NN = (((1,), (0,)), ((), ()))
NT = (((1,), (1,)), ((), ()))
TN = (((0,), (0,)), ((), ()))


def dot(a, b, dims):
    return lax.dot_general(a, b, dims, preferred_element_type=F32)


def wide(ref):
    return ref[...].astype(F32)


def column_sum(v):
    return jnp.sum(v, 0, keepdims=True)


def fixed(shape):
    return pl.BlockSpec(shape, lambda *i: (0,) * len(shape), pipeline_mode=pl.Buffered(1))


def rows(block, width):
    return pl.BlockSpec((block, width), lambda i: (i, 0))


def shape_of(shape, dtype=BF16):
    return jax.ShapeDtypeStruct(shape, dtype)


def cost(us):
    return pl.CostEstimate(flops=int(us * 1.15e9), bytes_accessed=0, transcendentals=0)


def params():
    return pltpu.CompilerParams(vmem_limit_bytes=VMEM_BYTES)


def norm_parts(v):
    centered = v - jnp.mean(v, -1, keepdims=True)
    scale = lax.rsqrt(jnp.mean(centered * centered, -1, keepdims=True) + EPS)
    return centered * scale, scale


def norm_backward(grad, gain, unit, scale):
    scaled = grad * gain
    return scale * (
        scaled
        - jnp.mean(scaled, -1, keepdims=True)
        - unit * jnp.mean(scaled * unit, -1, keepdims=True)
    )


TIME, MARK, SHARE, STEP = range(4)


def one_row(ref, at):
    return ref[at : at + 1].astype(F32)


def vector(ref):
    return ref[...].astype(F32).reshape(1, -1)


def whole_vector(v):
    return pl.BlockSpec(v.shape, lambda *i: (0,), pipeline_mode=pl.Buffered(1))


def known_rows(step, sequence, share, time_row):
    lane = lax.broadcasted_iota(jnp.int32, time_row.shape, 1)
    bucket = step * BUCKETS // TSTEPS
    return jnp.concatenate(
        [
            time_row,
            jnp.where(lane == bucket, 1.0, 0.0),
            jnp.where(lane == BUCKETS + bucket, share, 0.0),
            jnp.where(lane == sequence, step.astype(F32), 0.0),
        ],
        0,
    )


def project_rows(x, info_ref, small, weight_ref):
    width = x.shape[1]
    gain, shift, query_bias, value_bias = small
    unit, _ = norm_parts(x.astype(F32) + one_row(info_ref, TIME))
    normed = (unit * vector(gain) + vector(shift)).astype(BF16)

    def part(number):
        made = dot(normed, weight_ref[:, number * width : (number + 1) * width], NN)
        if number != 1:
            made = made + vector(query_bias if number == 0 else value_bias)
        made = made.astype(BF16)
        return made * jnp.asarray(HEAD_DIM ** (-0.5), BF16) if number == 0 else made

    return normed, part


def project_kernel(x_ref, info_ref, weight_ref, *refs):
    normed_ref, query_ref, kv_ref = refs[-3:]
    width = x_ref.shape[1]
    normed, part = project_rows(x_ref[...], info_ref, refs[:4], weight_ref)
    normed_ref[...] = normed
    query_ref[...] = part(0)
    kv_ref[:, :width] = part(1)
    kv_ref[:, width:] = part(2)


def project(x, info, small, weight, total, begun=None, block=256):
    count, width = x.shape
    first = 0 if begun is None else total // block - count // block
    later = pl.BlockSpec((block, width), lambda i: (i + first, 0))
    extra = [] if begun is None else list(begun)
    return pl.pallas_call(
        project_kernel,
        grid=(count // block,),
        in_specs=[rows(block, width), fixed(info.shape), fixed(weight.shape)]
        + [whole_vector(v) for v in small]
        + [pl.BlockSpec(memory_space=pl.ANY)] * len(extra),
        out_specs=[later, later, rows(block, 2 * width)],
        out_shape=[
            shape_of((total, width)),
            shape_of((total, width)),
            shape_of((count, 2 * width)),
        ],
        input_output_aliases={7: 0, 8: 1} if extra else {},
        compiler_params=params(),
        cost_estimate=cost(5),
        name="project",
    )(x, info, weight, *small, *extra)


def lane_parts():
    lane = lax.broadcasted_iota(jnp.int32, (1, LANES), 1)
    return lane < HEAD_DIM, lane % HEAD_DIM


def with_offset(own, place, base, offset):
    high = offset.astype(BF16)
    left = offset - high.astype(F32)
    mid = left.astype(BF16)
    low = (left - mid.astype(F32)).astype(BF16)
    zero = jnp.zeros_like(low)
    parts = jnp.where(place == 0, high, jnp.where(place == 1, mid, jnp.where(place == 2, low, zero)))
    return jnp.where(own, base, parts)


def attend_kernel(query_ref, *refs, pieces):
    key_refs, value_refs = refs[:pieces], refs[pieces : 2 * pieces]
    context_ref, logsum_ref = refs[2 * pieces :]
    count = query_ref.shape[0]
    low, place = lane_parts()
    row_half = lax.broadcasted_iota(jnp.int32, (LANES, LANES), 0) // HEAD_DIM
    lane_half = lax.broadcasted_iota(jnp.int32, (LANES, LANES), 1) // HEAD_DIM
    swapped = jnp.where(row_half != lane_half, 1.0, 0.0).astype(BF16)
    query = query_ref[...]

    def norms(v):
        v = v.astype(F32)
        return dot((v * v).astype(BF16), swapped, NN)

    key_norm = functools.reduce(
        jnp.maximum, [jnp.max(norms(ref[...]), 0, keepdims=True) for ref in key_refs]
    )
    bound = jnp.sqrt(norms(query) * key_norm) * 1.01
    ones_key = jnp.where(place < 3, 1.0, 0.0).astype(BF16)
    values = [ref[...].T for ref in value_refs]
    ones = jnp.ones((16, value_refs[0].shape[0]), BF16)

    def value_of(piece, head):
        return jnp.concatenate([values[piece][head * HEAD_DIM : (head + 1) * HEAD_DIM], ones], 0)

    def finish(mixed, offset):
        totals = [m[HEAD_DIM : HEAD_DIM + 1] for m in mixed]
        context = jnp.concatenate([m[:HEAD_DIM] / t for m, t in zip(mixed, totals)], 0)
        context_ref[...] = context.T.astype(BF16)
        logs = [jnp.broadcast_to(jnp.log(t), (HEAD_DIM, count)) for t in reversed(totals)]
        logsum_ref[...] = jnp.concatenate(logs, 0).T + offset

    mixed = []
    for head in range(2):
        own = low if head == 0 else ~low
        query_own = with_offset(own, place, query, -bound)
        out = 0.0
        for piece in range(pieces):
            key_own = jnp.where(own, key_refs[piece][...], ones_key)
            weights = jnp.exp(dot(key_own, query_own, NT)).astype(BF16)
            out = out + dot(value_of(piece, head), weights, NN)
        mixed.append(out)
    finish(mixed, bound)
    smallest = jnp.min(jnp.minimum(mixed[0][HEAD_DIM], mixed[1][HEAD_DIM]))

    @pl.when(smallest < 1e-25)
    def _():
        again, tops = [], []
        for head in range(2):
            own = low if head == 0 else ~low
            query_own = jnp.where(own, query, jnp.zeros_like(query))
            top = jnp.full((1, count), -jnp.inf, F32)
            for piece in range(pieces):
                scores = dot(key_refs[piece][...], query_own, NT)
                top = jnp.maximum(top, jnp.max(scores, 0, keepdims=True))
            out = 0.0
            for piece in range(pieces):
                scores = dot(key_refs[piece][...], query_own, NT)
                out = out + dot(value_of(piece, head), jnp.exp(scores - top).astype(BF16), NN)
            again.append(out)
            tops.append(jnp.broadcast_to(top, (HEAD_DIM, count)))
        finish(again, jnp.concatenate(tops[::-1], 0).T)


def attend(query, kvs):
    count, width = query.shape
    pairs, pieces, length = width // LANES, len(kvs), kvs[0].shape[0]
    row = pl.BlockSpec((count, LANES), lambda p: (0, p))
    return pl.pallas_call(
        functools.partial(attend_kernel, pieces=pieces),
        grid=(pairs,),
        in_specs=[row]
        + [pl.BlockSpec((length, LANES), lambda p: (0, p))] * pieces
        + [pl.BlockSpec((length, LANES), lambda p: (0, pairs + p))] * pieces,
        out_specs=[row, row],
        out_shape=[shape_of((count, width)), shape_of((count, width), F32)],
        compiler_params=params(),
        cost_estimate=cost(32),
        name="attend",
    )(query, *kvs, *kvs)


def attend_back_step(query_ref, grad_ref, context_ref, logsum_ref, pieces, query_grad_ref):
    low, place = lane_parts()
    query, grad = query_ref[...], grad_ref[...]
    count = query.shape[0]
    product = grad.astype(F32) * wide(context_ref)
    logsum = logsum_ref[...]
    ones_key = jnp.where(place < 3, 1.0, 0.0).astype(BF16)
    zero = jnp.zeros_like(query)
    heads = []
    for head in range(2):
        own = low if head == 0 else ~low
        inner = jnp.sum(jnp.where(own, product, 0.0), -1, keepdims=True)
        heads.append(
            (
                own,
                with_offset(own, place, query, -logsum),
                with_offset(own, place, grad, jnp.broadcast_to(-inner, logsum.shape)),
                jnp.where(own, query, zero),
                jnp.where(own, grad, zero),
            )
        )
    length = sum(piece[0].shape[0] for piece in pieces)
    query_grads = [0.0, 0.0]
    key_mean = 0.0
    for key_ref, value_ref, key_grad_ref, value_grad_ref, before in pieces:
        if before is not None:
            before()
        key, value = key_ref[...], value_ref[...]
        key_turned = key.T
        key_mean = key_mean + jnp.sum(key_turned.astype(F32), 1, keepdims=True) / length
        ones = jnp.ones((16, key.shape[0]), BF16)
        key_grad, value_grad = 0.0, 0.0
        for head, (own, query_off, grad_off, query_own, grad_own) in enumerate(heads):
            scores = dot(jnp.where(own, key, ones_key), query_off, NT)
            probs = jnp.exp(scores)
            prob_grad = dot(jnp.where(own, value, ones_key), grad_off, NT)
            score_grad = (probs * prob_grad).astype(BF16)
            value_grad = value_grad + dot(probs.astype(BF16), grad_own, NN)
            key_grad = key_grad + dot(score_grad, query_own, NN)
            lanes = slice(head * HEAD_DIM, (head + 1) * HEAD_DIM)
            turned = jnp.concatenate([key_turned[lanes], ones], 0)
            query_grads[head] = query_grads[head] + dot(turned, score_grad, NN)
        key_grad_ref[...] = key_grad.astype(BF16)
        value_grad_ref[...] = value_grad.astype(BF16)
    parts = [
        made[:HEAD_DIM]
        - key_mean[head * HEAD_DIM : (head + 1) * HEAD_DIM]
        * jnp.broadcast_to(made[HEAD_DIM : HEAD_DIM + 1], (HEAD_DIM, count))
        for head, made in enumerate(query_grads)
    ]
    query_grad_ref[...] = (jnp.concatenate(parts, 0) * HEAD_DIM ** (-0.5)).T.astype(BF16)


def attend_back_kernel(query_ref, grad_ref, context_ref, logsum_ref, *refs, pieces):
    key_refs, value_refs = refs[:pieces], refs[pieces : 2 * pieces]
    query_grad_ref = refs[2 * pieces]
    key_grad_refs = refs[2 * pieces + 1 : 3 * pieces + 1]
    value_grad_refs = refs[3 * pieces + 1 :]
    steps = list(zip(key_refs, value_refs, key_grad_refs, value_grad_refs, [None] * pieces))
    attend_back_step(query_ref, grad_ref, context_ref, logsum_ref, steps, query_grad_ref)


def attend_back(query, grad, context, logsum, kvs):
    count, width = query.shape
    pairs, pieces, length = width // LANES, len(kvs), kvs[0].shape[0]
    row = pl.BlockSpec((count, LANES), lambda p: (0, p))
    piece = pl.BlockSpec((length, LANES), lambda p: (0, p))
    return pl.pallas_call(
        functools.partial(attend_back_kernel, pieces=pieces),
        grid=(pairs,),
        in_specs=[row] * 4
        + [piece] * pieces
        + [pl.BlockSpec((length, LANES), lambda p: (0, pairs + p))] * pieces,
        out_specs=[row] + [piece] * (2 * pieces),
        out_shape=[shape_of((count, width))] + [shape_of((length, width))] * (2 * pieces),
        compiler_params=params(),
        cost_estimate=cost(75),
        name="attend_back",
    )(query, grad, context, logsum, *kvs, *kvs)


def here():
    d, z = lax.axis_index("dp"), lax.axis_index("seq")
    return d, z, d // 4, (d // 2) % 2, d % 2


def partners():
    d, z, y, x, core = here()
    return {
        "core": (d + 1 - 2 * core, z),
        "x": (d + 2 - 4 * x, z),
        "y": (d + 4 - 8 * y, z),
        "near": (d, z + 1 - 2 * (z % 2)),
        "inner": (d, 3 - z),
    }


def outer():
    z = lax.axis_index("seq")
    return (z == 0) | (z == 3)


def remote(source, target, sends, receives, send_index, receive_index, device):
    return pltpu.make_async_remote_copy(
        src_ref=source,
        dst_ref=target,
        send_sem=sends.at[send_index],
        recv_sem=receives.at[receive_index],
        device_id=device,
        device_id_type=pl.DeviceIdType.MESH,
    )


class Reduction:
    def __init__(self, source, out, scratch):
        self.source, self.out = source, out
        self.own = source.at[:, :, :, here()[4]]
        self.from_core, self.first, self.second, self.near, self.far = scratch[:5]
        self.sends, self.receives, self.local = scratch[5:8]
        self.parts, _, _, self.rows, self.width = self.from_core.shape
        self.half = self.width // 2

    @staticmethod
    def scratch(parts, block, width):
        half = width // 2
        return [
            pltpu.VMEM((parts, 2, 2, block, width), BF16),
            pltpu.VMEM((2, parts, 2, block, half), BF16),
            pltpu.VMEM((2, parts, block, half), BF16),
            pltpu.VMEM((parts, block, width), BF16),
            pltpu.VMEM((parts, block, width), BF16),
            pltpu.SemaphoreType.DMA((8,)),
            pltpu.SemaphoreType.DMA((8,)),
            pltpu.SemaphoreType.DMA((1,)),
        ]

    def copy(self, number):
        d, z, y, x, core = here()
        to = partners()
        left, right = pl.ds(0, self.half), pl.ds(self.half, self.half)
        source, target, device = (
            lambda: (self.source.at[:, :, :, 1 - core], self.from_core, to["core"]),
            lambda: (self.own.at[:, :, 1 - x, :, left], self.first.at[0], to["x"]),
            lambda: (self.own.at[:, 1 - y, :, :, right], self.first.at[1], to["y"]),
            lambda: (self.own.at[:, 1 - y, x, :, left], self.second.at[0], to["y"]),
            lambda: (self.own.at[:, y, 1 - x, :, right], self.second.at[1], to["x"]),
            lambda: (self.own.at[:, y, x], self.near, to["near"]),
            lambda: (self.own.at[:, y, x], self.far, to["inner"]),
            lambda: (self.own.at[:, y, x], self.near, to["near"]),
        )[number]()
        return remote(source, target, self.sends, self.receives, number, number, device)

    def to_cores(self):
        self.copy(0).start()

    def to_first(self):
        self.copy(0).wait()
        for part in range(self.parts):
            for i in range(2):
                for j in range(2):
                    self.own[part, i, j] = self.own[part, i, j] + self.from_core[part, i, j]
        self.copy(1).start()
        self.copy(2).start()

    def to_second(self):
        _, _, y, x, _ = here()
        self.copy(1).wait()
        self.copy(2).wait()
        left, right = slice(0, self.half), slice(self.half, self.width)
        for part in range(self.parts):
            for i in range(2):
                self.own[part, i, x, :, left] = self.own[part, i, x, :, left] + self.first[0, part, i]
                self.own[part, y, i, :, right] = self.own[part, y, i, :, right] + self.first[1, part, i]
        self.copy(3).start()
        self.copy(4).start()

    def to_near(self):
        _, _, y, x, _ = here()
        self.copy(3).wait()
        self.copy(4).wait()
        left, right = slice(0, self.half), slice(self.half, self.width)
        for part in range(self.parts):
            self.own[part, y, x, :, left] = self.own[part, y, x, :, left] + self.second[0, part]
            self.own[part, y, x, :, right] = self.own[part, y, x, :, right] + self.second[1, part]

        @pl.when(outer())
        def _():
            self.copy(5).start()

    def add_whole(self, received):
        _, _, y, x, _ = here()
        for part in range(self.parts):
            self.own[part, y, x] = self.own[part, y, x] + received[part]

    def to_far(self):
        @pl.when(jnp.logical_not(outer()))
        def _():
            self.copy(5).wait_recv()
            self.add_whole(self.near)
            self.copy(6).start()

    def to_other(self):
        @pl.when(jnp.logical_not(outer()))
        def _():
            self.copy(6).wait()
            self.add_whole(self.far)
            self.copy(7).start()

    def to_out(self):
        _, _, y, x, _ = here()

        @pl.when(outer())
        def _():
            self.copy(5).wait_send()
            self.copy(7).wait_recv()
            pltpu.make_async_copy(self.near, self.out, self.local.at[0]).start()

        @pl.when(jnp.logical_not(outer()))
        def _():
            pltpu.make_async_copy(self.own.at[:, y, x], self.out, self.local.at[0]).start()

    def finish(self):
        _, _, y, x, _ = here()

        @pl.when(outer())
        def _():
            pltpu.make_async_copy(self.near, self.out, self.local.at[0]).wait()

        @pl.when(jnp.logical_not(outer()))
        def _():
            self.copy(7).wait_send()
            pltpu.make_async_copy(self.own.at[:, y, x], self.out, self.local.at[0]).wait()


class Trade:
    def __init__(self, out, sends, receives, local, gather=False, parts=1):
        self.out, self.sends, self.receives, self.local = out, sends, receives, local
        self.gather, self.parts = gather, parts

    @staticmethod
    def semaphores(parts=1):
        return [pltpu.SemaphoreType.DMA((2, parts)), pltpu.SemaphoreType.DMA((2, parts)), pltpu.SemaphoreType.DMA((parts,))]

    def device(self, p):
        d, z, _, _, core = here()
        return (d - core + z // 2, 2 * core + (z + p) % 2)

    def stays(self):
        _, z, _, _, core = here()
        return z // 2 == core

    def slot(self, p):
        return p if self.gather else lax.axis_index("seq") % 2

    def own_slot(self, p):
        return p if self.gather else (lax.axis_index("seq") + p) % 2

    def greet(self, barrier):
        @pl.when(jnp.logical_not(self.stays()))
        def _():
            pl.semaphore_signal(barrier, inc=1, device_id=self.device(0), device_id_type=pl.DeviceIdType.MESH)

        pl.semaphore_signal(barrier, inc=1, device_id=self.device(1), device_id_type=pl.DeviceIdType.MESH)
        return jnp.where(self.stays(), 1, 2)

    def rows(self, ref, part):
        many = ref.shape[0] // self.parts
        return ref.at[pl.ds(part * many, many)]

    def keep(self, block, part):
        return pltpu.make_async_copy(
            self.rows(block, part), self.rows(self.out.at[self.own_slot(0)], part), self.local.at[part]
        )

    def copy(self, p, block, part):
        slot = self.slot(p)
        return pltpu.make_async_remote_copy(
            src_ref=self.rows(block, part),
            dst_ref=self.rows(self.out.at[slot], part),
            send_sem=self.sends.at[p, part],
            recv_sem=self.receives.at[slot, part],
            device_id=self.device(p),
            device_id_type=pl.DeviceIdType.MESH,
        )

    def each(self, p, far, near):
        if p == 1:
            far()
            return
        pl.when(jnp.logical_not(self.stays()))(far)
        pl.when(self.stays())(near)

    def begin(self, p, block, part=0):
        self.each(p, lambda: self.copy(p, block, part).start(), lambda: self.keep(block, part).start())

    def sent(self, p, block, part=0):
        self.each(p, lambda: self.copy(p, block, part).wait_send(), lambda: None)

    def arrived(self, p, block, part=0):
        slot = self.own_slot(p)
        target = self.rows(self.out.at[slot], part)

        def far():
            pltpu.make_async_remote_copy(
                src_ref=target,
                dst_ref=target,
                send_sem=self.sends.at[p, part],
                recv_sem=self.receives.at[slot, part],
                device_id=self.device(p),
                device_id_type=pl.DeviceIdType.MESH,
            ).wait_recv()

        self.each(p, far, lambda: self.keep(block, part).wait())


def meet(names, *trades):
    barrier = pltpu.get_barrier_semaphore()
    to = partners()
    for name in names:
        pl.semaphore_signal(barrier, inc=1, device_id=to[name], device_id_type=pl.DeviceIdType.MESH)
    expected = len(names)
    for one in trades:
        expected = expected + one.greet(barrier)
    pl.semaphore_wait(barrier, expected)


def front_kernel(
    tokens, weight, table, steps_ref, gain, shift, query_bias, value_bias,
    x0_out, x1_out, normed_out, query_out, near0_out, near1_out, far0_out, far1_out, info_out,
    x_v, weight_v, table_v, info_here, info_in, normed_v, query_v, near_v, far_v,
    load, stores, info_sends, info_receives, sends, receives, *trade, share,
):
    d, z, _, _, core = here()
    block, width = x_v.shape[1:]
    small = (gain, shift, query_bias, value_bias)
    trade = Trade(x_v, *trade, gather=True, parts=2)
    loaded = pltpu.make_async_copy(weight, weight_v, load.at[0])
    looked_up = pltpu.make_async_copy(table, table_v, load.at[1])
    meet(("core",), trade)
    held = [tokens.at[(z + p) % 2] for p in range(2)]
    pieces = [(p, part) for p in range(2) for part in range(2)]
    many = block // 2
    for p, part in pieces:
        trade.begin(p, held[p], part)
    looked_up.start()
    loaded.start()
    steps = [steps_ref[j] for j in range(2)]
    row = lax.broadcasted_iota(jnp.int32, (16, table.shape[0]), 0)
    place = lax.broadcasted_iota(jnp.int32, (16, table.shape[0]), 1)
    wanted = jnp.where(row == 0, steps[0], jnp.where(row == 1, steps[1], -1))
    chosen = jnp.where(place == wanted, 1.0, 0.0).astype(BF16)
    looked_up.wait()
    time_rows = dot(chosen, table_v[...], NN)
    for j in range(2):
        info_here[4 * j : 4 * j + 4] = known_rows(steps[j], 2 * d + j, share, time_rows[j : j + 1])
    known = remote(info_here, info_in, info_sends, info_receives, 0, 0, partners()["core"])
    known.start()
    known.wait()
    mine = jnp.where(z // 2 == core, info_here[...], info_in[...])
    info_out[0:4] = jnp.where(z % 2 == 0, mine[0:4], mine[4:8])
    info_out[4:8] = jnp.zeros_like(info_in[4:8])
    loaded.wait()
    copies, moved = [], []
    for number, (p, part) in enumerate(pieces):
        trade.arrived(p, held[p], part)
        inner = pl.ds(part * many, many)
        normed, made = project_rows(x_v[p, inner], info_out, small, weight_v)
        near_v[p, inner, :width] = made(1)
        near_v[p, inner, width:] = made(2)
        moved.append(
            remote(near_v.at[p, inner], far_v.at[p, inner], sends, receives, number, number, partners()["core"])
        )
        moved[number].start()
        normed_v[p, inner] = normed
        query_v[p, inner] = made(0)
        whole = pl.ds(number * many, many)
        for at, (source, target) in enumerate(
            (
                (x_v.at[p, inner], (x0_out, x1_out)[p].at[inner]), (normed_v.at[p, inner], normed_out.at[whole]),
                (query_v.at[p, inner], query_out.at[whole]), (near_v.at[p, inner], (near0_out, near1_out)[p].at[inner]),
            )
        ):
            copies.append(pltpu.make_async_copy(source, target, stores.at[number, at]))
            copies[-1].start()
    for number, (p, part) in enumerate(pieces):
        inner = pl.ds(part * many, many)
        moved[number].wait()
        copies.append(
            pltpu.make_async_copy(far_v.at[p, inner], (far0_out, far1_out)[p].at[inner], stores.at[number, 4])
        )
        copies[-1].start()
    for p, part in pieces:
        trade.sent(p, held[p], part)
    for copy in copies:
        copy.wait()


def front(tokens, weight, table, steps, small, share):
    _, block, width = tokens.shape
    info_shape = (8, width)
    any_spec = pl.BlockSpec(memory_space=pl.ANY)
    inside = pl.BlockSpec(memory_space=pltpu.VMEM)
    pair = pltpu.VMEM((2, block, width), BF16)
    wide_pair = pltpu.VMEM((2, block, 2 * width), BF16)
    one = pltpu.SemaphoreType.DMA((1,))
    two, four = pltpu.SemaphoreType.DMA((2,)), pltpu.SemaphoreType.DMA((4,))
    return pl.pallas_call(
        functools.partial(front_kernel, share=share),
        in_specs=[any_spec] * 3 + [pl.BlockSpec(memory_space=pltpu.SMEM)] + [inside] * 4,
        out_specs=[any_spec] * 8 + [inside],
        out_shape=[shape_of((block, width))] * 2
        + [shape_of((2 * block, width))] * 2
        + [shape_of((block, 2 * width))] * 4
        + [shape_of(info_shape, F32)],
        scratch_shapes=[
            pair, pltpu.VMEM(weight.shape, BF16), pltpu.VMEM(table.shape, BF16), pltpu.VMEM(info_shape, F32),
            pltpu.VMEM(info_shape, F32), pair, pair, wide_pair, wide_pair,
            two, pltpu.SemaphoreType.DMA((4, 5)), one, one, four, four,
        ]
        + Trade.semaphores(2),
        compiler_params=pltpu.CompilerParams(
            vmem_limit_bytes=VMEM_BYTES, collective_id=2, has_side_effects=True
        ),
        cost_estimate=cost(48),
        name="front",
    )(tokens, weight, table, steps, *small)


def fixed_any():
    return pl.BlockSpec(memory_space=pl.ANY)


def back_kernel(
    query_ref, grad_ref, context_ref, logsum_ref, *refs, pieces, parts, pairs
):
    key_refs, value_refs = refs[:pieces], refs[pieces : 2 * pieces]
    refs = refs[2 * pieces :]
    normed_ref, hidden_grad_ref, whole_context, branch, active_ref, cot0, cot1 = refs[:7]
    first_normed, layer_ref, query_grad_ref, key_out, value_out, layer_out, down_out, up_out, qkv_out = refs[7:16]
    refs = refs[16:]
    near = pieces // 2
    down_parts, up_parts = refs[:2]
    chunks = []
    for number, (which, at, many) in enumerate(back_chunks(down_parts.shape, up_parts.shape)):
        scratch = refs[2 + 8 * number : 10 + 8 * number]
        if which == "down":
            here_rows = pl.ds(at, many)
            chunks.append(
                Reduction(down_parts.at[:, :, :, :, here_rows], down_out.at[:, here_rows], scratch)
            )
        else:
            here_parts = pl.ds(at, many)
            chunks.append(Reduction(up_parts.at[here_parts], up_out.at[here_parts], scratch))
    qkv_parts = refs[34]
    for group in range(2):
        lanes = pl.ds(2 * group * LANES, 2 * LANES)
        scratch = refs[35 + 8 * group : 43 + 8 * group]
        chunks.append(Reduction(qkv_parts.at[group], qkv_out.at[:, :, lanes], scratch))
    one, two, three, four, five, six = chunks
    query_held, near_grads, far_grads, far_in, far_sends, far_receives = refs[51:57]
    whole_context_ref, branch_ref, cots_ref, first_normed_ref, loads = refs[57:62]
    back = Trade(layer_out, *refs[62:])
    block = key_refs[0].shape[0]
    layer_blocks = [layer_ref.at[pl.ds(p * block, block)] for p in range(2)]
    step = pl.program_id(0)
    made = 2 * parts + 1
    pair, last = step - made, pl.num_programs(0) - 1

    def far_copy(which):
        return remote(
            far_grads, far_in.at[which % 2], far_sends, far_receives, 0, which, partners()["core"]
        )

    loaded = [
        pltpu.make_async_copy(source, target, loads.at[number])
        for number, (source, target) in enumerate(
            (
                (whole_context, whole_context_ref), (branch, branch_ref), (cot0, cots_ref.at[pl.ds(0, block)]),
                (cot1, cots_ref.at[pl.ds(block, block)]), (first_normed, first_normed_ref),
            )
        )
    ]

    def begin():
        for copy in loaded:
            copy.start()
        meet(("core", "x", "y", "near", "inner"), back)
        back.begin(0, layer_blocks[0])
        back.begin(1, layer_blocks[1])

    def settle():
        which = pair - 1
        slot = which % 2
        far_copy(which).wait()
        key_grad = near_grads[slot, 0] + far_in[slot, 0]
        value_grad = near_grads[slot, 1] + far_in[slot, 1]
        key_out[...] = key_grad
        value_out[...] = value_grad

        @pl.when(which < 4)
        def _():
            grads = jnp.concatenate([query_held[slot], key_grad, value_grad], 1)
            product = dot(first_normed_ref[...], grads, TN).astype(BF16)
            lanes = pl.ds(pl.multiple_of(slot * LANES, LANES), LANES)
            for part in range(3):
                block_of = product[:, part * LANES : (part + 1) * LANES]
                qkv_parts[which // 2, part, :, :, :, :, lanes] = block_of.reshape(qkv_parts.shape[2:6] + (LANES,))

    plan = {
        (0, 0): [begin],
        (2, 0): [one.to_cores],
        (4, 0): [one.to_first],
        (5, 0): [two.to_cores],
        (8, 0): [two.to_first],
        (9, 0): [three.to_cores, one.to_second],
        (9, 1): [four.to_cores],
        (10, 0): [three.to_first, one.to_near],
        (10, 1): [two.to_second],
        (10, 2): [four.to_first],
        (10, 3): [one.to_far],
        (11, 0): [five.to_cores],
        (11, 1): [two.to_near],
        (11, 2): [three.to_second, one.to_other],
        (11, 3): [five.to_first, four.to_second],
        (12, 0): [two.to_far],
        (12, 1): [three.to_near],
        (12, 2): [five.to_second, four.to_near],
        (13, 0): [six.to_cores, five.to_near, three.to_far, two.to_other],
        (13, 1): [six.to_first, four.to_far, five.to_far],
        (13, 2): [three.to_other],
        (13, 3): [six.to_second],
        (14, 0): [four.to_other, five.to_other],
        (14, 1): [six.to_near, one.to_out],
        (14, 2): [six.to_far],
        (14, 3): [six.to_other],
        (15, 0): [two.to_out, three.to_out, four.to_out, five.to_out, six.to_out],
    }

    def run_plan(place, steps):
        for (at, where), actions in plan.items():
            if where == place and at in steps:

                @pl.when(step == at)
                def _():
                    for action in actions:
                        action()

    run_plan(0, range(made))

    @pl.when(step < parts)
    def _():
        part = dot(normed_ref[...], hidden_grad_ref[...], TN).astype(BF16)
        up_parts[step] = part.reshape(up_parts.shape[1:])

    @pl.when(step == parts)
    def _():
        for copy in loaded:
            copy.wait()
        part = dot(whole_context_ref[...], branch_ref[...], TN).astype(BF16)
        up_parts[parts] = part.reshape(up_parts.shape[1:])

    @pl.when((step > parts) & (step < made))
    def _():
        part = dot(active_ref[...], cots_ref[...], TN).astype(BF16).reshape(down_parts.shape[3:])
        at = step - parts - 1
        down_parts[0, at // 2, at % 2] = part

    def before(place):
        def run():
            run_plan(place, range(made, made + pairs))
            if place == near:
                far_copy(pair).start()

        return run

    pl.when(pair >= 1)(settle)

    @pl.when((step >= made) & (pair < pairs))
    def _():
        order = []
        slot = pair % 2
        for i in range(near):
            far_rows = pl.ds(i * block, block)
            order.append(
                (key_refs[near + i], value_refs[near + i], far_grads.at[0, far_rows], far_grads.at[1, far_rows])
            )
        for i in range(near):
            near_rows = pl.ds(i * block, block)
            order.append(
                (key_refs[i], value_refs[i], near_grads.at[slot, 0, near_rows], near_grads.at[slot, 1, near_rows])
            )
        steps = [one_piece + (before(place),) for place, one_piece in enumerate(order)]
        attend_back_step(query_ref, grad_ref, context_ref, logsum_ref, steps, query_grad_ref)
        query_held[slot] = query_grad_ref[...]

    @pl.when(step == last)
    def _():
        run_plan(0, [made + pairs])
        for p in range(2):
            back.sent(p, layer_blocks[p])
            back.arrived(p, layer_blocks[p])
        for chunk in chunks:
            chunk.finish()


def back_chunks(down_shape, up_shape):
    block, parts = down_shape[-2], up_shape[0]
    return [
        ("up", 0, parts // 2),
        ("up", parts // 2, parts - parts // 2),
        ("down", 0, block // 2),
        ("down", block // 2, block // 2),
    ]


def back(query, grad, context, logsum, kvs, normed, hidden_grad, branch, active, cots, first_normed, layer_out):
    count, width = query.shape
    pairs, pieces, length = width // LANES, len(kvs), kvs[0].shape[0]
    near = pieces // 2
    parts = hidden_grad.shape[1] // width
    made = 2 * parts + 1
    pair = lambda i: jnp.clip(i - made, 0, pairs - 1)
    row = pl.BlockSpec((count, LANES), lambda i: (0, pair(i)))
    settled = pl.BlockSpec((count, LANES), lambda i: (0, jnp.clip(i - made - 1, 0, pairs - 1)))
    piece = pl.BlockSpec((length, LANES), lambda i: (0, pair(i)))
    value = pl.BlockSpec((length, LANES), lambda i: (0, pairs + pair(i)))
    whole = fixed((count, width))
    up_rows, down_rows = width // 8, hidden_grad.shape[1] // 8
    down_shape, up_shape = (1, 2, 2, 2, down_rows, width), (parts + 1, 2, 2, 2, up_rows, width)
    return pl.pallas_call(
        functools.partial(back_kernel, pieces=pieces, parts=parts, pairs=pairs),
        grid=(made + pairs + 1,),
        in_specs=[row] * 4
        + [piece] * pieces
        + [value] * pieces
        + [
            whole,
            pl.BlockSpec((count, width), lambda i: (0, jnp.minimum(i, parts - 1))),
            fixed_any(),
            fixed_any(),
            pl.BlockSpec((count, width), lambda i: (0, jnp.clip(i - parts - 1, 0, parts - 1))),
        ]
        + [fixed_any()] * 4,
        out_specs=[row, settled, settled] + [fixed_any()] * 4,
        out_shape=[shape_of((count, width))] * 3
        + [
            shape_of((2, length, width)), shape_of((1, down_rows, width)), shape_of((parts + 1, up_rows, width)),
            shape_of((3, up_rows, 4 * LANES)),
        ],
        scratch_shapes=[pltpu.VMEM(down_shape, BF16), pltpu.VMEM(up_shape, BF16)]
        + [
            shape
            for which, _, many in back_chunks(down_shape, up_shape)
            for shape in Reduction.scratch(*((1, many) if which == "down" else (many, up_rows)), width)
        ]
        + [pltpu.VMEM((2, 3, 2, 2, 2, up_rows, 2 * LANES), BF16)]
        + Reduction.scratch(3, up_rows, 2 * LANES) * 2
        + [
            pltpu.VMEM((2, count, LANES), BF16),
            pltpu.VMEM((2, 2, count, LANES), BF16),
            pltpu.VMEM((2, count, LANES), BF16),
            pltpu.VMEM((2, 2, count, LANES), BF16),
            pltpu.SemaphoreType.DMA((1,)),
            pltpu.SemaphoreType.DMA((pairs,)),
        ]
        + [pltpu.VMEM((count, width), BF16)] * 4
        + [pltpu.SemaphoreType.DMA((5,))]
        + Trade.semaphores(),
        compiler_params=pltpu.CompilerParams(
            vmem_limit_bytes=VMEM_BYTES, collective_id=0, has_side_effects=True
        ),
        cost_estimate=cost(100),
        name="back",
    )(
        query, grad, context, logsum, *kvs, *kvs, normed, hidden_grad, context, branch, active, *cots,
        first_normed, layer_out
    )


def tail_kernel(
    query_grad, key_grad, value_grad, normed, x0, x1, middle_grad, weight,
    info_ref, gain_ref, feed_ref,
    tokens_out, qkv_out, sums_ref,
    query_v, key_v, value_v, normed_v, x_v, middle_v, weight_v, token_v, last_parts, *refs, total_tokens, parts,
):
    one = Reduction(last_parts, qkv_out, refs[:8])
    sums_in, sums_sends, sums_receives, loads = refs[8:12]
    back = Trade(tokens_out, *refs[12:], parts=TOKEN_PARTS)
    block, width = x0.shape
    d, z, _, _, core = here()
    total, ahead, many = 2 * TOKEN_PARTS, TOKEN_PARTS, block // 2
    top, bottom = pl.ds(0, block), pl.ds(block, block)
    later = ((query_grad, query_v), (key_grad, key_v), (value_grad, value_v), (middle_grad, middle_v))
    copies = [
        pltpu.make_async_copy(source, target, loads.at[number])
        for number, (source, target) in enumerate(
            (
                (weight, weight_v), (x0, x_v.at[0]),
                *((ref.at[top], held.at[top]) for ref, held in later),
                (normed, normed_v), (x1, x_v.at[1]),
                *((ref.at[bottom], held.at[bottom]) for ref, held in later),
            )
        )
    ]
    for copy in copies:
        copy.start()
    meet(("core", "x", "y", "near", "inner"), back)

    def start_block(number):
        p, at = divmod(number * many, block)
        held = pl.ds(number * many, many)
        inner = pl.ds(at, many)
        normed_grad = 0.0
        for part, grads in enumerate((query_v, key_v, value_v)):
            columns = slice(part * width, (part + 1) * width)
            normed_grad = normed_grad + dot(grads[held], weight_v[:, columns], NT)
        unit, scale = norm_parts(x_v[p, inner].astype(F32) + one_row(info_ref, TIME))
        token_grad = middle_v[held] + norm_backward(normed_grad, vector(gain_ref), unit, scale)
        token_v[p, inner] = token_grad.astype(BF16)
        return [
            column_sum(normed_grad * unit),
            column_sum(normed_grad),
            column_sum(query_v[held].astype(F32)),
            column_sum(value_v[held].astype(F32)),
            column_sum(token_grad),
        ]

    def sums_copy(number):
        to = partners()[("core", "x", "y", "near", "inner", "near")[number]]
        return remote(sums_ref, sums_in.at[number], sums_sends, sums_receives, number, number, to)

    def sums_next(number):
        def add_up():
            sums_ref[...] = sums_ref[...] + sums_in[number]

        if number < 3:
            sums_copy(number).wait()
            add_up()
            if number < 2:
                sums_copy(number + 1).start()
            else:
                pl.when(outer())(sums_copy(3).start)
            return

        @pl.when(outer())
        def _():
            if number == 3:
                sums_copy(3).wait_send()
            if number == 5:
                sums_copy(5).wait_recv()
                sums_ref[...] = sums_in[5]

        @pl.when(jnp.logical_not(outer()))
        def _():
            if number == 3:
                sums_copy(3).wait_recv()
                add_up()
                sums_copy(4).start()
            if number == 4:
                sums_copy(4).wait()
                add_up()
                sums_copy(5).start()
            if number == 5:
                sums_copy(5).wait_send()

    def move(number):
        if number >= ahead:
            p, part = divmod(number - ahead, TOKEN_PARTS)
            back.sent(p, token_v.at[p], part)
        p, part = divmod(number, TOKEN_PARTS)
        back.begin(p, token_v.at[p], part)

    for copy in copies[:6]:
        copy.wait()
    sums = start_block(0)
    for number in range(ahead // 2):
        move(number)
    sums = [a + b for a, b in zip(sums, start_block(1))]
    for number in range(ahead // 2, ahead):
        move(number)
    for copy in copies[6:]:
        copy.wait()
    lanes = slice(width - 2 * LANES, width)
    for part, grads in enumerate((query_v, key_v, value_v)):
        made = dot(normed_v[...], grads[:, lanes], TN).astype(BF16)
        last_parts[part] = made.reshape(last_parts.shape[1:])
    one.to_cores()
    sums = [a + b for a, b in zip(sums, start_block(2))]
    one.to_first()
    sums = [a + b for a, b in zip(sums, start_block(3))]
    sums_ref[...] = jnp.zeros_like(sums_ref)
    sums_ref[0:4] = feed_ref[0:4]
    sums_ref[4 : 4 + parts] = feed_ref[8 : 8 + parts]
    for number in range(4):
        sums_ref[4 + parts + number : 5 + parts + number] = sums[number]
    energy = jnp.sum(feed_ref[4:5], keepdims=True) / (width * total_tokens)
    sums_ref[8 + parts : 9 + parts] = info_ref[MARK : MARK + 1] * energy + info_ref[SHARE : SHARE + 1]
    sums_ref[9 + parts : 10 + parts] = info_ref[STEP : STEP + 1] * jnp.where(core == 0, 1.0, 0.0)
    sequence = (d - core + z // 2) * 2 + z % 2
    sums_ref[pl.ds(16 + sequence, 1)] = sums[4]
    sums_copy(0).start()
    for number in range(ahead, ahead + 2):
        move(number)
    sums_next(0)
    one.to_second()
    sums_next(1)
    one.to_near()
    sums_next(2)
    for number in range(ahead + 2, ahead + 4):
        move(number)
    one.to_far()
    sums_next(3)
    for number in range(ahead + 4, ahead + 6):
        move(number)
    one.to_other()
    sums_next(4)
    for number in range(ahead + 6, total):
        move(number)
    one.to_out()
    sums_next(5)
    for number in range(total - ahead, total):
        p, part = divmod(number, TOKEN_PARTS)
        back.sent(p, token_v.at[p], part)
    for number in range(total):
        p, part = divmod(number, TOKEN_PARTS)
        back.arrived(p, token_v.at[p], part)
    one.finish()


def tail(grads, normed, xs, middle_grad, weight, info, gain, feed_sums, total_tokens, hidden_parts):
    block, width = xs[0].shape
    count, total_seqs = 2 * block, 16
    any_spec = fixed_any()
    inside = pl.BlockSpec(memory_space=pltpu.VMEM)
    up_rows = width // 8
    held = lambda *shape, dtype=BF16: pltpu.VMEM(shape, dtype)
    sums_shape = (16 + total_seqs, width)
    return pl.pallas_call(
        functools.partial(tail_kernel, total_tokens=total_tokens, parts=hidden_parts),
        in_specs=[any_spec] * 8 + [inside] * 3,
        out_specs=[any_spec, any_spec, inside],
        out_shape=[
            shape_of((2, block, width)), shape_of((3, up_rows, 2 * LANES)), shape_of(sums_shape, F32),
        ],
        scratch_shapes=[
            held(count, width), held(count, width), held(count, width), held(count, width),
            held(2, block, width), held(count, width, dtype=F32), held(*weight.shape), held(2, block, width),
            held(3, 2, 2, 2, up_rows, 2 * LANES),
        ]
        + Reduction.scratch(3, up_rows, 2 * LANES)
        + [
            held(6, *sums_shape, dtype=F32),
            pltpu.SemaphoreType.DMA((6,)),
            pltpu.SemaphoreType.DMA((6,)),
            pltpu.SemaphoreType.DMA((12,)),
        ]
        + Trade.semaphores(TOKEN_PARTS),
        compiler_params=pltpu.CompilerParams(
            vmem_limit_bytes=VMEM_BYTES, collective_id=1, has_side_effects=True
        ),
        cost_estimate=cost(60),
        name="tail",
    )(*grads, normed, *xs, middle_grad, weight, info, gain, feed_sums)


def finish_kernel(
    token_ref, layer_ref, qkv_ref, last_qkv_ref, up_out_ref, out_part_ref, down_ref, sums_ref,
    token_out, layer_out, qkv_out, up_out, out_out, down_out, table_out, *small_outs, total_seqs, parts, table_rows,
):
    token_out[...] = wide(token_ref)
    layer_out[...] = layer_ref[...]
    qkv_out[...] = jnp.concatenate([qkv_ref[0], last_qkv_ref[0]], 1).astype(F32)
    up_out[...] = up_out_ref[0].astype(F32)
    out_out[...] = out_part_ref[0].astype(F32)
    down_out[...] = wide(down_ref)
    block, width = table_out.shape
    steps_row = 9 + parts
    first = lax.axis_index("dp") * table_rows + pl.program_id(0) * block
    place = (lax.broadcasted_iota(jnp.int32, (block, 1), 0) + first).astype(F32)
    total = jnp.zeros_like(table_out)
    for s in range(total_seqs):
        chosen = place == sums_ref[steps_row : steps_row + 1, s : s + 1]
        total = total + jnp.where(chosen, sums_ref[16 + s : 17 + s], 0.0)
    table_out[...] = total

    @pl.when(pl.program_id(0) == 0)
    def _():
        d = lax.axis_index("dp")
        piece = small_outs[0].shape[0]
        turned = pltpu.roll(sums_ref[0:16], lax.rem(width - d * piece, width), 1)
        order = [row for row in range(8 + parts) if not 4 <= row < 4 + parts]
        for row, out in zip(order, small_outs):
            out[...] = turned[row, :piece]
        up_piece = small_outs[8].shape[0]
        share = width // up_piece
        mine = sums_ref[pl.ds(4 + d // share, 1)]
        mine = pltpu.roll(mine, lax.rem(width - d % share * up_piece, width), 1)
        small_outs[8][...] = mine[0, :up_piece]
        small_outs[9][...] = sums_ref[8 + parts, :BUCKETS]
        small_outs[10][...] = sums_ref[8 + parts, BUCKETS : 2 * BUCKETS]


def finish(token, layer, qkv, last_qkv, up_out, down, sums, table_rows, dp):
    seqs, length, width = token.shape
    parts, block = up_out.shape[0] - 1, up_out.shape[1]
    steps = parts
    small = [width // dp] * 8 + [parts * width // dp] + [BUCKETS] * 2
    rows_at = lambda many: pl.BlockSpec((many // steps, width), lambda i: (i, 0))
    count = seqs * length
    wide_rows = rows_at(count)
    made = pl.pallas_call(
        functools.partial(
            finish_kernel, total_seqs=sums.shape[0] - 16, parts=parts, table_rows=table_rows
        ),
        grid=(steps,),
        in_specs=[
            wide_rows, wide_rows,
            pl.BlockSpec((1, block, qkv.shape[2]), lambda i: (jnp.minimum(i, 2), 0, 0)),
            pl.BlockSpec((1, block, last_qkv.shape[2]), lambda i: (jnp.minimum(i, 2), 0, 0)),
            pl.BlockSpec((1, block, width), lambda i: (i, 0, 0)),
            pl.BlockSpec((1, block, width), lambda i: (parts, 0, 0)),
            rows_at(down.shape[0]),
            fixed(sums.shape),
        ],
        out_specs=[
            wide_rows, wide_rows,
            pl.BlockSpec((block, width), lambda i: (0, jnp.minimum(i, 2))),
            pl.BlockSpec((block, width), lambda i: (0, i)),
            pl.BlockSpec((block, width), lambda i: (0, 0)),
            rows_at(down.shape[0]), rows_at(table_rows),
        ]
        + [pl.BlockSpec((many,), lambda i: (0,)) for many in small],
        out_shape=[
            shape_of((count, width), F32), shape_of((count, width)), shape_of((block, 3 * width), F32),
            shape_of((block, parts * width), F32), shape_of((block, width), F32), shape_of(down.shape, F32),
            shape_of((table_rows, width), F32),
        ]
        + [shape_of((many,), F32) for many in small],
        compiler_params=params(),
        cost_estimate=cost(6),
        name="finish",
    )(token.reshape(count, width), layer.reshape(count, width), qkv, last_qkv, up_out, up_out, down, sums)
    shape = (seqs, length, width)
    return [made[0].reshape(shape), made[1].reshape(shape)] + list(made[2:])


def gelu_parts(hidden):
    share = 0.5 + 0.5 * lax.erf(hidden * 2**-0.5)
    bell = jnp.exp(-0.5 * hidden * hidden) * 0.3989422804014327
    return hidden * share, share + hidden * bell


def feed_kernel(
    context_ref, x0_ref, x1_ref, info_ref, cot0_ref, cot1_ref, out_weight_ref, up_ref, down_ref,
    out_bias_ref, gain_ref, shift_ref, down_bias_ref, up_bias_ref,
    out_ref, active_ref, hidden_grad_ref, normed_ref, middle_grad_ref, branch_ref, context_grad_ref, sums_ref,
    out_weight_v, up_v, down_v, loads,
):
    step = pl.program_id(0)
    width, hidden_width = x0_ref.shape[1], up_ref.shape[1]

    parts = hidden_width // width
    out_copy = pltpu.make_async_copy(out_weight_ref, out_weight_v, loads.at[0, parts])
    copies = []
    for part in range(parts):
        columns = pl.ds(part * width, width)
        copies.append(
            (
                pltpu.make_async_copy(up_ref.at[:, columns], up_v.at[:, columns], loads.at[0, part]),
                pltpu.make_async_copy(down_ref.at[columns], down_v.at[columns], loads.at[1, part]),
            )
        )

    @pl.when(step == 0)
    def _():
        out_copy.start()
        for one, two in copies:
            one.start()
            two.start()
        sums_ref[...] = jnp.zeros_like(sums_ref)
        out_copy.wait()

    x = jnp.where(step == 0, x0_ref[...], x1_ref[...])
    cot = jnp.where(step == 0, cot0_ref[...], cot1_ref[...])
    middle = (
        x.astype(F32)
        + one_row(info_ref, TIME)
        + dot(context_ref[...], out_weight_v[...], NN)
        + vector(out_bias_ref)
    )
    unit, scale = norm_parts(middle)
    gain = vector(gain_ref)
    normed = (unit * gain + vector(shift_ref)).astype(BF16)
    normed_ref[...] = normed
    out = middle + vector(down_bias_ref)
    normed_grad = jnp.zeros_like(out)
    up_bias = vector(up_bias_ref)
    for part in range(parts):
        columns = slice(part * width, (part + 1) * width)

        @pl.when(step == 0)
        def _():
            for copy in copies[part]:
                copy.wait()

        hidden = dot(normed, up_v[:, columns], NN) + up_bias[:, columns]
        active, slope = gelu_parts(hidden)
        active = active.astype(BF16)
        active_ref[:, columns] = active
        out = out + dot(active, down_v[columns, :], NN)
        hidden_grad = (dot(cot, down_v[columns, :], NT) * slope).astype(BF16)
        hidden_grad_ref[:, columns] = hidden_grad
        sums_ref[8 + part : 9 + part] += column_sum(hidden_grad.astype(F32))
        normed_grad = normed_grad + dot(hidden_grad, up_v[:, columns], NT)
    out_ref[...] = out.astype(BF16)
    cot = cot.astype(F32)
    middle_grad = cot + norm_backward(normed_grad, gain, unit, scale)
    middle_grad_ref[...] = middle_grad
    branch = middle_grad.astype(BF16)
    branch_ref[...] = branch
    context_grad_ref[...] = dot(branch, out_weight_v[...], NT).astype(BF16)
    sums_ref[0:1] += column_sum(cot)
    sums_ref[1:2] += column_sum(normed_grad * unit)
    sums_ref[2:3] += column_sum(normed_grad)
    sums_ref[3:4] += column_sum(branch.astype(F32))
    sums_ref[4:5] += column_sum(out * out)


def feed(context, xs, info, small, cots, out_weight, up, down):
    block, width = xs[0].shape
    count, hidden_width = 2 * block, up.shape[1]
    sums_rows = 8 + hidden_width // width + (-(hidden_width // width)) % 8
    whole = fixed((block, width))
    return pl.pallas_call(
        feed_kernel,
        grid=(2,),
        in_specs=[
            rows(block, width), whole, whole, fixed(info.shape), whole, whole,
        ]
        + [pl.BlockSpec(memory_space=pl.ANY)] * 3
        + [whole_vector(v) for v in small],
        out_specs=[
            rows(block, width), rows(block, hidden_width), rows(block, hidden_width), rows(block, width),
            rows(block, width), rows(block, width), rows(block, width),
            pl.BlockSpec((sums_rows, width), lambda i: (0, 0)),
        ],
        out_shape=[
            shape_of((count, width)), shape_of((count, hidden_width)), shape_of((count, hidden_width)),
            shape_of((count, width)), shape_of((count, width), F32), shape_of((count, width)),
            shape_of((count, width)), shape_of((sums_rows, width), F32),
        ],
        scratch_shapes=[
            pltpu.VMEM(out_weight.shape, BF16), pltpu.VMEM(up.shape, BF16), pltpu.VMEM(down.shape, BF16),
            pltpu.SemaphoreType.DMA((2, hidden_width // width + 1)),
        ],
        compiler_params=params(),
        cost_estimate=cost(34),
        name="feed",
    )(context, *xs, info, *cots, out_weight, up, down, *small)


def down_grad_kernel(active_ref, cot0_ref, cot1_ref, out_ref):
    block = cot0_ref.shape[0]
    out_ref[...] = (
        dot(active_ref[:block], cot0_ref[...], TN) + dot(active_ref[block:], cot1_ref[...], TN)
    ).astype(BF16)


def down_grad(active, cots):
    block, width = cots[0].shape
    count, hidden_width = active.shape
    return pl.pallas_call(
        down_grad_kernel,
        grid=(hidden_width // width,),
        in_specs=[pl.BlockSpec((count, width), lambda i: (0, i))] + [fixed((block, width))] * 2,
        out_specs=rows(width, width),
        out_shape=shape_of((hidden_width, width)),
        compiler_params=params(),
        cost_estimate=cost(8),
        name="down_grad",
    )(active, *cots)


def up_out_grad_kernel(normed_ref, hidden_grad_ref, context_ref, branch_ref, out_ref):
    last = pl.num_programs(0) - 1

    @pl.when(pl.program_id(0) < last)
    def _():
        out_ref[0] = dot(normed_ref[...], hidden_grad_ref[...], TN).astype(BF16)

    @pl.when(pl.program_id(0) == last)
    def _():
        out_ref[0] = dot(context_ref[...], branch_ref[...], TN).astype(BF16)


def up_out_grad(normed, hidden_grad, context, branch):
    count, width = normed.shape
    parts = hidden_grad.shape[1] // width
    whole = fixed((count, width))
    return pl.pallas_call(
        up_out_grad_kernel,
        grid=(parts + 1,),
        in_specs=[
            whole,
            pl.BlockSpec((count, width), lambda i: (0, jnp.minimum(i, parts - 1))),
            whole,
            whole,
        ],
        out_specs=pl.BlockSpec((1, width, width), lambda i: (i, 0, 0)),
        out_shape=shape_of((parts + 1, width, width)),
        compiler_params=params(),
        cost_estimate=cost(10),
        name="up_out_grad",
    )(normed, hidden_grad, context, branch)


def qkv_grad_kernel(normed_ref, grad_ref, out_ref):
    out_ref[0] = dot(normed_ref[...], grad_ref[...], TN).astype(BF16)


def qkv_grad(normed, grads):
    count, width = normed.shape
    parts = grads.shape[1] // width
    return pl.pallas_call(
        qkv_grad_kernel,
        grid=(parts,),
        in_specs=[fixed((count, width)), pl.BlockSpec((count, width), lambda i: (0, i))],
        out_specs=pl.BlockSpec((1, width, width), lambda i: (i, 0, 0)),
        out_shape=shape_of((parts, width, width)),
        compiler_params=params(),
        cost_estimate=cost(7),
        name="qkv_grad",
    )(normed, grads)


def start_kernel(
    query_grad_ref, key0_ref, key1_ref, far_key0_ref, far_key1_ref, value0_ref, value1_ref, far_value0_ref,
    far_value1_ref, x0_ref, x1_ref, info_ref, middle_grad_ref, gain_ref, weight_ref,
    token0_ref, token1_ref, grads_ref, sums_ref,
):
    step = pl.program_id(0)
    width = x0_ref.shape[1]

    @pl.when(step == 0)
    def _():
        sums_ref[...] = jnp.zeros_like(sums_ref)

    def pick(first, second):
        return jnp.where(step == 0, first[...], second[...])

    query_grad = query_grad_ref[...]
    key_grad = (pick(key0_ref, key1_ref).astype(F32) + pick(far_key0_ref, far_key1_ref).astype(F32)).astype(BF16)
    value_grad = (
        pick(value0_ref, value1_ref).astype(F32) + pick(far_value0_ref, far_value1_ref).astype(F32)
    ).astype(BF16)
    normed_grad = 0.0
    for part, grad in enumerate((query_grad, key_grad, value_grad)):
        columns = slice(part * width, (part + 1) * width)
        grads_ref[:, columns] = grad
        normed_grad = normed_grad + dot(grad, weight_ref[:, columns], NT)
    unit, scale = norm_parts(pick(x0_ref, x1_ref).astype(F32) + one_row(info_ref, TIME))
    token_grad = middle_grad_ref[...] + norm_backward(normed_grad, vector(gain_ref), unit, scale)

    @pl.when(step == 0)
    def _():
        token0_ref[...] = token_grad.astype(BF16)

    @pl.when(step == 1)
    def _():
        token1_ref[...] = token_grad.astype(BF16)

    sums_ref[0:1] += column_sum(normed_grad * unit)
    sums_ref[1:2] += column_sum(normed_grad)
    sums_ref[2:3] += column_sum(query_grad.astype(F32))
    sums_ref[3:4] += column_sum(value_grad.astype(F32))
    sums_ref[4:5] += column_sum(token_grad)


def start_back(query_grad, key_grads, value_grads, xs, info, middle_grad, gain, weight):
    block, width = xs[0].shape
    count = 2 * block
    whole = fixed((block, width))
    kept = pl.BlockSpec((block, width), lambda i: (0, 0))
    return pl.pallas_call(
        start_kernel,
        grid=(2,),
        in_specs=[rows(block, width)]
        + [whole] * 10
        + [fixed(info.shape), rows(block, width), whole_vector(gain), fixed(weight.shape)],
        out_specs=[kept, kept, rows(block, 3 * width), pl.BlockSpec((8, width), lambda i: (0, 0))],
        out_shape=[
            shape_of((block, width)), shape_of((block, width)), shape_of((count, 3 * width)),
            shape_of((8, width), F32),
        ],
        compiler_params=params(),
        cost_estimate=cost(10),
        name="start_back",
    )(query_grad, *key_grads, *value_grads, *xs, info, middle_grad, gain, weight)


class Places:
    def __init__(self, dp, seq):
        self.dp, self.seq = dp, seq
        self.bits = dp.bit_length() - 1

    def flat(self, d, z):
        return d * self.seq + z

    def pairs(self, to):
        return [
            (self.flat(d, z), self.flat(*to(d, z))) for d in range(self.dp) for z in range(self.seq)
        ]

    def gather_order(self, turn):
        def to(d, z):
            core, j = d % 2, (z + turn) % 2
            return d - core + z // 2, 2 * core + j

        return self.pairs(to)

    def scatter_order(self, turn):
        return [(b, a) for a, b in self.gather_order(turn)]

    def swap(self, bit):
        return self.pairs(lambda d, z: (d ^ (1 << bit), z))

    def swap_seq(self, step):
        return self.pairs(lambda d, z: (d, z ^ step))


def send(x, order):
    return lax.ppermute(x, BOTH, order)


def add(a, b):
    return (a.astype(F32) + b.astype(F32)).astype(BF16)


def reduce_parts(parts, places):
    d, z = lax.axis_index("dp"), lax.axis_index("seq")
    count, height, width = parts.shape
    block = height // places.dp
    grid = parts.reshape((count,) + (2,) * places.bits + (block, width))

    def halve(value, bit, axes):
        axis = 1 + axes.index(bit)
        mine = (d >> bit) & 1
        kept = lax.dynamic_index_in_dim(value, mine, axis, keepdims=False)
        sent = lax.dynamic_index_in_dim(value, 1 - mine, axis, keepdims=False)
        axes.remove(bit)
        return add(kept, send(sent, places.swap(bit)))

    axes = list(range(places.bits - 1, -1, -1))
    grid = halve(grid, 0, axes)
    halves = []
    for number, order in enumerate((range(1, places.bits), range(places.bits - 1, 0, -1))):
        at = block // 2
        value = lax.slice_in_dim(grid, number * at, (number + 1) * at, axis=grid.ndim - 2)
        left = list(axes)
        for bit in order:
            value = halve(value, bit, left)
        halves.append(sum_along_seq(value, z, places))
    return jnp.concatenate(halves, 1)


def sum_along_seq(value, z, places):
    count, block, width = value.shape
    mine = z % 2
    grid = value.reshape(count, block, 2, width // 2)
    kept = lax.dynamic_index_in_dim(grid, mine, 2, keepdims=False)
    sent = lax.dynamic_index_in_dim(grid, 1 - mine, 2, keepdims=False)
    half = add(kept, send(sent, places.swap_seq(1)))
    half = add(half, send(half, places.swap_seq(2)))
    other = send(half, places.swap_seq(1))
    first = jnp.where(mine == 0, half, other)
    second = jnp.where(mine == 0, other, half)
    return jnp.concatenate([first, second], 2).astype(F32)


def sum_everywhere(value, places):
    for bit in range(places.bits):
        value = value + send(value, places.swap(bit))
    for step in (1, 2):
        value = value + send(value, places.swap_seq(step))
    return value


def per_device(
    tokens, timesteps, time_table, ln1_gain, ln1_bias, qkv_weight, q_bias, v_bias, out_weight, out_bias,
    ln2_gain, ln2_bias, up_weight, up_bias, down_weight, down_bias, cotangent,
):
    places = Places(lax.axis_size("dp"), lax.axis_size("seq"))
    seq_count, local_len, width = tokens.shape
    hidden_width = up_weight.shape[1]
    assert places.seq == 4 and seq_count == 2 and places.dp == 1 << places.bits
    d, z = lax.axis_index("dp"), lax.axis_index("seq")
    core = d % 2
    total_seqs = seq_count * places.dp
    total_tokens = total_seqs * local_len * places.seq

    def gathered(array):
        blocks = []
        for turn in range(2):
            mine = lax.dynamic_index_in_dim(array, (z + turn) % 2, 0, keepdims=False)
            blocks.append(send(mine, places.gather_order(turn)))
        return blocks

    count = 2 * local_len
    parts = hidden_width // width
    first_small = (ln1_gain, ln1_bias, q_bias, v_bias)
    second_small = (out_bias, ln2_gain, ln2_bias, down_bias, up_bias)
    sequence = (d - core + z // 2) * seq_count + z % 2
    if places.dp == 8:
        made = front(tokens, qkv_weight, time_table, timesteps, first_small, count / total_tokens)
        xs, (normed, query), kvs, info = made[:2], made[2:4], list(made[4:8]), made[8]
        cotangent, query = lax.optimization_barrier((cotangent, query))
        cots = gathered(cotangent)
    else:
        info = jnp.concatenate(
            [
                known_rows(
                    timesteps[j], seq_count * d + j, count / total_tokens,
                    lax.dynamic_slice_in_dim(time_table, timesteps[j], 1, 0).astype(F32),
                )
                for j in range(2)
            ]
        )
        far_info = send(info, places.swap(0))
        xs = gathered(tokens)
        cots = gathered(cotangent)
        info = jnp.where(z // 2 == core, info, far_info)
        info = jnp.pad(jnp.where(z % 2 == 0, info[:4], info[4:]), ((0, 4), (0, 0)))
        normed, query, kv0 = project(xs[0], info, first_small, qkv_weight, count)
        far0 = send(kv0, places.swap(0))
        normed, query, kv1 = project(xs[1], info, first_small, qkv_weight, count, (normed, query))
        kvs = [kv0, kv1, far0, send(kv1, places.swap(0))]
    context, logsum = attend(query, kvs)
    out, active, hidden_grad, normed_two, middle_grad, branch, context_grad, feed_sums = feed(
        context, xs, info, second_small, cots, out_weight, up_weight, down_weight
    )

    def scattered(blocks, dtype):
        back = [send(block, places.scatter_order(turn)) for turn, block in enumerate(blocks)]
        even = z % 2 == 0
        return jnp.stack(
            [jnp.where(even, back[0], back[1]), jnp.where(even, back[1], back[0])]
        ).astype(dtype)


    if places.dp == 8:
        made = back(
            query, context_grad, context, logsum, kvs, normed_two, hidden_grad, branch, active, cots,
            normed, out
        )
        tokens_grad, last_qkv, packed = tail(
            made[:3], normed, xs, middle_grad, qkv_weight, info, ln1_gain, feed_sums, total_tokens, parts
        )
        tokens_grad, layer_out, qkv_sum, up_sum, out_sum, down_sum, table_grad, *small = finish(
            tokens_grad, made[3], made[6], last_qkv, made[5], made[4][0], packed,
            time_table.shape[0] // places.dp, places.dp,
        )
    else:
        layer_out = scattered([out[:local_len], out[local_len:]], BF16)
        down_sum = reduce_parts(down_grad(active, cots)[None], places)[0]
        up_out_sum = reduce_parts(up_out_grad(normed_two, hidden_grad, context, branch), places)
        made = attend_back(query, context_grad, context, logsum, kvs)
        token0, token1, projected_grad, start_sums = start_back(
            made[0],
            list(made[1:3]) + [send(g, places.swap(0)) for g in made[3:5]],
            list(made[5:7]) + [send(g, places.swap(0)) for g in made[7:9]],
            xs, info, middle_grad, ln1_gain, qkv_weight,
        )
        tokens_grad = scattered([token0, token1], F32)
        qkv_sum = reduce_parts(qkv_grad(normed, projected_grad), places)
        energy = jnp.sum(feed_sums[4]) / (width * total_tokens)
        sequence_rows = jnp.where(jnp.arange(total_seqs)[:, None] == sequence, start_sums[4][None], 0.0)
        packed = jnp.concatenate(
            [
                feed_sums[0:4], feed_sums[8 : 8 + parts], start_sums[0:4],
                jnp.stack(
                    [info[MARK] * energy + info[SHARE], info[STEP] * jnp.where(core == 0, 1.0, 0.0)]
                ),
                sequence_rows,
            ]
        )
        packed = sum_everywhere(packed, places)
        steps = packed[9 + parts, :total_seqs].astype(jnp.int32)
        table_rows = time_table.shape[0] // places.dp
        chosen = (steps[None, :] == (jnp.arange(table_rows) + d * table_rows)[:, None]).astype(F32)
        table_grad = jnp.dot(chosen, packed[10 + parts :], precision=lax.Precision.HIGHEST)

        def side_by_side(stacked):
            return jnp.moveaxis(stacked, 0, 1).reshape(stacked.shape[1], -1)

        qkv_sum, out_sum = side_by_side(qkv_sum), up_out_sum[parts]
        up_sum = side_by_side(up_out_sum[:parts])
        piece = width // places.dp
        mine = lax.dynamic_slice_in_dim(packed[: 8 + parts], d * piece, piece, 1)
        up_piece = hidden_width // places.dp
        up_bias_sum = lax.dynamic_slice_in_dim(packed[4 : 4 + parts].reshape(-1), d * up_piece, up_piece, 0)
        stats = packed[8 + parts]
        small = [mine[row] for row in (0, 1, 2, 3, 4 + parts, 5 + parts, 6 + parts, 7 + parts)]
        small += [up_bias_sum, stats[:BUCKETS], stats[BUCKETS : 2 * BUCKETS]]
    down_bias_sum, gain_two, shift_two, out_bias_sum, gain_one, shift_one, q_sum, v_sum = small[:8]
    return (
        layer_out, tokens_grad, table_grad, gain_one, shift_one, qkv_sum, q_sum, v_sum, out_sum, out_bias_sum,
        gain_two, shift_two, up_sum, small[8], down_sum, down_bias_sum, small[9], small[10],
    )


def solution(mesh):
    split = P("dp", "seq", None)
    return jax.shard_map(
        per_device,
        mesh=mesh,
        in_specs=(split, P("dp")) + (P(),) * 14 + (split,),
        out_specs=(
            split, split, P("dp", None), P("dp"), P("dp"), P("dp", None), P("dp"), P("dp"), P("dp", None),
            P("dp"), P("dp"), P("dp"), P("dp", None), P("dp"), P("dp", None), P("dp"), P(), P(),
        ),
        check_vma=False,
    )
```
